32 devices in a mesh: ctx: 8 (over y, x, core), head: 4 (over z).
Axes of the slice: x: 2, y: 2, z: 4, core: 2. Of those that a mesh axis runs over, the one named last changes fastest.
Arguments:
- queries: bfloat16 [1024, 1024], P('ctx', 'head'), may hold values from -6 to 6
- key_vectors: bfloat16 [1024, 1024], P('ctx', 'head'), may hold values from -6 to 6
- value_rows: bfloat16 [1024, 2048], P('ctx', 'head'), may hold values from -6 to 6
- write_rate: float32 [16, 1024], P('head', 'ctx'), may hold values from 0.0078125 to 1
- log_decay: float32 [16, 1024], P('head', 'ctx'), may hold values from -0.9 to 0
- doc_offsets: int32 [5], replicated, may hold values from 0 to 1024, as said below
- out_weight: bfloat16 [2048, 2048], P('head'), may hold values from -0.125 to 0.125
- grad_out: bfloat16 [1024, 2048], P(('ctx', 'head')), may hold values from -6 to 6
Outputs:
- layer_out: float32 [1024, 2048], P(('ctx', 'head'))
- grad_q: float32 [1024, 1024], P('ctx', 'head')
- grad_k: float32 [1024, 1024], P('ctx', 'head')
- grad_v: float32 [1024, 2048], P('ctx', 'head')
- grad_rate: float32 [16, 1024], P('head', 'ctx')
- grad_decay: float32 [16, 1024], P('head', 'ctx')
- weight_grad: float32 [2048, 2048], P('ctx', 'head')
The draws below stay inside these ranges and needn't reach their ends.
Inputs may be any that keep to these rules, and one draw needn't show every extreme that they name: `doc_offsets`: Increasing; the first entry is 0 and the last is 1024.
All inputs are finite; a program needn't handle non-finite values.
Results may differ from the reference program's by a relative error of at most 0.0029.
Values may be sent and summed in bfloat16 or wider, within the bound.
No kernel may reach another device: no remote copies, remote signals or barrier semaphores. Data moves between devices by JAX's collectives and lax.ppermute only.
A program may use at most 64 MiB of HBM per device.

```python
import jax
import jax.numpy as jnp
from jax import lax

D = 2048
VHEADS = 16
KHEADS = 8
DK = 128
DV = 128
STRETCH = 64
DOCS = 4
TOKEN_TOTAL = 1024


def draw_write_rate(key, part):
    head_key, token_random_key = jax.random.split(key)
    lowest = DK / (4.0 * TOKEN_TOTAL)
    head_scale = jnp.exp(jax.random.uniform(head_key, (VHEADS, 1), jnp.float32, jnp.log(lowest), 0.0))
    factor = jax.random.uniform(token_random_key, (VHEADS, TOKEN_TOTAL), jnp.float32, 0.5, 1.0)
    return (head_scale * factor).astype(jnp.float32)


def draw_log_decay(key, part):
    rate_random_key, token_random_key, spurt_random_key, levels_random_key = jax.random.split(key, 4)
    slowest = 0.1 / TOKEN_TOTAL
    per_head_rate = jnp.exp(jax.random.uniform(rate_random_key, (VHEADS, 1), jnp.float32, jnp.log(slowest), jnp.log(0.06)))
    random_wobble = jax.random.uniform(token_random_key, (VHEADS, TOKEN_TOTAL), jnp.float32, 0.5, 1.5)
    spurt_groups = jax.random.uniform(spurt_random_key, (1, TOKEN_TOTAL), jnp.float32) < 6.0 / TOKEN_TOTAL
    layer_levels = jnp.log(jax.random.uniform(levels_random_key, (VHEADS, TOKEN_TOTAL), jnp.float32, 0.5, 0.8))
    return (-per_head_rate * random_wobble + jnp.where(spurt_groups, layer_levels, 0.0)).astype(jnp.float32)


def draw_doc_offsets(key, part):
    shuffled = jax.random.permutation(key, TOKEN_TOTAL - 1)[:DOCS - 1] + 1
    inner = jnp.sort(shuffled.astype(jnp.int32))
    return jnp.concatenate([jnp.zeros((1,), jnp.int32), inner, jnp.full((1,), TOKEN_TOTAL, jnp.int32)]).astype(jnp.int32)


def with_spikes(drawn, rng, source, target, parts, factor):
    owner, partner = [(jnp.arange(drawn.shape[axis_at]) // (drawn.shape[axis_at] // parts)).reshape([-1 if axis == axis_at else 1 for axis in range(drawn.ndim)]) for axis_at in (source, target)]
    chosen = jax.random.permutation(rng, parts)[partner]
    strong = (owner == chosen) | (owner == (partner + parts // 2) % parts)
    return jnp.where(strong, factor * drawn, drawn)


def levels(key, shape, cuts, least, largest):
    def one(position, shards_of):
        draws = jax.random.uniform(jax.random.fold_in(jax.random.fold_in(key, 6), position), (shards_of,), jnp.float32, least / len(cuts), largest / len(cuts))
        return jnp.repeat(jnp.exp(draws), shape[position] // shards_of).reshape((-1,) + (1,) * (len(shape) - position - 1))

    gain = one(*cuts[0])
    for cut in cuts[1:]:
        gain = gain * one(*cut)
    return gain


def noise(key, shape, deviation, most, cuts=(), kind=jnp.bfloat16):
    level = levels(key, shape, cuts, -0.22, 0.18) if cuts else 1.0
    values = jax.random.normal(key, shape, jnp.float32) * deviation * level
    return jnp.minimum(jnp.maximum(values, -most), most).astype(kind)


def gaussian_with(stream_key, shape, scale, bound, cuts, heavy, kind=jnp.bfloat16):
    entries = scale * jax.random.normal(stream_key, shape, jnp.float32)
    if cuts:
        entries = entries * levels(stream_key, shape, cuts, -0.22, 0.18)
    return jnp.clip(with_spikes(entries, jax.random.fold_in(stream_key, 3), *heavy), -bound, bound).astype(kind)


def setup_inputs(seed: int = 0) -> dict:
    streams_of = jax.random.split(jax.random.key(seed), 9)
    queries = noise(streams_of[0], (TOKEN_TOTAL, KHEADS * DK), 1.0, 6.0, ((0, 8), (1, 4)))
    key_vectors = noise(streams_of[1], (TOKEN_TOTAL, KHEADS * DK), 1.0, 6.0, ((0, 8), (1, 4)))
    value_rows = noise(streams_of[2], (TOKEN_TOTAL, VHEADS * DV), 1.0, 6.0, ((0, 8), (1, 4)))
    write_rate = draw_write_rate(jax.random.fold_in(streams_of[8], 71), 0)
    log_decay = draw_log_decay(jax.random.fold_in(streams_of[8], 71), 0)
    doc_offsets = draw_doc_offsets(jax.random.fold_in(streams_of[8], 71), 0)
    out_weight = noise(streams_of[6], (VHEADS * DV, D), (VHEADS * DV) ** -0.5, 0.125, ((0, 4),))
    grad_out = gaussian_with(streams_of[7], (TOKEN_TOTAL, D), 1.0, 6.0, ((0, 32),), (0, 1, 32, 2.75))
    return dict(queries=queries, key_vectors=key_vectors, value_rows=value_rows, write_rate=write_rate, log_decay=log_decay, doc_offsets=doc_offsets, out_weight=out_weight, grad_out=grad_out)


full_precision = lax.Precision.HIGHEST

def tri_inverse(strict_lower):
    order_size = strict_lower.shape[-1]
    identity = jnp.eye(order_size, dtype=strict_lower.dtype)
    powers = -strict_lower
    result = identity + powers
    reach_span = 2
    while reach_span < order_size:
        powers = jnp.einsum('hij,hjk->hik', powers, powers, precision=full_precision)
        result = jnp.einsum('hij,hjk->hik', result, identity + powers, precision=full_precision)
        reach_span = reach_span * 2
    return result

def block_step(state, inputs):
    query_blk, key_blk, value_blk, rate_blk, decay_blk, reset_blk = inputs
    dtype_f = decay_blk.dtype
    cumul = jnp.cumsum(decay_blk, axis=-1)
    segment = jnp.cumsum(reset_blk)
    block_len = reset_blk.shape[0]
    row_ids = lax.broadcasted_iota(jnp.int32, (block_len, block_len), 0)
    col_ids = lax.broadcasted_iota(jnp.int32, (block_len, block_len), 1)
    same_seg = segment[:, None] == segment[None, :]
    together = same_seg & (row_ids >= col_ids)
    strict = same_seg & (row_ids > col_ids)
    gaps = cumul[:, :, None] - cumul[:, None, :]
    ratio = jnp.exp(jnp.where(together, gaps, 0.0)) * together.astype(dtype_f)
    from_start = jnp.exp(cumul) * (segment == 0).astype(dtype_f)
    to_end = jnp.exp(cumul[:, -1:] - cumul) * (segment == segment[-1]).astype(dtype_f)
    whole_decay = jnp.exp(cumul[:, -1]) * (segment[-1] == 0).astype(dtype_f)
    key_dots = jnp.einsum('hik,hjk->hij', key_blk, key_blk, precision=full_precision)
    coupling = rate_blk[:, :, None] * key_dots * ratio * strict.astype(dtype_f)
    inverse = tri_inverse(coupling)
    right_side = jnp.concatenate([rate_blk[:, :, None] * value_blk, (rate_blk * from_start)[:, :, None] * key_blk], axis=-1)
    solved = jnp.einsum('hij,hjw->hiw', inverse, right_side, precision=full_precision)
    value_width = value_blk.shape[-1]
    pseudo = solved[..., :value_width] - jnp.einsum('hck,hvk->hcv', solved[..., value_width:], state, precision=full_precision)
    scores = jnp.einsum('hik,hjk->hij', query_blk, key_blk, precision=full_precision) * ratio
    outputs = from_start[:, :, None] * jnp.einsum('hck,hvk->hcv', query_blk, state, precision=full_precision)
    outputs = outputs + jnp.einsum('hij,hjv->hiv', scores, pseudo, precision=full_precision)
    new_state = whole_decay[:, None, None] * state + jnp.einsum('hcv,hck->hvk', pseudo, to_end[:, :, None] * key_blk, precision=full_precision)
    return (new_state, outputs)

def run_blocks(state, query_heads, key_heads, value_heads, rates, decays, resets, block_size):
    head_count, length = rates.shape
    blocks = length // block_size

    def split_rows(tensor):
        return jnp.moveaxis(tensor.reshape(head_count, blocks, block_size, tensor.shape[-1]), 1, 0)
    stacked = (split_rows(query_heads), split_rows(key_heads), split_rows(value_heads), jnp.moveaxis(rates.reshape(head_count, blocks, block_size), 1, 0), jnp.moveaxis(decays.reshape(head_count, blocks, block_size), 1, 0), resets.reshape(blocks, block_size))
    final_state, outputs = lax.scan(jax.checkpoint(block_step), state, stacked)
    outputs = jnp.moveaxis(outputs, 0, 1).reshape(head_count, length, outputs.shape[-1])
    return (final_state, outputs)

def to_heads(query_f, key_f, value_f):
    length = query_f.shape[0]

    def heads_first(tensor, width):
        return jnp.transpose(tensor.reshape(length, tensor.shape[1] // width, width), (1, 0, 2))

    def unit_rows(tensor):
        return tensor / jnp.sqrt(lax.optimization_barrier(jnp.sum(tensor * tensor, axis=-1, keepdims=True)) + 1e-06)
    value_heads = heads_first(value_f, DV)
    repeat_by = value_heads.shape[0] // (key_f.shape[1] // DK)
    query_heads = jnp.repeat(unit_rows(heads_first(query_f, DK)), repeat_by, axis=0)
    key_heads = jnp.repeat(unit_rows(heads_first(key_f, DK)), repeat_by, axis=0)
    return (query_heads, key_heads, value_heads)

def reference(queries, key_vectors, value_rows, write_rate, log_decay, doc_offsets, out_weight, grad_out):
    positions = jnp.arange(TOKEN_TOTAL, dtype=jnp.int32)
    resets = jnp.any(positions[:, None] == doc_offsets[None, :DOCS].astype(jnp.int32), axis=1).astype(jnp.int32)

    def core(query_f, key_f, value_f, rates, decays):
        query_heads, key_heads, value_heads = to_heads(query_f, key_f, value_f)
        head_count = value_heads.shape[0]
        start_state = jnp.zeros((head_count, DV, DK), dtype=value_f.dtype)
        final_state, outputs = run_blocks(start_state, query_heads, key_heads, value_heads, rates, decays, resets, STRETCH)
        return jnp.transpose(outputs, (1, 0, 2)).reshape(query_f.shape[0], head_count * DV)
    core_out, core_vjp = jax.vjp(core, queries.astype(jnp.float32), key_vectors.astype(jnp.float32), value_rows.astype(jnp.float32), write_rate, log_decay)
    mixed_in = core_out.astype(jnp.bfloat16)
    layer_out = jnp.dot(mixed_in, out_weight, preferred_element_type=jnp.float32)
    d_core = jnp.dot(grad_out, out_weight.T, preferred_element_type=jnp.float32)
    weight_grad = jnp.dot(grad_out.T, mixed_in, preferred_element_type=jnp.float32)
    grad_q, grad_k, grad_v, grad_rate, grad_decay = core_vjp(d_core)
    return (layer_out, grad_q, grad_k, grad_v, grad_rate, grad_decay, weight_grad)
```

```python
from functools import partial

import jax
import jax.numpy as jnp
from jax import lax
from jax.experimental import pallas as pl
from jax.experimental.pallas import tpu as pltpu
from jax.sharding import PartitionSpec as P

DK = 128
DV = 128
AUX = 16
EPS = 1e-06
F32 = jnp.float32
BF16 = jnp.bfloat16
VMEM_LIMIT = 56 * 1024 * 1024


def dot(a, b, ca, cb):
    return lax.dot_general(a, b, (((ca,), (cb,)), ((), ())), preferred_element_type=F32)


def halves(x):
    high = x.astype(BF16)
    return high, (x - high.astype(F32)).astype(BF16)


def thirds(x):
    high = x.astype(BF16).astype(F32)
    middle = (x - high).astype(BF16).astype(F32)
    return high, middle, x - high - middle


def mm(a, b, ca=1, cb=0):
    left = jnp.concatenate([a[0], a[0], a[1]], axis=ca)
    right = jnp.concatenate([b[0], b[1], b[0]], axis=cb)
    return dot(left, right, ca, cb)


def iotas(rows, columns):
    shape = (rows, columns)
    return lax.broadcasted_iota(jnp.int32, shape, 0), lax.broadcasted_iota(jnp.int32, shape, 1)


def call(kernel, outs, n_in, smem=(), scratch=()):
    spec = lambda i: pl.BlockSpec(memory_space=pltpu.SMEM if i in smem else pltpu.VMEM)
    return pl.pallas_call(
        kernel,
        out_shape=outs,
        in_specs=[spec(i) for i in range(n_in)],
        out_specs=jax.tree.map(lambda _: pl.BlockSpec(memory_space=pltpu.VMEM), outs),
        scratch_shapes=list(scratch),
        compiler_params=pltpu.CompilerParams(vmem_limit_bytes=VMEM_LIMIT),
    )


def arr(dtype, *shape):
    return jax.ShapeDtypeStruct(shape, dtype)


class Plan:
    def __init__(self, n, tok, hv, hk):
        self.n, self.tok, self.hv, self.hk = n, tok, hv, hk
        self.width = hv * DV // n
        self.padded = -(-self.width // 16) * 16
        self.v_at = 2 * tok
        self.aux_at = 2 * tok + self.padded
        self.rows = self.aux_at + AUX
        self.batch = max(b for b in (1, 2, 4) if n % b == 0)

    def value_head(self, g):
        return g * self.width // DV

    def key_head(self, g):
        return self.value_head(g) * self.hk // self.hv


def aux_rows(rows, columns):
    row_ids = lax.broadcasted_iota(jnp.int32, (AUX, columns), 0)
    out = jnp.zeros((AUX, columns), F32)
    for i, part in enumerate(p for r in rows for p in thirds(r)):
        out = jnp.where(row_ids == i, part, out)
    return out.astype(BF16)


def pack_kernel(plan, q_ref, k_ref, v_ref, rate_ref, decay_ref, out_ref):
    tok = plan.tok
    values = [
        jnp.transpose(v_ref[:, h * DV : (h + 1) * DV].astype(F32)) for h in range(plan.hv)
    ]
    for g in range(plan.n):
        h, kh = plan.value_head(g), plan.key_head(g)
        out_ref[g, :tok] = q_ref[:, kh * DK : (kh + 1) * DK]
        out_ref[g, tok : 2 * tok] = k_ref[:, kh * DK : (kh + 1) * DK]
        first = g * plan.width - h * DV
        piece = values[h][first : first + plan.width]
        if plan.padded > plan.width:
            blank = jnp.zeros((plan.padded - plan.width, tok), F32)
            piece = jnp.concatenate([piece, blank], axis=0)
        out_ref[g, plan.v_at : plan.aux_at] = piece.astype(BF16)
        rows = [rate_ref[h : h + 1, :], decay_ref[h : h + 1, :]]
        out_ref[g, plan.aux_at :] = aux_rows(rows, tok)


def unit(x):
    scale = lax.rsqrt(jnp.sum(x * x, axis=1, keepdims=True) + EPS)
    return x * scale, scale


def segments(off_ref, positions):
    total = jnp.zeros(positions.shape, jnp.int32)
    for j in range(off_ref.shape[0] - 1):
        total = total + (off_ref[j] <= positions).astype(jnp.int32)
    return total


def to_columns(rows, tok):
    row_ids = lax.broadcasted_iota(jnp.int32, (tok, tok), 0)
    stacked = jnp.zeros((tok, tok), F32)
    for i, r in enumerate(rows):
        stacked = jnp.where(row_ids == i, r, stacked)
    turned = jnp.transpose(stacked)
    return [turned[:, i : i + 1] for i in range(len(rows))]


def to_rows(columns, tok):
    column_ids = lax.broadcasted_iota(jnp.int32, (tok, tok), 1)
    stacked = jnp.zeros((tok, tok), F32)
    for i, c in enumerate(columns):
        stacked = jnp.where(column_ids == i, c, stacked)
    turned = jnp.transpose(stacked)
    return [turned[i : i + 1, :] for i in range(len(columns))]


def scalings(plan, off_ref, chunks, auxes):
    tok = plan.tok
    rows, columns = iotas(tok, tok)
    upto = (rows <= columns).astype(BF16)
    sums = [dot(a, upto, 1, 0) for a in auxes]
    rates = [jnp.sum(a[0:3].astype(F32), axis=0, keepdims=True) for a in auxes]
    cumuls = [s[3:4] + s[4:5] + s[5:6] for s in sums]
    turned = to_columns(rates + cumuls, tok)
    out = []
    for i, c in enumerate(chunks):
        b_col, c_col = turned[i], turned[len(chunks) + i]
        c_row = cumuls[i]
        start = c * tok
        seg_col = segments(off_ref, start + rows[:, :1])
        seg_row = segments(off_ref, start + columns[:1, :])
        before = jnp.int32(0)
        last = jnp.int32(0)
        for j in range(off_ref.shape[0] - 1):
            before = before + (off_ref[j] <= start - 1).astype(jnp.int32)
            last = last + (off_ref[j] <= start + tok - 1).astype(jnp.int32)
        c_last = c_row[:, tok - 1 : tok]
        together = (seg_col == seg_row) & (rows >= columns)
        ratio = jnp.where(together, jnp.exp(jnp.where(together, c_col - c_row, 0.0)), 0.0)
        start_col = jnp.where(seg_col == before, jnp.exp(c_col), 0.0)
        end_col = jnp.where(seg_col == last, jnp.exp(c_last - c_col), 0.0)
        whole = jnp.where(last == before, jnp.exp(c_last), 0.0)
        out.append((rates[i], b_col, ratio, start_col, end_col, whole))
    return out


def inverses(lowers):
    size = lowers[0].shape[0]
    rows, columns = iotas(size, size)
    identity = (rows == columns).astype(F32)
    block = min(16, size)
    near = (rows // block) == (columns // block)
    powers = [jnp.where(near, -m, 0.0) for m in lowers]
    results = [identity + p for p in powers]
    split = [halves(p) for p in powers]
    powers = [mm(s, s) for s in split]
    reach = 2
    while reach < block:
        split = [halves(p) for p in powers]
        more = reach * 2 < block
        both = []
        for r, s in zip(results, split):
            left = halves(r)
            if more:
                left = tuple(jnp.concatenate([x, y], axis=0) for x, y in zip(left, s))
            both.append(mm(left, s))
        results = [r + b[:size] for r, b in zip(results, both)]
        if more:
            powers = [b[size:] for b in both]
        reach *= 2
    while block < size:
        across = ((rows // (2 * block)) == (columns // (2 * block))) & (
            (rows // block) > (columns // block)
        )
        split = [halves(r) for r in results]
        middle = [mm(halves(jnp.where(across, m, 0.0)), s) for m, s in zip(lowers, split)]
        results = [r - mm(s, halves(m)) for r, s, m in zip(results, split, middle)]
        block *= 2
    return results


def forward_kernel(
    plan, off_ref, in_ref, out_ref, x_ref, a_ref, w_ref, t_ref, q_ref, ratio_ref, u_ref, s_ref, l_ref, ol_ref
):
    n, tok, width = plan.n, plan.tok, plan.width
    rows, columns = iotas(tok, tok)
    identity = (rows == columns).astype(F32)

    def put(ref, c, pair):
        ref[c, 0], ref[c, 1] = pair

    def group(step, carry):
        chunks = [step * plan.batch + i for i in range(plan.batch)]
        scales = scalings(plan, off_ref, chunks, [in_ref[c, plan.aux_at :] for c in chunks])
        qn = [unit(in_ref[c, :tok].astype(F32))[0] for c in chunks]
        kn = [unit(in_ref[c, tok : 2 * tok].astype(F32))[0] for c in chunks]
        kp = [halves(x) for x in kn]
        qp = [halves(x) for x in qn]
        dots = [
            mm(tuple(jnp.concatenate([a, b], axis=0) for a, b in zip(q, k)), k, 1, 1)
            for q, k in zip(qp, kp)
        ]
        strict = rows > columns
        lowers = [
            jnp.where(strict, s[1] * d[tok:] * s[2], 0.0) for s, d in zip(scales, dots)
        ]
        scores = [d[:tok] * s[2] for s, d in zip(scales, dots)]
        inv = inverses(lowers)
        rated = [halves(x * s[0]) for x, s in zip(inv, scales)]
        w = [mm(x, halves(s[3] * k)) for x, s, k in zip(rated, scales, kn)]
        values = [in_ref[c, plan.v_at : plan.aux_at][:width] for c in chunks]
        u = [
            dot(
                jnp.concatenate([v, v], axis=1), jnp.concatenate(x, axis=1), 1, 1
            )
            for v, x in zip(values, rated)
        ]
        wp = [halves(x) for x in w]
        up = [halves(x) for x in u]
        ap = [halves(x) for x in scores]
        ke = [halves(s[4] * k) for s, k in zip(scales, kn)]
        for i, c in enumerate(chunks):
            put(x_ref, c, halves(inv[i]))
            put(a_ref, c, ap[i])
            put(w_ref, c, wp[i])
            put(t_ref, c, halves(scales[i][5] * identity - mm(wp[i], ke[i], 0, 0)))
            put(q_ref, c, halves(scales[i][3] * qn[i] - mm(ap[i], wp[i])))
            ratio_ref[c] = scales[i][2]
            u_ref[c] = u[i]
            l_ref[c] = mm(up[i], ke[i])
            ol_ref[c] = mm(up[i], ap[i], 1, 1)
        return carry

    lax.fori_loop(0, n // plan.batch, group, 0)
    state = jnp.zeros((width, DK), F32)
    for c in range(n):
        s_ref[c] = state
        pair = halves(state)
        out_ref[c] = (ol_ref[c] + mm(pair, (q_ref[c, 0], q_ref[c, 1]), 1, 1)).astype(BF16)
        state = l_ref[c] + mm(pair, (t_ref[c, 0], t_ref[c, 1]))


def backward_kernel(
    plan, off_ref, in_ref, g_ref, x_ref, a_ref, w_ref, t_ref, q_ref, ratio_ref, u_ref, s_ref, out_ref, e_ref
):
    n, tok, width = plan.n, plan.tok, plan.width
    rows, columns = iotas(tok, tok)
    strict = rows > columns
    upto = (rows >= columns).astype(BF16)

    def get(ref, c):
        return ref[c, 0], ref[c, 1]

    def d_out(c):
        return g_ref[c, :width], g_ref[c, plan.padded : plan.padded + width]

    d_state = jnp.zeros((width, DK), F32)
    for c in reversed(range(n)):
        e_ref[c] = d_state
        d_state = mm(halves(d_state), get(t_ref, c), 1, 1) + mm(d_out(c), get(q_ref, c))

    def cat(pairs, axis):
        return tuple(jnp.concatenate(parts, axis=axis) for parts in zip(*pairs))

    def group(step, carry):
        chunks = [step * plan.batch + i for i in range(plan.batch)]
        scales = scalings(plan, off_ref, chunks, [in_ref[c, plan.aux_at :] for c in chunks])
        qu = [unit(in_ref[c, :tok].astype(F32)) for c in chunks]
        ku = [unit(in_ref[c, tok : 2 * tok].astype(F32)) for c in chunks]
        qp = [halves(x[0]) for x in qu]
        kp = [halves(x[0]) for x in ku]
        do = [d_out(c) for c in chunks]
        s0 = [s_ref[c] for c in chunks]
        ds = [e_ref[c] for c in chunks]
        s0p = [halves(x) for x in s0]
        dsp = [halves(x) for x in ds]
        pseudo = [u_ref[c] - mm(s, get(w_ref, c), 1, 1) for c, s in zip(chunks, s0p)]
        pp = [halves(x) for x in pseudo]
        ke = [halves(s[4] * k[0]) for s, k in zip(scales, ku)]
        dp = [
            mm(o, get(a_ref, c)) + mm(d, k, 1, 1) for c, o, d, k in zip(chunks, do, dsp, ke)
        ]
        dr = [mm(halves(d), get(x_ref, c)) for c, d in zip(chunks, dp)]
        drp = [halves(x) for x in dr]
        big = [
            mm(cat([o, r], 1), cat([p, s], 1), 0, 0) for o, r, p, s in zip(do, drp, pp, s0p)
        ]
        pds = [mm(p, d, 0, 0) for p, d in zip(pp, dsp)]
        da = [b[:tok, :tok] * ratio_ref[c] for b, c in zip(big, chunks)]
        dm = [
            jnp.where(strict, -b[tok:, :tok] * ratio_ref[c], 0.0) for b, c in zip(big, chunks)
        ]
        dap = [halves(x) for x in da]
        dmp = [halves(x) for x in dm]
        dbm = [halves(s[1] * x) for s, x in zip(scales, dm)]
        by_row = [mm(cat([x, y], 0), k) for x, y, k in zip(dap, dmp, kp)]
        by_column = [
            mm(cat([x, y], 0), cat([q, k], 0), 0, 0) for x, y, q, k in zip(dap, dbm, qp, kp)
        ]
        sums = []
        for i, c in enumerate(chunks):
            _, b_col, _, start_col, end_col, whole = scales[i]
            (qn, q_scale), (kn, k_scale) = qu[i], ku[i]
            dqn = by_row[i][:tok] + start_col * big[i][:tok, tok:]
            erase = by_row[i][tok:] - start_col * big[i][tok:, tok:]
            ends = end_col * pds[i]
            write = by_column[i] + ends
            dkn = b_col * erase + write
            s_q = jnp.sum(qn * dqn, axis=1, keepdims=True)
            s_e = jnp.sum(kn * erase, axis=1, keepdims=True)
            s_w = jnp.sum(kn * write, axis=1, keepdims=True)
            total = jnp.sum(jnp.sum(kn * ends, axis=1, keepdims=True), axis=0, keepdims=True)
            both = jnp.sum(jnp.sum(s0[i] * ds[i], axis=1, keepdims=True), axis=0, keepdims=True)
            out_ref[c, :tok] = (q_scale * (dqn - qn * s_q)).astype(BF16)
            out_ref[c, tok : 2 * tok] = (k_scale * (dkn - kn * (b_col * s_e + s_w))).astype(BF16)
            dv = scales[i][0] * dr[i]
            if plan.padded > width:
                dv = jnp.concatenate([dv, jnp.zeros((plan.padded - width, tok), F32)], axis=0)
            out_ref[c, plan.v_at : plan.aux_at] = dv.astype(BF16)
            sums.append((s_e, s_q + b_col * s_e - s_w, total + whole * both))
        turned = to_rows([s[0] for s in sums] + [s[1] for s in sums], tok)
        for i, c in enumerate(chunks):
            values = in_ref[c, plan.v_at : plan.aux_at][:width].astype(F32)
            d_rate = turned[i] + jnp.sum(dr[i] * values, axis=0, keepdims=True)
            parts = dot(aux_rows([turned[len(chunks) + i]], tok), upto, 1, 0)
            d_decay = parts[0:1] + parts[1:2] + parts[2:3] + sums[i][2]
            out_ref[c, plan.aux_at :] = aux_rows([d_rate, d_decay], tok)
        return carry

    lax.fori_loop(0, n // plan.batch, group, 0)


def cotangent_kernel(plan, parts, head_ref, *refs):
    pieces, w_ref, out_ref, all_ref = refs[:parts], refs[parts], refs[parts + 1], refs[parts + 2]
    rows = pieces[0].shape[0]
    for d in range(parts):
        at = lax.rem(head_ref[0] + parts - d, parts)
        all_ref[pl.ds(pl.multiple_of(at * rows, rows), rows), :] = pieces[d][...]
    tok, model = all_ref.shape
    share = model // plan.n
    whole = all_ref[...]
    core = dot(w_ref[...], whole, 1, 1)
    high, low = halves(core)
    width, padded = plan.width, plan.padded
    for g in range(plan.n):
        for i, x in enumerate((core, core - high.astype(F32))):
            piece = x[g * width : (g + 1) * width]
            if padded > width:
                piece = jnp.concatenate([piece, jnp.zeros((padded - width, tok), F32)], axis=0)
            out_ref[g, i * padded : (i + 1) * padded] = piece.astype(BF16)
    turned = jnp.transpose(whole.astype(F32)).astype(BF16)
    for g in range(plan.n):
        out_ref[g, 2 * padded :] = turned[g * share : (g + 1) * share]


def finish_kernel(plan, in_ref, q_ref, k_ref, v_ref, rate_ref, decay_ref):
    tok, n = plan.tok, plan.n
    for kh in range(plan.hk):
        mine = [g for g in range(n) if plan.key_head(g) == kh]
        for ref, at in ((q_ref, 0), (k_ref, tok)):
            total = in_ref[mine[0], at : at + tok].astype(F32)
            for g in mine[1:]:
                total = total + in_ref[g, at : at + tok].astype(F32)
            ref[:, kh * DK : (kh + 1) * DK] = total
    for h in range(plan.hv):
        mine = [g for g in range(n) if plan.value_head(g) == h]
        pieces = [in_ref[g, plan.v_at : plan.aux_at].astype(F32)[: plan.width] for g in mine]
        v_ref[:, h * DV : (h + 1) * DV] = jnp.transpose(jnp.concatenate(pieces, axis=0))
        aux = in_ref[mine[0], plan.aux_at :].astype(F32)
        for g in mine[1:]:
            aux = aux + in_ref[g, plan.aux_at :].astype(F32)
        rate_ref[h : h + 1, :] = aux[0:1] + aux[1:2] + aux[2:3]
        decay_ref[h : h + 1, :] = aux[3:4] + aux[4:5] + aux[5:6]


def exchange(x, axis):
    return lax.all_to_all(x, axis, split_axis=0, concat_axis=0, tiled=True)


def per_device(
    queries, key_vectors, value_rows, write_rate, log_decay, doc_offsets, out_weight, grad_out
):
    n, parts = lax.axis_size("ctx"), lax.axis_size("head")
    tok, hv = queries.shape[0], write_rate.shape[0]
    hk, model = queries.shape[1] // DK, grad_out.shape[1]
    plan = Plan(n, tok, hv, hk)
    width, share = plan.width, model // n

    sent = call(partial(pack_kernel, plan), arr(BF16, n, plan.rows, DK), 5)(
        queries, key_vectors, value_rows, write_rate, log_decay
    )
    got = exchange(sent, "ctx")

    pieces = [grad_out] + [
        lax.ppermute(grad_out, "head", [(i, (i + d) % parts) for i in range(parts)])
        for d in range(1, parts)
    ]
    head = lax.axis_index("head").astype(jnp.int32).reshape(1)
    cot_sent = call(
        partial(cotangent_kernel, plan, parts),
        arr(BF16, n, 2 * plan.padded + share, tok),
        parts + 2,
        smem=(0,),
        scratch=[pltpu.VMEM((tok, model), BF16)],
    )(head, *pieces, out_weight)
    cot = exchange(cot_sent, "ctx")

    pair = lambda r, c: arr(BF16, n, 2, r, c)
    out, x, a, w, t, q, ratio, u, s, _, _ = call(
        partial(forward_kernel, plan),
        (
            arr(BF16, n, width, tok),
            pair(tok, tok),
            pair(tok, tok),
            pair(tok, DK),
            pair(DK, DK),
            pair(tok, DK),
            arr(F32, n, tok, tok),
            arr(F32, n, width, tok),
            arr(F32, n, width, DK),
            arr(F32, n, width, DK),
            arr(F32, n, width, tok),
        ),
        2,
        smem=(0,),
    )(doc_offsets, got)

    mixed = exchange(out, "ctx").reshape(hv * DV, tok)
    projected = dot(mixed, out_weight, 0, 0).astype(BF16)
    layer_parts = exchange(projected, "head").reshape(parts, tok // parts, model)
    layer_out = jnp.sum(layer_parts.astype(F32), axis=0)

    all_mixed = lax.all_gather(out, "ctx", axis=0)
    grads = cot[:, 2 * plan.padded :]
    weight_grad = jnp.einsum(
        "cdt,gcvt->dgv", grads, all_mixed, preferred_element_type=F32
    ).reshape(share, hv * DV)

    back_sent = call(
        partial(backward_kernel, plan),
        arr(BF16, n, plan.rows, DK),
        11,
        smem=(0,),
        scratch=[pltpu.VMEM((n, width, DK), F32)],
    )(doc_offsets, got, cot, x, a, w, t, q, ratio, u, s)
    back = exchange(back_sent, "ctx")
    grad_q, grad_k, grad_v, grad_rate, grad_decay = call(
        partial(finish_kernel, plan),
        (
            arr(F32, tok, hk * DK),
            arr(F32, tok, hk * DK),
            arr(F32, tok, hv * DV),
            arr(F32, hv, tok),
            arr(F32, hv, tok),
        ),
        1,
    )(back)
    return (layer_out, grad_q, grad_k, grad_v, grad_rate, grad_decay, weight_grad)


def solution(mesh):
    placed = (
        P("ctx", "head"),
        P("ctx", "head"),
        P("ctx", "head"),
        P("head", "ctx"),
        P("head", "ctx"),
        P(),
        P("head", None),
        P(("ctx", "head"), None),
    )
    return jax.shard_map(
        per_device,
        mesh=mesh,
        in_specs=placed,
        out_specs=(
            P(("ctx", "head"), None),
            P("ctx", "head"),
            P("ctx", "head"),
            P("ctx", "head"),
            P("head", "ctx"),
            P("head", "ctx"),
            P("ctx", "head"),
        ),
        check_vma=False,
    )
```

```python
from functools import partial

import jax
import jax.numpy as jnp
from jax import lax
from jax.experimental import pallas as pl
from jax.experimental.pallas import tpu as pltpu
from jax.sharding import PartitionSpec as P

DK = 128
DV = 128
AUX = 16
EPS = 1e-06
F32 = jnp.float32
BF16 = jnp.bfloat16
VMEM_LIMIT = 56 * 1024 * 1024


def dot(a, b, ca, cb):
    return lax.dot_general(a, b, (((ca,), (cb,)), ((), ())), preferred_element_type=F32)


def halves(x):
    high = x.astype(BF16)
    return high, (x - high.astype(F32)).astype(BF16)


def thirds(x):
    high = x.astype(BF16).astype(F32)
    middle = (x - high).astype(BF16).astype(F32)
    return high, middle, x - high - middle


def mm(a, b, ca=1, cb=0):
    left = jnp.concatenate([a[0], a[0], a[1]], axis=ca)
    right = jnp.concatenate([b[0], b[1], b[0]], axis=cb)
    return dot(left, right, ca, cb)


def iotas(rows, columns):
    shape = (rows, columns)
    return lax.broadcasted_iota(jnp.int32, shape, 0), lax.broadcasted_iota(jnp.int32, shape, 1)


def call(kernel, outs, n_in, smem=(), scratch=()):
    spec = lambda i: pl.BlockSpec(memory_space=pltpu.SMEM if i in smem else pltpu.VMEM)
    return pl.pallas_call(
        kernel,
        out_shape=outs,
        in_specs=[spec(i) for i in range(n_in)],
        out_specs=jax.tree.map(lambda _: pl.BlockSpec(memory_space=pltpu.VMEM), outs),
        scratch_shapes=list(scratch),
        compiler_params=pltpu.CompilerParams(vmem_limit_bytes=VMEM_LIMIT),
    )


def arr(dtype, *shape):
    return jax.ShapeDtypeStruct(shape, dtype)


class Plan:
    def __init__(self, n, tok, hv, hk):
        self.n, self.tok, self.hv, self.hk = n, tok, hv, hk
        self.width = hv * DV // n
        self.padded = -(-self.width // 16) * 16
        self.v_at = 2 * tok
        self.aux_at = 2 * tok + self.padded
        self.rows = self.aux_at + AUX
        self.batch = max(b for b in (1, 2, 4) if n % b == 0)

    def value_head(self, g):
        return g * self.width // DV

    def key_head(self, g):
        return self.value_head(g) * self.hk // self.hv


def aux_rows(rows, columns):
    row_ids = lax.broadcasted_iota(jnp.int32, (AUX, columns), 0)
    out = jnp.zeros((AUX, columns), F32)
    for i, part in enumerate(p for r in rows for p in thirds(r)):
        out = jnp.where(row_ids == i, part, out)
    return out.astype(BF16)


def pack_kernel(plan, q_ref, k_ref, v_ref, rate_ref, decay_ref, out_ref):
    tok = plan.tok
    values = [
        jnp.transpose(v_ref[:, h * DV : (h + 1) * DV].astype(F32)) for h in range(plan.hv)
    ]
    for g in range(plan.n):
        h, kh = plan.value_head(g), plan.key_head(g)
        out_ref[g, :tok] = q_ref[:, kh * DK : (kh + 1) * DK]
        out_ref[g, tok : 2 * tok] = k_ref[:, kh * DK : (kh + 1) * DK]
        first = g * plan.width - h * DV
        piece = values[h][first : first + plan.width]
        if plan.padded > plan.width:
            blank = jnp.zeros((plan.padded - plan.width, tok), F32)
            piece = jnp.concatenate([piece, blank], axis=0)
        out_ref[g, plan.v_at : plan.aux_at] = piece.astype(BF16)
        rows = [rate_ref[h : h + 1, :], decay_ref[h : h + 1, :]]
        out_ref[g, plan.aux_at :] = aux_rows(rows, tok)


def unit(x):
    scale = lax.rsqrt(jnp.sum(x * x, axis=1, keepdims=True) + EPS)
    return x * scale, scale


def segments(off_ref, positions):
    total = jnp.zeros(positions.shape, jnp.int32)
    for j in range(off_ref.shape[0] - 1):
        total = total + (off_ref[j] <= positions).astype(jnp.int32)
    return total


def to_columns(rows, tok):
    row_ids = lax.broadcasted_iota(jnp.int32, (tok, tok), 0)
    stacked = jnp.zeros((tok, tok), F32)
    for i, r in enumerate(rows):
        stacked = jnp.where(row_ids == i, r, stacked)
    turned = jnp.transpose(stacked)
    return [turned[:, i : i + 1] for i in range(len(rows))]


def to_rows(columns, tok):
    column_ids = lax.broadcasted_iota(jnp.int32, (tok, tok), 1)
    stacked = jnp.zeros((tok, tok), F32)
    for i, c in enumerate(columns):
        stacked = jnp.where(column_ids == i, c, stacked)
    turned = jnp.transpose(stacked)
    return [turned[i : i + 1, :] for i in range(len(columns))]


def scalings(plan, off_ref, chunks, auxes):
    tok = plan.tok
    rows, columns = iotas(tok, tok)
    upto = (rows <= columns).astype(BF16)
    sums = [dot(a, upto, 1, 0) for a in auxes]
    rates = [jnp.sum(a[0:3].astype(F32), axis=0, keepdims=True) for a in auxes]
    cumuls = [s[3:4] + s[4:5] + s[5:6] for s in sums]
    turned = to_columns(rates + cumuls, tok)
    out = []
    for i, c in enumerate(chunks):
        b_col, c_col = turned[i], turned[len(chunks) + i]
        c_row = cumuls[i]
        start = c * tok
        seg_col = segments(off_ref, start + rows[:, :1])
        seg_row = segments(off_ref, start + columns[:1, :])
        before = jnp.int32(0)
        last = jnp.int32(0)
        for j in range(off_ref.shape[0] - 1):
            before = before + (off_ref[j] <= start - 1).astype(jnp.int32)
            last = last + (off_ref[j] <= start + tok - 1).astype(jnp.int32)
        c_last = c_row[:, tok - 1 : tok]
        together = (seg_col == seg_row) & (rows >= columns)
        ratio = jnp.where(together, jnp.exp(jnp.where(together, c_col - c_row, 0.0)), 0.0)
        start_col = jnp.where(seg_col == before, jnp.exp(c_col), 0.0)
        end_col = jnp.where(seg_col == last, jnp.exp(c_last - c_col), 0.0)
        whole = jnp.where(last == before, jnp.exp(c_last), 0.0)
        out.append((rates[i], b_col, ratio, start_col, end_col, whole))
    return out


def inverses(lowers):
    size = lowers[0].shape[0]
    rows, columns = iotas(size, size)
    identity = (rows == columns).astype(F32)
    block = min(16, size)
    near = (rows // block) == (columns // block)
    powers = [jnp.where(near, -m, 0.0) for m in lowers]
    results = [identity + p for p in powers]
    split = [halves(p) for p in powers]
    powers = [mm(s, s) for s in split]
    reach = 2
    while reach < block:
        split = [halves(p) for p in powers]
        more = reach * 2 < block
        both = []
        for r, s in zip(results, split):
            left = halves(r)
            if more:
                left = tuple(jnp.concatenate([x, y], axis=0) for x, y in zip(left, s))
            both.append(mm(left, s))
        results = [r + b[:size] for r, b in zip(results, both)]
        if more:
            powers = [b[size:] for b in both]
        reach *= 2
    while block < size:
        across = ((rows // (2 * block)) == (columns // (2 * block))) & (
            (rows // block) > (columns // block)
        )
        split = [halves(r) for r in results]
        middle = [mm(halves(jnp.where(across, m, 0.0)), s) for m, s in zip(lowers, split)]
        results = [r - mm(s, halves(m)) for r, s, m in zip(results, split, middle)]
        block *= 2
    return results


def forward_kernel(
    plan, off_ref, in_ref, out_ref, x_ref, a_ref, w_ref, t_ref, q_ref, ratio_ref, u_ref, s_ref, l_ref, ol_ref
):
    n, tok, width = plan.n, plan.tok, plan.width
    rows, columns = iotas(tok, tok)
    identity = (rows == columns).astype(F32)

    def put(ref, c, pair):
        ref[c, 0], ref[c, 1] = pair

    def group(step, carry):
        chunks = [step * plan.batch + i for i in range(plan.batch)]
        scales = scalings(plan, off_ref, chunks, [in_ref[c, plan.aux_at :] for c in chunks])
        qn = [unit(in_ref[c, :tok].astype(F32))[0] for c in chunks]
        kn = [unit(in_ref[c, tok : 2 * tok].astype(F32))[0] for c in chunks]
        kp = [halves(x) for x in kn]
        qp = [halves(x) for x in qn]
        dots = [
            mm(tuple(jnp.concatenate([a, b], axis=0) for a, b in zip(q, k)), k, 1, 1)
            for q, k in zip(qp, kp)
        ]
        strict = rows > columns
        lowers = [
            jnp.where(strict, s[1] * d[tok:] * s[2], 0.0) for s, d in zip(scales, dots)
        ]
        scores = [d[:tok] * s[2] for s, d in zip(scales, dots)]
        inv = inverses(lowers)
        rated = [halves(x * s[0]) for x, s in zip(inv, scales)]
        w = [mm(x, halves(s[3] * k)) for x, s, k in zip(rated, scales, kn)]
        values = [in_ref[c, plan.v_at : plan.aux_at][:width] for c in chunks]
        u = [
            dot(
                jnp.concatenate([v, v], axis=1), jnp.concatenate(x, axis=1), 1, 1
            )
            for v, x in zip(values, rated)
        ]
        wp = [halves(x) for x in w]
        up = [halves(x) for x in u]
        ap = [halves(x) for x in scores]
        ke = [halves(s[4] * k) for s, k in zip(scales, kn)]
        for i, c in enumerate(chunks):
            put(x_ref, c, halves(inv[i]))
            put(a_ref, c, ap[i])
            put(w_ref, c, wp[i])
            put(t_ref, c, halves(scales[i][5] * identity - mm(wp[i], ke[i], 0, 0)))
            put(q_ref, c, halves(scales[i][3] * qn[i] - mm(ap[i], wp[i])))
            ratio_ref[c] = scales[i][2]
            u_ref[c] = u[i]
            l_ref[c] = mm(up[i], ke[i])
            ol_ref[c] = mm(up[i], ap[i], 1, 1)
        return carry

    lax.fori_loop(0, n // plan.batch, group, 0)
    state = jnp.zeros((width, DK), F32)
    for c in range(n):
        s_ref[c] = state
        pair = halves(state)
        core = ol_ref[c] + mm(pair, (q_ref[c, 0], q_ref[c, 1]), 1, 1)
        if plan.padded > width:
            core = jnp.concatenate([core, jnp.zeros((plan.padded - width, tok), F32)], axis=0)
        core = core.astype(BF16)
        for g in range(n):
            out_ref[g, (c - g) % n] = core
        state = l_ref[c] + mm(pair, (t_ref[c, 0], t_ref[c, 1]))


def backward_kernel(
    plan, off_ref, in_ref, g_ref, x_ref, a_ref, w_ref, t_ref, q_ref, ratio_ref, u_ref, s_ref, out_ref, e_ref
):
    n, tok, width = plan.n, plan.tok, plan.width
    rows, columns = iotas(tok, tok)
    strict = rows > columns
    upto = (rows >= columns).astype(BF16)

    def get(ref, c):
        return ref[c, 0], ref[c, 1]

    def d_out(c):
        return g_ref[c, :width], g_ref[c, plan.padded : plan.padded + width]

    d_state = jnp.zeros((width, DK), F32)
    for c in reversed(range(n)):
        e_ref[c] = d_state
        d_state = mm(halves(d_state), get(t_ref, c), 1, 1) + mm(d_out(c), get(q_ref, c))

    def cat(pairs, axis):
        return tuple(jnp.concatenate(parts, axis=axis) for parts in zip(*pairs))

    def group(step, carry):
        chunks = [step * plan.batch + i for i in range(plan.batch)]
        scales = scalings(plan, off_ref, chunks, [in_ref[c, plan.aux_at :] for c in chunks])
        qu = [unit(in_ref[c, :tok].astype(F32)) for c in chunks]
        ku = [unit(in_ref[c, tok : 2 * tok].astype(F32)) for c in chunks]
        qp = [halves(x[0]) for x in qu]
        kp = [halves(x[0]) for x in ku]
        do = [d_out(c) for c in chunks]
        s0 = [s_ref[c] for c in chunks]
        ds = [e_ref[c] for c in chunks]
        s0p = [halves(x) for x in s0]
        dsp = [halves(x) for x in ds]
        pseudo = [u_ref[c] - mm(s, get(w_ref, c), 1, 1) for c, s in zip(chunks, s0p)]
        pp = [halves(x) for x in pseudo]
        ke = [halves(s[4] * k[0]) for s, k in zip(scales, ku)]
        dp = [
            mm(o, get(a_ref, c)) + mm(d, k, 1, 1) for c, o, d, k in zip(chunks, do, dsp, ke)
        ]
        dr = [mm(halves(d), get(x_ref, c)) for c, d in zip(chunks, dp)]
        drp = [halves(x) for x in dr]
        big = [
            mm(cat([o, r], 1), cat([p, s], 1), 0, 0) for o, r, p, s in zip(do, drp, pp, s0p)
        ]
        pds = [mm(p, d, 0, 0) for p, d in zip(pp, dsp)]
        da = [b[:tok, :tok] * ratio_ref[c] for b, c in zip(big, chunks)]
        dm = [
            jnp.where(strict, -b[tok:, :tok] * ratio_ref[c], 0.0) for b, c in zip(big, chunks)
        ]
        dap = [halves(x) for x in da]
        dmp = [halves(x) for x in dm]
        dbm = [halves(s[1] * x) for s, x in zip(scales, dm)]
        by_row = [mm(cat([x, y], 0), k) for x, y, k in zip(dap, dmp, kp)]
        by_column = [
            mm(cat([x, y], 0), cat([q, k], 0), 0, 0) for x, y, q, k in zip(dap, dbm, qp, kp)
        ]
        sums = []
        for i, c in enumerate(chunks):
            _, b_col, _, start_col, end_col, whole = scales[i]
            (qn, q_scale), (kn, k_scale) = qu[i], ku[i]
            dqn = by_row[i][:tok] + start_col * big[i][:tok, tok:]
            erase = by_row[i][tok:] - start_col * big[i][tok:, tok:]
            ends = end_col * pds[i]
            write = by_column[i] + ends
            dkn = b_col * erase + write
            s_q = jnp.sum(qn * dqn, axis=1, keepdims=True)
            s_e = jnp.sum(kn * erase, axis=1, keepdims=True)
            s_w = jnp.sum(kn * write, axis=1, keepdims=True)
            total = jnp.sum(jnp.sum(kn * ends, axis=1, keepdims=True), axis=0, keepdims=True)
            both = jnp.sum(jnp.sum(s0[i] * ds[i], axis=1, keepdims=True), axis=0, keepdims=True)
            out_ref[c, :tok] = (q_scale * (dqn - qn * s_q)).astype(BF16)
            out_ref[c, tok : 2 * tok] = (k_scale * (dkn - kn * (b_col * s_e + s_w))).astype(BF16)
            dv = scales[i][0] * dr[i]
            if plan.padded > width:
                dv = jnp.concatenate([dv, jnp.zeros((plan.padded - width, tok), F32)], axis=0)
            out_ref[c, plan.v_at : plan.aux_at] = dv.astype(BF16)
            sums.append((s_e, s_q + b_col * s_e - s_w, total + whole * both))
        turned = to_rows([s[0] for s in sums] + [s[1] for s in sums], tok)
        for i, c in enumerate(chunks):
            values = in_ref[c, plan.v_at : plan.aux_at][:width].astype(F32)
            d_rate = turned[i] + jnp.sum(dr[i] * values, axis=0, keepdims=True)
            parts = dot(aux_rows([turned[len(chunks) + i]], tok), upto, 1, 0)
            d_decay = parts[0:1] + parts[1:2] + parts[2:3] + sums[i][2]
            out_ref[c, plan.aux_at :] = aux_rows([d_rate, d_decay], tok)
        return carry

    lax.fori_loop(0, n // plan.batch, group, 0)


def cotangent_kernel(plan, grad_ref, w_ref, out_ref):
    whole = grad_ref[...]
    tok, model = whole.shape
    share = model // plan.n
    core = dot(w_ref[...], whole, 1, 1)
    high, low = halves(core)
    width, padded = plan.width, plan.padded
    for g in range(plan.n):
        for i, x in enumerate((core, core - high.astype(F32))):
            piece = x[g * width : (g + 1) * width]
            if padded > width:
                piece = jnp.concatenate([piece, jnp.zeros((padded - width, tok), F32)], axis=0)
            out_ref[g, i * padded : (i + 1) * padded] = piece.astype(BF16)
    turned = jnp.transpose(whole.astype(F32)).astype(BF16)
    for g in range(plan.n):
        out_ref[g, 2 * padded :] = turned[g * share : (g + 1) * share]


def finish_kernel(plan, in_ref, q_ref, k_ref, v_ref, rate_ref, decay_ref):
    tok, n = plan.tok, plan.n
    for kh in range(plan.hk):
        mine = [g for g in range(n) if plan.key_head(g) == kh]
        for ref, at in ((q_ref, 0), (k_ref, tok)):
            total = in_ref[mine[0], at : at + tok].astype(F32)
            for g in mine[1:]:
                total = total + in_ref[g, at : at + tok].astype(F32)
            ref[:, kh * DK : (kh + 1) * DK] = total
    for h in range(plan.hv):
        mine = [g for g in range(n) if plan.value_head(g) == h]
        pieces = [in_ref[g, plan.v_at : plan.aux_at].astype(F32)[: plan.width] for g in mine]
        v_ref[:, h * DV : (h + 1) * DV] = jnp.transpose(jnp.concatenate(pieces, axis=0))
        aux = in_ref[mine[0], plan.aux_at :].astype(F32)
        for g in mine[1:]:
            aux = aux + in_ref[g, plan.aux_at :].astype(F32)
        rate_ref[h : h + 1, :] = aux[0:1] + aux[1:2] + aux[2:3]
        decay_ref[h : h + 1, :] = aux[3:4] + aux[4:5] + aux[5:6]


def all_columns(plan, pieces):
    if plan.padded > plan.width:
        pieces = [p.astype(F32)[: plan.width] for p in pieces]
    return jnp.concatenate(pieces, axis=0).astype(BF16)


def project_kernel(plan, mixed_ref, w_ref, out_ref):
    mixed = all_columns(plan, [mixed_ref[g, 0] for g in range(plan.n)])
    out_ref[...] = dot(mixed, w_ref[...], 0, 0).astype(BF16)


def weight_kernel(plan, place_ref, cot_ref, mixed_ref, out_ref):
    total = None
    for step in range(plan.n):
        chunk = lax.rem(place_ref[0] + step, plan.n)
        mixed = all_columns(plan, [mixed_ref[g, step] for g in range(plan.n)])
        part = dot(cot_ref[chunk, 2 * plan.padded :], mixed, 1, 1)
        total = part if total is None else total + part
    out_ref[...] = total


def exchange(x, axis):
    return lax.all_to_all(x, axis, split_axis=0, concat_axis=0, tiled=True)


def per_device(
    queries, key_vectors, value_rows, write_rate, log_decay, doc_offsets, out_weight, grad_out
):
    n, parts = lax.axis_size("ctx"), lax.axis_size("head")
    tok, hv = queries.shape[0], write_rate.shape[0]
    hk, model = queries.shape[1] // DK, grad_out.shape[1]
    plan = Plan(n, tok, hv, hk)
    width, share = plan.width, model // n

    sent = call(partial(pack_kernel, plan), arr(BF16, n, plan.rows, DK), 5)(
        queries, key_vectors, value_rows, write_rate, log_decay
    )
    got = exchange(sent, "ctx")

    copies = jnp.broadcast_to(grad_out[None], (parts,) + grad_out.shape)
    whole_grad = exchange(copies, "head").reshape(tok, model)
    cot_sent = call(
        partial(cotangent_kernel, plan), arr(BF16, n, 2 * plan.padded + share, tok), 2
    )(whole_grad, out_weight)
    cot = exchange(cot_sent, "ctx")

    pair = lambda r, c: arr(BF16, n, 2, r, c)
    out, x, a, w, t, q, ratio, u, s, _, _ = call(
        partial(forward_kernel, plan),
        (
            arr(BF16, n, n, plan.padded, tok),
            pair(tok, tok),
            pair(tok, tok),
            pair(tok, DK),
            pair(DK, DK),
            pair(tok, DK),
            arr(F32, n, tok, tok),
            arr(F32, n, width, tok),
            arr(F32, n, width, DK),
            arr(F32, n, width, DK),
            arr(F32, n, width, tok),
        ),
        2,
        smem=(0,),
    )(doc_offsets, got)

    mixed = exchange(out, "ctx")
    back_sent = call(
        partial(backward_kernel, plan),
        arr(BF16, n, plan.rows, DK),
        11,
        smem=(0,),
        scratch=[pltpu.VMEM((n, width, DK), F32)],
    )(doc_offsets, got, cot, x, a, w, t, q, ratio, u, s)
    back = exchange(back_sent, "ctx")
    block = pl.BlockSpec((n, 1, plan.padded, tok), lambda i: (0, 0, 0, 0))
    projected = pl.pallas_call(
        partial(project_kernel, plan),
        out_shape=arr(BF16, tok, model),
        grid=(1,),
        in_specs=[block, pl.BlockSpec(out_weight.shape, lambda i: (0, 0))],
        out_specs=pl.BlockSpec((tok, model), lambda i: (0, 0)),
        compiler_params=pltpu.CompilerParams(vmem_limit_bytes=VMEM_LIMIT),
    )(mixed, out_weight)
    layer_parts = exchange(projected, "head").reshape(parts, tok // parts, model)
    layer_out = jnp.sum(layer_parts.astype(F32), axis=0)
    place = lax.axis_index("ctx").astype(jnp.int32).reshape(1)
    weight_grad = call(
        partial(weight_kernel, plan), arr(F32, share, hv * DV), 3, smem=(0,)
    )(place, cot, mixed)

    grad_q, grad_k, grad_v, grad_rate, grad_decay = call(
        partial(finish_kernel, plan),
        (
            arr(F32, tok, hk * DK),
            arr(F32, tok, hk * DK),
            arr(F32, tok, hv * DV),
            arr(F32, hv, tok),
            arr(F32, hv, tok),
        ),
        1,
    )(back)
    return (layer_out, grad_q, grad_k, grad_v, grad_rate, grad_decay, weight_grad)


def solution(mesh):
    placed = (
        P("ctx", "head"),
        P("ctx", "head"),
        P("ctx", "head"),
        P("head", "ctx"),
        P("head", "ctx"),
        P(),
        P("head", None),
        P(("ctx", "head"), None),
    )
    return jax.shard_map(
        per_device,
        mesh=mesh,
        in_specs=placed,
        out_specs=(
            P(("ctx", "head"), None),
            P("ctx", "head"),
            P("ctx", "head"),
            P("ctx", "head"),
            P("head", "ctx"),
            P("head", "ctx"),
            P("ctx", "head"),
        ),
        check_vma=False,
    )
```

```python
from functools import partial

import jax
import jax.numpy as jnp
from jax import lax
from jax.experimental import pallas as pl
from jax.experimental.pallas import tpu as pltpu
from jax.sharding import PartitionSpec as P

DK = 128
DV = 128
AUX = 16
EPS = 1e-06
F32 = jnp.float32
BF16 = jnp.bfloat16
VMEM_LIMIT = 56 * 1024 * 1024


def dot(a, b, ca, cb):
    return lax.dot_general(a, b, (((ca,), (cb,)), ((), ())), preferred_element_type=F32)


def halves(x):
    high = x.astype(BF16)
    return high, (x - high.astype(F32)).astype(BF16)


def thirds(x):
    high = x.astype(BF16).astype(F32)
    middle = (x - high).astype(BF16).astype(F32)
    return high, middle, x - high - middle


def mm(a, b, ca=1, cb=0):
    left = jnp.concatenate([a[0], a[0], a[1]], axis=ca)
    right = jnp.concatenate([b[0], b[1], b[0]], axis=cb)
    return dot(left, right, ca, cb)


def cat(pairs, axis):
    return tuple(jnp.concatenate(parts, axis=axis) for parts in zip(*pairs))


def put(ref, i, pair):
    ref[i, 0], ref[i, 1] = pair


def get(ref, i):
    return ref[i, 0], ref[i, 1]


def iotas(rows, columns):
    shape = (rows, columns)
    return lax.broadcasted_iota(jnp.int32, shape, 0), lax.broadcasted_iota(jnp.int32, shape, 1)


def call(kernel, outs, n_in, smem=(), scratch=()):
    spec = lambda i: pl.BlockSpec(memory_space=pltpu.SMEM if i in smem else pltpu.VMEM)
    return pl.pallas_call(
        kernel,
        out_shape=outs,
        in_specs=[spec(i) for i in range(n_in)],
        out_specs=jax.tree.map(lambda _: pl.BlockSpec(memory_space=pltpu.VMEM), outs),
        scratch_shapes=list(scratch),
        compiler_params=pltpu.CompilerParams(vmem_limit_bytes=VMEM_LIMIT),
    )


def arr(dtype, *shape):
    return jax.ShapeDtypeStruct(shape, dtype)


class Plan:
    def __init__(self, n, tok, hv, hk):
        self.n, self.tok, self.hv, self.hk = n, tok, hv, hk
        self.mates = n // hv
        self.v_at = 2 * tok
        self.aux_at = 2 * tok + DV
        self.rows = self.aux_at + AUX
        self.groups = [[m * self.mates + b for m in range(hv)] for b in range(self.mates)]

    def key_head(self, head):
        return head * self.hk // self.hv

    def exchange(self, x):
        return lax.all_to_all(
            x, "ctx", split_axis=0, concat_axis=0, axis_index_groups=self.groups, tiled=True
        )

    def from_mate(self, x, d):
        s = self.mates
        pairs = [(i // s * s + (i + d) % s, i) for i in range(self.n)]
        return lax.ppermute(x, "ctx", pairs)


def aux_rows(rows, columns):
    row_ids = lax.broadcasted_iota(jnp.int32, (AUX, columns), 0)
    out = jnp.zeros((AUX, columns), F32)
    for i, part in enumerate(p for r in rows for p in thirds(r)):
        out = jnp.where(row_ids == i, part, out)
    return out.astype(BF16)


def pack_kernel(plan, q_ref, k_ref, v_ref, rate_ref, decay_ref, out_ref):
    tok = plan.tok
    for h in range(plan.hv):
        kh = plan.key_head(h)
        out_ref[h, :tok] = q_ref[:, kh * DK : (kh + 1) * DK]
        out_ref[h, tok : 2 * tok] = k_ref[:, kh * DK : (kh + 1) * DK]
        turned = jnp.transpose(v_ref[:, h * DV : (h + 1) * DV].astype(F32))
        out_ref[h, plan.v_at : plan.aux_at] = turned.astype(BF16)
        rows = [rate_ref[h : h + 1, :], decay_ref[h : h + 1, :]]
        out_ref[h, plan.aux_at :] = aux_rows(rows, tok)


def unit(x):
    scale = lax.rsqrt(jnp.sum(x * x, axis=1, keepdims=True) + EPS)
    return x * scale, scale


def segments(off_ref, positions):
    total = jnp.zeros(positions.shape, jnp.int32)
    for j in range(off_ref.shape[0] - 1):
        total = total + (off_ref[j] <= positions).astype(jnp.int32)
    return total


def to_columns(rows, tok):
    row_ids = lax.broadcasted_iota(jnp.int32, (tok, tok), 0)
    stacked = jnp.zeros((tok, tok), F32)
    for i, r in enumerate(rows):
        stacked = jnp.where(row_ids == i, r, stacked)
    turned = jnp.transpose(stacked)
    return [turned[:, i : i + 1] for i in range(len(rows))]


def to_rows(columns, tok):
    column_ids = lax.broadcasted_iota(jnp.int32, (tok, tok), 1)
    stacked = jnp.zeros((tok, tok), F32)
    for i, c in enumerate(columns):
        stacked = jnp.where(column_ids == i, c, stacked)
    turned = jnp.transpose(stacked)
    return [turned[i : i + 1, :] for i in range(len(columns))]


def scalings(plan, off_ref, chunks, auxes):
    tok = plan.tok
    rows, columns = iotas(tok, tok)
    upto = (rows <= columns).astype(BF16)
    sums = [dot(a, upto, 1, 0) for a in auxes]
    rates = [jnp.sum(a[0:3].astype(F32), axis=0, keepdims=True) for a in auxes]
    cumuls = [s[3:4] + s[4:5] + s[5:6] for s in sums]
    turned = to_columns(rates + cumuls, tok)
    out = []
    for i, c in enumerate(chunks):
        b_col, c_col = turned[i], turned[len(chunks) + i]
        c_row = cumuls[i]
        start = c * tok
        seg_col = segments(off_ref, start + rows[:, :1])
        seg_row = segments(off_ref, start + columns[:1, :])
        before = jnp.int32(0)
        last = jnp.int32(0)
        for j in range(off_ref.shape[0] - 1):
            before = before + (off_ref[j] <= start - 1).astype(jnp.int32)
            last = last + (off_ref[j] <= start + tok - 1).astype(jnp.int32)
        c_last = c_row[:, tok - 1 : tok]
        together = (seg_col == seg_row) & (rows >= columns)
        ratio = jnp.where(together, jnp.exp(jnp.where(together, c_col - c_row, 0.0)), 0.0)
        start_col = jnp.where(seg_col == before, jnp.exp(c_col), 0.0)
        end_col = jnp.where(seg_col == last, jnp.exp(c_last - c_col), 0.0)
        whole = jnp.where(last == before, jnp.exp(c_last), 0.0)
        out.append((rates[i], b_col, ratio, start_col, end_col, whole))
    return out


def inverses(lowers):
    size = lowers[0].shape[0]
    rows, columns = iotas(size, size)
    identity = (rows == columns).astype(F32)
    block = min(16, size)
    near = (rows // block) == (columns // block)
    powers = [jnp.where(near, -m, 0.0) for m in lowers]
    results = [identity + p for p in powers]
    split = [halves(p) for p in powers]
    powers = [mm(s, s) for s in split]
    reach = 2
    while reach < block:
        split = [halves(p) for p in powers]
        more = reach * 2 < block
        both = []
        for r, s in zip(results, split):
            left = halves(r)
            if more:
                left = cat([left, s], 0)
            both.append(mm(left, s))
        results = [r + b[:size] for r, b in zip(results, both)]
        if more:
            powers = [b[size:] for b in both]
        reach *= 2
    while block < size:
        across = ((rows // (2 * block)) == (columns // (2 * block))) & (
            (rows // block) > (columns // block)
        )
        split = [halves(r) for r in results]
        middle = [mm(halves(jnp.where(across, m, 0.0)), s) for m, s in zip(lowers, split)]
        results = [r - mm(s, halves(m)) for r, s, m in zip(results, split, middle)]
        block *= 2
    return results


def prepare_kernel(
    plan, off_ref, mate_ref, in_ref, link_ref, x_ref, a_ref, w_ref, q_ref, ratio_ref, u_ref, ol_ref
):
    tok = plan.tok
    rows, columns = iotas(tok, tok)
    identity = (lax.broadcasted_iota(jnp.int32, (DK, DK), 0) == lax.broadcasted_iota(jnp.int32, (DK, DK), 1)).astype(F32)
    mine = range(plan.hv)
    chunks = [mate_ref[0] + plan.mates * m for m in mine]
    scales = scalings(plan, off_ref, chunks, [in_ref[m, plan.aux_at :] for m in mine])
    qn = [unit(in_ref[m, :tok].astype(F32))[0] for m in mine]
    kn = [unit(in_ref[m, tok : 2 * tok].astype(F32))[0] for m in mine]
    kp = [halves(x) for x in kn]
    qp = [halves(x) for x in qn]
    dots = [mm(cat([q, k], 0), k, 1, 1) for q, k in zip(qp, kp)]
    strict = rows > columns
    lowers = [jnp.where(strict, s[1] * d[tok:] * s[2], 0.0) for s, d in zip(scales, dots)]
    scores = [d[:tok] * s[2] for s, d in zip(scales, dots)]
    inv = inverses(lowers)
    rated = [halves(x * s[0]) for x, s in zip(inv, scales)]
    w = [mm(x, halves(s[3] * k)) for x, s, k in zip(rated, scales, kn)]
    values = [in_ref[m, plan.v_at : plan.aux_at] for m in mine]
    u = [
        dot(jnp.concatenate([v, v], axis=1), jnp.concatenate(x, axis=1), 1, 1)
        for v, x in zip(values, rated)
    ]
    wp = [halves(x) for x in w]
    up = [halves(x) for x in u]
    ap = [halves(x) for x in scores]
    ke = [halves(s[4] * k) for s, k in zip(scales, kn)]
    for m in mine:
        link_ref[m, 0] = scales[m][5] * identity - mm(wp[m], ke[m], 0, 0)
        link_ref[m, 1] = mm(up[m], ke[m])
    for m in mine:
        put(x_ref, m, halves(inv[m]))
        put(a_ref, m, ap[m])
        put(w_ref, m, wp[m])
        put(q_ref, m, halves(scales[m][3] * qn[m] - mm(ap[m], wp[m])))
        ratio_ref[m] = scales[m][2]
        u_ref[m] = u[m]
        ol_ref[m] = mm(up[m], ap[m], 1, 1)


def lay_out(plan, mate, refs, all_ref):
    for d, ref in enumerate(refs):
        all_ref[lax.rem(mate + d, plan.mates)] = ref[...]


def scan_kernel(plan, mate_ref, *refs):
    s = plan.mates
    links, (cot_ref, q_ref, ol_ref, out_ref, s_ref, back_ref, all_ref, states_ref) = refs[:s], refs[s:]
    mate = mate_ref[0]
    lay_out(plan, mate, links, all_ref)
    state = jnp.zeros((DV, DK), F32)
    for c in range(plan.n):
        states_ref[c] = state
        if c < plan.n - 1:
            link = all_ref.at[c % s, c // s]
            state = link[1] + mm(halves(state), halves(link[0]))
    for m in range(plan.hv):
        state = states_ref[mate + s * m]
        s_ref[m] = state
        core = (ol_ref[m] + mm(halves(state), get(q_ref, m), 1, 1)).astype(BF16)
        for g in range(plan.hv):
            out_ref[g, (m - g) % plan.hv] = core
        back_ref[m] = mm(d_out(cot_ref, m), get(q_ref, m))


def d_out(cot_ref, m):
    return cot_ref[m, :DV], cot_ref[m, DV : 2 * DV]


def backward_kernel(plan, off_ref, mate_ref, *refs):
    s, n, tok = plan.mates, plan.n, plan.tok
    links, backs, refs = refs[:s], refs[s : 2 * s], refs[2 * s :]
    in_ref, cot_ref, x_ref, a_ref, w_ref, ratio_ref, u_ref, s_ref, out_ref = refs[:9]
    links_ref, backs_ref, cots_ref = refs[9:]
    mate = mate_ref[0]
    lay_out(plan, mate, links, links_ref)
    lay_out(plan, mate, backs, backs_ref)
    d_state = jnp.zeros((DV, DK), F32)
    for c in reversed(range(n)):
        cots_ref[c] = d_state
        if c:
            d_state = backs_ref[c % s, c // s] + mm(
                halves(d_state), halves(links_ref[c % s, c // s, 0]), 1, 1
            )
    rows, columns = iotas(tok, tok)
    strict = rows > columns
    upto = (rows >= columns).astype(BF16)
    mine = range(plan.hv)
    chunks = [mate + s * m for m in mine]
    scales = scalings(plan, off_ref, chunks, [in_ref[m, plan.aux_at :] for m in mine])
    qu = [unit(in_ref[m, :tok].astype(F32)) for m in mine]
    ku = [unit(in_ref[m, tok : 2 * tok].astype(F32)) for m in mine]
    qp = [halves(x[0]) for x in qu]
    kp = [halves(x[0]) for x in ku]
    do = [d_out(cot_ref, m) for m in mine]
    s0 = [s_ref[m] for m in mine]
    ds = [cots_ref[c] for c in chunks]
    s0p = [halves(x) for x in s0]
    dsp = [halves(x) for x in ds]
    pseudo = [u_ref[m] - mm(s0p[m], get(w_ref, m), 1, 1) for m in mine]
    pp = [halves(x) for x in pseudo]
    ke = [halves(s[4] * k[0]) for s, k in zip(scales, ku)]
    dp = [mm(do[m], get(a_ref, m)) + mm(dsp[m], ke[m], 1, 1) for m in mine]
    dr = [mm(halves(dp[m]), get(x_ref, m)) for m in mine]
    drp = [halves(x) for x in dr]
    big = [mm(cat([o, r], 1), cat([p, s], 1), 0, 0) for o, r, p, s in zip(do, drp, pp, s0p)]
    pds = [mm(p, d, 0, 0) for p, d in zip(pp, dsp)]
    da = [big[m][:tok, :tok] * ratio_ref[m] for m in mine]
    dm = [jnp.where(strict, -big[m][tok:, :tok] * ratio_ref[m], 0.0) for m in mine]
    dap = [halves(x) for x in da]
    dmp = [halves(x) for x in dm]
    dbm = [halves(s[1] * x) for s, x in zip(scales, dm)]
    by_row = [mm(cat([x, y], 0), k) for x, y, k in zip(dap, dmp, kp)]
    by_column = [
        mm(cat([x, y], 0), cat([q, k], 0), 0, 0) for x, y, q, k in zip(dap, dbm, qp, kp)
    ]
    sums = []
    for m in mine:
        _, b_col, _, start_col, end_col, whole = scales[m]
        (qn, q_scale), (kn, k_scale) = qu[m], ku[m]
        dqn = by_row[m][:tok] + start_col * big[m][:tok, tok:]
        erase = by_row[m][tok:] - start_col * big[m][tok:, tok:]
        ends = end_col * pds[m]
        write = by_column[m] + ends
        dkn = b_col * erase + write
        s_q = jnp.sum(qn * dqn, axis=1, keepdims=True)
        s_e = jnp.sum(kn * erase, axis=1, keepdims=True)
        s_w = jnp.sum(kn * write, axis=1, keepdims=True)
        total = jnp.sum(jnp.sum(kn * ends, axis=1, keepdims=True), axis=0, keepdims=True)
        both = jnp.sum(jnp.sum(s0[m] * ds[m], axis=1, keepdims=True), axis=0, keepdims=True)
        out_ref[m, :tok] = (q_scale * (dqn - qn * s_q)).astype(BF16)
        out_ref[m, tok : 2 * tok] = (k_scale * (dkn - kn * (b_col * s_e + s_w))).astype(BF16)
        out_ref[m, plan.v_at : plan.aux_at] = (scales[m][0] * dr[m]).astype(BF16)
        sums.append((s_e, s_q + b_col * s_e - s_w, total + whole * both))
    turned = to_rows([s[0] for s in sums] + [s[1] for s in sums], tok)
    for m in mine:
        values = in_ref[m, plan.v_at : plan.aux_at].astype(F32)
        d_rate = turned[m] + jnp.sum(dr[m] * values, axis=0, keepdims=True)
        parts = dot(aux_rows([turned[plan.hv + m]], tok), upto, 1, 0)
        d_decay = parts[0:1] + parts[1:2] + parts[2:3] + sums[m][2]
        out_ref[m, plan.aux_at :] = aux_rows([d_rate, d_decay], tok)


def cotangent_kernel(plan, parts, head_ref, *refs):
    pieces, (w_ref, out_ref, all_ref) = refs[:parts], refs[parts:]
    rows = pieces[0].shape[0]
    for d in range(parts):
        at = lax.rem(head_ref[0] + d, parts)
        all_ref[pl.ds(pl.multiple_of(at * rows, rows), rows), :] = pieces[d][...]
    whole = all_ref[...]
    share = whole.shape[1] // plan.hv
    high, low = halves(dot(w_ref[...], whole, 1, 1))
    for m in range(plan.hv):
        out_ref[m, :DV] = high[m * DV : (m + 1) * DV]
        out_ref[m, DV : 2 * DV] = low[m * DV : (m + 1) * DV]
        turned = jnp.transpose(whole[:, m * share : (m + 1) * share].astype(F32))
        out_ref[m, 2 * DV :] = turned.astype(BF16)


def project_kernel(plan, parts, head_ref, mixed_ref, w_ref, *refs):
    outs, total_ref = refs[:parts], refs[parts]
    mixed = jnp.concatenate([mixed_ref[g, 0] for g in range(plan.hv)], axis=0)
    total_ref[...] = dot(mixed, w_ref[...], 0, 0)
    rows = outs[0].shape[0]
    for d in range(parts):
        at = lax.rem(head_ref[0] + parts - d, parts)
        block = total_ref[pl.ds(pl.multiple_of(at * rows, rows), rows), :]
        outs[d][...] = block.astype(outs[d].dtype)


def weight_kernel(plan, place_ref, mate_ref, cot_ref, mixed_ref, *outs):
    share = outs[0].shape[0]
    mixed = [
        jnp.concatenate([mixed_ref[g, step] for g in range(plan.hv)], axis=0)
        for step in range(plan.hv)
    ]
    for d, out_ref in enumerate(outs):
        at = lax.rem(mate_ref[0] + plan.mates - d, plan.mates)
        at = pl.multiple_of(2 * DV + at * share, share)
        total = None
        for step in range(plan.hv):
            chunk = lax.rem(place_ref[0] + step, plan.hv)
            part = dot(cot_ref[chunk, pl.ds(at, share), :], mixed[step], 1, 1)
            total = part if total is None else total + part
        out_ref[...] = total


def finish_kernel(plan, in_ref, q_ref, k_ref, v_ref, rate_ref, decay_ref):
    tok = plan.tok
    for kh in range(plan.hk):
        mine = [h for h in range(plan.hv) if plan.key_head(h) == kh]
        for ref, at in ((q_ref, 0), (k_ref, tok)):
            total = in_ref[mine[0], at : at + tok].astype(F32)
            for h in mine[1:]:
                total = total + in_ref[h, at : at + tok].astype(F32)
            ref[:, kh * DK : (kh + 1) * DK] = total
    for h in range(plan.hv):
        v_ref[:, h * DV : (h + 1) * DV] = jnp.transpose(
            in_ref[h, plan.v_at : plan.aux_at].astype(F32)
        )
        aux = in_ref[h, plan.aux_at :].astype(F32)
        rate_ref[h : h + 1, :] = aux[0:1] + aux[1:2] + aux[2:3]
        decay_ref[h : h + 1, :] = aux[3:4] + aux[4:5] + aux[5:6]


def per_device(
    queries, key_vectors, value_rows, write_rate, log_decay, doc_offsets, out_weight, grad_out
):
    n, parts = lax.axis_size("ctx"), lax.axis_size("head")
    tok, hv = queries.shape[0], write_rate.shape[0]
    hk, model = queries.shape[1] // DK, grad_out.shape[1]
    plan = Plan(n, tok, hv, hk)
    s = plan.mates
    index = lax.axis_index("ctx").astype(jnp.int32)
    place, mate = (index // s).reshape(1), (index % s).reshape(1)
    head = lax.axis_index("head").astype(jnp.int32).reshape(1)

    def from_head(x, d):
        return lax.ppermute(x, "head", [((i + d) % parts, i) for i in range(parts)])

    pieces = [grad_out] + [from_head(grad_out, d) for d in range(1, parts)]

    sent = call(partial(pack_kernel, plan), arr(BF16, hv, plan.rows, DK), 5)(
        queries, key_vectors, value_rows, write_rate, log_decay
    )
    got = plan.exchange(sent)

    cot_sent = call(
        partial(cotangent_kernel, plan, parts),
        arr(BF16, hv, 2 * DV + model // hv, tok),
        parts + 2,
        smem=(0,),
        scratch=[pltpu.VMEM((tok, model), BF16)],
    )(head, *pieces, out_weight)
    cot = plan.exchange(cot_sent)

    pair = lambda r, c: arr(BF16, hv, 2, r, c)
    link, x, a, w, q, ratio, u, ol = call(
        partial(prepare_kernel, plan),
        (
            arr(F32, hv, 2, DK, DK),
            pair(tok, tok),
            pair(tok, tok),
            pair(tok, DK),
            pair(tok, DK),
            arr(F32, hv, tok, tok),
            arr(F32, hv, DV, tok),
            arr(F32, hv, DV, tok),
        ),
        3,
        smem=(0, 1),
    )(doc_offsets, mate, got)
    links = [link] + [plan.from_mate(link, d) for d in range(1, s)]
    out, states, back = call(
        partial(scan_kernel, plan),
        (arr(BF16, hv, hv, DV, tok), arr(F32, hv, DV, DK), arr(F32, hv, DV, DK)),
        s + 4,
        smem=(0,),
        scratch=[pltpu.VMEM((s, hv, 2, DK, DK), F32), pltpu.VMEM((n, DV, DK), F32)],
    )(mate, *links, cot, q, ol)
    mixed = plan.exchange(out)
    backs = [back] + [plan.from_mate(back, d) for d in range(1, s)]

    grad_sent = call(
        partial(backward_kernel, plan),
        arr(BF16, hv, plan.rows, DK),
        2 * s + 10,
        smem=(0, 1),
        scratch=[
            pltpu.VMEM((s, hv, 2, DK, DK), F32),
            pltpu.VMEM((s, hv, DV, DK), F32),
            pltpu.VMEM((n, DV, DK), F32),
        ],
    )(doc_offsets, mate, *links, *backs, got, cot, x, a, w, ratio, u, states)

    block = pl.BlockSpec((hv, 1, DV, tok), lambda i: (0, 0, 0, 0))
    rows = tok // parts
    projected = pl.pallas_call(
        partial(project_kernel, plan, parts),
        out_shape=[arr(BF16 if d else F32, rows, model) for d in range(parts)],
        grid=(1,),
        in_specs=[
            pl.BlockSpec(memory_space=pltpu.SMEM),
            block,
            pl.BlockSpec(out_weight.shape, lambda i: (0, 0)),
        ],
        out_specs=[pl.BlockSpec((rows, model), lambda i: (0, 0))] * parts,
        scratch_shapes=[pltpu.VMEM((tok, model), F32)],
        compiler_params=pltpu.CompilerParams(vmem_limit_bytes=VMEM_LIMIT),
    )(head, mixed, out_weight)
    layer_out = projected[0]
    for d in range(1, parts):
        layer_out = layer_out + from_head(projected[d], d).astype(F32)

    shares = call(
        partial(weight_kernel, plan), [arr(F32, model // n, hv * DV)] * s, 4, smem=(0, 1)
    )(place, mate, cot, mixed)
    weight_grad = shares[0]
    for d in range(1, s):
        weight_grad = weight_grad + plan.from_mate(shares[d], d)

    grads = plan.exchange(grad_sent)
    grad_q, grad_k, grad_v, grad_rate, grad_decay = call(
        partial(finish_kernel, plan),
        (
            arr(F32, tok, hk * DK),
            arr(F32, tok, hk * DK),
            arr(F32, tok, hv * DV),
            arr(F32, hv, tok),
            arr(F32, hv, tok),
        ),
        1,
    )(grads)
    return (layer_out, grad_q, grad_k, grad_v, grad_rate, grad_decay, weight_grad)


def solution(mesh):
    placed = (
        P("ctx", "head"),
        P("ctx", "head"),
        P("ctx", "head"),
        P("head", "ctx"),
        P("head", "ctx"),
        P(),
        P("head", None),
        P(("ctx", "head"), None),
    )
    return jax.shard_map(
        per_device,
        mesh=mesh,
        in_specs=placed,
        out_specs=(
            P(("ctx", "head"), None),
            P("ctx", "head"),
            P("ctx", "head"),
            P("ctx", "head"),
            P("head", "ctx"),
            P("head", "ctx"),
            P("ctx", "head"),
        ),
        check_vma=False,
    )
```

```python
from functools import partial

import jax
import jax.numpy as jnp
from jax import lax
from jax.experimental import pallas as pl
from jax.experimental.pallas import tpu as pltpu
from jax.sharding import PartitionSpec as P

DK = 128
DV = 128
AUX = 16
EPS = 1e-06
F32 = jnp.float32
BF16 = jnp.bfloat16
VMEM_LIMIT = 24 * 1024 * 1024


def dot(a, b, ca, cb):
    return lax.dot_general(a, b, (((ca,), (cb,)), ((), ())), preferred_element_type=F32)


def halves(x):
    high = x.astype(BF16)
    return high, (x - high.astype(F32)).astype(BF16)


def thirds(x):
    high = x.astype(BF16).astype(F32)
    middle = (x - high).astype(BF16).astype(F32)
    return high, middle, x - high - middle


def mm(a, b, ca=1, cb=0):
    left = jnp.concatenate([a[0], a[0], a[1]], axis=ca)
    right = jnp.concatenate([b[0], b[1], b[0]], axis=cb)
    return dot(left, right, ca, cb)


def cat(pairs, axis):
    return tuple(jnp.concatenate(parts, axis=axis) for parts in zip(*pairs))


def put(ref, i, pair):
    ref[i, 0], ref[i, 1] = pair


def get(ref, i):
    return ref[i, 0], ref[i, 1]


def iotas(rows, columns):
    shape = (rows, columns)
    return lax.broadcasted_iota(jnp.int32, shape, 0), lax.broadcasted_iota(jnp.int32, shape, 1)


def call(kernel, outs, n_in, smem=(), scratch=(), flops=0, inside=True, fetch=False):
    spec = lambda i: pl.BlockSpec(memory_space=pltpu.SMEM if i in smem else pltpu.VMEM)
    if inside:
        outs = jax.tree.map(lambda o: pltpu.VMEM(o.shape, o.dtype), outs)
    run = pl.pallas_call(
        kernel,
        out_shape=outs,
        in_specs=[spec(i) for i in range(n_in)],
        out_specs=jax.tree.map(lambda _: pl.BlockSpec(memory_space=pltpu.VMEM), outs),
        scratch_shapes=list(scratch),
        compiler_params=pltpu.CompilerParams(vmem_limit_bytes=VMEM_LIMIT),
        cost_estimate=pl.CostEstimate(flops=flops, bytes_accessed=0, transcendentals=0),
    )

    def placed(*args):
        hold = lambda x: pltpu.with_memory_space_constraint(x, pltpu.VMEM)
        return run(*(x if fetch or i in smem else hold(x) for i, x in enumerate(args)))

    return placed


def arr(dtype, *shape):
    return jax.ShapeDtypeStruct(shape, dtype)


class Plan:
    def __init__(self, n, tok, hv, hk):
        self.n, self.tok, self.hv, self.hk = n, tok, hv, hk
        self.mates = n // hv
        self.v_at = 2 * tok
        self.aux_at = 2 * tok + DV
        self.rows = self.aux_at + AUX
        self.groups = [[m * self.mates + b for m in range(hv)] for b in range(self.mates)]

    def key_head(self, head):
        return head * self.hk // self.hv

    def exchange(self, x):
        return lax.all_to_all(
            x, "ctx", split_axis=0, concat_axis=0, axis_index_groups=self.groups, tiled=True
        )

    def from_mate(self, x, d):
        s = self.mates
        pairs = [(i // s * s + (i + d) % s, i) for i in range(self.n)]
        return lax.ppermute(x, "ctx", pairs)


def aux_rows(rows, columns):
    row_ids = lax.broadcasted_iota(jnp.int32, (AUX, columns), 0)
    out = jnp.zeros((AUX, columns), F32)
    for i, part in enumerate(p for r in rows for p in thirds(r)):
        out = jnp.where(row_ids == i, part, out)
    return out.astype(BF16)


def pack_kernel(plan, q_ref, k_ref, v_ref, rate_ref, decay_ref, out_ref):
    tok = plan.tok
    for h in range(plan.hv):
        kh = plan.key_head(h)
        out_ref[h, :tok] = q_ref[:, kh * DK : (kh + 1) * DK]
        out_ref[h, tok : 2 * tok] = k_ref[:, kh * DK : (kh + 1) * DK]
        turned = jnp.transpose(v_ref[:, h * DV : (h + 1) * DV].astype(F32))
        out_ref[h, plan.v_at : plan.aux_at] = turned.astype(BF16)
        rows = [rate_ref[h : h + 1, :], decay_ref[h : h + 1, :]]
        out_ref[h, plan.aux_at :] = aux_rows(rows, tok)


def unit(x):
    scale = lax.rsqrt(jnp.sum(x * x, axis=1, keepdims=True) + EPS)
    return x * scale, scale


def segments(off_ref, positions):
    total = jnp.zeros(positions.shape, jnp.int32)
    for j in range(off_ref.shape[0] - 1):
        total = total + (off_ref[j] <= positions).astype(jnp.int32)
    return total


def to_columns(rows, tok):
    row_ids = lax.broadcasted_iota(jnp.int32, (tok, tok), 0)
    stacked = jnp.zeros((tok, tok), F32)
    for i, r in enumerate(rows):
        stacked = jnp.where(row_ids == i, r, stacked)
    turned = jnp.transpose(stacked)
    return [turned[:, i : i + 1] for i in range(len(rows))]


def to_rows(columns, tok):
    column_ids = lax.broadcasted_iota(jnp.int32, (tok, tok), 1)
    stacked = jnp.zeros((tok, tok), F32)
    for i, c in enumerate(columns):
        stacked = jnp.where(column_ids == i, c, stacked)
    turned = jnp.transpose(stacked)
    return [turned[i : i + 1, :] for i in range(len(columns))]


def scalings(plan, off_ref, chunks, auxes):
    tok = plan.tok
    rows, columns = iotas(tok, tok)
    upto = (rows <= columns).astype(BF16)
    sums = [dot(a, upto, 1, 0) for a in auxes]
    rates = [jnp.sum(a[0:3].astype(F32), axis=0, keepdims=True) for a in auxes]
    cumuls = [s[3:4] + s[4:5] + s[5:6] for s in sums]
    turned = to_columns(rates + cumuls, tok)
    out = []
    for i, c in enumerate(chunks):
        b_col, c_col = turned[i], turned[len(chunks) + i]
        c_row = cumuls[i]
        start = c * tok
        seg_col = segments(off_ref, start + rows[:, :1])
        seg_row = segments(off_ref, start + columns[:1, :])
        before = jnp.int32(0)
        last = jnp.int32(0)
        for j in range(off_ref.shape[0] - 1):
            before = before + (off_ref[j] <= start - 1).astype(jnp.int32)
            last = last + (off_ref[j] <= start + tok - 1).astype(jnp.int32)
        c_last = c_row[:, tok - 1 : tok]
        together = (seg_col == seg_row) & (rows >= columns)
        ratio = jnp.where(together, jnp.exp(jnp.where(together, c_col - c_row, 0.0)), 0.0)
        start_col = jnp.where(seg_col == before, jnp.exp(c_col), 0.0)
        end_col = jnp.where(seg_col == last, jnp.exp(c_last - c_col), 0.0)
        whole = jnp.where(last == before, jnp.exp(c_last), 0.0)
        out.append((rates[i], b_col, ratio, start_col, end_col, whole))
    return out


def inverses(lowers):
    size = lowers[0].shape[0]
    rows, columns = iotas(size, size)
    identity = (rows == columns).astype(F32)
    block = min(16, size)
    near = (rows // block) == (columns // block)
    powers = [jnp.where(near, -m, 0.0) for m in lowers]
    results = [identity + p for p in powers]
    split = [halves(p) for p in powers]
    powers = [mm(s, s) for s in split]
    reach = 2
    while reach < block:
        split = [halves(p) for p in powers]
        more = reach * 2 < block
        both = []
        for r, s in zip(results, split):
            left = halves(r)
            if more:
                left = cat([left, s], 0)
            both.append(mm(left, s))
        results = [r + b[:size] for r, b in zip(results, both)]
        if more:
            powers = [b[size:] for b in both]
        reach *= 2
    while block < size:
        across = ((rows // (2 * block)) == (columns // (2 * block))) & (
            (rows // block) > (columns // block)
        )
        split = [halves(r) for r in results]
        middle = [mm(halves(jnp.where(across, m, 0.0)), s) for m, s in zip(lowers, split)]
        results = [r - mm(s, halves(m)) for r, s, m in zip(results, split, middle)]
        block *= 2
    return results


def prepare_kernel(
    plan, off_ref, mate_ref, in_ref, link_ref, x_ref, a_ref, w_ref, q_ref, ratio_ref, u_ref, ol_ref
):
    tok = plan.tok
    rows, columns = iotas(tok, tok)
    identity = (lax.broadcasted_iota(jnp.int32, (DK, DK), 0) == lax.broadcasted_iota(jnp.int32, (DK, DK), 1)).astype(F32)
    mine = range(plan.hv)
    chunks = [mate_ref[0] + plan.mates * m for m in mine]
    scales = scalings(plan, off_ref, chunks, [in_ref[m, plan.aux_at :] for m in mine])
    qn = [unit(in_ref[m, :tok].astype(F32))[0] for m in mine]
    kn = [unit(in_ref[m, tok : 2 * tok].astype(F32))[0] for m in mine]
    kp = [halves(x) for x in kn]
    qp = [halves(x) for x in qn]
    dots = [mm(cat([q, k], 0), k, 1, 1) for q, k in zip(qp, kp)]
    strict = rows > columns
    lowers = [jnp.where(strict, s[1] * d[tok:] * s[2], 0.0) for s, d in zip(scales, dots)]
    scores = [d[:tok] * s[2] for s, d in zip(scales, dots)]
    inv = inverses(lowers)
    rated = [halves(x * s[0]) for x, s in zip(inv, scales)]
    w = [mm(x, halves(s[3] * k)) for x, s, k in zip(rated, scales, kn)]
    values = [in_ref[m, plan.v_at : plan.aux_at] for m in mine]
    u = [
        dot(jnp.concatenate([v, v], axis=1), jnp.concatenate(x, axis=1), 1, 1)
        for v, x in zip(values, rated)
    ]
    wp = [halves(x) for x in w]
    up = [halves(x) for x in u]
    ap = [halves(x) for x in scores]
    ke = [halves(s[4] * k) for s, k in zip(scales, kn)]
    for m in mine:
        link_ref[m, 0] = scales[m][5] * identity - mm(wp[m], ke[m], 0, 0)
        link_ref[m, 1] = mm(up[m], ke[m])
    for m in mine:
        put(x_ref, m, halves(inv[m]))
        put(a_ref, m, ap[m])
        put(w_ref, m, wp[m])
        put(q_ref, m, halves(scales[m][3] * qn[m] - mm(ap[m], wp[m])))
        ratio_ref[m] = scales[m][2]
        u_ref[m] = u[m]
        ol_ref[m] = mm(up[m], ap[m], 1, 1)


def lay_out(plan, mate, refs, all_ref):
    for d, ref in enumerate(refs):
        all_ref[lax.rem(mate + d, plan.mates)] = ref[...]


def scan_kernel(plan, mate_ref, *refs):
    s = plan.mates
    links, (cot_ref, q_ref, ol_ref, out_ref, s_ref, back_ref, all_ref, states_ref) = refs[:s], refs[s:]
    mate = mate_ref[0]
    lay_out(plan, mate, links, all_ref)
    state = jnp.zeros((DV, DK), F32)
    for c in range(plan.n):
        states_ref[c] = state
        if c < plan.n - 1:
            link = all_ref.at[c % s, c // s]
            state = link[1] + mm(halves(state), halves(link[0]))
    for m in range(plan.hv):
        state = states_ref[mate + s * m]
        s_ref[m] = state
        core = (ol_ref[m] + mm(halves(state), get(q_ref, m), 1, 1)).astype(BF16)
        for g in range(plan.hv):
            out_ref[g, (m - g) % plan.hv] = core
        back_ref[m] = mm(d_out(cot_ref, m), get(q_ref, m))


def d_out(cot_ref, m):
    return cot_ref[m, :DV], cot_ref[m, DV : 2 * DV]


def backward_kernel(plan, off_ref, mate_ref, *refs):
    s, n, tok = plan.mates, plan.n, plan.tok
    links, backs, refs = refs[:s], refs[s : 2 * s], refs[2 * s :]
    in_ref, cot_ref, x_ref, a_ref, w_ref, ratio_ref, u_ref, s_ref, out_ref = refs[:9]
    links_ref, backs_ref, cots_ref = refs[9:]
    mate = mate_ref[0]
    lay_out(plan, mate, links, links_ref)
    lay_out(plan, mate, backs, backs_ref)
    d_state = jnp.zeros((DV, DK), F32)
    for c in reversed(range(n)):
        cots_ref[c] = d_state
        if c:
            d_state = backs_ref[c % s, c // s] + mm(
                halves(d_state), halves(links_ref[c % s, c // s, 0]), 1, 1
            )
    rows, columns = iotas(tok, tok)
    strict = rows > columns
    upto = (rows >= columns).astype(BF16)
    mine = range(plan.hv)
    chunks = [mate + s * m for m in mine]
    scales = scalings(plan, off_ref, chunks, [in_ref[m, plan.aux_at :] for m in mine])
    qu = [unit(in_ref[m, :tok].astype(F32)) for m in mine]
    ku = [unit(in_ref[m, tok : 2 * tok].astype(F32)) for m in mine]
    qp = [halves(x[0]) for x in qu]
    kp = [halves(x[0]) for x in ku]
    do = [d_out(cot_ref, m) for m in mine]
    s0 = [s_ref[m] for m in mine]
    ds = [cots_ref[c] for c in chunks]
    s0p = [halves(x) for x in s0]
    dsp = [halves(x) for x in ds]
    pseudo = [u_ref[m] - mm(s0p[m], get(w_ref, m), 1, 1) for m in mine]
    pp = [halves(x) for x in pseudo]
    ke = [halves(s[4] * k[0]) for s, k in zip(scales, ku)]
    dp = [mm(do[m], get(a_ref, m)) + mm(dsp[m], ke[m], 1, 1) for m in mine]
    dr = [mm(halves(dp[m]), get(x_ref, m)) for m in mine]
    drp = [halves(x) for x in dr]
    big = [mm(cat([o, r], 1), cat([p, s], 1), 0, 0) for o, r, p, s in zip(do, drp, pp, s0p)]
    pds = [mm(p, d, 0, 0) for p, d in zip(pp, dsp)]
    da = [big[m][:tok, :tok] * ratio_ref[m] for m in mine]
    dm = [jnp.where(strict, -big[m][tok:, :tok] * ratio_ref[m], 0.0) for m in mine]
    dap = [halves(x) for x in da]
    dmp = [halves(x) for x in dm]
    dbm = [halves(s[1] * x) for s, x in zip(scales, dm)]
    by_row = [mm(cat([x, y], 0), k) for x, y, k in zip(dap, dmp, kp)]
    by_column = [
        mm(cat([x, y], 0), cat([q, k], 0), 0, 0) for x, y, q, k in zip(dap, dbm, qp, kp)
    ]
    sums = []
    for m in mine:
        _, b_col, _, start_col, end_col, whole = scales[m]
        (qn, q_scale), (kn, k_scale) = qu[m], ku[m]
        dqn = by_row[m][:tok] + start_col * big[m][:tok, tok:]
        erase = by_row[m][tok:] - start_col * big[m][tok:, tok:]
        ends = end_col * pds[m]
        write = by_column[m] + ends
        dkn = b_col * erase + write
        s_q = jnp.sum(qn * dqn, axis=1, keepdims=True)
        s_e = jnp.sum(kn * erase, axis=1, keepdims=True)
        s_w = jnp.sum(kn * write, axis=1, keepdims=True)
        total = jnp.sum(jnp.sum(kn * ends, axis=1, keepdims=True), axis=0, keepdims=True)
        both = jnp.sum(jnp.sum(s0[m] * ds[m], axis=1, keepdims=True), axis=0, keepdims=True)
        out_ref[m, :tok] = (q_scale * (dqn - qn * s_q)).astype(BF16)
        out_ref[m, tok : 2 * tok] = (k_scale * (dkn - kn * (b_col * s_e + s_w))).astype(BF16)
        out_ref[m, plan.v_at : plan.aux_at] = (scales[m][0] * dr[m]).astype(BF16)
        sums.append((s_e, s_q + b_col * s_e - s_w, total + whole * both))
    turned = to_rows([s[0] for s in sums] + [s[1] for s in sums], tok)
    for m in mine:
        values = in_ref[m, plan.v_at : plan.aux_at].astype(F32)
        d_rate = turned[m] + jnp.sum(dr[m] * values, axis=0, keepdims=True)
        parts = dot(aux_rows([turned[plan.hv + m]], tok), upto, 1, 0)
        d_decay = parts[0:1] + parts[1:2] + parts[2:3] + sums[m][2]
        out_ref[m, plan.aux_at :] = aux_rows([d_rate, d_decay], tok)


def cotangent_kernel(plan, parts, head_ref, *refs):
    pieces, (w_ref, out_ref, all_ref) = refs[:parts], refs[parts:]
    rows = pieces[0].shape[0]
    for d in range(parts):
        at = lax.rem(head_ref[0] + d, parts)
        all_ref[pl.ds(pl.multiple_of(at * rows, rows), rows), :] = pieces[d][...]
    whole = all_ref[...]
    share = whole.shape[1] // plan.hv
    high, low = halves(dot(w_ref[...], whole, 1, 1))
    for m in range(plan.hv):
        out_ref[m, :DV] = high[m * DV : (m + 1) * DV]
        out_ref[m, DV : 2 * DV] = low[m * DV : (m + 1) * DV]
        turned = jnp.transpose(whole[:, m * share : (m + 1) * share].astype(F32))
        out_ref[m, 2 * DV :] = turned.astype(BF16)


def project_kernel(plan, parts, head_ref, mixed_ref, w_ref, *refs):
    outs, total_ref = refs[:parts], refs[parts]
    mixed = jnp.concatenate([mixed_ref[g, 0] for g in range(plan.hv)], axis=0)
    total_ref[...] = dot(mixed, w_ref[...], 0, 0)
    rows = outs[0].shape[0]
    for d in range(parts):
        at = lax.rem(head_ref[0] + parts - d, parts)
        block = total_ref[pl.ds(pl.multiple_of(at * rows, rows), rows), :]
        outs[d][...] = block.astype(outs[d].dtype)


def weight_kernel(plan, place_ref, mate_ref, cot_ref, mixed_ref, *outs):
    share = outs[0].shape[0]
    mixed = [
        jnp.concatenate([mixed_ref[g, step] for g in range(plan.hv)], axis=0)
        for step in range(plan.hv)
    ]
    for d, out_ref in enumerate(outs):
        at = lax.rem(mate_ref[0] + plan.mates - d, plan.mates)
        at = pl.multiple_of(2 * DV + at * share, share)
        total = None
        for step in range(plan.hv):
            chunk = lax.rem(place_ref[0] + step, plan.hv)
            part = dot(cot_ref[chunk, pl.ds(at, share), :], mixed[step], 1, 1)
            total = part if total is None else total + part
        out_ref[...] = total


def finish_kernel(plan, in_ref, q_ref, k_ref, v_ref, rate_ref, decay_ref):
    tok = plan.tok
    for kh in range(plan.hk):
        mine = [h for h in range(plan.hv) if plan.key_head(h) == kh]
        for ref, at in ((q_ref, 0), (k_ref, tok)):
            total = in_ref[mine[0], at : at + tok].astype(F32)
            for h in mine[1:]:
                total = total + in_ref[h, at : at + tok].astype(F32)
            ref[:, kh * DK : (kh + 1) * DK] = total
    for h in range(plan.hv):
        v_ref[:, h * DV : (h + 1) * DV] = jnp.transpose(
            in_ref[h, plan.v_at : plan.aux_at].astype(F32)
        )
        aux = in_ref[h, plan.aux_at :].astype(F32)
        rate_ref[h : h + 1, :] = aux[0:1] + aux[1:2] + aux[2:3]
        decay_ref[h : h + 1, :] = aux[3:4] + aux[4:5] + aux[5:6]


def per_device(
    queries, key_vectors, value_rows, write_rate, log_decay, doc_offsets, out_weight, grad_out
):
    n, parts = lax.axis_size("ctx"), lax.axis_size("head")
    tok, hv = queries.shape[0], write_rate.shape[0]
    hk, model = queries.shape[1] // DK, grad_out.shape[1]
    plan = Plan(n, tok, hv, hk)
    s = plan.mates
    index = lax.axis_index("ctx").astype(jnp.int32)
    place, mate = (index // s).reshape(1), (index % s).reshape(1)
    head = lax.axis_index("head").astype(jnp.int32).reshape(1)

    def from_head(x, d):
        return lax.ppermute(x, "head", [((i + d) % parts, i) for i in range(parts)])

    pieces = [grad_out] + [from_head(grad_out, d) for d in range(1, parts)]

    sent = call(partial(pack_kernel, plan), arr(BF16, hv, plan.rows, DK), 5, flops=20_000_000_000, fetch=True)(
        queries, key_vectors, value_rows, write_rate, log_decay
    )
    got = plan.exchange(sent)

    cot_sent = call(
        partial(cotangent_kernel, plan, parts),
        arr(BF16, hv, 2 * DV + model // hv, tok),
        parts + 2,
        smem=(0,),
        scratch=[pltpu.VMEM((tok, model), BF16)],
        flops=4_000_000_000,
    )(head, *pieces, out_weight)
    cot = plan.exchange(cot_sent)

    pair = lambda r, c: arr(BF16, hv, 2, r, c)
    link, x, a, w, q, ratio, u, ol = call(
        partial(prepare_kernel, plan),
        (
            arr(F32, hv, 2, DK, DK),
            pair(tok, tok),
            pair(tok, tok),
            pair(tok, DK),
            pair(tok, DK),
            arr(F32, hv, tok, tok),
            arr(F32, hv, DV, tok),
            arr(F32, hv, DV, tok),
        ),
        3,
        smem=(0, 1),
        flops=6_000_000_000,
    )(doc_offsets, mate, got)
    links = [link] + [plan.from_mate(link, d) for d in range(1, s)]
    out, states, back = call(
        partial(scan_kernel, plan),
        (arr(BF16, hv, hv, DV, tok), arr(F32, hv, DV, DK), arr(F32, hv, DV, DK)),
        s + 4,
        smem=(0,),
        scratch=[pltpu.VMEM((s, hv, 2, DK, DK), F32), pltpu.VMEM((n, DV, DK), F32)],
        flops=4_000_000_000,
    )(mate, *links, cot, q, ol)
    mixed = plan.exchange(out)
    backs = [back] + [plan.from_mate(back, d) for d in range(1, s)]

    grad_sent = call(
        partial(backward_kernel, plan),
        arr(BF16, hv, plan.rows, DK),
        2 * s + 10,
        smem=(0, 1),
        scratch=[
            pltpu.VMEM((s, hv, 2, DK, DK), F32),
            pltpu.VMEM((s, hv, DV, DK), F32),
            pltpu.VMEM((n, DV, DK), F32),
        ],
        flops=20_000_000_000,
    )(doc_offsets, mate, *links, *backs, got, cot, x, a, w, ratio, u, states)

    rows = tok // parts
    projected = call(
        partial(project_kernel, plan, parts),
        [arr(BF16 if d else F32, rows, model) for d in range(parts)],
        3,
        smem=(0,),
        scratch=[pltpu.VMEM((tok, model), F32)],
        flops=3_000_000_000,
    )(head, mixed, out_weight)
    layer_out = projected[0]
    for d in range(1, parts):
        layer_out = layer_out + from_head(projected[d], d).astype(F32)

    shares = call(
        partial(weight_kernel, plan), [arr(F32, model // n, hv * DV)] * s, 4, smem=(0, 1), flops=3_000_000_000
    )(place, mate, cot, mixed)
    weight_grad = shares[0]
    for d in range(1, s):
        weight_grad = weight_grad + plan.from_mate(shares[d], d)

    grads = plan.exchange(grad_sent)
    grad_q, grad_k, grad_v, grad_rate, grad_decay = call(
        partial(finish_kernel, plan),
        (
            arr(F32, tok, hk * DK),
            arr(F32, tok, hk * DK),
            arr(F32, tok, hv * DV),
            arr(F32, hv, tok),
            arr(F32, hv, tok),
        ),
        1,
        flops=2_000_000_000,
        inside=False,
    )(grads)
    return (layer_out, grad_q, grad_k, grad_v, grad_rate, grad_decay, weight_grad)


def solution(mesh):
    placed = (
        P("ctx", "head"),
        P("ctx", "head"),
        P("ctx", "head"),
        P("head", "ctx"),
        P("head", "ctx"),
        P(),
        P("head", None),
        P(("ctx", "head"), None),
    )
    return jax.shard_map(
        per_device,
        mesh=mesh,
        in_specs=placed,
        out_specs=(
            P(("ctx", "head"), None),
            P("ctx", "head"),
            P("ctx", "head"),
            P("ctx", "head"),
            P("head", "ctx"),
            P("head", "ctx"),
            P("ctx", "head"),
        ),
        check_vma=False,
    )
```

```python
import math
from functools import partial

import jax
import jax.numpy as jnp
from jax import lax
from jax.experimental import pallas as pl
from jax.experimental.pallas import tpu as pltpu
from jax.sharding import PartitionSpec as P

DK = 128
DV = 128
AUX = 16
EPS = 1e-06
F32 = jnp.float32
BF16 = jnp.bfloat16
SPARE_VMEM = 8 * 1024 * 1024


def dot(a, b, ca, cb):
    return lax.dot_general(a, b, (((ca,), (cb,)), ((), ())), preferred_element_type=F32)


def halves(x):
    high = x.astype(BF16)
    return high, (x - high.astype(F32)).astype(BF16)


def thirds(x):
    high = x.astype(BF16).astype(F32)
    middle = (x - high).astype(BF16).astype(F32)
    return high, middle, x - high - middle


def mm(a, b, ca=1, cb=0):
    left = jnp.concatenate([a[0], a[0], a[1]], axis=ca)
    right = jnp.concatenate([b[0], b[1], b[0]], axis=cb)
    return dot(left, right, ca, cb)


def cat(pairs, axis):
    return tuple(jnp.concatenate(parts, axis=axis) for parts in zip(*pairs))


def put(ref, i, pair):
    ref[i, 0], ref[i, 1] = pair


def get(ref, i):
    return ref[i, 0], ref[i, 1]


def iotas(rows, columns):
    shape = (rows, columns)
    return lax.broadcasted_iota(jnp.int32, shape, 0), lax.broadcasted_iota(jnp.int32, shape, 1)


def call(kernel, outs, n_in, smem=(), scratch=(), flops=0, inside=True, fetch=False):
    spec = lambda i: pl.BlockSpec(memory_space=pltpu.SMEM if i in smem else pltpu.VMEM)
    if inside:
        outs = jax.tree.map(lambda o: pltpu.VMEM(o.shape, o.dtype), outs)
    run = pl.pallas_call(
        kernel,
        out_shape=outs,
        in_specs=[spec(i) for i in range(n_in)],
        out_specs=jax.tree.map(lambda _: pl.BlockSpec(memory_space=pltpu.VMEM), outs),
        scratch_shapes=list(scratch),
        compiler_params=pltpu.CompilerParams(
            vmem_limit_bytes=SPARE_VMEM + sum(x.dtype.itemsize * math.prod(x.shape) for x in scratch)
        ),
        cost_estimate=pl.CostEstimate(flops=flops, bytes_accessed=0, transcendentals=0),
    )

    def placed(*args):
        space = pltpu.HBM if fetch else pltpu.VMEM
        hold = lambda x: pltpu.with_memory_space_constraint(x, space)
        return run(*(x if i in smem else hold(x) for i, x in enumerate(args)))

    return placed


def arr(dtype, *shape):
    return jax.ShapeDtypeStruct(shape, dtype)


class Plan:
    def __init__(self, n, tok, hv, hk):
        self.n, self.tok, self.hv, self.hk = n, tok, hv, hk
        self.mates = n // hv
        self.v_at = 2 * tok
        self.aux_at = 2 * tok + DV
        self.rows = self.aux_at + AUX
        self.groups = [[m * self.mates + b for m in range(hv)] for b in range(self.mates)]

    def key_head(self, head):
        return head * self.hk // self.hv

    def exchange(self, x):
        return lax.all_to_all(
            x, "ctx", split_axis=0, concat_axis=0, axis_index_groups=self.groups, tiled=True
        )

    def from_mate(self, x, d):
        s = self.mates
        pairs = [(i // s * s + (i + d) % s, i) for i in range(self.n)]
        return lax.ppermute(x, "ctx", pairs)


def aux_rows(rows, columns):
    row_ids = lax.broadcasted_iota(jnp.int32, (AUX, columns), 0)
    out = jnp.zeros((AUX, columns), F32)
    for i, part in enumerate(p for r in rows for p in thirds(r)):
        out = jnp.where(row_ids == i, part, out)
    return out.astype(BF16)


def pack_kernel(plan, q_ref, k_ref, v_ref, rate_ref, decay_ref, out_ref):
    tok = plan.tok
    for h in range(plan.hv):
        kh = plan.key_head(h)
        out_ref[h, :tok] = q_ref[:, kh * DK : (kh + 1) * DK]
        out_ref[h, tok : 2 * tok] = k_ref[:, kh * DK : (kh + 1) * DK]
        turned = jnp.transpose(v_ref[:, h * DV : (h + 1) * DV].astype(F32))
        out_ref[h, plan.v_at : plan.aux_at] = turned.astype(BF16)
        rows = [rate_ref[h : h + 1, :], decay_ref[h : h + 1, :]]
        out_ref[h, plan.aux_at :] = aux_rows(rows, tok)


def unit(x):
    scale = lax.rsqrt(jnp.sum(x * x, axis=1, keepdims=True) + EPS)
    return x * scale, scale


def segments(off_ref, positions):
    total = jnp.zeros(positions.shape, jnp.int32)
    for j in range(off_ref.shape[0] - 1):
        total = total + (off_ref[j] <= positions).astype(jnp.int32)
    return total


def to_columns(rows, tok):
    row_ids = lax.broadcasted_iota(jnp.int32, (tok, tok), 0)
    stacked = jnp.zeros((tok, tok), F32)
    for i, r in enumerate(rows):
        stacked = jnp.where(row_ids == i, r, stacked)
    turned = jnp.transpose(stacked)
    return [turned[:, i : i + 1] for i in range(len(rows))]


def to_rows(columns, tok):
    column_ids = lax.broadcasted_iota(jnp.int32, (tok, tok), 1)
    stacked = jnp.zeros((tok, tok), F32)
    for i, c in enumerate(columns):
        stacked = jnp.where(column_ids == i, c, stacked)
    turned = jnp.transpose(stacked)
    return [turned[i : i + 1, :] for i in range(len(columns))]


def scalings(plan, off_ref, chunks, auxes):
    tok = plan.tok
    rows, columns = iotas(tok, tok)
    upto = (rows <= columns).astype(BF16)
    sums = [dot(a, upto, 1, 0) for a in auxes]
    rates = [jnp.sum(a[0:3].astype(F32), axis=0, keepdims=True) for a in auxes]
    cumuls = [s[3:4] + s[4:5] + s[5:6] for s in sums]
    turned = to_columns(rates + cumuls, tok)
    out = []
    for i, c in enumerate(chunks):
        b_col, c_col = turned[i], turned[len(chunks) + i]
        c_row = cumuls[i]
        start = c * tok
        seg_col = segments(off_ref, start + rows[:, :1])
        seg_row = segments(off_ref, start + columns[:1, :])
        before = jnp.int32(0)
        last = jnp.int32(0)
        for j in range(off_ref.shape[0] - 1):
            before = before + (off_ref[j] <= start - 1).astype(jnp.int32)
            last = last + (off_ref[j] <= start + tok - 1).astype(jnp.int32)
        c_last = c_row[:, tok - 1 : tok]
        together = (seg_col == seg_row) & (rows >= columns)
        ratio = jnp.where(together, jnp.exp(jnp.where(together, c_col - c_row, 0.0)), 0.0)
        start_col = jnp.where(seg_col == before, jnp.exp(c_col), 0.0)
        end_col = jnp.where(seg_col == last, jnp.exp(c_last - c_col), 0.0)
        whole = jnp.where(last == before, jnp.exp(c_last), 0.0)
        out.append((rates[i], b_col, ratio, start_col, end_col, whole))
    return out


def inverses(lowers):
    size = lowers[0].shape[0]
    rows, columns = iotas(size, size)
    identity = (rows == columns).astype(F32)
    block = min(16, size)
    near = (rows // block) == (columns // block)
    powers = [jnp.where(near, -m, 0.0) for m in lowers]
    results = [identity + p for p in powers]
    split = [halves(p) for p in powers]
    powers = [mm(s, s) for s in split]
    reach = 2
    while reach < block:
        split = [halves(p) for p in powers]
        more = reach * 2 < block
        both = []
        for r, s in zip(results, split):
            left = halves(r)
            if more:
                left = cat([left, s], 0)
            both.append(mm(left, s))
        results = [r + b[:size] for r, b in zip(results, both)]
        if more:
            powers = [b[size:] for b in both]
        reach *= 2
    while block < size:
        across = ((rows // (2 * block)) == (columns // (2 * block))) & (
            (rows // block) > (columns // block)
        )
        split = [halves(r) for r in results]
        middle = [mm(halves(jnp.where(across, m, 0.0)), s) for m, s in zip(lowers, split)]
        results = [r - mm(s, halves(m)) for r, s, m in zip(results, split, middle)]
        block *= 2
    return results


def prepare_kernel(
    plan, off_ref, mate_ref, in_ref, link_ref, x_ref, a_ref, w_ref, q_ref, ratio_ref, u_ref, ol_ref
):
    tok = plan.tok
    rows, columns = iotas(tok, tok)
    identity = (lax.broadcasted_iota(jnp.int32, (DK, DK), 0) == lax.broadcasted_iota(jnp.int32, (DK, DK), 1)).astype(F32)
    mine = range(plan.hv)
    chunks = [mate_ref[0] + plan.mates * m for m in mine]
    scales = scalings(plan, off_ref, chunks, [in_ref[m, plan.aux_at :] for m in mine])
    qn = [unit(in_ref[m, :tok].astype(F32))[0] for m in mine]
    kn = [unit(in_ref[m, tok : 2 * tok].astype(F32))[0] for m in mine]
    kp = [halves(x) for x in kn]
    qp = [halves(x) for x in qn]
    dots = [mm(cat([q, k], 0), k, 1, 1) for q, k in zip(qp, kp)]
    strict = rows > columns
    lowers = [jnp.where(strict, s[1] * d[tok:] * s[2], 0.0) for s, d in zip(scales, dots)]
    scores = [d[:tok] * s[2] for s, d in zip(scales, dots)]
    inv = inverses(lowers)
    rated = [halves(x * s[0]) for x, s in zip(inv, scales)]
    w = [mm(x, halves(s[3] * k)) for x, s, k in zip(rated, scales, kn)]
    values = [in_ref[m, plan.v_at : plan.aux_at] for m in mine]
    u = [
        dot(jnp.concatenate([v, v], axis=1), jnp.concatenate(x, axis=1), 1, 1)
        for v, x in zip(values, rated)
    ]
    wp = [halves(x) for x in w]
    up = [halves(x) for x in u]
    ap = [halves(x) for x in scores]
    ke = [halves(s[4] * k) for s, k in zip(scales, kn)]
    for m in mine:
        link_ref[m, 0] = scales[m][5] * identity - mm(wp[m], ke[m], 0, 0)
        link_ref[m, 1] = mm(up[m], ke[m])
    for m in mine:
        put(x_ref, m, halves(inv[m]))
        put(a_ref, m, ap[m])
        put(w_ref, m, wp[m])
        put(q_ref, m, halves(scales[m][3] * qn[m] - mm(ap[m], wp[m])))
        ratio_ref[m] = scales[m][2]
        u_ref[m] = u[m]
        ol_ref[m] = mm(up[m], ap[m], 1, 1)


def lay_out(plan, mate, refs, all_ref):
    for d, ref in enumerate(refs):
        all_ref[lax.rem(mate + d, plan.mates)] = ref[...]


def scan_kernel(plan, mate_ref, *refs):
    s = plan.mates
    links, (cot_ref, q_ref, ol_ref, out_ref, s_ref, back_ref, all_ref, states_ref) = refs[:s], refs[s:]
    mate = mate_ref[0]
    lay_out(plan, mate, links, all_ref)
    state = jnp.zeros((DV, DK), F32)
    for c in range(plan.n):
        states_ref[c] = state
        if c < plan.n - 1:
            link = all_ref.at[c % s, c // s]
            state = link[1] + mm(halves(state), halves(link[0]))
    for m in range(plan.hv):
        state = states_ref[mate + s * m]
        s_ref[m] = state
        core = (ol_ref[m] + mm(halves(state), get(q_ref, m), 1, 1)).astype(BF16)
        for g in range(plan.hv):
            out_ref[g, (m - g) % plan.hv] = core
        back_ref[m] = mm(d_out(cot_ref, m), get(q_ref, m))


def d_out(cot_ref, m):
    return cot_ref[m, :DV], cot_ref[m, DV : 2 * DV]


def backward_kernel(plan, off_ref, mate_ref, *refs):
    s, n, tok = plan.mates, plan.n, plan.tok
    links, backs, refs = refs[:s], refs[s : 2 * s], refs[2 * s :]
    in_ref, cot_ref, x_ref, a_ref, w_ref, ratio_ref, u_ref, s_ref, out_ref = refs[:9]
    links_ref, backs_ref, cots_ref = refs[9:]
    mate = mate_ref[0]
    lay_out(plan, mate, links, links_ref)
    lay_out(plan, mate, backs, backs_ref)
    d_state = jnp.zeros((DV, DK), F32)
    for c in reversed(range(n)):
        cots_ref[c] = d_state
        if c:
            d_state = backs_ref[c % s, c // s] + mm(
                halves(d_state), halves(links_ref[c % s, c // s, 0]), 1, 1
            )
    rows, columns = iotas(tok, tok)
    strict = rows > columns
    upto = (rows >= columns).astype(BF16)
    mine = range(plan.hv)
    chunks = [mate + s * m for m in mine]
    scales = scalings(plan, off_ref, chunks, [in_ref[m, plan.aux_at :] for m in mine])
    qu = [unit(in_ref[m, :tok].astype(F32)) for m in mine]
    ku = [unit(in_ref[m, tok : 2 * tok].astype(F32)) for m in mine]
    qp = [halves(x[0]) for x in qu]
    kp = [halves(x[0]) for x in ku]
    do = [d_out(cot_ref, m) for m in mine]
    s0 = [s_ref[m] for m in mine]
    ds = [cots_ref[c] for c in chunks]
    s0p = [halves(x) for x in s0]
    dsp = [halves(x) for x in ds]
    pseudo = [u_ref[m] - mm(s0p[m], get(w_ref, m), 1, 1) for m in mine]
    pp = [halves(x) for x in pseudo]
    ke = [halves(s[4] * k[0]) for s, k in zip(scales, ku)]
    dp = [mm(do[m], get(a_ref, m)) + mm(dsp[m], ke[m], 1, 1) for m in mine]
    dr = [mm(halves(dp[m]), get(x_ref, m)) for m in mine]
    drp = [halves(x) for x in dr]
    big = [mm(cat([o, r], 1), cat([p, s], 1), 0, 0) for o, r, p, s in zip(do, drp, pp, s0p)]
    pds = [mm(p, d, 0, 0) for p, d in zip(pp, dsp)]
    da = [big[m][:tok, :tok] * ratio_ref[m] for m in mine]
    dm = [jnp.where(strict, -big[m][tok:, :tok] * ratio_ref[m], 0.0) for m in mine]
    dap = [halves(x) for x in da]
    dmp = [halves(x) for x in dm]
    dbm = [halves(s[1] * x) for s, x in zip(scales, dm)]
    by_row = [mm(cat([x, y], 0), k) for x, y, k in zip(dap, dmp, kp)]
    by_column = [
        mm(cat([x, y], 0), cat([q, k], 0), 0, 0) for x, y, q, k in zip(dap, dbm, qp, kp)
    ]
    sums = []
    for m in mine:
        _, b_col, _, start_col, end_col, whole = scales[m]
        (qn, q_scale), (kn, k_scale) = qu[m], ku[m]
        dqn = by_row[m][:tok] + start_col * big[m][:tok, tok:]
        erase = by_row[m][tok:] - start_col * big[m][tok:, tok:]
        ends = end_col * pds[m]
        write = by_column[m] + ends
        dkn = b_col * erase + write
        s_q = jnp.sum(qn * dqn, axis=1, keepdims=True)
        s_e = jnp.sum(kn * erase, axis=1, keepdims=True)
        s_w = jnp.sum(kn * write, axis=1, keepdims=True)
        total = jnp.sum(jnp.sum(kn * ends, axis=1, keepdims=True), axis=0, keepdims=True)
        both = jnp.sum(jnp.sum(s0[m] * ds[m], axis=1, keepdims=True), axis=0, keepdims=True)
        out_ref[m, :tok] = (q_scale * (dqn - qn * s_q)).astype(BF16)
        out_ref[m, tok : 2 * tok] = (k_scale * (dkn - kn * (b_col * s_e + s_w))).astype(BF16)
        out_ref[m, plan.v_at : plan.aux_at] = (scales[m][0] * dr[m]).astype(BF16)
        sums.append((s_e, s_q + b_col * s_e - s_w, total + whole * both))
    turned = to_rows([s[0] for s in sums] + [s[1] for s in sums], tok)
    for m in mine:
        values = in_ref[m, plan.v_at : plan.aux_at].astype(F32)
        d_rate = turned[m] + jnp.sum(dr[m] * values, axis=0, keepdims=True)
        parts = dot(aux_rows([turned[plan.hv + m]], tok), upto, 1, 0)
        d_decay = parts[0:1] + parts[1:2] + parts[2:3] + sums[m][2]
        out_ref[m, plan.aux_at :] = aux_rows([d_rate, d_decay], tok)


def cotangent_kernel(plan, parts, head_ref, *refs):
    pieces, (w_ref, out_ref, all_ref) = refs[:parts], refs[parts:]
    rows = pieces[0].shape[0]
    for d in range(parts):
        at = lax.rem(head_ref[0] + d, parts)
        all_ref[pl.ds(pl.multiple_of(at * rows, rows), rows), :] = pieces[d][...]
    whole = all_ref[...]
    share = whole.shape[1] // plan.hv
    high, low = halves(dot(w_ref[...], whole, 1, 1))
    for m in range(plan.hv):
        out_ref[m, :DV] = high[m * DV : (m + 1) * DV]
        out_ref[m, DV : 2 * DV] = low[m * DV : (m + 1) * DV]
        turned = jnp.transpose(whole[:, m * share : (m + 1) * share].astype(F32))
        out_ref[m, 2 * DV :] = turned.astype(BF16)


def project_kernel(plan, parts, head_ref, mixed_ref, w_ref, *refs):
    outs, total_ref = refs[:parts], refs[parts]
    mixed = jnp.concatenate([mixed_ref[g, 0] for g in range(plan.hv)], axis=0)
    total_ref[...] = dot(mixed, w_ref[...], 0, 0)
    rows = outs[0].shape[0]
    for d in range(parts):
        at = lax.rem(head_ref[0] + parts - d, parts)
        block = total_ref[pl.ds(pl.multiple_of(at * rows, rows), rows), :]
        outs[d][...] = block.astype(outs[d].dtype)


def weight_kernel(plan, place_ref, mate_ref, cot_ref, mixed_ref, *outs):
    share = outs[0].shape[0]
    mixed = [
        jnp.concatenate([mixed_ref[g, step] for g in range(plan.hv)], axis=0)
        for step in range(plan.hv)
    ]
    for d, out_ref in enumerate(outs):
        at = lax.rem(mate_ref[0] + plan.mates - d, plan.mates)
        at = pl.multiple_of(2 * DV + at * share, share)
        total = None
        for step in range(plan.hv):
            chunk = lax.rem(place_ref[0] + step, plan.hv)
            part = dot(cot_ref[chunk, pl.ds(at, share), :], mixed[step], 1, 1)
            total = part if total is None else total + part
        out_ref[...] = total


def finish_kernel(plan, in_ref, q_ref, k_ref, v_ref, rate_ref, decay_ref):
    tok = plan.tok
    for kh in range(plan.hk):
        mine = [h for h in range(plan.hv) if plan.key_head(h) == kh]
        for ref, at in ((q_ref, 0), (k_ref, tok)):
            total = in_ref[mine[0], at : at + tok].astype(F32)
            for h in mine[1:]:
                total = total + in_ref[h, at : at + tok].astype(F32)
            ref[:, kh * DK : (kh + 1) * DK] = total
    for h in range(plan.hv):
        v_ref[:, h * DV : (h + 1) * DV] = jnp.transpose(
            in_ref[h, plan.v_at : plan.aux_at].astype(F32)
        )
        aux = in_ref[h, plan.aux_at :].astype(F32)
        rate_ref[h : h + 1, :] = aux[0:1] + aux[1:2] + aux[2:3]
        decay_ref[h : h + 1, :] = aux[3:4] + aux[4:5] + aux[5:6]


def per_device(
    queries, key_vectors, value_rows, write_rate, log_decay, doc_offsets, out_weight, grad_out
):
    n, parts = lax.axis_size("ctx"), lax.axis_size("head")
    tok, hv = queries.shape[0], write_rate.shape[0]
    hk, model = queries.shape[1] // DK, grad_out.shape[1]
    plan = Plan(n, tok, hv, hk)
    s = plan.mates
    index = lax.axis_index("ctx").astype(jnp.int32)
    place, mate = (index // s).reshape(1), (index % s).reshape(1)
    head = lax.axis_index("head").astype(jnp.int32).reshape(1)

    def from_head(x, d):
        return lax.ppermute(x, "head", [((i + d) % parts, i) for i in range(parts)])

    pieces = [grad_out] + [from_head(grad_out, d) for d in range(1, parts)]

    sent = call(partial(pack_kernel, plan), arr(BF16, hv, plan.rows, DK), 5, flops=20_000_000_000, fetch=True)(
        queries, key_vectors, value_rows, write_rate, log_decay
    )
    got = plan.exchange(sent)

    cot_sent = call(
        partial(cotangent_kernel, plan, parts),
        arr(BF16, hv, 2 * DV + model // hv, tok),
        parts + 2,
        smem=(0,),
        scratch=[pltpu.VMEM((tok, model), BF16)],
        flops=4_000_000_000,
    )(head, *pieces, out_weight)
    cot = plan.exchange(cot_sent)

    pair = lambda r, c: arr(BF16, hv, 2, r, c)
    link, x, a, w, q, ratio, u, ol = call(
        partial(prepare_kernel, plan),
        (
            arr(F32, hv, 2, DK, DK),
            pair(tok, tok),
            pair(tok, tok),
            pair(tok, DK),
            pair(tok, DK),
            arr(F32, hv, tok, tok),
            arr(F32, hv, DV, tok),
            arr(F32, hv, DV, tok),
        ),
        3,
        smem=(0, 1),
        flops=6_000_000_000,
    )(doc_offsets, mate, got)
    links = [link] + [plan.from_mate(link, d) for d in range(1, s)]
    out, states, back = call(
        partial(scan_kernel, plan),
        (arr(BF16, hv, hv, DV, tok), arr(F32, hv, DV, DK), arr(F32, hv, DV, DK)),
        s + 4,
        smem=(0,),
        scratch=[pltpu.VMEM((s, hv, 2, DK, DK), F32), pltpu.VMEM((n, DV, DK), F32)],
        flops=4_000_000_000,
    )(mate, *links, cot, q, ol)
    mixed = plan.exchange(out)
    backs = [back] + [plan.from_mate(back, d) for d in range(1, s)]

    grad_sent = call(
        partial(backward_kernel, plan),
        arr(BF16, hv, plan.rows, DK),
        2 * s + 10,
        smem=(0, 1),
        scratch=[
            pltpu.VMEM((s, hv, 2, DK, DK), F32),
            pltpu.VMEM((s, hv, DV, DK), F32),
            pltpu.VMEM((n, DV, DK), F32),
        ],
        flops=20_000_000_000,
    )(doc_offsets, mate, *links, *backs, got, cot, x, a, w, ratio, u, states)

    rows = tok // parts
    projected = call(
        partial(project_kernel, plan, parts),
        [arr(BF16 if d else F32, rows, model) for d in range(parts)],
        3,
        smem=(0,),
        scratch=[pltpu.VMEM((tok, model), F32)],
        flops=3_000_000_000,
    )(head, mixed, out_weight)
    shares = call(
        partial(weight_kernel, plan), [arr(F32, model // n, hv * DV)] * s, 4, smem=(0, 1), flops=3_000_000_000
    )(place, mate, cot, mixed)
    weight_grad = shares[0]
    for d in range(1, s):
        weight_grad = weight_grad + plan.from_mate(shares[d], d)

    grad_sent, _ = lax.optimization_barrier((grad_sent, projected[1]))
    grads = plan.exchange(grad_sent)
    layer_out = projected[0]
    for d in range(1, parts):
        layer_out = layer_out + from_head(projected[d], d).astype(F32)
    grad_q, grad_k, grad_v, grad_rate, grad_decay = call(
        partial(finish_kernel, plan),
        (
            arr(F32, tok, hk * DK),
            arr(F32, tok, hk * DK),
            arr(F32, tok, hv * DV),
            arr(F32, hv, tok),
            arr(F32, hv, tok),
        ),
        1,
        flops=2_000_000_000,
        inside=False,
    )(grads)
    return (layer_out, grad_q, grad_k, grad_v, grad_rate, grad_decay, weight_grad)


def solution(mesh):
    placed = (
        P("ctx", "head"),
        P("ctx", "head"),
        P("ctx", "head"),
        P("head", "ctx"),
        P("head", "ctx"),
        P(),
        P("head", None),
        P(("ctx", "head"), None),
    )
    return jax.shard_map(
        per_device,
        mesh=mesh,
        in_specs=placed,
        out_specs=(
            P(("ctx", "head"), None),
            P("ctx", "head"),
            P("ctx", "head"),
            P("ctx", "head"),
            P("head", "ctx"),
            P("head", "ctx"),
            P("ctx", "head"),
        ),
        check_vma=False,
    )
```

```python
import math
from functools import partial

import jax
import jax.numpy as jnp
from jax import lax
from jax.experimental import pallas as pl
from jax.experimental.pallas import tpu as pltpu
from jax.sharding import PartitionSpec as P

DK = 128
DV = 128
AUX = 16
INVERSE, SCORES, FROM_STATE, READS, RATIO, WRITES, STATE, KEPT = range(8)
EPS = 1e-06
F32 = jnp.float32
BF16 = jnp.bfloat16
SPARE_VMEM = 8 * 1024 * 1024


def dot(a, b, ca, cb):
    return lax.dot_general(a, b, (((ca,), (cb,)), ((), ())), preferred_element_type=F32)


def halves(x):
    high = x.astype(BF16)
    return high, (x - high.astype(F32)).astype(BF16)


def thirds(x):
    high = x.astype(BF16).astype(F32)
    middle = (x - high).astype(BF16).astype(F32)
    return high, middle, x - high - middle


def mm(a, b, ca=1, cb=0):
    left = jnp.concatenate([a[0], a[0], a[1]], axis=ca)
    right = jnp.concatenate([b[0], b[1], b[0]], axis=cb)
    return dot(left, right, ca, cb)


def cat(pairs, axis):
    return tuple(jnp.concatenate(parts, axis=axis) for parts in zip(*pairs))


def iotas(rows, columns):
    shape = (rows, columns)
    return lax.broadcasted_iota(jnp.int32, shape, 0), lax.broadcasted_iota(jnp.int32, shape, 1)


def call(kernel, outs, n_in, smem=(), scratch=(), flops=0, inside=True, fetch=()):
    spec = lambda i: pl.BlockSpec(memory_space=pltpu.SMEM if i in smem else pltpu.VMEM)
    if inside:
        outs = jax.tree.map(lambda o: pltpu.VMEM(o.shape, o.dtype), outs)
    run = pl.pallas_call(
        kernel,
        out_shape=outs,
        in_specs=[spec(i) for i in range(n_in)],
        out_specs=jax.tree.map(lambda _: pl.BlockSpec(memory_space=pltpu.VMEM), outs),
        scratch_shapes=list(scratch),
        compiler_params=pltpu.CompilerParams(
            vmem_limit_bytes=SPARE_VMEM + sum(x.dtype.itemsize * math.prod(x.shape) for x in scratch)
        ),
        cost_estimate=pl.CostEstimate(flops=flops, bytes_accessed=0, transcendentals=0),
    )

    def placed(*args):
        hold = pltpu.with_memory_space_constraint
        space = lambda i: pltpu.HBM if i in fetch else pltpu.VMEM
        return run(*(x if i in smem else hold(x, space(i)) for i, x in enumerate(args)))

    return placed


def arr(dtype, *shape):
    return jax.ShapeDtypeStruct(shape, dtype)


class Plan:
    def __init__(self, n, tok, hv, hk):
        self.n, self.tok, self.hv, self.hk = n, tok, hv, hk
        self.mates = n // hv
        self.v_at = 2 * tok
        self.aux_at = 2 * tok + DV
        self.rows = self.aux_at + AUX
        self.groups = [[m * self.mates + b for m in range(hv)] for b in range(self.mates)]

    def key_head(self, head):
        return head * self.hk // self.hv

    def exchange(self, x):
        return lax.all_to_all(
            x, "ctx", split_axis=0, concat_axis=0, axis_index_groups=self.groups, tiled=True
        )

    def from_mate(self, x, d):
        s = self.mates
        pairs = [(i // s * s + (i + d) % s, i) for i in range(self.n)]
        return lax.ppermute(x, "ctx", pairs)


def aux_rows(rows, columns):
    row_ids = lax.broadcasted_iota(jnp.int32, (AUX, columns), 0)
    out = jnp.zeros((AUX, columns), F32)
    for i, part in enumerate(p for r in rows for p in thirds(r)):
        out = jnp.where(row_ids == i, part, out)
    return out.astype(BF16)


def pack_kernel(plan, q_ref, k_ref, v_ref, rate_ref, decay_ref, out_ref):
    tok = plan.tok
    for h in range(plan.hv):
        kh = plan.key_head(h)
        out_ref[h, :tok] = q_ref[:, kh * DK : (kh + 1) * DK]
        out_ref[h, tok : 2 * tok] = k_ref[:, kh * DK : (kh + 1) * DK]
        turned = jnp.transpose(v_ref[:, h * DV : (h + 1) * DV].astype(F32))
        out_ref[h, plan.v_at : plan.aux_at] = turned.astype(BF16)
        rows = [rate_ref[h : h + 1, :], decay_ref[h : h + 1, :]]
        out_ref[h, plan.aux_at :] = aux_rows(rows, tok)


def unit(x):
    scale = lax.rsqrt(jnp.sum(x * x, axis=1, keepdims=True) + EPS)
    return x * scale, scale


def segments(off_ref, positions):
    total = jnp.zeros(positions.shape, jnp.int32)
    for j in range(off_ref.shape[0] - 1):
        total = total + (off_ref[j] <= positions).astype(jnp.int32)
    return total


def to_columns(rows, tok):
    row_ids = lax.broadcasted_iota(jnp.int32, (tok, tok), 0)
    stacked = jnp.zeros((tok, tok), F32)
    for i, r in enumerate(rows):
        stacked = jnp.where(row_ids == i, r, stacked)
    turned = jnp.transpose(stacked)
    return [turned[:, i : i + 1] for i in range(len(rows))]


def to_rows(columns, tok):
    column_ids = lax.broadcasted_iota(jnp.int32, (tok, tok), 1)
    stacked = jnp.zeros((tok, tok), F32)
    for i, c in enumerate(columns):
        stacked = jnp.where(column_ids == i, c, stacked)
    turned = jnp.transpose(stacked)
    return [turned[i : i + 1, :] for i in range(len(columns))]


def scalings(plan, off_ref, chunks, auxes):
    tok = plan.tok
    rows, columns = iotas(tok, tok)
    upto = (rows <= columns).astype(BF16)
    sums = [dot(a, upto, 1, 0) for a in auxes]
    rates = [jnp.sum(a[0:3].astype(F32), axis=0, keepdims=True) for a in auxes]
    cumuls = [s[3:4] + s[4:5] + s[5:6] for s in sums]
    turned = to_columns(rates + cumuls, tok)
    out = []
    for i, c in enumerate(chunks):
        b_col, c_col = turned[i], turned[len(chunks) + i]
        c_row = cumuls[i]
        start = c * tok
        seg_col = segments(off_ref, start + rows[:, :1])
        seg_row = segments(off_ref, start + columns[:1, :])
        before = jnp.int32(0)
        last = jnp.int32(0)
        for j in range(off_ref.shape[0] - 1):
            before = before + (off_ref[j] <= start - 1).astype(jnp.int32)
            last = last + (off_ref[j] <= start + tok - 1).astype(jnp.int32)
        c_last = c_row[:, tok - 1 : tok]
        together = (seg_col == seg_row) & (rows >= columns)
        ratio = jnp.where(together, jnp.exp(jnp.where(together, c_col - c_row, 0.0)), 0.0)
        start_col = jnp.where(seg_col == before, jnp.exp(c_col), 0.0)
        end_col = jnp.where(seg_col == last, jnp.exp(c_last - c_col), 0.0)
        whole = jnp.where(last == before, jnp.exp(c_last), 0.0)
        out.append((rates[i], b_col, ratio, start_col, end_col, whole))
    return out


def inverses(lowers):
    size = lowers[0].shape[0]
    rows, columns = iotas(size, size)
    identity = (rows == columns).astype(F32)
    block = min(16, size)
    near = (rows // block) == (columns // block)
    powers = [jnp.where(near, -m, 0.0) for m in lowers]
    results = [identity + p for p in powers]
    split = [halves(p) for p in powers]
    powers = [mm(s, s) for s in split]
    reach = 2
    while reach < block:
        split = [halves(p) for p in powers]
        more = reach * 2 < block
        both = []
        for r, s in zip(results, split):
            left = halves(r)
            if more:
                left = cat([left, s], 0)
            both.append(mm(left, s))
        results = [r + b[:size] for r, b in zip(results, both)]
        if more:
            powers = [b[size:] for b in both]
        reach *= 2
    while block < size:
        across = ((rows // (2 * block)) == (columns // (2 * block))) & (
            (rows // block) > (columns // block)
        )
        split = [halves(r) for r in results]
        middle = [mm(halves(jnp.where(across, m, 0.0)), s) for m, s in zip(lowers, split)]
        results = [r - mm(s, halves(m)) for r, s, m in zip(results, split, middle)]
        block *= 2
    return results


def prepare_kernel(
    plan, off_ref, mate_ref, in_ref, link_ref, kept_ref
):
    tok = plan.tok
    rows, columns = iotas(tok, tok)
    identity = (lax.broadcasted_iota(jnp.int32, (DK, DK), 0) == lax.broadcasted_iota(jnp.int32, (DK, DK), 1)).astype(F32)
    mine = range(plan.hv)
    chunks = [mate_ref[0] + plan.mates * m for m in mine]
    scales = scalings(plan, off_ref, chunks, [in_ref[m, plan.aux_at :] for m in mine])
    qn = [unit(in_ref[m, :tok].astype(F32))[0] for m in mine]
    kn = [unit(in_ref[m, tok : 2 * tok].astype(F32))[0] for m in mine]
    kp = [halves(x) for x in kn]
    qp = [halves(x) for x in qn]
    dots = [mm(cat([q, k], 0), k, 1, 1) for q, k in zip(qp, kp)]
    strict = rows > columns
    lowers = [jnp.where(strict, s[1] * d[tok:] * s[2], 0.0) for s, d in zip(scales, dots)]
    scores = [d[:tok] * s[2] for s, d in zip(scales, dots)]
    inv = inverses(lowers)
    rated = [halves(x * s[0]) for x, s in zip(inv, scales)]
    w = [mm(x, halves(s[3] * k)) for x, s, k in zip(rated, scales, kn)]
    values = [in_ref[m, plan.v_at : plan.aux_at] for m in mine]
    u = [
        dot(jnp.concatenate([v, v], axis=1), jnp.concatenate(x, axis=1), 1, 1)
        for v, x in zip(values, rated)
    ]
    wp = [halves(x) for x in w]
    up = [halves(x) for x in u]
    ap = [halves(x) for x in scores]
    ke = [halves(s[4] * k) for s, k in zip(scales, kn)]
    for m in mine:
        link_ref[m, 0] = scales[m][5] * identity - mm(wp[m], ke[m], 0, 0)
        link_ref[m, 1] = mm(up[m], ke[m])
    for m in mine:
        kept_ref[m, INVERSE] = inv[m]
        kept_ref[m, SCORES] = scores[m]
        kept_ref[m, FROM_STATE] = w[m]
        kept_ref[m, READS] = scales[m][3] * qn[m] - mm(ap[m], wp[m])
        kept_ref[m, RATIO] = scales[m][2]
        kept_ref[m, WRITES] = u[m]
        kept_ref[m, STATE] = mm(up[m], ap[m], 1, 1)


def lay_out(plan, mate, refs, all_ref):
    for d, ref in enumerate(refs):
        all_ref[lax.rem(mate + d, plan.mates)] = ref[...]


def scan_kernel(plan, mate_ref, *refs):
    s = plan.mates
    links, (cot_ref, kept_ref, out_ref, all_kept_ref, back_ref, all_ref, states_ref) = refs[:s], refs[s:]
    mate = mate_ref[0]
    lay_out(plan, mate, links, all_ref)
    state = jnp.zeros((DV, DK), F32)
    for c in range(plan.n):
        states_ref[c] = state
        if c < plan.n - 1:
            link = all_ref.at[c % s, c // s]
            state = link[1] + mm(halves(state), halves(link[0]))
    for m in range(plan.hv):
        state = states_ref[mate + s * m]
        reads = halves(kept_ref[m, READS])
        core = (kept_ref[m, STATE] + mm(halves(state), reads, 1, 1)).astype(BF16)
        for g in range(plan.hv):
            out_ref[g, (m - g) % plan.hv] = core
        back_ref[m] = mm(d_out(cot_ref, m), reads)
        all_kept_ref[m, STATE] = state
        for i in range(STATE):
            all_kept_ref[m, i] = kept_ref[m, i]


def d_out(cot_ref, m):
    return cot_ref[m, :DV], cot_ref[m, DV : 2 * DV]


def backward_kernel(plan, off_ref, mate_ref, *refs):
    s, n, tok = plan.mates, plan.n, plan.tok
    links, backs, refs = refs[:s], refs[s : 2 * s], refs[2 * s :]
    in_ref, cot_ref, kept_ref, out_ref, links_ref, backs_ref, cots_ref = refs
    mate = mate_ref[0]
    lay_out(plan, mate, links, links_ref)
    lay_out(plan, mate, backs, backs_ref)
    d_state = jnp.zeros((DV, DK), F32)
    for c in reversed(range(n)):
        cots_ref[c] = d_state
        if c:
            d_state = backs_ref[c % s, c // s] + mm(
                halves(d_state), halves(links_ref[c % s, c // s, 0]), 1, 1
            )
    rows, columns = iotas(tok, tok)
    strict = rows > columns
    upto = (rows >= columns).astype(BF16)
    mine = range(plan.hv)
    chunks = [mate + s * m for m in mine]
    scales = scalings(plan, off_ref, chunks, [in_ref[m, plan.aux_at :] for m in mine])
    qu = [unit(in_ref[m, :tok].astype(F32)) for m in mine]
    ku = [unit(in_ref[m, tok : 2 * tok].astype(F32)) for m in mine]
    qp = [halves(x[0]) for x in qu]
    kp = [halves(x[0]) for x in ku]
    do = [d_out(cot_ref, m) for m in mine]
    s0 = [kept_ref[m, STATE] for m in mine]
    ds = [cots_ref[c] for c in chunks]
    s0p = [halves(x) for x in s0]
    dsp = [halves(x) for x in ds]
    pseudo = [kept_ref[m, WRITES] - mm(s0p[m], halves(kept_ref[m, FROM_STATE]), 1, 1) for m in mine]
    pp = [halves(x) for x in pseudo]
    ke = [halves(s[4] * k[0]) for s, k in zip(scales, ku)]
    dp = [mm(do[m], halves(kept_ref[m, SCORES])) + mm(dsp[m], ke[m], 1, 1) for m in mine]
    dr = [mm(halves(dp[m]), halves(kept_ref[m, INVERSE])) for m in mine]
    drp = [halves(x) for x in dr]
    big = [mm(cat([o, r], 1), cat([p, s], 1), 0, 0) for o, r, p, s in zip(do, drp, pp, s0p)]
    pds = [mm(p, d, 0, 0) for p, d in zip(pp, dsp)]
    da = [big[m][:tok, :tok] * kept_ref[m, RATIO] for m in mine]
    dm = [jnp.where(strict, -big[m][tok:, :tok] * kept_ref[m, RATIO], 0.0) for m in mine]
    dap = [halves(x) for x in da]
    dmp = [halves(x) for x in dm]
    dbm = [halves(s[1] * x) for s, x in zip(scales, dm)]
    by_row = [mm(cat([x, y], 0), k) for x, y, k in zip(dap, dmp, kp)]
    by_column = [
        mm(cat([x, y], 0), cat([q, k], 0), 0, 0) for x, y, q, k in zip(dap, dbm, qp, kp)
    ]
    sums = []
    for m in mine:
        _, b_col, _, start_col, end_col, whole = scales[m]
        (qn, q_scale), (kn, k_scale) = qu[m], ku[m]
        dqn = by_row[m][:tok] + start_col * big[m][:tok, tok:]
        erase = by_row[m][tok:] - start_col * big[m][tok:, tok:]
        ends = end_col * pds[m]
        write = by_column[m] + ends
        dkn = b_col * erase + write
        s_q = jnp.sum(qn * dqn, axis=1, keepdims=True)
        s_e = jnp.sum(kn * erase, axis=1, keepdims=True)
        s_w = jnp.sum(kn * write, axis=1, keepdims=True)
        total = jnp.sum(jnp.sum(kn * ends, axis=1, keepdims=True), axis=0, keepdims=True)
        both = jnp.sum(jnp.sum(s0[m] * ds[m], axis=1, keepdims=True), axis=0, keepdims=True)
        out_ref[m, :tok] = (q_scale * (dqn - qn * s_q)).astype(BF16)
        out_ref[m, tok : 2 * tok] = (k_scale * (dkn - kn * (b_col * s_e + s_w))).astype(BF16)
        out_ref[m, plan.v_at : plan.aux_at] = (scales[m][0] * dr[m]).astype(BF16)
        sums.append((s_e, s_q + b_col * s_e - s_w, total + whole * both))
    turned = to_rows([s[0] for s in sums] + [s[1] for s in sums], tok)
    for m in mine:
        values = in_ref[m, plan.v_at : plan.aux_at].astype(F32)
        d_rate = turned[m] + jnp.sum(dr[m] * values, axis=0, keepdims=True)
        parts = dot(aux_rows([turned[plan.hv + m]], tok), upto, 1, 0)
        d_decay = parts[0:1] + parts[1:2] + parts[2:3] + sums[m][2]
        out_ref[m, plan.aux_at :] = aux_rows([d_rate, d_decay], tok)


def cotangent_kernel(plan, parts, head_ref, *refs):
    pieces, (w_ref, out_ref, all_ref) = refs[:parts], refs[parts:]
    rows = pieces[0].shape[0]
    for d in range(parts):
        at = lax.rem(head_ref[0] + d, parts)
        all_ref[pl.ds(pl.multiple_of(at * rows, rows), rows), :] = pieces[d][...]
    whole = all_ref[...]
    share = whole.shape[1] // plan.hv
    high, low = halves(dot(w_ref[...], whole, 1, 1))
    for m in range(plan.hv):
        out_ref[m, :DV] = high[m * DV : (m + 1) * DV]
        out_ref[m, DV : 2 * DV] = low[m * DV : (m + 1) * DV]
        turned = jnp.transpose(whole[:, m * share : (m + 1) * share].astype(F32))
        out_ref[m, 2 * DV :] = turned.astype(BF16)


def project_kernel(plan, parts, head_ref, mixed_ref, w_ref, *refs):
    outs, total_ref = refs[:parts], refs[parts]
    mixed = jnp.concatenate([mixed_ref[g, 0] for g in range(plan.hv)], axis=0)
    total_ref[...] = dot(mixed, w_ref[...], 0, 0)
    rows = outs[0].shape[0]
    for d in range(parts):
        at = lax.rem(head_ref[0] + parts - d, parts)
        block = total_ref[pl.ds(pl.multiple_of(at * rows, rows), rows), :]
        outs[d][...] = block.astype(outs[d].dtype)


def weight_kernel(plan, place_ref, mate_ref, cot_ref, mixed_ref, *outs):
    share = outs[0].shape[0]
    mixed = [
        jnp.concatenate([mixed_ref[g, step] for g in range(plan.hv)], axis=0)
        for step in range(plan.hv)
    ]
    for d, out_ref in enumerate(outs):
        at = lax.rem(mate_ref[0] + plan.mates - d, plan.mates)
        at = pl.multiple_of(2 * DV + at * share, share)
        total = None
        for step in range(plan.hv):
            chunk = lax.rem(place_ref[0] + step, plan.hv)
            part = dot(cot_ref[chunk, pl.ds(at, share), :], mixed[step], 1, 1)
            total = part if total is None else total + part
        out_ref[...] = total


def finish_kernel(plan, in_ref, q_ref, k_ref, v_ref, rate_ref, decay_ref):
    tok = plan.tok
    for kh in range(plan.hk):
        mine = [h for h in range(plan.hv) if plan.key_head(h) == kh]
        for ref, at in ((q_ref, 0), (k_ref, tok)):
            total = in_ref[mine[0], at : at + tok].astype(F32)
            for h in mine[1:]:
                total = total + in_ref[h, at : at + tok].astype(F32)
            ref[:, kh * DK : (kh + 1) * DK] = total
    for h in range(plan.hv):
        v_ref[:, h * DV : (h + 1) * DV] = jnp.transpose(
            in_ref[h, plan.v_at : plan.aux_at].astype(F32)
        )
        aux = in_ref[h, plan.aux_at :].astype(F32)
        rate_ref[h : h + 1, :] = aux[0:1] + aux[1:2] + aux[2:3]
        decay_ref[h : h + 1, :] = aux[3:4] + aux[4:5] + aux[5:6]


def per_device(
    queries, key_vectors, value_rows, write_rate, log_decay, doc_offsets, out_weight, grad_out
):
    n, parts = lax.axis_size("ctx"), lax.axis_size("head")
    tok, hv = queries.shape[0], write_rate.shape[0]
    hk, model = queries.shape[1] // DK, grad_out.shape[1]
    plan = Plan(n, tok, hv, hk)
    s = plan.mates
    index = lax.axis_index("ctx").astype(jnp.int32)
    place, mate = (index // s).reshape(1), (index % s).reshape(1)
    head = lax.axis_index("head").astype(jnp.int32).reshape(1)

    def from_head(x, d):
        return lax.ppermute(x, "head", [((i + d) % parts, i) for i in range(parts)])

    pieces = [grad_out] + [from_head(grad_out, d) for d in range(1, parts)]

    sent = call(partial(pack_kernel, plan), arr(BF16, hv, plan.rows, DK), 5, flops=20_000_000_000, fetch=range(5))(
        queries, key_vectors, value_rows, write_rate, log_decay
    )
    got = plan.exchange(sent)

    cot_sent = call(
        partial(cotangent_kernel, plan, parts),
        arr(BF16, hv, 2 * DV + model // hv, tok),
        parts + 2,
        smem=(0,),
        scratch=[pltpu.VMEM((tok, model), BF16)],
        flops=4_000_000_000,
    )(head, *pieces, out_weight)
    cot = plan.exchange(cot_sent)

    kept_shape = arr(F32, hv, KEPT, tok, DK)
    link, kept = call(
        partial(prepare_kernel, plan),
        (arr(F32, hv, 2, DK, DK), kept_shape),
        3,
        smem=(0, 1),
        flops=6_000_000_000,
    )(doc_offsets, mate, got)
    links = [link] + [plan.from_mate(link, d) for d in range(1, s)]
    out, kept, back = call(
        partial(scan_kernel, plan),
        (arr(BF16, hv, hv, DV, tok), kept_shape, arr(F32, hv, DV, DK)),
        s + 3,
        smem=(0,),
        scratch=[pltpu.VMEM((s, hv, 2, DK, DK), F32), pltpu.VMEM((n, DV, DK), F32)],
        flops=4_000_000_000,
    )(mate, *links, cot, kept)
    mixed = plan.exchange(out)
    backs = [back] + [plan.from_mate(back, d) for d in range(1, s)]

    grad_sent = call(
        partial(backward_kernel, plan),
        arr(BF16, hv, plan.rows, DK),
        2 * s + 5,
        smem=(0, 1),
        scratch=[
            pltpu.VMEM((s, hv, 2, DK, DK), F32),
            pltpu.VMEM((s, hv, DV, DK), F32),
            pltpu.VMEM((n, DV, DK), F32),
        ],
        flops=20_000_000_000,
    )(doc_offsets, mate, *links, *backs, got, cot, kept)

    rows = tok // parts
    projected = call(
        partial(project_kernel, plan, parts),
        [arr(BF16 if d else F32, rows, model) for d in range(parts)],
        3,
        smem=(0,),
        scratch=[pltpu.VMEM((tok, model), F32)],
        flops=3_000_000_000,
        fetch=(2,),
    )(head, mixed, out_weight)
    shares = call(
        partial(weight_kernel, plan), [arr(F32, model // n, hv * DV)] * s, 4, smem=(0, 1), flops=3_000_000_000
    )(place, mate, cot, mixed)
    weight_grad = shares[0]
    for d in range(1, s):
        weight_grad = weight_grad + plan.from_mate(shares[d], d)

    grad_sent, _ = lax.optimization_barrier((grad_sent, projected[1]))
    grads = plan.exchange(grad_sent)
    grad_q, grad_k, grad_v, grad_rate, grad_decay = call(
        partial(finish_kernel, plan),
        (
            arr(F32, tok, hk * DK),
            arr(F32, tok, hk * DK),
            arr(F32, tok, hv * DV),
            arr(F32, hv, tok),
            arr(F32, hv, tok),
        ),
        1,
        flops=2_000_000_000,
        inside=False,
    )(grads)
    pieces = [from_head(projected[d], d) for d in range(1, parts)]
    layer_out, _, _ = lax.optimization_barrier((projected[0], grad_q, weight_grad))
    for piece in pieces:
        layer_out = layer_out + piece.astype(F32)
    return (layer_out, grad_q, grad_k, grad_v, grad_rate, grad_decay, weight_grad)


def solution(mesh):
    placed = (
        P("ctx", "head"),
        P("ctx", "head"),
        P("ctx", "head"),
        P("head", "ctx"),
        P("head", "ctx"),
        P(),
        P("head", None),
        P(("ctx", "head"), None),
    )
    return jax.shard_map(
        per_device,
        mesh=mesh,
        in_specs=placed,
        out_specs=(
            P(("ctx", "head"), None),
            P("ctx", "head"),
            P("ctx", "head"),
            P("ctx", "head"),
            P("head", "ctx"),
            P("head", "ctx"),
            P("ctx", "head"),
        ),
        check_vma=False,
    )
```

```python
import math
from functools import partial

import jax
import jax.numpy as jnp
from jax import lax
from jax.experimental import pallas as pl
from jax.experimental.pallas import tpu as pltpu
from jax.sharding import PartitionSpec as P

DK = 128
DV = 128
AUX = 16
INVERSE, SCORES, FROM_STATE, READS, RATIO, WRITES, LOCAL, KEPT = range(8)
EPS = 1e-06
F32 = jnp.float32
BF16 = jnp.bfloat16
SPARE_VMEM = 8 * 1024 * 1024


def dot(a, b, ca, cb):
    return lax.dot_general(a, b, (((ca,), (cb,)), ((), ())), preferred_element_type=F32)


def halves(x):
    high = x.astype(BF16)
    return high, (x - high.astype(F32)).astype(BF16)


def thirds(x):
    high = x.astype(BF16).astype(F32)
    middle = (x - high).astype(BF16).astype(F32)
    return high, middle, x - high - middle


def mm(a, b, ca=1, cb=0):
    left = jnp.concatenate([a[0], a[0], a[1]], axis=ca)
    right = jnp.concatenate([b[0], b[1], b[0]], axis=cb)
    return dot(left, right, ca, cb)


def cat(pairs, axis):
    return tuple(jnp.concatenate(parts, axis=axis) for parts in zip(*pairs))


def iotas(rows, columns):
    shape = (rows, columns)
    return lax.broadcasted_iota(jnp.int32, shape, 0), lax.broadcasted_iota(jnp.int32, shape, 1)


def call(kernel, outs, smem=(), scratch=(), flops=0, inside=True, fetch=()):
    if inside:
        outs = jax.tree.map(lambda o: pltpu.VMEM(o.shape, o.dtype), outs)
    scoped = SPARE_VMEM + sum(x.dtype.itemsize * math.prod(x.shape) for x in scratch)

    def run(*args):
        spec = lambda i: pl.BlockSpec(memory_space=pltpu.SMEM if i in smem else pltpu.VMEM)
        space = lambda i: pltpu.HBM if i in fetch else pltpu.VMEM
        hold = pltpu.with_memory_space_constraint
        return pl.pallas_call(
            kernel,
            out_shape=outs,
            in_specs=[spec(i) for i in range(len(args))],
            out_specs=jax.tree.map(lambda _: pl.BlockSpec(memory_space=pltpu.VMEM), outs),
            scratch_shapes=list(scratch),
            compiler_params=pltpu.CompilerParams(vmem_limit_bytes=scoped),
            cost_estimate=pl.CostEstimate(flops=flops, bytes_accessed=0, transcendentals=0),
        )(*(x if i in smem else hold(x, space(i)) for i, x in enumerate(args)))

    return run


def arr(dtype, *shape):
    return jax.ShapeDtypeStruct(shape, dtype)


class Ring:
    def __init__(self, size):
        self.size = size
        self.paired = size & (size - 1) == 0

    def source(self, i, d):
        return i ^ d if self.paired else (i + d) % self.size

    def target(self, i, d):
        return i ^ d if self.paired else (i + self.size - d) % self.size

    def seen(self, d, k):
        return d ^ k if self.paired else (k - d) % self.size

    def pairs(self, d):
        return [(self.source(i, d), i) for i in range(self.size)]


class Plan:
    def __init__(self, n, tok, hv, hk):
        self.n, self.tok, self.hv, self.hk = n, tok, hv, hk
        self.mates = n // hv
        self.v_at = 2 * tok
        self.aux_at = 2 * tok + DV
        self.rows = self.aux_at + AUX
        self.ring = Ring(hv)

    def key_head(self, head):
        return head * self.hk // self.hv

    def exchange(self, pieces):
        s = self.mates
        moved = [pieces[0]]
        for d in range(1, self.hv):
            pairs = [(i * s + b, j * s + b) for i, j in self.ring.pairs(d) for b in range(s)]
            moved.append(lax.ppermute(pieces[d], "ctx", pairs))
        return moved

    def from_mate(self, x, d):
        s = self.mates
        pairs = [(i // s * s + (i + d) % s, i) for i in range(self.n)]
        return lax.ppermute(x, "ctx", pairs)


def aux_rows(rows, columns):
    row_ids = lax.broadcasted_iota(jnp.int32, (AUX, columns), 0)
    out = jnp.zeros((AUX, columns), F32)
    for i, part in enumerate(p for r in rows for p in thirds(r)):
        out = jnp.where(row_ids == i, part, out)
    return out.astype(BF16)


def pack_kernel(plan, place_ref, q_ref, k_ref, v_ref, rate_ref, decay_ref, *refs):
    outs, out_ref = refs[:-1], refs[-1]
    tok = plan.tok
    for h in range(plan.hv):
        kh = plan.key_head(h)
        out_ref[h, :tok] = q_ref[:, kh * DK : (kh + 1) * DK]
        out_ref[h, tok : 2 * tok] = k_ref[:, kh * DK : (kh + 1) * DK]
        turned = jnp.transpose(v_ref[:, h * DV : (h + 1) * DV].astype(F32))
        out_ref[h, plan.v_at : plan.aux_at] = turned.astype(BF16)
        rows = [rate_ref[h : h + 1, :], decay_ref[h : h + 1, :]]
        out_ref[h, plan.aux_at :] = aux_rows(rows, tok)
    hand_out(plan, place_ref[0], out_ref, outs)


def hand_out(plan, place, all_ref, outs):
    for d, ref in enumerate(outs):
        ref[...] = all_ref[plan.ring.target(place, d)]


def unit(x):
    scale = lax.rsqrt(jnp.sum(x * x, axis=1, keepdims=True) + EPS)
    return x * scale, scale


def segments(off_ref, positions):
    total = jnp.zeros(positions.shape, jnp.int32)
    for j in range(off_ref.shape[0] - 1):
        total = total + (off_ref[j] <= positions).astype(jnp.int32)
    return total


def to_columns(rows, tok):
    row_ids = lax.broadcasted_iota(jnp.int32, (tok, tok), 0)
    stacked = jnp.zeros((tok, tok), F32)
    for i, r in enumerate(rows):
        stacked = jnp.where(row_ids == i, r, stacked)
    turned = jnp.transpose(stacked)
    return [turned[:, i : i + 1] for i in range(len(rows))]


def to_rows(columns, tok):
    column_ids = lax.broadcasted_iota(jnp.int32, (tok, tok), 1)
    stacked = jnp.zeros((tok, tok), F32)
    for i, c in enumerate(columns):
        stacked = jnp.where(column_ids == i, c, stacked)
    turned = jnp.transpose(stacked)
    return [turned[i : i + 1, :] for i in range(len(columns))]


def scalings(plan, off_ref, chunks, auxes):
    tok = plan.tok
    rows, columns = iotas(tok, tok)
    upto = (rows <= columns).astype(BF16)
    sums = [dot(a, upto, 1, 0) for a in auxes]
    rates = [jnp.sum(a[0:3].astype(F32), axis=0, keepdims=True) for a in auxes]
    cumuls = [s[3:4] + s[4:5] + s[5:6] for s in sums]
    turned = to_columns(rates + cumuls, tok)
    out = []
    for i, c in enumerate(chunks):
        b_col, c_col = turned[i], turned[len(chunks) + i]
        c_row = cumuls[i]
        start = c * tok
        seg_col = segments(off_ref, start + rows[:, :1])
        seg_row = segments(off_ref, start + columns[:1, :])
        before = jnp.int32(0)
        last = jnp.int32(0)
        for j in range(off_ref.shape[0] - 1):
            before = before + (off_ref[j] <= start - 1).astype(jnp.int32)
            last = last + (off_ref[j] <= start + tok - 1).astype(jnp.int32)
        c_last = c_row[:, tok - 1 : tok]
        together = (seg_col == seg_row) & (rows >= columns)
        ratio = jnp.where(together, jnp.exp(jnp.where(together, c_col - c_row, 0.0)), 0.0)
        start_col = jnp.where(seg_col == before, jnp.exp(c_col), 0.0)
        end_col = jnp.where(seg_col == last, jnp.exp(c_last - c_col), 0.0)
        whole = jnp.where(last == before, jnp.exp(c_last), 0.0)
        out.append((rates[i], b_col, ratio, start_col, end_col, whole))
    return out


def inverses(lowers):
    size = lowers[0].shape[0]
    rows, columns = iotas(size, size)
    identity = (rows == columns).astype(F32)
    block = min(16, size)
    near = (rows // block) == (columns // block)
    powers = [jnp.where(near, -m, 0.0) for m in lowers]
    results = [identity + p for p in powers]
    split = [halves(p) for p in powers]
    powers = [mm(s, s) for s in split]
    reach = 2
    while reach < block:
        split = [halves(p) for p in powers]
        more = reach * 2 < block
        both = []
        for r, s in zip(results, split):
            left = halves(r)
            if more:
                left = cat([left, s], 0)
            both.append(mm(left, s))
        results = [r + b[:size] for r, b in zip(results, both)]
        if more:
            powers = [b[size:] for b in both]
        reach *= 2
    while block < size:
        across = ((rows // (2 * block)) == (columns // (2 * block))) & (
            (rows // block) > (columns // block)
        )
        split = [halves(r) for r in results]
        middle = [mm(halves(jnp.where(across, m, 0.0)), s) for m, s in zip(lowers, split)]
        results = [r - mm(s, halves(m)) for r, s, m in zip(results, split, middle)]
        block *= 2
    return results


def chunks_of(plan, place, mate):
    return [mate + plan.mates * plan.ring.source(place, d) for d in range(plan.hv)]


def prepare_kernel(plan, off_ref, place_ref, mate_ref, *refs):
    in_refs, (link_ref, kept_ref) = refs[: plan.hv], refs[plan.hv :]
    tok = plan.tok
    rows, columns = iotas(tok, tok)
    key_rows, key_columns = iotas(DK, DK)
    identity = (key_rows == key_columns).astype(F32)
    mine = range(plan.hv)
    chunks = chunks_of(plan, place_ref[0], mate_ref[0])
    scales = scalings(plan, off_ref, chunks, [r[plan.aux_at :] for r in in_refs])
    qn = [unit(in_refs[m][:tok].astype(F32))[0] for m in mine]
    kn = [unit(in_refs[m][tok : 2 * tok].astype(F32))[0] for m in mine]
    kp = [halves(x) for x in kn]
    qp = [halves(x) for x in qn]
    dots = [mm(cat([q, k], 0), k, 1, 1) for q, k in zip(qp, kp)]
    strict = rows > columns
    lowers = [jnp.where(strict, s[1] * d[tok:] * s[2], 0.0) for s, d in zip(scales, dots)]
    scores = [d[:tok] * s[2] for s, d in zip(scales, dots)]
    inv = inverses(lowers)
    rated = [halves(x * s[0]) for x, s in zip(inv, scales)]
    w = [mm(x, halves(s[3] * k)) for x, s, k in zip(rated, scales, kn)]
    values = [in_refs[m][plan.v_at : plan.aux_at] for m in mine]
    u = [
        dot(jnp.concatenate([v, v], axis=1), jnp.concatenate(x, axis=1), 1, 1)
        for v, x in zip(values, rated)
    ]
    wp = [halves(x) for x in w]
    up = [halves(x) for x in u]
    ap = [halves(x) for x in scores]
    ke = [halves(s[4] * k) for s, k in zip(scales, kn)]
    for m in mine:
        link_ref[m, 0] = scales[m][5] * identity - mm(wp[m], ke[m], 0, 0)
        link_ref[m, 1] = mm(up[m], ke[m])
    for m in mine:
        kept_ref[m, INVERSE] = inv[m]
        kept_ref[m, SCORES] = scores[m]
        kept_ref[m, FROM_STATE] = w[m]
        kept_ref[m, READS] = scales[m][3] * qn[m] - mm(ap[m], wp[m])
        kept_ref[m, RATIO] = scales[m][2]
        kept_ref[m, WRITES] = u[m]
        kept_ref[m, LOCAL] = mm(up[m], ap[m], 1, 1)


def lay_out(plan, place, mate, refs, all_ref):
    for d, ref in enumerate(refs):
        for m in range(plan.hv):
            all_ref[lax.rem(mate + d, plan.mates), plan.ring.source(place, m)] = ref[m]


def scan_kernel(plan, place_ref, mate_ref, *refs):
    s, hv = plan.mates, plan.hv
    links, kept_ref, state_ref = refs[:s], refs[s], refs[s + 1]
    outs, (all_ref, states_ref) = refs[s + 2 : -2], refs[-2:]
    place, mate = place_ref[0], mate_ref[0]
    lay_out(plan, place, mate, links, all_ref)
    state = jnp.zeros((DV, DK), F32)
    for c in range(plan.n):
        states_ref[c] = state
        if c < plan.n - 1:
            link = all_ref.at[c % s, c // s]
            state = link[1] + mm(halves(state), halves(link[0]))
    cores = []
    for m, c in enumerate(chunks_of(plan, place, mate)):
        state = states_ref[c]
        state_ref[m] = state
        core = kept_ref[m, LOCAL] + mm(halves(state), halves(kept_ref[m, READS]), 1, 1)
        cores.append(core.astype(BF16))
    for d in range(hv):
        for k in range(hv):
            outs[d][k] = cores[plan.ring.seen(d, k)]


def state_cotangent_kernel(plan, kept_ref, *refs):
    for m in range(plan.hv):
        refs[-1][m] = mm(d_out(refs[m]), halves(kept_ref[m, READS]))


def d_out(ref):
    return ref[:DV], ref[DV:]


def backward_kernel(plan, off_ref, place_ref, mate_ref, *refs):
    s, n, tok, hv = plan.mates, plan.n, plan.tok, plan.hv
    links, backs, refs = refs[:s], refs[s : 2 * s], refs[2 * s :]
    in_refs, d_refs, kept_ref, state_ref = refs[:hv], refs[hv : 2 * hv], refs[2 * hv], refs[2 * hv + 1]
    outs, (links_ref, backs_ref, cots_ref) = refs[2 * hv + 2 : -3], refs[-3:]
    place, mate = place_ref[0], mate_ref[0]
    lay_out(plan, place, mate, links, links_ref)
    lay_out(plan, place, mate, backs, backs_ref)
    d_state = jnp.zeros((DV, DK), F32)
    for c in reversed(range(n)):
        cots_ref[c] = d_state
        if c:
            d_state = backs_ref[c % s, c // s] + mm(
                halves(d_state), halves(links_ref[c % s, c // s, 0]), 1, 1
            )
    rows, columns = iotas(tok, tok)
    strict = rows > columns
    upto = (rows >= columns).astype(BF16)
    mine = range(hv)
    chunks = chunks_of(plan, place, mate)
    scales = scalings(plan, off_ref, chunks, [r[plan.aux_at :] for r in in_refs])
    qu = [unit(in_refs[m][:tok].astype(F32)) for m in mine]
    ku = [unit(in_refs[m][tok : 2 * tok].astype(F32)) for m in mine]
    qp = [halves(x[0]) for x in qu]
    kp = [halves(x[0]) for x in ku]
    do = [d_out(r) for r in d_refs]
    s0 = [state_ref[m] for m in mine]
    ds = [cots_ref[c] for c in chunks]
    s0p = [halves(x) for x in s0]
    dsp = [halves(x) for x in ds]
    pseudo = [kept_ref[m, WRITES] - mm(s0p[m], halves(kept_ref[m, FROM_STATE]), 1, 1) for m in mine]
    pp = [halves(x) for x in pseudo]
    ke = [halves(s[4] * k[0]) for s, k in zip(scales, ku)]
    dp = [mm(do[m], halves(kept_ref[m, SCORES])) + mm(dsp[m], ke[m], 1, 1) for m in mine]
    dr = [mm(halves(dp[m]), halves(kept_ref[m, INVERSE])) for m in mine]
    drp = [halves(x) for x in dr]
    big = [mm(cat([o, r], 1), cat([p, s], 1), 0, 0) for o, r, p, s in zip(do, drp, pp, s0p)]
    pds = [mm(p, d, 0, 0) for p, d in zip(pp, dsp)]
    da = [big[m][:tok, :tok] * kept_ref[m, RATIO] for m in mine]
    dm = [jnp.where(strict, -big[m][tok:, :tok] * kept_ref[m, RATIO], 0.0) for m in mine]
    dap = [halves(x) for x in da]
    dmp = [halves(x) for x in dm]
    dbm = [halves(s[1] * x) for s, x in zip(scales, dm)]
    by_row = [mm(cat([x, y], 0), k) for x, y, k in zip(dap, dmp, kp)]
    by_column = [
        mm(cat([x, y], 0), cat([q, k], 0), 0, 0) for x, y, q, k in zip(dap, dbm, qp, kp)
    ]
    sums = []
    for m in mine:
        _, b_col, _, start_col, end_col, whole = scales[m]
        (qn, q_scale), (kn, k_scale) = qu[m], ku[m]
        out_ref = outs[plan.ring.seen(m, 0)]
        dqn = by_row[m][:tok] + start_col * big[m][:tok, tok:]
        erase = by_row[m][tok:] - start_col * big[m][tok:, tok:]
        ends = end_col * pds[m]
        write = by_column[m] + ends
        dkn = b_col * erase + write
        s_q = jnp.sum(qn * dqn, axis=1, keepdims=True)
        s_e = jnp.sum(kn * erase, axis=1, keepdims=True)
        s_w = jnp.sum(kn * write, axis=1, keepdims=True)
        total = jnp.sum(jnp.sum(kn * ends, axis=1, keepdims=True), axis=0, keepdims=True)
        both = jnp.sum(jnp.sum(s0[m] * ds[m], axis=1, keepdims=True), axis=0, keepdims=True)
        out_ref[:tok] = (q_scale * (dqn - qn * s_q)).astype(BF16)
        out_ref[tok : 2 * tok] = (k_scale * (dkn - kn * (b_col * s_e + s_w))).astype(BF16)
        out_ref[plan.v_at : plan.aux_at] = (scales[m][0] * dr[m]).astype(BF16)
        sums.append((s_e, s_q + b_col * s_e - s_w, total + whole * both))
    turned = to_rows([s[0] for s in sums] + [s[1] for s in sums], tok)
    for m in mine:
        values = in_refs[m][plan.v_at : plan.aux_at].astype(F32)
        d_rate = turned[m] + jnp.sum(dr[m] * values, axis=0, keepdims=True)
        parts = dot(aux_rows([turned[plan.hv + m]], tok), upto, 1, 0)
        d_decay = parts[0:1] + parts[1:2] + parts[2:3] + sums[m][2]
        outs[plan.ring.seen(m, 0)][plan.aux_at :] = aux_rows([d_rate, d_decay], tok)


def gather_rows(head, pieces, all_ref):
    rows, ring = pieces[0].shape[0], Ring(len(pieces))
    for d, piece in enumerate(pieces):
        at = ring.source(head, d) * rows
        all_ref[pl.ds(pl.multiple_of(at, rows), rows), :] = piece[...]


def cotangent_kernel(plan, parts, head_ref, place_ref, *refs):
    pieces, w_ref, outs, (all_ref, core_ref) = refs[:parts], refs[parts], refs[parts + 1 : -2], refs[-2:]
    gather_rows(head_ref[0], pieces, all_ref)
    high, low = halves(dot(w_ref[...], all_ref[...], 1, 1))
    for m in range(plan.hv):
        core_ref[m, :DV] = high[m * DV : (m + 1) * DV]
        core_ref[m, DV:] = low[m * DV : (m + 1) * DV]
    hand_out(plan, place_ref[0], core_ref, outs)


def turn_kernel(plan, parts, head_ref, place_ref, *refs):
    pieces, outs, (all_ref, turned_ref) = refs[:parts], refs[parts:-2], refs[-2:]
    gather_rows(head_ref[0], pieces, all_ref)
    share = turned_ref.shape[1]
    for m in range(plan.hv):
        part = all_ref[:, m * share : (m + 1) * share].astype(F32)
        turned_ref[m] = jnp.transpose(part).astype(BF16)
    hand_out(plan, place_ref[0], turned_ref, outs)


def project_kernel(plan, parts, head_ref, place_ref, *refs):
    mixed_refs, w_ref, outs, (all_ref, total_ref) = (
        refs[: plan.hv],
        refs[plan.hv],
        refs[plan.hv + 1 : -2],
        refs[-2:],
    )
    for d, ref in enumerate(mixed_refs):
        all_ref[plan.ring.source(place_ref[0], d)] = ref[0]
    mixed = all_ref[...].reshape(plan.hv * DV, plan.tok)
    total_ref[...] = dot(mixed, w_ref[...], 0, 0)
    rows, ring = outs[0].shape[0], Ring(parts)
    for d in range(parts):
        at = ring.target(head_ref[0], d) * rows
        block = total_ref[pl.ds(pl.multiple_of(at, rows), rows), :]
        outs[d][...] = block.astype(outs[d].dtype)


def weight_kernel(plan, place_ref, mate_ref, *refs):
    hv = plan.hv
    turned, mixed_refs, outs, all_ref = refs[:hv], refs[hv : 2 * hv], refs[2 * hv : -1], refs[-1]
    for d, ref in enumerate(mixed_refs):
        head = plan.ring.source(place_ref[0], d)
        for k in range(hv):
            all_ref[k, head] = ref[k]
    share = outs[0].shape[0]
    for d, out_ref in enumerate(outs):
        at = lax.rem(mate_ref[0] + plan.mates - d, plan.mates) * share
        at = pl.multiple_of(at, share)
        total = None
        for k in range(hv):
            mixed = all_ref[k].reshape(hv * DV, plan.tok)
            part = dot(turned[k][pl.ds(at, share), :], mixed, 1, 1)
            total = part if total is None else total + part
        out_ref[...] = total


def finish_kernel(plan, place_ref, *refs):
    pieces, (q_ref, k_ref, v_ref, rate_ref, decay_ref, in_ref) = refs[: plan.hv], refs[plan.hv :]
    tok = plan.tok
    for d, ref in enumerate(pieces):
        in_ref[plan.ring.source(place_ref[0], d)] = ref[...]
    for kh in range(plan.hk):
        mine = [h for h in range(plan.hv) if plan.key_head(h) == kh]
        for ref, at in ((q_ref, 0), (k_ref, tok)):
            total = in_ref[mine[0], at : at + tok].astype(F32)
            for h in mine[1:]:
                total = total + in_ref[h, at : at + tok].astype(F32)
            ref[:, kh * DK : (kh + 1) * DK] = total
    for h in range(plan.hv):
        v_ref[:, h * DV : (h + 1) * DV] = jnp.transpose(
            in_ref[h, plan.v_at : plan.aux_at].astype(F32)
        )
        aux = in_ref[h, plan.aux_at :].astype(F32)
        rate_ref[h : h + 1, :] = aux[0:1] + aux[1:2] + aux[2:3]
        decay_ref[h : h + 1, :] = aux[3:4] + aux[4:5] + aux[5:6]


def per_device(
    queries, key_vectors, value_rows, write_rate, log_decay, doc_offsets, out_weight, grad_out
):
    n, parts = lax.axis_size("ctx"), lax.axis_size("head")
    tok, hv = queries.shape[0], write_rate.shape[0]
    hk, model = queries.shape[1] // DK, grad_out.shape[1]
    plan = Plan(n, tok, hv, hk)
    s = plan.mates
    index = lax.axis_index("ctx").astype(jnp.int32)
    place, mate = (index // s).reshape(1), (index % s).reshape(1)
    head = lax.axis_index("head").astype(jnp.int32).reshape(1)

    def across_heads(pieces):
        moved = [lax.ppermute(pieces[d], "head", Ring(parts).pairs(d)) for d in range(1, parts)]
        return [pieces[0]] + moved

    vmem = lambda dtype, *shape: pltpu.VMEM(shape, dtype)
    rows = across_heads([grad_out] * parts)

    packed = call(
        partial(pack_kernel, plan),
        [arr(BF16, plan.rows, DK)] * hv,
        smem=(0,),
        scratch=[vmem(BF16, hv, plan.rows, DK)],
        fetch=range(6),
        flops=2_000_000_000,
    )(place, queries, key_vectors, value_rows, write_rate, log_decay)
    got = plan.exchange(packed)

    link, kept = call(
        partial(prepare_kernel, plan),
        (arr(F32, hv, 2, DK, DK), arr(F32, hv, KEPT, tok, DK)),
        smem=(0, 1, 2),
        flops=4_500_000_000,
    )(doc_offsets, place, mate, *got)
    links = [link] + [plan.from_mate(link, d) for d in range(1, s)]

    d_core = call(
        partial(cotangent_kernel, plan, parts),
        [arr(BF16, 2 * DV, tok)] * hv,
        smem=(0, 1),
        scratch=[vmem(BF16, tok, model), vmem(BF16, hv, 2 * DV, tok)],
        flops=1_500_000_000,
    )(head, place, *rows, out_weight)
    d_core = plan.exchange(d_core)
    turned = call(
        partial(turn_kernel, plan, parts),
        [arr(BF16, model // hv, tok)] * hv,
        smem=(0, 1),
        scratch=[vmem(BF16, tok, model), vmem(BF16, hv, model // hv, tok)],
        flops=1_000_000_000,
    )(head, place, *rows)
    turned = plan.exchange(turned)

    states, *mixed = call(
        partial(scan_kernel, plan),
        [arr(F32, hv, DV, DK)] + [arr(BF16, hv, DV, tok)] * hv,
        smem=(0, 1),
        scratch=[vmem(F32, s, hv, 2, DK, DK), vmem(F32, n, DV, DK)],
        flops=2_500_000_000,
    )(place, mate, *links, kept)
    mixed = plan.exchange(mixed)
    back = call(
        partial(state_cotangent_kernel, plan), arr(F32, hv, DV, DK), flops=500_000_000
    )(kept, *d_core)
    backs = [back] + [plan.from_mate(back, d) for d in range(1, s)]

    projected = call(
        partial(project_kernel, plan, parts),
        [arr(BF16 if d else F32, tok // parts, model) for d in range(parts)],
        smem=(0, 1),
        scratch=[vmem(BF16, hv, DV, tok), vmem(F32, tok, model)],
        flops=1_000_000_000,
    )(head, place, *mixed, out_weight)
    layer_parts = across_heads(projected)

    grads = call(
        partial(backward_kernel, plan),
        [arr(BF16, plan.rows, DK)] * hv,
        smem=(0, 1, 2),
        scratch=[
            vmem(F32, s, hv, 2, DK, DK),
            vmem(F32, s, hv, DV, DK),
            vmem(F32, n, DV, DK),
        ],
        flops=6_000_000_000,
    )(doc_offsets, place, mate, *links, *backs, *got, *d_core, kept, states)
    grads = plan.exchange(grads)

    shares = call(
        partial(weight_kernel, plan),
        [arr(F32, model // n, hv * DV)] * s,
        smem=(0, 1),
        scratch=[vmem(BF16, hv, hv, DV, tok)],
        flops=1_000_000_000,
    )(place, mate, *turned, *mixed)
    weight_grad = shares[0]
    for d in range(1, s):
        weight_grad = weight_grad + plan.from_mate(shares[d], d)

    grad_q, grad_k, grad_v, grad_rate, grad_decay = call(
        partial(finish_kernel, plan),
        (
            arr(F32, tok, hk * DK),
            arr(F32, tok, hk * DK),
            arr(F32, tok, hv * DV),
            arr(F32, hv, tok),
            arr(F32, hv, tok),
        ),
        smem=(0,),
        scratch=[vmem(BF16, hv, plan.rows, DK)],
        flops=1_000_000_000,
        inside=False,
    )(place, *grads)
    layer_out, _, _ = lax.optimization_barrier((layer_parts[0], grad_q, weight_grad))
    for part in layer_parts[1:]:
        layer_out = layer_out + part.astype(F32)
    return (layer_out, grad_q, grad_k, grad_v, grad_rate, grad_decay, weight_grad)


def solution(mesh):
    placed = (
        P("ctx", "head"),
        P("ctx", "head"),
        P("ctx", "head"),
        P("head", "ctx"),
        P("head", "ctx"),
        P(),
        P("head", None),
        P(("ctx", "head"), None),
    )
    return jax.shard_map(
        per_device,
        mesh=mesh,
        in_specs=placed,
        out_specs=(
            P(("ctx", "head"), None),
            P("ctx", "head"),
            P("ctx", "head"),
            P("ctx", "head"),
            P("head", "ctx"),
            P("head", "ctx"),
            P("ctx", "head"),
        ),
        check_vma=False,
    )
```

```python
import math
from functools import partial

import jax
import jax.numpy as jnp
from jax import lax
from jax.experimental import pallas as pl
from jax.experimental.pallas import tpu as pltpu
from jax.sharding import PartitionSpec as P

DK = 128
DV = 128
AUX = 16
INVERSE, SCORES, FROM_STATE, READS, RATIO, WRITES, LOCAL, KEPT = range(8)
EPS = 1e-06
F32 = jnp.float32
BF16 = jnp.bfloat16
SPARE_VMEM = 8 * 1024 * 1024


def dot(a, b, ca, cb):
    return lax.dot_general(a, b, (((ca,), (cb,)), ((), ())), preferred_element_type=F32)


def halves(x):
    high = x.astype(BF16)
    return high, (x - high.astype(F32)).astype(BF16)


def thirds(x):
    high = x.astype(BF16).astype(F32)
    middle = (x - high).astype(BF16).astype(F32)
    return high, middle, x - high - middle


def mm(a, b, ca=1, cb=0):
    left = jnp.concatenate([a[0], a[0], a[1]], axis=ca)
    right = jnp.concatenate([b[0], b[1], b[0]], axis=cb)
    return dot(left, right, ca, cb)


def cat(pairs, axis):
    return tuple(jnp.concatenate(parts, axis=axis) for parts in zip(*pairs))


def iotas(rows, columns):
    shape = (rows, columns)
    return lax.broadcasted_iota(jnp.int32, shape, 0), lax.broadcasted_iota(jnp.int32, shape, 1)


def call(kernel, outs, smem=(), scratch=(), flops=0, inside=True, fetch=()):
    if inside:
        outs = jax.tree.map(lambda o: pltpu.VMEM(o.shape, o.dtype), outs)
    scoped = SPARE_VMEM + sum(x.dtype.itemsize * math.prod(x.shape) for x in scratch)

    def run(*args):
        spec = lambda i: pl.BlockSpec(memory_space=pltpu.SMEM if i in smem else pltpu.VMEM)
        space = lambda i: pltpu.HBM if i in fetch else pltpu.VMEM
        hold = pltpu.with_memory_space_constraint
        return pl.pallas_call(
            kernel,
            out_shape=outs,
            in_specs=[spec(i) for i in range(len(args))],
            out_specs=jax.tree.map(lambda _: pl.BlockSpec(memory_space=pltpu.VMEM), outs),
            scratch_shapes=list(scratch),
            compiler_params=pltpu.CompilerParams(vmem_limit_bytes=scoped),
            cost_estimate=pl.CostEstimate(flops=flops, bytes_accessed=0, transcendentals=0),
        )(*(x if i in smem else hold(x, space(i)) for i, x in enumerate(args)))

    return run


def arr(dtype, *shape):
    return jax.ShapeDtypeStruct(shape, dtype)


class Ring:
    def __init__(self, size):
        self.size = size
        self.paired = size & (size - 1) == 0

    def source(self, i, d):
        return i ^ d if self.paired else (i + d) % self.size

    def target(self, i, d):
        return i ^ d if self.paired else (i + self.size - d) % self.size

    def seen(self, d, k):
        return d ^ k if self.paired else (k - d) % self.size

    def pairs(self, d):
        return [(self.source(i, d), i) for i in range(self.size)]


class Plan:
    def __init__(self, n, tok, hv, hk):
        self.n, self.tok, self.hv, self.hk = n, tok, hv, hk
        self.mates = n // hv
        self.v_at = 2 * tok
        self.aux_at = 2 * tok + DV
        self.rows = self.aux_at + AUX
        self.ring = Ring(hv)

    def key_head(self, head):
        return head * self.hk // self.hv

    def exchange(self, pieces):
        s = self.mates
        moved = [pieces[0]]
        for d in range(1, self.hv):
            pairs = [(i * s + b, j * s + b) for i, j in self.ring.pairs(d) for b in range(s)]
            moved.append(lax.ppermute(pieces[d], "ctx", pairs))
        return moved

    def exchange_at_once(self, pieces):
        s = self.mates
        groups = [[m * s + b for m in range(self.hv)] for b in range(s)]
        return lax.all_to_all(
            pieces, "ctx", split_axis=0, concat_axis=0, axis_index_groups=groups, tiled=True
        )

    def from_mate(self, x, d):
        s = self.mates
        pairs = [(i // s * s + (i + d) % s, i) for i in range(self.n)]
        return lax.ppermute(x, "ctx", pairs)


def aux_rows(rows, columns):
    row_ids = lax.broadcasted_iota(jnp.int32, (AUX, columns), 0)
    out = jnp.zeros((AUX, columns), F32)
    for i, part in enumerate(p for r in rows for p in thirds(r)):
        out = jnp.where(row_ids == i, part, out)
    return out.astype(BF16)


def pack_kernel(plan, q_ref, k_ref, v_ref, rate_ref, decay_ref, out_ref):
    tok = plan.tok
    for h in range(plan.hv):
        kh = plan.key_head(h)
        out_ref[h, :tok] = q_ref[:, kh * DK : (kh + 1) * DK]
        out_ref[h, tok : 2 * tok] = k_ref[:, kh * DK : (kh + 1) * DK]
        turned = jnp.transpose(v_ref[:, h * DV : (h + 1) * DV].astype(F32))
        out_ref[h, plan.v_at : plan.aux_at] = turned.astype(BF16)
        rows = [rate_ref[h : h + 1, :], decay_ref[h : h + 1, :]]
        out_ref[h, plan.aux_at :] = aux_rows(rows, tok)


def hand_out(plan, place, all_ref, outs):
    for d, ref in enumerate(outs):
        ref[...] = all_ref[plan.ring.target(place, d)]


def unit(x):
    scale = lax.rsqrt(jnp.sum(x * x, axis=1, keepdims=True) + EPS)
    return x * scale, scale


def segments(off_ref, positions):
    total = jnp.zeros(positions.shape, jnp.int32)
    for j in range(off_ref.shape[0] - 1):
        total = total + (off_ref[j] <= positions).astype(jnp.int32)
    return total


def to_columns(rows, tok):
    row_ids = lax.broadcasted_iota(jnp.int32, (tok, tok), 0)
    stacked = jnp.zeros((tok, tok), F32)
    for i, r in enumerate(rows):
        stacked = jnp.where(row_ids == i, r, stacked)
    turned = jnp.transpose(stacked)
    return [turned[:, i : i + 1] for i in range(len(rows))]


def to_rows(columns, tok):
    column_ids = lax.broadcasted_iota(jnp.int32, (tok, tok), 1)
    stacked = jnp.zeros((tok, tok), F32)
    for i, c in enumerate(columns):
        stacked = jnp.where(column_ids == i, c, stacked)
    turned = jnp.transpose(stacked)
    return [turned[i : i + 1, :] for i in range(len(columns))]


def scalings(plan, off_ref, chunks, auxes):
    tok = plan.tok
    rows, columns = iotas(tok, tok)
    upto = (rows <= columns).astype(BF16)
    sums = [dot(a, upto, 1, 0) for a in auxes]
    rates = [jnp.sum(a[0:3].astype(F32), axis=0, keepdims=True) for a in auxes]
    cumuls = [s[3:4] + s[4:5] + s[5:6] for s in sums]
    turned = to_columns(rates + cumuls, tok)
    out = []
    for i, c in enumerate(chunks):
        b_col, c_col = turned[i], turned[len(chunks) + i]
        c_row = cumuls[i]
        start = c * tok
        seg_col = segments(off_ref, start + rows[:, :1])
        seg_row = segments(off_ref, start + columns[:1, :])
        before = jnp.int32(0)
        last = jnp.int32(0)
        for j in range(off_ref.shape[0] - 1):
            before = before + (off_ref[j] <= start - 1).astype(jnp.int32)
            last = last + (off_ref[j] <= start + tok - 1).astype(jnp.int32)
        c_last = c_row[:, tok - 1 : tok]
        together = (seg_col == seg_row) & (rows >= columns)
        ratio = jnp.where(together, jnp.exp(jnp.where(together, c_col - c_row, 0.0)), 0.0)
        start_col = jnp.where(seg_col == before, jnp.exp(c_col), 0.0)
        end_col = jnp.where(seg_col == last, jnp.exp(c_last - c_col), 0.0)
        whole = jnp.where(last == before, jnp.exp(c_last), 0.0)
        out.append((rates[i], b_col, ratio, start_col, end_col, whole))
    return out


def inverses(lowers):
    size = lowers[0].shape[0]
    rows, columns = iotas(size, size)
    identity = (rows == columns).astype(F32)
    block = min(16, size)
    near = (rows // block) == (columns // block)
    powers = [jnp.where(near, -m, 0.0) for m in lowers]
    results = [identity + p for p in powers]
    split = [halves(p) for p in powers]
    powers = [mm(s, s) for s in split]
    reach = 2
    while reach < block:
        split = [halves(p) for p in powers]
        more = reach * 2 < block
        both = []
        for r, s in zip(results, split):
            left = halves(r)
            if more:
                left = cat([left, s], 0)
            both.append(mm(left, s))
        results = [r + b[:size] for r, b in zip(results, both)]
        if more:
            powers = [b[size:] for b in both]
        reach *= 2
    while block < size:
        across = ((rows // (2 * block)) == (columns // (2 * block))) & (
            (rows // block) > (columns // block)
        )
        split = [halves(r) for r in results]
        middle = [mm(halves(jnp.where(across, m, 0.0)), s) for m, s in zip(lowers, split)]
        results = [r - mm(s, halves(m)) for r, s, m in zip(results, split, middle)]
        block *= 2
    return results


def chunks_of(plan, place, mate):
    return [mate + plan.mates * plan.ring.source(place, d) for d in range(plan.hv)]


def in_place_order(plan, place, ref):
    return [ref.at[plan.ring.source(place, d)] for d in range(plan.hv)]


def prepare_kernel(plan, off_ref, place_ref, mate_ref, *refs):
    in_ref, link_ref, kept_ref = refs
    in_refs = in_place_order(plan, place_ref[0], in_ref)
    tok = plan.tok
    rows, columns = iotas(tok, tok)
    key_rows, key_columns = iotas(DK, DK)
    identity = (key_rows == key_columns).astype(F32)
    mine = range(plan.hv)
    chunks = chunks_of(plan, place_ref[0], mate_ref[0])
    scales = scalings(plan, off_ref, chunks, [r[plan.aux_at :] for r in in_refs])
    qn = [unit(in_refs[m][:tok].astype(F32))[0] for m in mine]
    kn = [unit(in_refs[m][tok : 2 * tok].astype(F32))[0] for m in mine]
    kp = [halves(x) for x in kn]
    qp = [halves(x) for x in qn]
    dots = [mm(cat([q, k], 0), k, 1, 1) for q, k in zip(qp, kp)]
    strict = rows > columns
    lowers = [jnp.where(strict, s[1] * d[tok:] * s[2], 0.0) for s, d in zip(scales, dots)]
    scores = [d[:tok] * s[2] for s, d in zip(scales, dots)]
    inv = inverses(lowers)
    rated = [halves(x * s[0]) for x, s in zip(inv, scales)]
    w = [mm(x, halves(s[3] * k)) for x, s, k in zip(rated, scales, kn)]
    values = [in_refs[m][plan.v_at : plan.aux_at] for m in mine]
    u = [
        dot(jnp.concatenate([v, v], axis=1), jnp.concatenate(x, axis=1), 1, 1)
        for v, x in zip(values, rated)
    ]
    wp = [halves(x) for x in w]
    up = [halves(x) for x in u]
    ap = [halves(x) for x in scores]
    ke = [halves(s[4] * k) for s, k in zip(scales, kn)]
    for m in mine:
        link_ref[m, 0] = scales[m][5] * identity - mm(wp[m], ke[m], 0, 0)
        link_ref[m, 1] = mm(up[m], ke[m])
    for m in mine:
        kept_ref[m, INVERSE] = inv[m]
        kept_ref[m, SCORES] = scores[m]
        kept_ref[m, FROM_STATE] = w[m]
        kept_ref[m, READS] = scales[m][3] * qn[m] - mm(ap[m], wp[m])
        kept_ref[m, RATIO] = scales[m][2]
        kept_ref[m, WRITES] = u[m]
        kept_ref[m, LOCAL] = mm(up[m], ap[m], 1, 1)


def lay_out(plan, place, mate, refs, all_ref):
    for d, ref in enumerate(refs):
        for m in range(plan.hv):
            all_ref[lax.rem(mate + d, plan.mates), plan.ring.source(place, m)] = ref[m]


def scan_kernel(plan, place_ref, mate_ref, *refs):
    s, hv = plan.mates, plan.hv
    links, kept_ref, state_ref = refs[:s], refs[s], refs[s + 1]
    outs, (all_ref, states_ref) = refs[s + 2 : -2], refs[-2:]
    place, mate = place_ref[0], mate_ref[0]
    lay_out(plan, place, mate, links, all_ref)
    state = jnp.zeros((DV, DK), F32)
    for c in range(plan.n):
        states_ref[c] = state
        if c < plan.n - 1:
            link = all_ref.at[c % s, c // s]
            state = link[1] + mm(halves(state), halves(link[0]))
    cores = []
    for m, c in enumerate(chunks_of(plan, place, mate)):
        state = states_ref[c]
        state_ref[m] = state
        core = kept_ref[m, LOCAL] + mm(halves(state), halves(kept_ref[m, READS]), 1, 1)
        cores.append(core.astype(BF16))
    for d in range(hv):
        for k in range(hv):
            outs[d][k] = cores[plan.ring.seen(d, k)]


def state_cotangent_kernel(plan, kept_ref, *refs):
    for m in range(plan.hv):
        refs[-1][m] = mm(d_out(refs[m]), halves(kept_ref[m, READS]))


def d_out(ref):
    return ref[:DV], ref[DV : 2 * DV]


def backward_kernel(plan, off_ref, place_ref, mate_ref, *refs):
    s, n, tok, hv = plan.mates, plan.n, plan.tok, plan.hv
    links, backs, in_ref, refs = refs[:s], refs[s : 2 * s], refs[2 * s], refs[2 * s + 1 :]
    d_refs, (kept_ref, state_ref, out_ref, links_ref, backs_ref, cots_ref) = refs[:hv], refs[hv:]
    place, mate = place_ref[0], mate_ref[0]
    in_refs = in_place_order(plan, place, in_ref)
    outs = in_place_order(plan, place, out_ref)
    lay_out(plan, place, mate, links, links_ref)
    lay_out(plan, place, mate, backs, backs_ref)
    d_state = jnp.zeros((DV, DK), F32)
    for c in reversed(range(n)):
        cots_ref[c] = d_state
        if c:
            d_state = backs_ref[c % s, c // s] + mm(
                halves(d_state), halves(links_ref[c % s, c // s, 0]), 1, 1
            )
    rows, columns = iotas(tok, tok)
    strict = rows > columns
    upto = (rows >= columns).astype(BF16)
    mine = range(hv)
    chunks = chunks_of(plan, place, mate)
    scales = scalings(plan, off_ref, chunks, [r[plan.aux_at :] for r in in_refs])
    qu = [unit(in_refs[m][:tok].astype(F32)) for m in mine]
    ku = [unit(in_refs[m][tok : 2 * tok].astype(F32)) for m in mine]
    qp = [halves(x[0]) for x in qu]
    kp = [halves(x[0]) for x in ku]
    do = [d_out(r) for r in d_refs]
    s0 = [state_ref[m] for m in mine]
    ds = [cots_ref[c] for c in chunks]
    s0p = [halves(x) for x in s0]
    dsp = [halves(x) for x in ds]
    pseudo = [kept_ref[m, WRITES] - mm(s0p[m], halves(kept_ref[m, FROM_STATE]), 1, 1) for m in mine]
    pp = [halves(x) for x in pseudo]
    ke = [halves(s[4] * k[0]) for s, k in zip(scales, ku)]
    dp = [mm(do[m], halves(kept_ref[m, SCORES])) + mm(dsp[m], ke[m], 1, 1) for m in mine]
    dr = [mm(halves(dp[m]), halves(kept_ref[m, INVERSE])) for m in mine]
    drp = [halves(x) for x in dr]
    big = [mm(cat([o, r], 1), cat([p, s], 1), 0, 0) for o, r, p, s in zip(do, drp, pp, s0p)]
    pds = [mm(p, d, 0, 0) for p, d in zip(pp, dsp)]
    da = [big[m][:tok, :tok] * kept_ref[m, RATIO] for m in mine]
    dm = [jnp.where(strict, -big[m][tok:, :tok] * kept_ref[m, RATIO], 0.0) for m in mine]
    dap = [halves(x) for x in da]
    dmp = [halves(x) for x in dm]
    dbm = [halves(s[1] * x) for s, x in zip(scales, dm)]
    by_row = [mm(cat([x, y], 0), k) for x, y, k in zip(dap, dmp, kp)]
    by_column = [
        mm(cat([x, y], 0), cat([q, k], 0), 0, 0) for x, y, q, k in zip(dap, dbm, qp, kp)
    ]
    sums = []
    for m in mine:
        _, b_col, _, start_col, end_col, whole = scales[m]
        (qn, q_scale), (kn, k_scale) = qu[m], ku[m]
        out = outs[m]
        dqn = by_row[m][:tok] + start_col * big[m][:tok, tok:]
        erase = by_row[m][tok:] - start_col * big[m][tok:, tok:]
        ends = end_col * pds[m]
        write = by_column[m] + ends
        dkn = b_col * erase + write
        s_q = jnp.sum(qn * dqn, axis=1, keepdims=True)
        s_e = jnp.sum(kn * erase, axis=1, keepdims=True)
        s_w = jnp.sum(kn * write, axis=1, keepdims=True)
        total = jnp.sum(jnp.sum(kn * ends, axis=1, keepdims=True), axis=0, keepdims=True)
        both = jnp.sum(jnp.sum(s0[m] * ds[m], axis=1, keepdims=True), axis=0, keepdims=True)
        out[:tok] = (q_scale * (dqn - qn * s_q)).astype(BF16)
        out[tok : 2 * tok] = (k_scale * (dkn - kn * (b_col * s_e + s_w))).astype(BF16)
        out[plan.v_at : plan.aux_at] = (scales[m][0] * dr[m]).astype(BF16)
        sums.append((s_e, s_q + b_col * s_e - s_w, total + whole * both))
    turned = to_rows([s[0] for s in sums] + [s[1] for s in sums], tok)
    for m in mine:
        values = in_refs[m][plan.v_at : plan.aux_at].astype(F32)
        d_rate = turned[m] + jnp.sum(dr[m] * values, axis=0, keepdims=True)
        parts = dot(aux_rows([turned[plan.hv + m]], tok), upto, 1, 0)
        d_decay = parts[0:1] + parts[1:2] + parts[2:3] + sums[m][2]
        outs[m][plan.aux_at :] = aux_rows([d_rate, d_decay], tok)


def gather_rows(head, pieces, all_ref):
    rows, ring = pieces[0].shape[0], Ring(len(pieces))
    for d, piece in enumerate(pieces):
        at = ring.source(head, d) * rows
        all_ref[pl.ds(pl.multiple_of(at, rows), rows), :] = piece[...]


def cotangent_kernel(plan, parts, head_ref, place_ref, *refs):
    pieces, w_ref, outs, (all_ref, out_ref) = refs[:parts], refs[parts], refs[parts + 1 : -2], refs[-2:]
    gather_rows(head_ref[0], pieces, all_ref)
    high, low = halves(dot(w_ref[...], all_ref[...], 1, 1))
    share = all_ref.shape[1] // plan.hv
    for m in range(plan.hv):
        out_ref[m, :DV] = high[m * DV : (m + 1) * DV]
        out_ref[m, DV : 2 * DV] = low[m * DV : (m + 1) * DV]
        part = all_ref[:, m * share : (m + 1) * share].astype(F32)
        out_ref[m, 2 * DV :] = jnp.transpose(part).astype(BF16)
    hand_out(plan, place_ref[0], out_ref, outs)


def project_kernel(plan, parts, head_ref, place_ref, *refs):
    mixed_refs, w_ref, outs, (all_ref, total_ref) = (
        refs[: plan.hv],
        refs[plan.hv],
        refs[plan.hv + 1 : -2],
        refs[-2:],
    )
    for d, ref in enumerate(mixed_refs):
        all_ref[plan.ring.source(place_ref[0], d)] = ref[0]
    mixed = all_ref[...].reshape(plan.hv * DV, plan.tok)
    total_ref[...] = dot(mixed, w_ref[...], 0, 0)
    rows, ring = outs[0].shape[0], Ring(parts)
    for d in range(parts):
        at = ring.target(head_ref[0], d) * rows
        block = total_ref[pl.ds(pl.multiple_of(at, rows), rows), :]
        outs[d][...] = block.astype(outs[d].dtype)


def weight_kernel(plan, place_ref, mate_ref, *refs):
    hv = plan.hv
    cot_refs, mixed_refs, outs, all_ref = refs[:hv], refs[hv : 2 * hv], refs[2 * hv : -1], refs[-1]
    for d, ref in enumerate(mixed_refs):
        head = plan.ring.source(place_ref[0], d)
        for k in range(hv):
            all_ref[k, head] = ref[k]
    share = outs[0].shape[0]
    for d, out_ref in enumerate(outs):
        at = lax.rem(mate_ref[0] + plan.mates - d, plan.mates) * share
        at = 2 * DV + pl.multiple_of(at, share)
        total = None
        for k in range(hv):
            mixed = all_ref[k].reshape(hv * DV, plan.tok)
            part = dot(cot_refs[k][pl.ds(at, share), :], mixed, 1, 1)
            total = part if total is None else total + part
        out_ref[...] = total


def finish_kernel(plan, in_ref, q_ref, k_ref, v_ref, rate_ref, decay_ref):
    tok = plan.tok
    for kh in range(plan.hk):
        mine = [h for h in range(plan.hv) if plan.key_head(h) == kh]
        for ref, at in ((q_ref, 0), (k_ref, tok)):
            total = in_ref[mine[0], at : at + tok].astype(F32)
            for h in mine[1:]:
                total = total + in_ref[h, at : at + tok].astype(F32)
            ref[:, kh * DK : (kh + 1) * DK] = total
    for h in range(plan.hv):
        v_ref[:, h * DV : (h + 1) * DV] = jnp.transpose(
            in_ref[h, plan.v_at : plan.aux_at].astype(F32)
        )
        aux = in_ref[h, plan.aux_at :].astype(F32)
        rate_ref[h : h + 1, :] = aux[0:1] + aux[1:2] + aux[2:3]
        decay_ref[h : h + 1, :] = aux[3:4] + aux[4:5] + aux[5:6]


def after(x, y):
    return lax.optimization_barrier((x, y))[0]


def per_device(
    queries, key_vectors, value_rows, write_rate, log_decay, doc_offsets, out_weight, grad_out
):
    n, parts = lax.axis_size("ctx"), lax.axis_size("head")
    tok, hv = queries.shape[0], write_rate.shape[0]
    hk, model = queries.shape[1] // DK, grad_out.shape[1]
    plan = Plan(n, tok, hv, hk)
    s = plan.mates
    index = lax.axis_index("ctx").astype(jnp.int32)
    place, mate = (index // s).reshape(1), (index % s).reshape(1)
    head = lax.axis_index("head").astype(jnp.int32).reshape(1)

    def across_heads(pieces):
        moved = [lax.ppermute(pieces[d], "head", Ring(parts).pairs(d)) for d in range(1, parts)]
        return [pieces[0]] + moved

    vmem = lambda dtype, *shape: pltpu.VMEM(shape, dtype)

    packed = call(
        partial(pack_kernel, plan),
        arr(BF16, hv, plan.rows, DK),
        fetch=range(5),
    )(queries, key_vectors, value_rows, write_rate, log_decay)
    got = plan.exchange_at_once(packed)
    rows = across_heads([after(grad_out, packed)] * parts)

    link, kept = call(
        partial(prepare_kernel, plan),
        (arr(F32, hv, 2, DK, DK), arr(F32, hv, KEPT, tok, DK)),
        smem=(0, 1, 2),
        flops=20_000_000_000,
    )(doc_offsets, place, mate, got)
    links = [link] + [plan.from_mate(link, d) for d in range(1, s)]

    cot = call(
        partial(cotangent_kernel, plan, parts),
        [arr(BF16, 2 * DV + model // hv, tok)] * hv,
        smem=(0, 1),
        scratch=[vmem(BF16, tok, model), vmem(BF16, hv, 2 * DV + model // hv, tok)],
        flops=30_000_000_000,
    )(head, place, *after(rows, link), out_weight)
    kept = after(kept, cot[0])
    cot = plan.exchange(cot)

    states, *mixed = call(
        partial(scan_kernel, plan),
        [arr(F32, hv, DV, DK)] + [arr(BF16, hv, DV, tok)] * hv,
        smem=(0, 1),
        scratch=[vmem(F32, s, hv, 2, DK, DK), vmem(F32, n, DV, DK)],
        flops=2_500_000_000,
    )(place, mate, *links, kept)
    mixed = plan.exchange(mixed)
    back = call(
        partial(state_cotangent_kernel, plan), arr(F32, hv, DV, DK), flops=500_000_000
    )(kept, *after(cot, states))
    backs = [back] + [plan.from_mate(back, d) for d in range(1, s)]

    projected = call(
        partial(project_kernel, plan, parts),
        [arr(BF16 if d else F32, tok // parts, model) for d in range(parts)],
        smem=(0, 1),
        scratch=[vmem(BF16, hv, DV, tok), vmem(F32, tok, model)],
        flops=1_000_000_000,
    )(head, place, *mixed, out_weight)
    layer_parts = across_heads(projected)

    grads = call(
        partial(backward_kernel, plan),
        arr(BF16, hv, plan.rows, DK),
        smem=(0, 1, 2),
        scratch=[
            vmem(F32, s, hv, 2, DK, DK),
            vmem(F32, s, hv, DV, DK),
            vmem(F32, n, DV, DK),
        ],
        flops=6_000_000_000,
    )(doc_offsets, place, mate, *links, *backs, got, *cot, kept, states)
    grads = plan.exchange_at_once(grads)

    shares = call(
        partial(weight_kernel, plan),
        [arr(F32, model // n, hv * DV)] * s,
        smem=(0, 1),
        scratch=[vmem(BF16, hv, hv, DV, tok)],
        flops=1_000_000_000,
    )(place, mate, *cot, *mixed)
    weight_grad = shares[0]
    for d in range(1, s):
        weight_grad = weight_grad + plan.from_mate(shares[d], d)

    grad_q, grad_k, grad_v, grad_rate, grad_decay = call(
        partial(finish_kernel, plan),
        (
            arr(F32, tok, hk * DK),
            arr(F32, tok, hk * DK),
            arr(F32, tok, hv * DV),
            arr(F32, hv, tok),
            arr(F32, hv, tok),
        ),
        flops=1_000_000_000,
        inside=False,
    )(grads)
    layer_out = after(layer_parts[0], (grad_q, weight_grad))
    for part in layer_parts[1:]:
        layer_out = layer_out + part.astype(F32)
    return (layer_out, grad_q, grad_k, grad_v, grad_rate, grad_decay, weight_grad)


def solution(mesh):
    placed = (
        P("ctx", "head"),
        P("ctx", "head"),
        P("ctx", "head"),
        P("head", "ctx"),
        P("head", "ctx"),
        P(),
        P("head", None),
        P(("ctx", "head"), None),
    )
    return jax.shard_map(
        per_device,
        mesh=mesh,
        in_specs=placed,
        out_specs=(
            P(("ctx", "head"), None),
            P("ctx", "head"),
            P("ctx", "head"),
            P("ctx", "head"),
            P("head", "ctx"),
            P("head", "ctx"),
            P("ctx", "head"),
        ),
        check_vma=False,
    )
```

```python
import math
from functools import partial

import jax
import jax.numpy as jnp
from jax import lax
from jax.experimental import pallas as pl
from jax.experimental.pallas import tpu as pltpu
from jax.sharding import PartitionSpec as P

DK = 128
DV = 128
AUX = 16
INVERSE, SCORES, FROM_STATE, READS, RATIO, WRITES, LOCAL, KEPT = range(8)
EPS = 1e-06
F32 = jnp.float32
BF16 = jnp.bfloat16
SPARE_VMEM = 8 * 1024 * 1024


def dot(a, b, ca, cb):
    return lax.dot_general(a, b, (((ca,), (cb,)), ((), ())), preferred_element_type=F32)


def halves(x):
    high = x.astype(BF16)
    return high, (x - high.astype(F32)).astype(BF16)


def thirds(x):
    high = x.astype(BF16).astype(F32)
    middle = (x - high).astype(BF16).astype(F32)
    return high, middle, x - high - middle


def mm(a, b, ca=1, cb=0):
    left = jnp.concatenate([a[0], a[0], a[1]], axis=ca)
    right = jnp.concatenate([b[0], b[1], b[0]], axis=cb)
    return dot(left, right, ca, cb)


def cat(pairs, axis):
    return tuple(jnp.concatenate(parts, axis=axis) for parts in zip(*pairs))


def iotas(rows, columns):
    shape = (rows, columns)
    return lax.broadcasted_iota(jnp.int32, shape, 0), lax.broadcasted_iota(jnp.int32, shape, 1)


def call(kernel, outs, smem=(), scratch=(), flops=0, inside=True, fetch=()):
    if inside:
        outs = jax.tree.map(lambda o: pltpu.VMEM(o.shape, o.dtype), outs)
    scoped = SPARE_VMEM + sum(x.dtype.itemsize * math.prod(x.shape) for x in scratch)

    def run(*args):
        spec = lambda i: pl.BlockSpec(memory_space=pltpu.SMEM if i in smem else pltpu.VMEM)
        space = lambda i: pltpu.HBM if i in fetch else pltpu.VMEM
        hold = pltpu.with_memory_space_constraint
        return pl.pallas_call(
            kernel,
            out_shape=outs,
            in_specs=[spec(i) for i in range(len(args))],
            out_specs=jax.tree.map(lambda _: pl.BlockSpec(memory_space=pltpu.VMEM), outs),
            scratch_shapes=list(scratch),
            compiler_params=pltpu.CompilerParams(vmem_limit_bytes=scoped),
            cost_estimate=pl.CostEstimate(flops=flops, bytes_accessed=0, transcendentals=0),
        )(*(x if i in smem else hold(x, space(i)) for i, x in enumerate(args)))

    return run


def arr(dtype, *shape):
    return jax.ShapeDtypeStruct(shape, dtype)


class Ring:
    def __init__(self, size):
        self.size = size
        self.paired = size & (size - 1) == 0

    def source(self, i, d):
        return i ^ d if self.paired else (i + d) % self.size

    def target(self, i, d):
        return i ^ d if self.paired else (i + self.size - d) % self.size

    def seen(self, d, k):
        return d ^ k if self.paired else (k - d) % self.size

    def pairs(self, d):
        return [(self.source(i, d), i) for i in range(self.size)]


class Plan:
    def __init__(self, n, tok, hv, hk):
        self.n, self.tok, self.hv, self.hk = n, tok, hv, hk
        self.mates = n // hv
        self.v_at = 2 * tok
        self.aux_at = 2 * tok + DV
        self.rows = self.aux_at + AUX
        self.ring = Ring(hv)

    def key_head(self, head):
        return head * self.hk // self.hv

    def exchange(self, pieces):
        s = self.mates
        moved = [pieces[0]]
        for d in range(1, self.hv):
            pairs = [(i * s + b, j * s + b) for i, j in self.ring.pairs(d) for b in range(s)]
            moved.append(lax.ppermute(pieces[d], "ctx", pairs))
        return moved

    def exchange_at_once(self, pieces):
        s = self.mates
        groups = [[m * s + b for m in range(self.hv)] for b in range(s)]
        return lax.all_to_all(
            pieces, "ctx", split_axis=0, concat_axis=0, axis_index_groups=groups, tiled=True
        )

    def from_mate(self, x, d):
        s = self.mates
        pairs = [(i // s * s + (i + d) % s, i) for i in range(self.n)]
        return lax.ppermute(x, "ctx", pairs)


def aux_rows(rows, columns):
    row_ids = lax.broadcasted_iota(jnp.int32, (AUX, columns), 0)
    out = jnp.zeros((AUX, columns), F32)
    for i, part in enumerate(p for r in rows for p in thirds(r)):
        out = jnp.where(row_ids == i, part, out)
    return out.astype(BF16)


def pack_kernel(plan, q_ref, k_ref, v_ref, rate_ref, decay_ref, out_ref):
    tok = plan.tok
    for h in range(plan.hv):
        kh = plan.key_head(h)
        out_ref[h, :tok] = q_ref[:, kh * DK : (kh + 1) * DK]
        out_ref[h, tok : 2 * tok] = k_ref[:, kh * DK : (kh + 1) * DK]
        turned = jnp.transpose(v_ref[:, h * DV : (h + 1) * DV].astype(F32))
        out_ref[h, plan.v_at : plan.aux_at] = turned.astype(BF16)
        rows = [rate_ref[h : h + 1, :], decay_ref[h : h + 1, :]]
        out_ref[h, plan.aux_at :] = aux_rows(rows, tok)


def hand_out(plan, place, all_ref, outs):
    for d, ref in enumerate(outs):
        ref[...] = all_ref[plan.ring.target(place, d)]


def unit(x):
    scale = lax.rsqrt(jnp.sum(x * x, axis=1, keepdims=True) + EPS)
    return x * scale, scale


def segments(off_ref, positions):
    total = jnp.zeros(positions.shape, jnp.int32)
    for j in range(off_ref.shape[0] - 1):
        total = total + (off_ref[j] <= positions).astype(jnp.int32)
    return total


def to_columns(rows, tok):
    row_ids = lax.broadcasted_iota(jnp.int32, (tok, tok), 0)
    stacked = jnp.zeros((tok, tok), F32)
    for i, r in enumerate(rows):
        stacked = jnp.where(row_ids == i, r, stacked)
    turned = jnp.transpose(stacked)
    return [turned[:, i : i + 1] for i in range(len(rows))]


def to_rows(columns, tok):
    column_ids = lax.broadcasted_iota(jnp.int32, (tok, tok), 1)
    stacked = jnp.zeros((tok, tok), F32)
    for i, c in enumerate(columns):
        stacked = jnp.where(column_ids == i, c, stacked)
    turned = jnp.transpose(stacked)
    return [turned[i : i + 1, :] for i in range(len(columns))]


def scalings(plan, off_ref, chunks, auxes):
    tok = plan.tok
    rows, columns = iotas(tok, tok)
    upto = (rows <= columns).astype(BF16)
    sums = [dot(a, upto, 1, 0) for a in auxes]
    rates = [jnp.sum(a[0:3].astype(F32), axis=0, keepdims=True) for a in auxes]
    cumuls = [s[3:4] + s[4:5] + s[5:6] for s in sums]
    turned = to_columns(rates + cumuls, tok)
    out = []
    for i, c in enumerate(chunks):
        b_col, c_col = turned[i], turned[len(chunks) + i]
        c_row = cumuls[i]
        start = c * tok
        seg_col = segments(off_ref, start + rows[:, :1])
        seg_row = segments(off_ref, start + columns[:1, :])
        before = jnp.int32(0)
        last = jnp.int32(0)
        for j in range(off_ref.shape[0] - 1):
            before = before + (off_ref[j] <= start - 1).astype(jnp.int32)
            last = last + (off_ref[j] <= start + tok - 1).astype(jnp.int32)
        c_last = c_row[:, tok - 1 : tok]
        together = (seg_col == seg_row) & (rows >= columns)
        ratio = jnp.where(together, jnp.exp(jnp.where(together, c_col - c_row, 0.0)), 0.0)
        start_col = jnp.where(seg_col == before, jnp.exp(c_col), 0.0)
        end_col = jnp.where(seg_col == last, jnp.exp(c_last - c_col), 0.0)
        whole = jnp.where(last == before, jnp.exp(c_last), 0.0)
        out.append((rates[i], b_col, ratio, start_col, end_col, whole))
    return out


def inverses(lowers):
    size = lowers[0].shape[0]
    rows, columns = iotas(size, size)
    identity = (rows == columns).astype(F32)
    block = min(16, size)
    near = (rows // block) == (columns // block)
    powers = [jnp.where(near, -m, 0.0) for m in lowers]
    results = [identity + p for p in powers]
    split = [halves(p) for p in powers]
    powers = [mm(s, s) for s in split]
    reach = 2
    while reach < block:
        split = [halves(p) for p in powers]
        more = reach * 2 < block
        both = []
        for r, s in zip(results, split):
            left = halves(r)
            if more:
                left = cat([left, s], 0)
            both.append(mm(left, s))
        results = [r + b[:size] for r, b in zip(results, both)]
        if more:
            powers = [b[size:] for b in both]
        reach *= 2
    while block < size:
        across = ((rows // (2 * block)) == (columns // (2 * block))) & (
            (rows // block) > (columns // block)
        )
        split = [halves(r) for r in results]
        middle = [mm(halves(jnp.where(across, m, 0.0)), s) for m, s in zip(lowers, split)]
        results = [r - mm(s, halves(m)) for r, s, m in zip(results, split, middle)]
        block *= 2
    return results


def chunks_of(plan, place, mate):
    return [mate + plan.mates * plan.ring.source(place, d) for d in range(plan.hv)]


def in_place_order(plan, place, ref):
    return [ref.at[plan.ring.source(place, d)] for d in range(plan.hv)]


def prepare_kernel(plan, off_ref, place_ref, mate_ref, *refs):
    in_ref, link_ref, kept_ref = refs
    in_refs = in_place_order(plan, place_ref[0], in_ref)
    tok = plan.tok
    rows, columns = iotas(tok, tok)
    key_rows, key_columns = iotas(DK, DK)
    identity = (key_rows == key_columns).astype(F32)
    mine = range(plan.hv)
    chunks = chunks_of(plan, place_ref[0], mate_ref[0])
    scales = scalings(plan, off_ref, chunks, [r[plan.aux_at :] for r in in_refs])
    qn = [unit(in_refs[m][:tok].astype(F32))[0] for m in mine]
    kn = [unit(in_refs[m][tok : 2 * tok].astype(F32))[0] for m in mine]
    kp = [halves(x) for x in kn]
    qp = [halves(x) for x in qn]
    dots = [mm(cat([q, k], 0), k, 1, 1) for q, k in zip(qp, kp)]
    strict = rows > columns
    lowers = [jnp.where(strict, s[1] * d[tok:] * s[2], 0.0) for s, d in zip(scales, dots)]
    scores = [d[:tok] * s[2] for s, d in zip(scales, dots)]
    inv = inverses(lowers)
    rated = [halves(x * s[0]) for x, s in zip(inv, scales)]
    w = [mm(x, halves(s[3] * k)) for x, s, k in zip(rated, scales, kn)]
    values = [in_refs[m][plan.v_at : plan.aux_at] for m in mine]
    u = [
        dot(jnp.concatenate([v, v], axis=1), jnp.concatenate(x, axis=1), 1, 1)
        for v, x in zip(values, rated)
    ]
    wp = [halves(x) for x in w]
    up = [halves(x) for x in u]
    ap = [halves(x) for x in scores]
    ke = [halves(s[4] * k) for s, k in zip(scales, kn)]
    for m in mine:
        link_ref[m, 0] = scales[m][5] * identity - mm(wp[m], ke[m], 0, 0)
        link_ref[m, 1] = mm(up[m], ke[m])
    for m in mine:
        kept_ref[m, INVERSE] = inv[m]
        kept_ref[m, SCORES] = scores[m]
        kept_ref[m, FROM_STATE] = w[m]
        kept_ref[m, READS] = scales[m][3] * qn[m] - mm(ap[m], wp[m])
        kept_ref[m, RATIO] = scales[m][2]
        kept_ref[m, WRITES] = u[m]
        kept_ref[m, LOCAL] = mm(up[m], ap[m], 1, 1)


def lay_out(plan, place, mate, refs, all_ref):
    for d, ref in enumerate(refs):
        for m in range(plan.hv):
            all_ref[lax.rem(mate + d, plan.mates), plan.ring.source(place, m)] = ref[m]


def scan_kernel(plan, place_ref, mate_ref, *refs):
    s, hv = plan.mates, plan.hv
    links, kept_ref, state_ref = refs[:s], refs[s], refs[s + 1]
    outs, (all_ref, states_ref) = refs[s + 2 : -2], refs[-2:]
    place, mate = place_ref[0], mate_ref[0]
    lay_out(plan, place, mate, links, all_ref)
    state = jnp.zeros((DV, DK), F32)
    for c in range(plan.n):
        states_ref[c] = state
        if c < plan.n - 1:
            link = all_ref.at[c % s, c // s]
            state = link[1] + mm(halves(state), halves(link[0]))
    cores = []
    for m, c in enumerate(chunks_of(plan, place, mate)):
        state = states_ref[c]
        state_ref[m] = state
        core = kept_ref[m, LOCAL] + mm(halves(state), halves(kept_ref[m, READS]), 1, 1)
        cores.append(core.astype(BF16))
    for d in range(hv):
        for k in range(hv):
            outs[d][k] = cores[plan.ring.seen(d, k)]


def state_cotangent_kernel(plan, kept_ref, *refs):
    for m in range(plan.hv):
        refs[-1][m] = mm(d_out(refs[m]), halves(kept_ref[m, READS]))


def d_out(ref):
    return ref[:DV], ref[DV : 2 * DV]


def backward_kernel(plan, off_ref, place_ref, mate_ref, *refs):
    s, n, tok, hv = plan.mates, plan.n, plan.tok, plan.hv
    links, backs, in_ref, refs = refs[:s], refs[s : 2 * s], refs[2 * s], refs[2 * s + 1 :]
    d_refs, (kept_ref, state_ref, out_ref, links_ref, backs_ref, cots_ref) = refs[:hv], refs[hv:]
    place, mate = place_ref[0], mate_ref[0]
    in_refs = in_place_order(plan, place, in_ref)
    outs = in_place_order(plan, place, out_ref)
    lay_out(plan, place, mate, links, links_ref)
    lay_out(plan, place, mate, backs, backs_ref)
    d_state = jnp.zeros((DV, DK), F32)
    for c in reversed(range(n)):
        cots_ref[c] = d_state
        if c:
            d_state = backs_ref[c % s, c // s] + mm(
                halves(d_state), halves(links_ref[c % s, c // s, 0]), 1, 1
            )
    rows, columns = iotas(tok, tok)
    strict = rows > columns
    upto = (rows >= columns).astype(BF16)
    mine = range(hv)
    chunks = chunks_of(plan, place, mate)
    scales = scalings(plan, off_ref, chunks, [r[plan.aux_at :] for r in in_refs])
    qu = [unit(in_refs[m][:tok].astype(F32)) for m in mine]
    ku = [unit(in_refs[m][tok : 2 * tok].astype(F32)) for m in mine]
    qp = [halves(x[0]) for x in qu]
    kp = [halves(x[0]) for x in ku]
    do = [d_out(r) for r in d_refs]
    s0 = [state_ref[m] for m in mine]
    ds = [cots_ref[c] for c in chunks]
    s0p = [halves(x) for x in s0]
    dsp = [halves(x) for x in ds]
    pseudo = [kept_ref[m, WRITES] - mm(s0p[m], halves(kept_ref[m, FROM_STATE]), 1, 1) for m in mine]
    pp = [halves(x) for x in pseudo]
    ke = [halves(s[4] * k[0]) for s, k in zip(scales, ku)]
    dp = [mm(do[m], halves(kept_ref[m, SCORES])) + mm(dsp[m], ke[m], 1, 1) for m in mine]
    dr = [mm(halves(dp[m]), halves(kept_ref[m, INVERSE])) for m in mine]
    drp = [halves(x) for x in dr]
    big = [mm(cat([o, r], 1), cat([p, s], 1), 0, 0) for o, r, p, s in zip(do, drp, pp, s0p)]
    pds = [mm(p, d, 0, 0) for p, d in zip(pp, dsp)]
    da = [big[m][:tok, :tok] * kept_ref[m, RATIO] for m in mine]
    dm = [jnp.where(strict, -big[m][tok:, :tok] * kept_ref[m, RATIO], 0.0) for m in mine]
    dap = [halves(x) for x in da]
    dmp = [halves(x) for x in dm]
    dbm = [halves(s[1] * x) for s, x in zip(scales, dm)]
    by_row = [mm(cat([x, y], 0), k) for x, y, k in zip(dap, dmp, kp)]
    by_column = [
        mm(cat([x, y], 0), cat([q, k], 0), 0, 0) for x, y, q, k in zip(dap, dbm, qp, kp)
    ]
    sums = []
    for m in mine:
        _, b_col, _, start_col, end_col, whole = scales[m]
        (qn, q_scale), (kn, k_scale) = qu[m], ku[m]
        out = outs[m]
        dqn = by_row[m][:tok] + start_col * big[m][:tok, tok:]
        erase = by_row[m][tok:] - start_col * big[m][tok:, tok:]
        ends = end_col * pds[m]
        write = by_column[m] + ends
        dkn = b_col * erase + write
        s_q = jnp.sum(qn * dqn, axis=1, keepdims=True)
        s_e = jnp.sum(kn * erase, axis=1, keepdims=True)
        s_w = jnp.sum(kn * write, axis=1, keepdims=True)
        total = jnp.sum(jnp.sum(kn * ends, axis=1, keepdims=True), axis=0, keepdims=True)
        both = jnp.sum(jnp.sum(s0[m] * ds[m], axis=1, keepdims=True), axis=0, keepdims=True)
        out[:tok] = (q_scale * (dqn - qn * s_q)).astype(BF16)
        out[tok : 2 * tok] = (k_scale * (dkn - kn * (b_col * s_e + s_w))).astype(BF16)
        out[plan.v_at : plan.aux_at] = (scales[m][0] * dr[m]).astype(BF16)
        sums.append((s_e, s_q + b_col * s_e - s_w, total + whole * both))
    turned = to_rows([s[0] for s in sums] + [s[1] for s in sums], tok)
    for m in mine:
        values = in_refs[m][plan.v_at : plan.aux_at].astype(F32)
        d_rate = turned[m] + jnp.sum(dr[m] * values, axis=0, keepdims=True)
        parts = dot(aux_rows([turned[plan.hv + m]], tok), upto, 1, 0)
        d_decay = parts[0:1] + parts[1:2] + parts[2:3] + sums[m][2]
        outs[m][plan.aux_at :] = aux_rows([d_rate, d_decay], tok)


def gather_rows(head, pieces, all_ref):
    rows, ring = pieces[0].shape[0], Ring(len(pieces))
    for d, piece in enumerate(pieces):
        at = ring.source(head, d) * rows
        all_ref[pl.ds(pl.multiple_of(at, rows), rows), :] = piece[...]


def cotangent_kernel(plan, parts, head_ref, place_ref, *refs):
    pieces, w_ref, outs, (all_ref, out_ref) = refs[:parts], refs[parts], refs[parts + 1 : -2], refs[-2:]
    gather_rows(head_ref[0], pieces, all_ref)
    high, low = halves(dot(w_ref[...], all_ref[...], 1, 1))
    share = all_ref.shape[1] // plan.hv
    for m in range(plan.hv):
        out_ref[m, :DV] = high[m * DV : (m + 1) * DV]
        out_ref[m, DV : 2 * DV] = low[m * DV : (m + 1) * DV]
        part = all_ref[:, m * share : (m + 1) * share].astype(F32)
        out_ref[m, 2 * DV :] = jnp.transpose(part).astype(BF16)
    hand_out(plan, place_ref[0], out_ref, outs)


def project_kernel(plan, parts, head_ref, place_ref, *refs):
    mixed_refs, w_ref, outs, (all_ref, total_ref) = (
        refs[: plan.hv],
        refs[plan.hv],
        refs[plan.hv + 1 : -2],
        refs[-2:],
    )
    for d, ref in enumerate(mixed_refs):
        all_ref[plan.ring.source(place_ref[0], d)] = ref[0]
    mixed = all_ref[...].reshape(plan.hv * DV, plan.tok)
    total_ref[...] = dot(mixed, w_ref[...], 0, 0)
    rows, ring = outs[0].shape[0], Ring(parts)
    for d in range(parts):
        at = ring.target(head_ref[0], d) * rows
        block = total_ref[pl.ds(pl.multiple_of(at, rows), rows), :]
        outs[d][...] = block.astype(outs[d].dtype)


def weight_kernel(plan, place_ref, mate_ref, *refs):
    hv = plan.hv
    cot_refs, mixed_refs, outs, all_ref = refs[:hv], refs[hv : 2 * hv], refs[2 * hv : -1], refs[-1]
    for d, ref in enumerate(mixed_refs):
        head = plan.ring.source(place_ref[0], d)
        for k in range(hv):
            all_ref[k, head] = ref[k]
    share = outs[0].shape[0]
    for d, out_ref in enumerate(outs):
        at = lax.rem(mate_ref[0] + plan.mates - d, plan.mates) * share
        at = 2 * DV + pl.multiple_of(at, share)
        total = None
        for k in range(hv):
            mixed = all_ref[k].reshape(hv * DV, plan.tok)
            part = dot(cot_refs[k][pl.ds(at, share), :], mixed, 1, 1)
            total = part if total is None else total + part
        out_ref[...] = total


def finish_kernel(plan, in_ref, q_ref, k_ref, v_ref, rate_ref, decay_ref):
    tok = plan.tok
    for kh in range(plan.hk):
        mine = [h for h in range(plan.hv) if plan.key_head(h) == kh]
        for ref, at in ((q_ref, 0), (k_ref, tok)):
            total = in_ref[mine[0], at : at + tok].astype(F32)
            for h in mine[1:]:
                total = total + in_ref[h, at : at + tok].astype(F32)
            ref[:, kh * DK : (kh + 1) * DK] = total
    for h in range(plan.hv):
        v_ref[:, h * DV : (h + 1) * DV] = jnp.transpose(
            in_ref[h, plan.v_at : plan.aux_at].astype(F32)
        )
        aux = in_ref[h, plan.aux_at :].astype(F32)
        rate_ref[h : h + 1, :] = aux[0:1] + aux[1:2] + aux[2:3]
        decay_ref[h : h + 1, :] = aux[3:4] + aux[4:5] + aux[5:6]


def after(x, y):
    return lax.optimization_barrier((x, y))[0]


def per_device(
    queries, key_vectors, value_rows, write_rate, log_decay, doc_offsets, out_weight, grad_out
):
    n, parts = lax.axis_size("ctx"), lax.axis_size("head")
    tok, hv = queries.shape[0], write_rate.shape[0]
    hk, model = queries.shape[1] // DK, grad_out.shape[1]
    plan = Plan(n, tok, hv, hk)
    s = plan.mates
    index = lax.axis_index("ctx").astype(jnp.int32)
    place, mate = (index // s).reshape(1), (index % s).reshape(1)
    head = lax.axis_index("head").astype(jnp.int32).reshape(1)

    def across_heads(pieces):
        moved = [lax.ppermute(pieces[d], "head", Ring(parts).pairs(d)) for d in range(1, parts)]
        return [pieces[0]] + moved

    vmem = lambda dtype, *shape: pltpu.VMEM(shape, dtype)

    packed = call(
        partial(pack_kernel, plan),
        arr(BF16, hv, plan.rows, DK),
        fetch=range(5),
    )(queries, key_vectors, value_rows, write_rate, log_decay)
    got = plan.exchange_at_once(packed)
    rows = across_heads([after(grad_out, packed)] * parts)

    link, kept = call(
        partial(prepare_kernel, plan),
        (arr(F32, hv, 2, DK, DK), arr(F32, hv, KEPT, tok, DK)),
        smem=(0, 1, 2),
        flops=20_000_000_000,
    )(doc_offsets, place, mate, got)
    links = [link] + [plan.from_mate(link, d) for d in range(1, s)]

    cot = call(
        partial(cotangent_kernel, plan, parts),
        [arr(BF16, 2 * DV + model // hv, tok)] * hv,
        smem=(0, 1),
        scratch=[vmem(BF16, tok, model), vmem(BF16, hv, 2 * DV + model // hv, tok)],
        flops=30_000_000_000,
    )(head, place, *after(rows, link), out_weight)
    kept = after(kept, cot[0])
    cot = plan.exchange(cot)

    states, *mixed = call(
        partial(scan_kernel, plan),
        [arr(F32, hv, DV, DK)] + [arr(BF16, hv, DV, tok)] * hv,
        smem=(0, 1),
        scratch=[vmem(F32, s, hv, 2, DK, DK), vmem(F32, n, DV, DK)],
        flops=2_500_000_000,
    )(place, mate, *links, kept)
    mixed = plan.exchange(mixed)
    back = call(
        partial(state_cotangent_kernel, plan), arr(F32, hv, DV, DK), flops=30_000_000_000
    )(kept, *after(cot, mixed[1]))
    backs = [back] + [plan.from_mate(back, d) for d in range(1, s)]

    projected = call(
        partial(project_kernel, plan, parts),
        [arr(BF16 if d else F32, tok // parts, model) for d in range(parts)],
        smem=(0, 1),
        scratch=[vmem(BF16, hv, DV, tok), vmem(F32, tok, model)],
        flops=1_000_000_000,
    )(head, place, *mixed, out_weight)
    layer_parts = across_heads(projected)

    grads = call(
        partial(backward_kernel, plan),
        arr(BF16, hv, plan.rows, DK),
        smem=(0, 1, 2),
        scratch=[
            vmem(F32, s, hv, 2, DK, DK),
            vmem(F32, s, hv, DV, DK),
            vmem(F32, n, DV, DK),
        ],
        flops=6_000_000_000,
    )(doc_offsets, place, mate, *links, *backs, got, *cot, kept, after(states, projected[1]))

    shares = call(
        partial(weight_kernel, plan),
        [arr(F32, model // n, hv * DV)] * s,
        smem=(0, 1),
        scratch=[vmem(BF16, hv, hv, DV, tok)],
        flops=1_000_000_000,
    )(place, mate, *cot, *mixed)
    grads = plan.exchange_at_once(after(grads, shares[0]))
    weight_grad = shares[0]
    for d in range(1, s):
        weight_grad = weight_grad + plan.from_mate(shares[d], d)

    grad_q, grad_k, grad_v, grad_rate, grad_decay = call(
        partial(finish_kernel, plan),
        (
            arr(F32, tok, hk * DK),
            arr(F32, tok, hk * DK),
            arr(F32, tok, hv * DV),
            arr(F32, hv, tok),
            arr(F32, hv, tok),
        ),
        flops=1_000_000_000,
        inside=False,
    )(grads)
    layer_out = after(layer_parts[0], (grad_q, weight_grad))
    for part in layer_parts[1:]:
        layer_out = layer_out + part.astype(F32)
    return (layer_out, grad_q, grad_k, grad_v, grad_rate, grad_decay, weight_grad)


def solution(mesh):
    placed = (
        P("ctx", "head"),
        P("ctx", "head"),
        P("ctx", "head"),
        P("head", "ctx"),
        P("head", "ctx"),
        P(),
        P("head", None),
        P(("ctx", "head"), None),
    )
    return jax.shard_map(
        per_device,
        mesh=mesh,
        in_specs=placed,
        out_specs=(
            P(("ctx", "head"), None),
            P("ctx", "head"),
            P("ctx", "head"),
            P("ctx", "head"),
            P("head", "ctx"),
            P("head", "ctx"),
            P("ctx", "head"),
        ),
        check_vma=False,
    )
```

```python
import math
from functools import partial

import jax
import jax.numpy as jnp
from jax import lax
from jax.experimental import pallas as pl
from jax.experimental.pallas import tpu as pltpu
from jax.sharding import PartitionSpec as P

DK = 128
DV = 128
AUX = 16
INVERSE, SCORES, FROM_STATE, READS, RATIO, WRITES, LOCAL, KEPT = range(8)
EPS = 1e-06
F32 = jnp.float32
BF16 = jnp.bfloat16
SPARE_VMEM = 8 * 1024 * 1024


def dot(a, b, ca, cb):
    return lax.dot_general(a, b, (((ca,), (cb,)), ((), ())), preferred_element_type=F32)


def halves(x):
    high = x.astype(BF16)
    return high, (x - high.astype(F32)).astype(BF16)


def thirds(x):
    high = x.astype(BF16).astype(F32)
    middle = (x - high).astype(BF16).astype(F32)
    return high, middle, x - high - middle


def mm(a, b, ca=1, cb=0):
    left = jnp.concatenate([a[0], a[0], a[1]], axis=ca)
    right = jnp.concatenate([b[0], b[1], b[0]], axis=cb)
    return dot(left, right, ca, cb)


def cat(pairs, axis):
    return tuple(jnp.concatenate(parts, axis=axis) for parts in zip(*pairs))


def iotas(rows, columns):
    shape = (rows, columns)
    return lax.broadcasted_iota(jnp.int32, shape, 0), lax.broadcasted_iota(jnp.int32, shape, 1)


def call(kernel, outs, smem=(), scratch=(), flops=0, inside=True, fetch=()):
    if inside:
        outs = jax.tree.map(lambda o: pltpu.VMEM(o.shape, o.dtype), outs)
    scoped = SPARE_VMEM + sum(x.dtype.itemsize * math.prod(x.shape) for x in scratch)

    def run(*args):
        spec = lambda i: pl.BlockSpec(memory_space=pltpu.SMEM if i in smem else pltpu.VMEM)
        space = lambda i: pltpu.HBM if i in fetch else pltpu.VMEM
        hold = pltpu.with_memory_space_constraint
        return pl.pallas_call(
            kernel,
            out_shape=outs,
            in_specs=[spec(i) for i in range(len(args))],
            out_specs=jax.tree.map(lambda _: pl.BlockSpec(memory_space=pltpu.VMEM), outs),
            scratch_shapes=list(scratch),
            compiler_params=pltpu.CompilerParams(vmem_limit_bytes=scoped),
            cost_estimate=pl.CostEstimate(flops=flops, bytes_accessed=0, transcendentals=0),
        )(*(hold(x, space(i)) if i in fetch or i not in smem else x for i, x in enumerate(args)))

    return run


def arr(dtype, *shape):
    return jax.ShapeDtypeStruct(shape, dtype)


class Ring:
    def __init__(self, size):
        self.size = size
        self.paired = size & (size - 1) == 0

    def source(self, i, d):
        return i ^ d if self.paired else (i + d) % self.size

    def target(self, i, d):
        return i ^ d if self.paired else (i + self.size - d) % self.size

    def seen(self, d, k):
        return d ^ k if self.paired else (k - d) % self.size

    def pairs(self, d):
        return [(self.source(i, d), i) for i in range(self.size)]


class Plan:
    def __init__(self, n, tok, hv, hk):
        self.n, self.tok, self.hv, self.hk = n, tok, hv, hk
        self.mates = n // hv
        self.v_at = 2 * tok
        self.aux_at = 2 * tok + DV
        self.rows = self.aux_at + AUX
        self.ring = Ring(hv)

    def key_head(self, head):
        return head * self.hk // self.hv

    def exchange(self, pieces):
        s = self.mates
        moved = [pieces[0]]
        for d in range(1, self.hv):
            pairs = [(i * s + b, j * s + b) for i, j in self.ring.pairs(d) for b in range(s)]
            moved.append(lax.ppermute(pieces[d], "ctx", pairs))
        return moved

    def from_mate(self, x, d):
        s = self.mates
        pairs = [(i // s * s + (i + d) % s, i) for i in range(self.n)]
        return lax.ppermute(x, "ctx", pairs)


def aux_rows(rows, columns):
    row_ids = lax.broadcasted_iota(jnp.int32, (AUX, columns), 0)
    out = jnp.zeros((AUX, columns), F32)
    for i, part in enumerate(p for r in rows for p in thirds(r)):
        out = jnp.where(row_ids == i, part, out)
    return out.astype(BF16)


def pack_kernel(plan, place_ref, q_ref, k_ref, v_ref, rate_ref, decay_ref, *refs):
    outs, out_ref = refs[:-1], refs[-1]
    tok = plan.tok
    for h in range(plan.hv):
        kh = plan.key_head(h)
        out_ref[h, :tok] = q_ref[:, kh * DK : (kh + 1) * DK]
        out_ref[h, tok : 2 * tok] = k_ref[:, kh * DK : (kh + 1) * DK]
        turned = jnp.transpose(v_ref[:, h * DV : (h + 1) * DV].astype(F32))
        out_ref[h, plan.v_at : plan.aux_at] = turned.astype(BF16)
        rows = [rate_ref[h : h + 1, :], decay_ref[h : h + 1, :]]
        out_ref[h, plan.aux_at :] = aux_rows(rows, tok)
    hand_out(plan, place_ref[0], out_ref, outs)


def hand_out(plan, place, all_ref, outs):
    for d, ref in enumerate(outs):
        ref[...] = all_ref[plan.ring.target(place, d)]


def unit(x):
    scale = lax.rsqrt(jnp.sum(x * x, axis=1, keepdims=True) + EPS)
    return x * scale, scale


def segments(off_ref, positions):
    total = jnp.zeros(positions.shape, jnp.int32)
    for j in range(off_ref.shape[0] - 1):
        total = total + (off_ref[j] <= positions).astype(jnp.int32)
    return total


def to_columns(rows, tok):
    row_ids = lax.broadcasted_iota(jnp.int32, (tok, tok), 0)
    stacked = jnp.zeros((tok, tok), F32)
    for i, r in enumerate(rows):
        stacked = jnp.where(row_ids == i, r, stacked)
    turned = jnp.transpose(stacked)
    return [turned[:, i : i + 1] for i in range(len(rows))]


def to_rows(columns, tok):
    column_ids = lax.broadcasted_iota(jnp.int32, (tok, tok), 1)
    stacked = jnp.zeros((tok, tok), F32)
    for i, c in enumerate(columns):
        stacked = jnp.where(column_ids == i, c, stacked)
    turned = jnp.transpose(stacked)
    return [turned[i : i + 1, :] for i in range(len(columns))]


def scalings(plan, off_ref, chunks, auxes):
    tok = plan.tok
    rows, columns = iotas(tok, tok)
    upto = (rows <= columns).astype(BF16)
    sums = [dot(a, upto, 1, 0) for a in auxes]
    rates = [jnp.sum(a[0:3].astype(F32), axis=0, keepdims=True) for a in auxes]
    cumuls = [s[3:4] + s[4:5] + s[5:6] for s in sums]
    turned = to_columns(rates + cumuls, tok)
    out = []
    for i, c in enumerate(chunks):
        b_col, c_col = turned[i], turned[len(chunks) + i]
        c_row = cumuls[i]
        start = c * tok
        seg_col = segments(off_ref, start + rows[:, :1])
        seg_row = segments(off_ref, start + columns[:1, :])
        before = jnp.int32(0)
        last = jnp.int32(0)
        for j in range(off_ref.shape[0] - 1):
            before = before + (off_ref[j] <= start - 1).astype(jnp.int32)
            last = last + (off_ref[j] <= start + tok - 1).astype(jnp.int32)
        c_last = c_row[:, tok - 1 : tok]
        together = (seg_col == seg_row) & (rows >= columns)
        ratio = jnp.where(together, jnp.exp(jnp.where(together, c_col - c_row, 0.0)), 0.0)
        start_col = jnp.where(seg_col == before, jnp.exp(c_col), 0.0)
        end_col = jnp.where(seg_col == last, jnp.exp(c_last - c_col), 0.0)
        whole = jnp.where(last == before, jnp.exp(c_last), 0.0)
        out.append((rates[i], b_col, ratio, start_col, end_col, whole))
    return out


def inverses(lowers):
    size = lowers[0].shape[0]
    rows, columns = iotas(size, size)
    identity = (rows == columns).astype(F32)
    block = min(16, size)
    near = (rows // block) == (columns // block)
    powers = [jnp.where(near, -m, 0.0) for m in lowers]
    results = [identity + p for p in powers]
    split = [halves(p) for p in powers]
    powers = [mm(s, s) for s in split]
    reach = 2
    while reach < block:
        split = [halves(p) for p in powers]
        more = reach * 2 < block
        both = []
        for r, s in zip(results, split):
            left = halves(r)
            if more:
                left = cat([left, s], 0)
            both.append(mm(left, s))
        results = [r + b[:size] for r, b in zip(results, both)]
        if more:
            powers = [b[size:] for b in both]
        reach *= 2
    while block < size:
        across = ((rows // (2 * block)) == (columns // (2 * block))) & (
            (rows // block) > (columns // block)
        )
        split = [halves(r) for r in results]
        middle = [mm(halves(jnp.where(across, m, 0.0)), s) for m, s in zip(lowers, split)]
        results = [r - mm(s, halves(m)) for r, s, m in zip(results, split, middle)]
        block *= 2
    return results


def chunks_of(plan, place, mate):
    return [mate + plan.mates * plan.ring.source(place, d) for d in range(plan.hv)]


def prepare_kernel(plan, off_ref, place_ref, mate_ref, *refs):
    in_refs, (link_ref, kept_ref) = refs[: plan.hv], refs[plan.hv :]
    tok = plan.tok
    rows, columns = iotas(tok, tok)
    key_rows, key_columns = iotas(DK, DK)
    identity = (key_rows == key_columns).astype(F32)
    mine = range(plan.hv)
    chunks = chunks_of(plan, place_ref[0], mate_ref[0])
    scales = scalings(plan, off_ref, chunks, [r[plan.aux_at :] for r in in_refs])
    qn = [unit(in_refs[m][:tok].astype(F32))[0] for m in mine]
    kn = [unit(in_refs[m][tok : 2 * tok].astype(F32))[0] for m in mine]
    kp = [halves(x) for x in kn]
    qp = [halves(x) for x in qn]
    dots = [mm(cat([q, k], 0), k, 1, 1) for q, k in zip(qp, kp)]
    strict = rows > columns
    lowers = [jnp.where(strict, s[1] * d[tok:] * s[2], 0.0) for s, d in zip(scales, dots)]
    scores = [d[:tok] * s[2] for s, d in zip(scales, dots)]
    inv = inverses(lowers)
    rated = [halves(x * s[0]) for x, s in zip(inv, scales)]
    w = [mm(x, halves(s[3] * k)) for x, s, k in zip(rated, scales, kn)]
    values = [in_refs[m][plan.v_at : plan.aux_at] for m in mine]
    u = [
        dot(jnp.concatenate([v, v], axis=1), jnp.concatenate(x, axis=1), 1, 1)
        for v, x in zip(values, rated)
    ]
    wp = [halves(x) for x in w]
    up = [halves(x) for x in u]
    ap = [halves(x) for x in scores]
    ke = [halves(s[4] * k) for s, k in zip(scales, kn)]
    for m in mine:
        link_ref[m, 0] = scales[m][5] * identity - mm(wp[m], ke[m], 0, 0)
        link_ref[m, 1] = mm(up[m], ke[m])
    for m in mine:
        kept_ref[m, INVERSE] = inv[m]
        kept_ref[m, SCORES] = scores[m]
        kept_ref[m, FROM_STATE] = w[m]
        kept_ref[m, READS] = scales[m][3] * qn[m] - mm(ap[m], wp[m])
        kept_ref[m, RATIO] = scales[m][2]
        kept_ref[m, WRITES] = u[m]
        kept_ref[m, LOCAL] = mm(up[m], ap[m], 1, 1)


def lay_out(plan, place, mate, refs, all_ref):
    for d, ref in enumerate(refs):
        for m in range(plan.hv):
            all_ref[lax.rem(mate + d, plan.mates), plan.ring.source(place, m)] = ref[m]


def scan_kernel(plan, place_ref, mate_ref, *refs):
    s, hv = plan.mates, plan.hv
    links, kept_ref, state_ref = refs[:s], refs[s], refs[s + 1]
    outs, (all_ref, states_ref) = refs[s + 2 : -2], refs[-2:]
    place, mate = place_ref[0], mate_ref[0]
    lay_out(plan, place, mate, links, all_ref)
    state = jnp.zeros((DV, DK), F32)
    for c in range(plan.n):
        states_ref[c] = state
        if c < plan.n - 1:
            link = all_ref.at[c % s, c // s]
            state = link[1] + mm(halves(state), halves(link[0]))
    cores = []
    for m, c in enumerate(chunks_of(plan, place, mate)):
        state = states_ref[c]
        state_ref[m] = state
        core = kept_ref[m, LOCAL] + mm(halves(state), halves(kept_ref[m, READS]), 1, 1)
        cores.append(core.astype(BF16))
    for d in range(hv):
        for k in range(hv):
            outs[d][k] = cores[plan.ring.seen(d, k)]


def state_cotangent_kernel(plan, kept_ref, *refs):
    for m in range(plan.hv):
        refs[-1][m] = mm(d_out(refs[m]), halves(kept_ref[m, READS]))


def d_out(ref):
    return ref[:DV], ref[DV : 2 * DV]


def backward_kernel(plan, off_ref, place_ref, mate_ref, *refs):
    s, n, tok, hv = plan.mates, plan.n, plan.tok, plan.hv
    links, backs, refs = refs[:s], refs[s : 2 * s], refs[2 * s :]
    in_refs, d_refs, kept_ref, state_ref = refs[:hv], refs[hv : 2 * hv], refs[2 * hv], refs[2 * hv + 1]
    outs, (links_ref, backs_ref, cots_ref) = refs[2 * hv + 2 : -3], refs[-3:]
    outs = [outs[plan.ring.seen(m, 0)] for m in range(hv)]
    place, mate = place_ref[0], mate_ref[0]
    lay_out(plan, place, mate, links, links_ref)
    lay_out(plan, place, mate, backs, backs_ref)
    d_state = jnp.zeros((DV, DK), F32)
    for c in reversed(range(n)):
        cots_ref[c] = d_state
        if c:
            d_state = backs_ref[c % s, c // s] + mm(
                halves(d_state), halves(links_ref[c % s, c // s, 0]), 1, 1
            )
    rows, columns = iotas(tok, tok)
    strict = rows > columns
    upto = (rows >= columns).astype(BF16)
    mine = range(hv)
    chunks = chunks_of(plan, place, mate)
    scales = scalings(plan, off_ref, chunks, [r[plan.aux_at :] for r in in_refs])
    qu = [unit(in_refs[m][:tok].astype(F32)) for m in mine]
    ku = [unit(in_refs[m][tok : 2 * tok].astype(F32)) for m in mine]
    qp = [halves(x[0]) for x in qu]
    kp = [halves(x[0]) for x in ku]
    do = [d_out(r) for r in d_refs]
    s0 = [state_ref[m] for m in mine]
    ds = [cots_ref[c] for c in chunks]
    s0p = [halves(x) for x in s0]
    dsp = [halves(x) for x in ds]
    pseudo = [kept_ref[m, WRITES] - mm(s0p[m], halves(kept_ref[m, FROM_STATE]), 1, 1) for m in mine]
    pp = [halves(x) for x in pseudo]
    ke = [halves(s[4] * k[0]) for s, k in zip(scales, ku)]
    dp = [mm(do[m], halves(kept_ref[m, SCORES])) + mm(dsp[m], ke[m], 1, 1) for m in mine]
    dr = [mm(halves(dp[m]), halves(kept_ref[m, INVERSE])) for m in mine]
    drp = [halves(x) for x in dr]
    big = [mm(cat([o, r], 1), cat([p, s], 1), 0, 0) for o, r, p, s in zip(do, drp, pp, s0p)]
    pds = [mm(p, d, 0, 0) for p, d in zip(pp, dsp)]
    da = [big[m][:tok, :tok] * kept_ref[m, RATIO] for m in mine]
    dm = [jnp.where(strict, -big[m][tok:, :tok] * kept_ref[m, RATIO], 0.0) for m in mine]
    dap = [halves(x) for x in da]
    dmp = [halves(x) for x in dm]
    dbm = [halves(s[1] * x) for s, x in zip(scales, dm)]
    by_row = [mm(cat([x, y], 0), k) for x, y, k in zip(dap, dmp, kp)]
    by_column = [
        mm(cat([x, y], 0), cat([q, k], 0), 0, 0) for x, y, q, k in zip(dap, dbm, qp, kp)
    ]
    sums = []
    for m in mine:
        _, b_col, _, start_col, end_col, whole = scales[m]
        (qn, q_scale), (kn, k_scale) = qu[m], ku[m]
        out = outs[m]
        dqn = by_row[m][:tok] + start_col * big[m][:tok, tok:]
        erase = by_row[m][tok:] - start_col * big[m][tok:, tok:]
        ends = end_col * pds[m]
        write = by_column[m] + ends
        dkn = b_col * erase + write
        s_q = jnp.sum(qn * dqn, axis=1, keepdims=True)
        s_e = jnp.sum(kn * erase, axis=1, keepdims=True)
        s_w = jnp.sum(kn * write, axis=1, keepdims=True)
        total = jnp.sum(jnp.sum(kn * ends, axis=1, keepdims=True), axis=0, keepdims=True)
        both = jnp.sum(jnp.sum(s0[m] * ds[m], axis=1, keepdims=True), axis=0, keepdims=True)
        out[:tok] = (q_scale * (dqn - qn * s_q)).astype(BF16)
        out[tok : 2 * tok] = (k_scale * (dkn - kn * (b_col * s_e + s_w))).astype(BF16)
        out[plan.v_at : plan.aux_at] = (scales[m][0] * dr[m]).astype(BF16)
        sums.append((s_e, s_q + b_col * s_e - s_w, total + whole * both))
    turned = to_rows([s[0] for s in sums] + [s[1] for s in sums], tok)
    for m in mine:
        values = in_refs[m][plan.v_at : plan.aux_at].astype(F32)
        d_rate = turned[m] + jnp.sum(dr[m] * values, axis=0, keepdims=True)
        parts = dot(aux_rows([turned[plan.hv + m]], tok), upto, 1, 0)
        d_decay = parts[0:1] + parts[1:2] + parts[2:3] + sums[m][2]
        outs[m][plan.aux_at :] = aux_rows([d_rate, d_decay], tok)


def gather_rows(head, pieces, all_ref):
    rows, ring = pieces[0].shape[0], Ring(len(pieces))
    for d, piece in enumerate(pieces):
        at = ring.source(head, d) * rows
        all_ref[pl.ds(pl.multiple_of(at, rows), rows), :] = piece[...]


def cotangent_kernel(plan, parts, head_ref, place_ref, *refs):
    pieces, w_ref, outs, (all_ref, out_ref) = refs[:parts], refs[parts], refs[parts + 1 : -2], refs[-2:]
    gather_rows(head_ref[0], pieces, all_ref)
    high, low = halves(dot(w_ref[...], all_ref[...], 1, 1))
    share = all_ref.shape[1] // plan.hv
    for m in range(plan.hv):
        out_ref[m, :DV] = high[m * DV : (m + 1) * DV]
        out_ref[m, DV : 2 * DV] = low[m * DV : (m + 1) * DV]
        part = all_ref[:, m * share : (m + 1) * share].astype(F32)
        out_ref[m, 2 * DV :] = jnp.transpose(part).astype(BF16)
    hand_out(plan, place_ref[0], out_ref, outs)


def project_kernel(plan, parts, head_ref, place_ref, *refs):
    mixed_refs, w_ref, outs, (all_ref, total_ref) = (
        refs[: plan.hv],
        refs[plan.hv],
        refs[plan.hv + 1 : -2],
        refs[-2:],
    )
    for d, ref in enumerate(mixed_refs):
        all_ref[plan.ring.source(place_ref[0], d)] = ref[0]
    mixed = all_ref[...].reshape(plan.hv * DV, plan.tok)
    total_ref[...] = dot(mixed, w_ref[...], 0, 0)
    rows, ring = outs[0].shape[0], Ring(parts)
    for d in range(parts):
        at = ring.target(head_ref[0], d) * rows
        block = total_ref[pl.ds(pl.multiple_of(at, rows), rows), :]
        outs[d][...] = block.astype(outs[d].dtype)


def weight_kernel(plan, place_ref, mate_ref, *refs):
    hv = plan.hv
    cot_refs, mixed_refs, outs, all_ref = refs[:hv], refs[hv : 2 * hv], refs[2 * hv : -1], refs[-1]
    for d, ref in enumerate(mixed_refs):
        head = plan.ring.source(place_ref[0], d)
        for k in range(hv):
            all_ref[k, head] = ref[k]
    share = outs[0].shape[0]
    for d, out_ref in enumerate(outs):
        at = lax.rem(mate_ref[0] + plan.mates - d, plan.mates) * share
        at = 2 * DV + pl.multiple_of(at, share)
        total = None
        for k in range(hv):
            mixed = all_ref[k].reshape(hv * DV, plan.tok)
            part = dot(cot_refs[k][pl.ds(at, share), :], mixed, 1, 1)
            total = part if total is None else total + part
        out_ref[...] = total


def finish_kernel(plan, place_ref, *refs):
    pieces, (q_ref, k_ref, v_ref, rate_ref, decay_ref, in_ref) = refs[: plan.hv], refs[plan.hv :]
    tok = plan.tok
    for d, ref in enumerate(pieces):
        in_ref[plan.ring.source(place_ref[0], d)] = ref[...]
    for kh in range(plan.hk):
        mine = [h for h in range(plan.hv) if plan.key_head(h) == kh]
        for ref, at in ((q_ref, 0), (k_ref, tok)):
            total = in_ref[mine[0], at : at + tok].astype(F32)
            for h in mine[1:]:
                total = total + in_ref[h, at : at + tok].astype(F32)
            ref[:, kh * DK : (kh + 1) * DK] = total
    for h in range(plan.hv):
        v_ref[:, h * DV : (h + 1) * DV] = jnp.transpose(
            in_ref[h, plan.v_at : plan.aux_at].astype(F32)
        )
        aux = in_ref[h, plan.aux_at :].astype(F32)
        rate_ref[h : h + 1, :] = aux[0:1] + aux[1:2] + aux[2:3]
        decay_ref[h : h + 1, :] = aux[3:4] + aux[4:5] + aux[5:6]


def after(x, y):
    return lax.optimization_barrier((x, y))[0]


def per_device(
    queries, key_vectors, value_rows, write_rate, log_decay, doc_offsets, out_weight, grad_out
):
    n, parts = lax.axis_size("ctx"), lax.axis_size("head")
    tok, hv = queries.shape[0], write_rate.shape[0]
    hk, model = queries.shape[1] // DK, grad_out.shape[1]
    plan = Plan(n, tok, hv, hk)
    s = plan.mates
    index = lax.axis_index("ctx").astype(jnp.int32)
    place, mate = (index // s).reshape(1), (index % s).reshape(1)
    head = lax.axis_index("head").astype(jnp.int32).reshape(1)

    def across_heads(pieces):
        moved = [lax.ppermute(pieces[d], "head", Ring(parts).pairs(d)) for d in range(1, parts)]
        return [pieces[0]] + moved

    vmem = lambda dtype, *shape: pltpu.VMEM(shape, dtype)

    packed = call(
        partial(pack_kernel, plan),
        [arr(BF16, plan.rows, DK)] * hv,
        smem=(0,),
        scratch=[vmem(BF16, hv, plan.rows, DK)],
        fetch=range(1, 6),
    )(place, queries, key_vectors, value_rows, write_rate, log_decay)
    got = plan.exchange(packed)
    rows = across_heads([grad_out] * parts)

    link, kept = call(
        partial(prepare_kernel, plan),
        (arr(F32, hv, 2, DK, DK), arr(F32, hv, KEPT, tok, DK)),
        smem=(0, 1, 2),
        fetch=(0,),
        flops=20_000_000_000,
    )(doc_offsets, place, mate, *got)
    links = [link] + [plan.from_mate(link, d) for d in range(1, s)]

    cot = call(
        partial(cotangent_kernel, plan, parts),
        [arr(BF16, 2 * DV + model // hv, tok)] * hv,
        smem=(0, 1),
        scratch=[vmem(BF16, tok, model), vmem(BF16, hv, 2 * DV + model // hv, tok)],
        flops=30_000_000_000,
    )(head, place, *rows, after(out_weight, link))
    kept = after(kept, cot[0])
    cot = plan.exchange(cot)

    states, *mixed = call(
        partial(scan_kernel, plan),
        [arr(F32, hv, DV, DK)] + [arr(BF16, hv, DV, tok)] * hv,
        smem=(0, 1),
        scratch=[vmem(F32, s, hv, 2, DK, DK), vmem(F32, n, DV, DK)],
        flops=2_500_000_000,
    )(place, mate, *links, kept)
    mixed = plan.exchange(mixed)
    back = call(
        partial(state_cotangent_kernel, plan), arr(F32, hv, DV, DK), flops=30_000_000_000
    )(kept, *after(cot, mixed[1]))
    backs = [back] + [plan.from_mate(back, d) for d in range(1, s)]

    projected = call(
        partial(project_kernel, plan, parts),
        [arr(BF16 if d else F32, tok // parts, model) for d in range(parts)],
        smem=(0, 1),
        scratch=[vmem(BF16, hv, DV, tok), vmem(F32, tok, model)],
        flops=1_000_000_000,
    )(head, place, *mixed, out_weight)
    layer_parts = across_heads(projected)

    grads = call(
        partial(backward_kernel, plan),
        [arr(BF16, plan.rows, DK)] * hv,
        smem=(0, 1, 2),
        fetch=(0,),
        scratch=[
            vmem(F32, s, hv, 2, DK, DK),
            vmem(F32, s, hv, DV, DK),
            vmem(F32, n, DV, DK),
        ],
        flops=6_000_000_000,
    )(doc_offsets, place, mate, *links, *backs, *got, *cot, kept, after(states, projected[1]))

    shares = call(
        partial(weight_kernel, plan),
        [arr(F32, model // n, hv * DV)] * s,
        smem=(0, 1),
        scratch=[vmem(BF16, hv, hv, DV, tok)],
        flops=1_000_000_000,
    )(place, mate, *cot, *mixed)
    grads = plan.exchange(after(grads, shares[0]))
    weight_grad = shares[0]
    for d in range(1, s):
        weight_grad = weight_grad + plan.from_mate(shares[d], d)

    layer_out = layer_parts[0]
    for part in layer_parts[1:]:
        layer_out = layer_out + part.astype(F32)
    grads = after(grads, layer_out)
    grad_q, grad_k, grad_v, grad_rate, grad_decay = call(
        partial(finish_kernel, plan),
        (
            arr(F32, tok, hk * DK),
            arr(F32, tok, hk * DK),
            arr(F32, tok, hv * DV),
            arr(F32, hv, tok),
            arr(F32, hv, tok),
        ),
        smem=(0,),
        scratch=[vmem(BF16, hv, plan.rows, DK)],
        flops=1_000_000_000,
        inside=False,
    )(place, *grads)
    return (layer_out, grad_q, grad_k, grad_v, grad_rate, grad_decay, weight_grad)


def solution(mesh):
    placed = (
        P("ctx", "head"),
        P("ctx", "head"),
        P("ctx", "head"),
        P("head", "ctx"),
        P("head", "ctx"),
        P(),
        P("head", None),
        P(("ctx", "head"), None),
    )
    return jax.shard_map(
        per_device,
        mesh=mesh,
        in_specs=placed,
        out_specs=(
            P(("ctx", "head"), None),
            P("ctx", "head"),
            P("ctx", "head"),
            P("ctx", "head"),
            P("head", "ctx"),
            P("head", "ctx"),
            P("ctx", "head"),
        ),
        check_vma=False,
    )
```

```python
import math
from functools import partial

import jax
import jax.numpy as jnp
from jax import lax
from jax.experimental import pallas as pl
from jax.experimental.pallas import tpu as pltpu
from jax.sharding import PartitionSpec as P

DK = 128
DV = 128
AUX = 16
INVERSE, SCORES, FROM_STATE, READS, RATIO, WRITES, LOCAL, KEPT = range(8)
EPS = 1e-06
F32 = jnp.float32
BF16 = jnp.bfloat16
SPARE_VMEM = 8 * 1024 * 1024


def dot(a, b, ca, cb):
    return lax.dot_general(a, b, (((ca,), (cb,)), ((), ())), preferred_element_type=F32)


def halves(x):
    high = x.astype(BF16)
    return high, (x - high.astype(F32)).astype(BF16)


def thirds(x):
    high = x.astype(BF16).astype(F32)
    middle = (x - high).astype(BF16).astype(F32)
    return high, middle, x - high - middle


def mm(a, b, ca=1, cb=0):
    left = jnp.concatenate([a[0], a[0], a[1]], axis=ca)
    right = jnp.concatenate([b[0], b[1], b[0]], axis=cb)
    return dot(left, right, ca, cb)


def cat(pairs, axis):
    return tuple(jnp.concatenate(parts, axis=axis) for parts in zip(*pairs))


def iotas(rows, columns):
    shape = (rows, columns)
    return lax.broadcasted_iota(jnp.int32, shape, 0), lax.broadcasted_iota(jnp.int32, shape, 1)


def call(kernel, outs, smem=(), scratch=(), flops=0, inside=True, fetch=()):
    if inside:
        outs = jax.tree.map(lambda o: pltpu.VMEM(o.shape, o.dtype), outs)
    scoped = SPARE_VMEM + sum(x.dtype.itemsize * math.prod(x.shape) for x in scratch)

    def run(*args):
        spec = lambda i: pl.BlockSpec(memory_space=pltpu.SMEM if i in smem else pltpu.VMEM)
        space = lambda i: pltpu.HBM if i in fetch else pltpu.VMEM
        hold = pltpu.with_memory_space_constraint
        return pl.pallas_call(
            kernel,
            out_shape=outs,
            in_specs=[spec(i) for i in range(len(args))],
            out_specs=jax.tree.map(lambda _: pl.BlockSpec(memory_space=pltpu.VMEM), outs),
            scratch_shapes=list(scratch),
            compiler_params=pltpu.CompilerParams(vmem_limit_bytes=scoped),
            cost_estimate=pl.CostEstimate(flops=flops, bytes_accessed=0, transcendentals=0),
        )(*(hold(x, space(i)) if i in fetch or i not in smem else x for i, x in enumerate(args)))

    return run


def arr(dtype, *shape):
    return jax.ShapeDtypeStruct(shape, dtype)


class Ring:
    def __init__(self, size):
        self.size = size
        self.paired = size & (size - 1) == 0

    def source(self, i, d):
        return i ^ d if self.paired else (i + d) % self.size

    def target(self, i, d):
        return i ^ d if self.paired else (i + self.size - d) % self.size

    def seen(self, d, k):
        return d ^ k if self.paired else (k - d) % self.size

    def pairs(self, d):
        return [(self.source(i, d), i) for i in range(self.size)]


class Plan:
    def __init__(self, n, tok, hv, hk):
        self.n, self.tok, self.hv, self.hk = n, tok, hv, hk
        self.mates = n // hv
        self.v_at = 2 * tok
        self.aux_at = 2 * tok + DV
        self.rows = self.aux_at + AUX
        self.ring = Ring(hv)

    def key_head(self, head):
        return head * self.hk // self.hv

    def exchange(self, pieces):
        s = self.mates
        moved = [pieces[0]]
        for d in range(1, self.hv):
            pairs = [(i * s + b, j * s + b) for i, j in self.ring.pairs(d) for b in range(s)]
            moved.append(lax.ppermute(pieces[d], "ctx", pairs))
        return moved

    def from_mate(self, x, d):
        s = self.mates
        pairs = [(i // s * s + (i + d) % s, i) for i in range(self.n)]
        return lax.ppermute(x, "ctx", pairs)


def aux_rows(rows, columns):
    row_ids = lax.broadcasted_iota(jnp.int32, (AUX, columns), 0)
    out = jnp.zeros((AUX, columns), F32)
    for i, part in enumerate(p for r in rows for p in thirds(r)):
        out = jnp.where(row_ids == i, part, out)
    return out.astype(BF16)


def pack_kernel(plan, place_ref, q_ref, k_ref, v_ref, rate_ref, decay_ref, *refs):
    outs, out_ref = refs[:-1], refs[-1]
    tok = plan.tok
    for h in range(plan.hv):
        kh = plan.key_head(h)
        out_ref[h, :tok] = q_ref[:, kh * DK : (kh + 1) * DK]
        out_ref[h, tok : 2 * tok] = k_ref[:, kh * DK : (kh + 1) * DK]
        turned = jnp.transpose(v_ref[:, h * DV : (h + 1) * DV].astype(F32))
        out_ref[h, plan.v_at : plan.aux_at] = turned.astype(BF16)
        rows = [rate_ref[h : h + 1, :], decay_ref[h : h + 1, :]]
        out_ref[h, plan.aux_at :] = aux_rows(rows, tok)
    hand_out(plan, place_ref[0], out_ref, outs)


def hand_out(plan, place, all_ref, outs):
    for d, ref in enumerate(outs):
        ref[...] = all_ref[plan.ring.target(place, d)]


def unit(x):
    scale = lax.rsqrt(jnp.sum(x * x, axis=1, keepdims=True) + EPS)
    return x * scale, scale


def segments(off_ref, positions):
    total = jnp.zeros(positions.shape, jnp.int32)
    for j in range(off_ref.shape[0] - 1):
        total = total + (off_ref[j] <= positions).astype(jnp.int32)
    return total


def to_columns(rows, tok):
    row_ids = lax.broadcasted_iota(jnp.int32, (tok, tok), 0)
    stacked = jnp.zeros((tok, tok), F32)
    for i, r in enumerate(rows):
        stacked = jnp.where(row_ids == i, r, stacked)
    turned = jnp.transpose(stacked)
    return [turned[:, i : i + 1] for i in range(len(rows))]


def to_rows(columns, tok):
    column_ids = lax.broadcasted_iota(jnp.int32, (tok, tok), 1)
    stacked = jnp.zeros((tok, tok), F32)
    for i, c in enumerate(columns):
        stacked = jnp.where(column_ids == i, c, stacked)
    turned = jnp.transpose(stacked)
    return [turned[i : i + 1, :] for i in range(len(columns))]


def scalings(plan, off_ref, chunks, auxes):
    tok = plan.tok
    rows, columns = iotas(tok, tok)
    upto = (rows <= columns).astype(BF16)
    sums = [dot(a, upto, 1, 0) for a in auxes]
    rates = [jnp.sum(a[0:3].astype(F32), axis=0, keepdims=True) for a in auxes]
    cumuls = [s[3:4] + s[4:5] + s[5:6] for s in sums]
    turned = to_columns(rates + cumuls, tok)
    out = []
    for i, c in enumerate(chunks):
        b_col, c_col = turned[i], turned[len(chunks) + i]
        c_row = cumuls[i]
        start = c * tok
        seg_col = segments(off_ref, start + rows[:, :1])
        seg_row = segments(off_ref, start + columns[:1, :])
        before = jnp.int32(0)
        last = jnp.int32(0)
        for j in range(off_ref.shape[0] - 1):
            before = before + (off_ref[j] <= start - 1).astype(jnp.int32)
            last = last + (off_ref[j] <= start + tok - 1).astype(jnp.int32)
        c_last = c_row[:, tok - 1 : tok]
        together = (seg_col == seg_row) & (rows >= columns)
        ratio = jnp.where(together, jnp.exp(jnp.where(together, c_col - c_row, 0.0)), 0.0)
        start_col = jnp.where(seg_col == before, jnp.exp(c_col), 0.0)
        end_col = jnp.where(seg_col == last, jnp.exp(c_last - c_col), 0.0)
        whole = jnp.where(last == before, jnp.exp(c_last), 0.0)
        out.append((rates[i], b_col, ratio, start_col, end_col, whole))
    return out


def inverses(lowers):
    size = lowers[0].shape[0]
    rows, columns = iotas(size, size)
    identity = (rows == columns).astype(F32)
    block = min(16, size)
    near = (rows // block) == (columns // block)
    powers = [jnp.where(near, -m, 0.0) for m in lowers]
    results = [identity + p for p in powers]
    split = [halves(p) for p in powers]
    powers = [mm(s, s) for s in split]
    reach = 2
    while reach < block:
        split = [halves(p) for p in powers]
        more = reach * 2 < block
        both = []
        for r, s in zip(results, split):
            left = halves(r)
            if more:
                left = cat([left, s], 0)
            both.append(mm(left, s))
        results = [r + b[:size] for r, b in zip(results, both)]
        if more:
            powers = [b[size:] for b in both]
        reach *= 2
    while block < size:
        across = ((rows // (2 * block)) == (columns // (2 * block))) & (
            (rows // block) > (columns // block)
        )
        split = [halves(r) for r in results]
        middle = [mm(halves(jnp.where(across, m, 0.0)), s) for m, s in zip(lowers, split)]
        results = [r - mm(s, halves(m)) for r, s, m in zip(results, split, middle)]
        block *= 2
    return results


def chunks_of(plan, place, mate):
    return [mate + plan.mates * plan.ring.source(place, d) for d in range(plan.hv)]


def prepare_kernel(plan, off_ref, place_ref, mate_ref, *refs):
    in_refs, (link_ref, kept_ref) = refs[: plan.hv], refs[plan.hv :]
    tok = plan.tok
    rows, columns = iotas(tok, tok)
    key_rows, key_columns = iotas(DK, DK)
    identity = (key_rows == key_columns).astype(F32)
    mine = range(plan.hv)
    chunks = chunks_of(plan, place_ref[0], mate_ref[0])
    scales = scalings(plan, off_ref, chunks, [r[plan.aux_at :] for r in in_refs])
    qn = [unit(in_refs[m][:tok].astype(F32))[0] for m in mine]
    kn = [unit(in_refs[m][tok : 2 * tok].astype(F32))[0] for m in mine]
    kp = [halves(x) for x in kn]
    qp = [halves(x) for x in qn]
    dots = [mm(cat([q, k], 0), k, 1, 1) for q, k in zip(qp, kp)]
    strict = rows > columns
    lowers = [jnp.where(strict, s[1] * d[tok:] * s[2], 0.0) for s, d in zip(scales, dots)]
    scores = [d[:tok] * s[2] for s, d in zip(scales, dots)]
    inv = inverses(lowers)
    rated = [halves(x * s[0]) for x, s in zip(inv, scales)]
    w = [mm(x, halves(s[3] * k)) for x, s, k in zip(rated, scales, kn)]
    values = [in_refs[m][plan.v_at : plan.aux_at] for m in mine]
    u = [
        dot(jnp.concatenate([v, v], axis=1), jnp.concatenate(x, axis=1), 1, 1)
        for v, x in zip(values, rated)
    ]
    wp = [halves(x) for x in w]
    up = [halves(x) for x in u]
    ap = [halves(x) for x in scores]
    ke = [halves(s[4] * k) for s, k in zip(scales, kn)]
    for m in mine:
        link_ref[m, 0] = scales[m][5] * identity - mm(wp[m], ke[m], 0, 0)
        link_ref[m, 1] = mm(up[m], ke[m])
    for m in mine:
        kept_ref[m, INVERSE] = inv[m]
        kept_ref[m, SCORES] = scores[m]
        kept_ref[m, FROM_STATE] = w[m]
        kept_ref[m, READS] = scales[m][3] * qn[m] - mm(ap[m], wp[m])
        kept_ref[m, RATIO] = scales[m][2]
        kept_ref[m, WRITES] = u[m]
        kept_ref[m, LOCAL] = mm(up[m], ap[m], 1, 1)


def lay_out(plan, place, mate, refs, all_ref):
    for d, ref in enumerate(refs):
        for m in range(plan.hv):
            all_ref[lax.rem(mate + d, plan.mates), plan.ring.source(place, m)] = ref[m]


def scan_kernel(plan, place_ref, mate_ref, *refs):
    s, hv = plan.mates, plan.hv
    links, kept_ref, state_ref = refs[:s], refs[s], refs[s + 1]
    outs, (all_ref, states_ref) = refs[s + 2 : -2], refs[-2:]
    place, mate = place_ref[0], mate_ref[0]
    lay_out(plan, place, mate, links, all_ref)
    state = jnp.zeros((DV, DK), F32)
    for c in range(plan.n):
        states_ref[c] = state
        if c < plan.n - 1:
            link = all_ref.at[c % s, c // s]
            state = link[1] + mm(halves(state), halves(link[0]))
    cores = []
    for m, c in enumerate(chunks_of(plan, place, mate)):
        state = states_ref[c]
        state_ref[m] = state
        core = kept_ref[m, LOCAL] + mm(halves(state), halves(kept_ref[m, READS]), 1, 1)
        cores.append(core.astype(BF16))
    for d in range(hv):
        for k in range(hv):
            outs[d][k] = cores[plan.ring.seen(d, k)]


def state_cotangent_kernel(plan, kept_ref, *refs):
    for m in range(plan.hv):
        refs[-1][m] = mm(d_out(refs[m]), halves(kept_ref[m, READS]))


def d_out(ref):
    return ref[:DV], ref[DV : 2 * DV]


def backward_kernel(plan, off_ref, place_ref, mate_ref, *refs):
    s, n, tok, hv = plan.mates, plan.n, plan.tok, plan.hv
    links, backs, refs = refs[:s], refs[s : 2 * s], refs[2 * s :]
    in_refs, d_refs, kept_ref, state_ref = refs[:hv], refs[hv : 2 * hv], refs[2 * hv], refs[2 * hv + 1]
    outs, (links_ref, backs_ref, cots_ref) = refs[2 * hv + 2 : -3], refs[-3:]
    outs = [outs[plan.ring.seen(m, 0)] for m in range(hv)]
    place, mate = place_ref[0], mate_ref[0]
    lay_out(plan, place, mate, links, links_ref)
    lay_out(plan, place, mate, backs, backs_ref)
    d_state = jnp.zeros((DV, DK), F32)
    for c in reversed(range(n)):
        cots_ref[c] = d_state
        if c:
            d_state = backs_ref[c % s, c // s] + mm(
                halves(d_state), halves(links_ref[c % s, c // s, 0]), 1, 1
            )
    rows, columns = iotas(tok, tok)
    strict = rows > columns
    upto = (rows >= columns).astype(BF16)
    mine = range(hv)
    chunks = chunks_of(plan, place, mate)
    scales = scalings(plan, off_ref, chunks, [r[plan.aux_at :] for r in in_refs])
    qu = [unit(in_refs[m][:tok].astype(F32)) for m in mine]
    ku = [unit(in_refs[m][tok : 2 * tok].astype(F32)) for m in mine]
    qp = [halves(x[0]) for x in qu]
    kp = [halves(x[0]) for x in ku]
    do = [d_out(r) for r in d_refs]
    s0 = [state_ref[m] for m in mine]
    ds = [cots_ref[c] for c in chunks]
    s0p = [halves(x) for x in s0]
    dsp = [halves(x) for x in ds]
    pseudo = [kept_ref[m, WRITES] - mm(s0p[m], halves(kept_ref[m, FROM_STATE]), 1, 1) for m in mine]
    pp = [halves(x) for x in pseudo]
    ke = [halves(s[4] * k[0]) for s, k in zip(scales, ku)]
    dp = [mm(do[m], halves(kept_ref[m, SCORES])) + mm(dsp[m], ke[m], 1, 1) for m in mine]
    dr = [mm(halves(dp[m]), halves(kept_ref[m, INVERSE])) for m in mine]
    drp = [halves(x) for x in dr]
    big = [mm(cat([o, r], 1), cat([p, s], 1), 0, 0) for o, r, p, s in zip(do, drp, pp, s0p)]
    pds = [mm(p, d, 0, 0) for p, d in zip(pp, dsp)]
    da = [big[m][:tok, :tok] * kept_ref[m, RATIO] for m in mine]
    dm = [jnp.where(strict, -big[m][tok:, :tok] * kept_ref[m, RATIO], 0.0) for m in mine]
    dap = [halves(x) for x in da]
    dmp = [halves(x) for x in dm]
    dbm = [halves(s[1] * x) for s, x in zip(scales, dm)]
    by_row = [mm(cat([x, y], 0), k) for x, y, k in zip(dap, dmp, kp)]
    by_column = [
        mm(cat([x, y], 0), cat([q, k], 0), 0, 0) for x, y, q, k in zip(dap, dbm, qp, kp)
    ]
    sums = []
    for m in mine:
        _, b_col, _, start_col, end_col, whole = scales[m]
        (qn, q_scale), (kn, k_scale) = qu[m], ku[m]
        out = outs[m]
        dqn = by_row[m][:tok] + start_col * big[m][:tok, tok:]
        erase = by_row[m][tok:] - start_col * big[m][tok:, tok:]
        ends = end_col * pds[m]
        write = by_column[m] + ends
        dkn = b_col * erase + write
        s_q = jnp.sum(qn * dqn, axis=1, keepdims=True)
        s_e = jnp.sum(kn * erase, axis=1, keepdims=True)
        s_w = jnp.sum(kn * write, axis=1, keepdims=True)
        total = jnp.sum(jnp.sum(kn * ends, axis=1, keepdims=True), axis=0, keepdims=True)
        both = jnp.sum(jnp.sum(s0[m] * ds[m], axis=1, keepdims=True), axis=0, keepdims=True)
        out[:tok] = (q_scale * (dqn - qn * s_q)).astype(BF16)
        out[tok : 2 * tok] = (k_scale * (dkn - kn * (b_col * s_e + s_w))).astype(BF16)
        out[plan.v_at : plan.aux_at] = (scales[m][0] * dr[m]).astype(BF16)
        sums.append((s_e, s_q + b_col * s_e - s_w, total + whole * both))
    turned = to_rows([s[0] for s in sums] + [s[1] for s in sums], tok)
    for m in mine:
        values = in_refs[m][plan.v_at : plan.aux_at].astype(F32)
        d_rate = turned[m] + jnp.sum(dr[m] * values, axis=0, keepdims=True)
        parts = dot(aux_rows([turned[plan.hv + m]], tok), upto, 1, 0)
        d_decay = parts[0:1] + parts[1:2] + parts[2:3] + sums[m][2]
        outs[m][plan.aux_at :] = aux_rows([d_rate, d_decay], tok)


def gather_rows(head, pieces, all_ref):
    rows, ring = pieces[0].shape[0], Ring(len(pieces))
    for d, piece in enumerate(pieces):
        at = ring.source(head, d) * rows
        all_ref[pl.ds(pl.multiple_of(at, rows), rows), :] = piece[...]


def cotangent_kernel(plan, parts, head_ref, place_ref, *refs):
    pieces, w_ref, outs, (all_ref, out_ref) = refs[:parts], refs[parts], refs[parts + 1 : -2], refs[-2:]
    gather_rows(head_ref[0], pieces, all_ref)
    high, low = halves(dot(w_ref[...], all_ref[...], 1, 1))
    share = all_ref.shape[1] // plan.hv
    for m in range(plan.hv):
        out_ref[m, :DV] = high[m * DV : (m + 1) * DV]
        out_ref[m, DV : 2 * DV] = low[m * DV : (m + 1) * DV]
        part = all_ref[:, m * share : (m + 1) * share].astype(F32)
        out_ref[m, 2 * DV :] = jnp.transpose(part).astype(BF16)
    hand_out(plan, place_ref[0], out_ref, outs)


def project_kernel(plan, parts, head_ref, place_ref, *refs):
    mixed_refs, w_ref, outs, (all_ref, total_ref) = (
        refs[: plan.hv],
        refs[plan.hv],
        refs[plan.hv + 1 : -2],
        refs[-2:],
    )
    for d, ref in enumerate(mixed_refs):
        all_ref[plan.ring.source(place_ref[0], d)] = ref[0]
    mixed = all_ref[...].reshape(plan.hv * DV, plan.tok)
    total_ref[...] = dot(mixed, w_ref[...], 0, 0)
    rows, ring = outs[0].shape[0], Ring(parts)
    for d in range(parts):
        at = ring.target(head_ref[0], d) * rows
        block = total_ref[pl.ds(pl.multiple_of(at, rows), rows), :]
        outs[d][...] = block.astype(outs[d].dtype)


def weight_kernel(plan, place_ref, mate_ref, *refs):
    hv = plan.hv
    cot_refs, mixed_refs, outs, all_ref = refs[:hv], refs[hv : 2 * hv], refs[2 * hv : -1], refs[-1]
    for d, ref in enumerate(mixed_refs):
        head = plan.ring.source(place_ref[0], d)
        for k in range(hv):
            all_ref[k, head] = ref[k]
    share = outs[0].shape[0]
    for d, out_ref in enumerate(outs):
        at = lax.rem(mate_ref[0] + plan.mates - d, plan.mates) * share
        at = 2 * DV + pl.multiple_of(at, share)
        total = None
        for k in range(hv):
            mixed = all_ref[k].reshape(hv * DV, plan.tok)
            part = dot(cot_refs[k][pl.ds(at, share), :], mixed, 1, 1)
            total = part if total is None else total + part
        out_ref[...] = total


def finish_kernel(plan, place_ref, *refs):
    pieces, (q_ref, k_ref, v_ref, rate_ref, decay_ref, in_ref) = refs[: plan.hv], refs[plan.hv :]
    tok = plan.tok
    for d, ref in enumerate(pieces):
        in_ref[plan.ring.source(place_ref[0], d)] = ref[...]
    for kh in range(plan.hk):
        mine = [h for h in range(plan.hv) if plan.key_head(h) == kh]
        for ref, at in ((q_ref, 0), (k_ref, tok)):
            total = in_ref[mine[0], at : at + tok].astype(F32)
            for h in mine[1:]:
                total = total + in_ref[h, at : at + tok].astype(F32)
            ref[:, kh * DK : (kh + 1) * DK] = total
    for h in range(plan.hv):
        v_ref[:, h * DV : (h + 1) * DV] = jnp.transpose(
            in_ref[h, plan.v_at : plan.aux_at].astype(F32)
        )
        aux = in_ref[h, plan.aux_at :].astype(F32)
        rate_ref[h : h + 1, :] = aux[0:1] + aux[1:2] + aux[2:3]
        decay_ref[h : h + 1, :] = aux[3:4] + aux[4:5] + aux[5:6]


def after(x, y):
    return lax.optimization_barrier((x, y))[0]


def per_device(
    queries, key_vectors, value_rows, write_rate, log_decay, doc_offsets, out_weight, grad_out
):
    n, parts = lax.axis_size("ctx"), lax.axis_size("head")
    tok, hv = queries.shape[0], write_rate.shape[0]
    hk, model = queries.shape[1] // DK, grad_out.shape[1]
    plan = Plan(n, tok, hv, hk)
    s = plan.mates
    index = lax.axis_index("ctx").astype(jnp.int32)
    place, mate = (index // s).reshape(1), (index % s).reshape(1)
    head = lax.axis_index("head").astype(jnp.int32).reshape(1)

    def across_heads(pieces):
        moved = [lax.ppermute(pieces[d], "head", Ring(parts).pairs(d)) for d in range(1, parts)]
        return [pieces[0]] + moved

    vmem = lambda dtype, *shape: pltpu.VMEM(shape, dtype)

    packed = call(
        partial(pack_kernel, plan),
        [arr(BF16, plan.rows, DK)] * hv,
        smem=(0,),
        scratch=[vmem(BF16, hv, plan.rows, DK)],
        fetch=range(1, 6),
    )(place, queries, key_vectors, value_rows, write_rate, log_decay)
    got = plan.exchange(packed)
    rows = across_heads([grad_out] * parts)

    link, kept = call(
        partial(prepare_kernel, plan),
        (arr(F32, hv, 2, DK, DK), arr(F32, hv, KEPT, tok, DK)),
        smem=(0, 1, 2),
        fetch=(0,),
        flops=20_000_000_000,
    )(doc_offsets, place, mate, *got)
    links = [link] + [plan.from_mate(link, d) for d in range(1, s)]

    cot = call(
        partial(cotangent_kernel, plan, parts),
        [arr(BF16, 2 * DV + model // hv, tok)] * hv,
        smem=(0, 1),
        scratch=[vmem(BF16, tok, model), vmem(BF16, hv, 2 * DV + model // hv, tok)],
        flops=30_000_000_000,
    )(head, place, *rows, after(out_weight, link))
    kept = after(kept, cot[0])
    states, *mixed = call(
        partial(scan_kernel, plan),
        [arr(F32, hv, DV, DK)] + [arr(BF16, hv, DV, tok)] * hv,
        smem=(0, 1),
        scratch=[vmem(F32, s, hv, 2, DK, DK), vmem(F32, n, DV, DK)],
        flops=2_500_000_000,
    )(place, mate, *links, kept)
    mixed = plan.exchange(mixed)
    cot = plan.exchange(after(cot, states))
    projected = call(
        partial(project_kernel, plan, parts),
        [arr(BF16 if d else F32, tok // parts, model) for d in range(parts)],
        smem=(0, 1),
        scratch=[vmem(BF16, hv, DV, tok), vmem(F32, tok, model)],
        flops=1_000_000_000,
    )(head, place, *mixed, out_weight)
    layer_parts = across_heads(projected)
    back = call(
        partial(state_cotangent_kernel, plan), arr(F32, hv, DV, DK), flops=30_000_000_000
    )(after(kept, layer_parts[1]), *cot)
    backs = [back] + [plan.from_mate(back, d) for d in range(1, s)]


    grads = call(
        partial(backward_kernel, plan),
        [arr(BF16, plan.rows, DK)] * hv,
        smem=(0, 1, 2),
        fetch=(0,),
        scratch=[
            vmem(F32, s, hv, 2, DK, DK),
            vmem(F32, s, hv, DV, DK),
            vmem(F32, n, DV, DK),
        ],
        flops=6_000_000_000,
    )(doc_offsets, place, mate, *links, *backs, *got, *cot, kept, after(states, projected[1]))

    shares_of = after(cot, grads[0])
    grads = plan.exchange(grads)
    shares = call(
        partial(weight_kernel, plan),
        [arr(F32, model // n, hv * DV)] * s,
        smem=(0, 1),
        scratch=[vmem(BF16, hv, hv, DV, tok)],
        flops=1_000_000_000,
    )(place, mate, *shares_of, *mixed)
    weight_grad = shares[0]
    for d in range(1, s):
        weight_grad = weight_grad + plan.from_mate(shares[d], d)

    layer_out = layer_parts[0]
    for part in layer_parts[1:]:
        layer_out = layer_out + part.astype(F32)
    grads = after(grads, (layer_out, weight_grad))
    grad_q, grad_k, grad_v, grad_rate, grad_decay = call(
        partial(finish_kernel, plan),
        (
            arr(F32, tok, hk * DK),
            arr(F32, tok, hk * DK),
            arr(F32, tok, hv * DV),
            arr(F32, hv, tok),
            arr(F32, hv, tok),
        ),
        smem=(0,),
        scratch=[vmem(BF16, hv, plan.rows, DK)],
        flops=1_000_000_000,
        inside=False,
    )(place, *grads)
    return (layer_out, grad_q, grad_k, grad_v, grad_rate, grad_decay, weight_grad)


def solution(mesh):
    placed = (
        P("ctx", "head"),
        P("ctx", "head"),
        P("ctx", "head"),
        P("head", "ctx"),
        P("head", "ctx"),
        P(),
        P("head", None),
        P(("ctx", "head"), None),
    )
    return jax.shard_map(
        per_device,
        mesh=mesh,
        in_specs=placed,
        out_specs=(
            P(("ctx", "head"), None),
            P("ctx", "head"),
            P("ctx", "head"),
            P("ctx", "head"),
            P("head", "ctx"),
            P("head", "ctx"),
            P("ctx", "head"),
        ),
        check_vma=False,
    )
```

```python
import math
from functools import partial

import jax
import jax.numpy as jnp
from jax import lax
from jax.experimental import pallas as pl
from jax.experimental.pallas import tpu as pltpu
from jax.sharding import PartitionSpec as P

DK = 128
DV = 128
AUX = 16
INVERSE, SCORES, FROM_STATE, READS, RATIO, WRITES, LOCAL, KEPT = range(8)
EPS = 1e-06
F32 = jnp.float32
BF16 = jnp.bfloat16
SPARE_VMEM = 8 * 1024 * 1024


def dot(a, b, ca, cb):
    return lax.dot_general(a, b, (((ca,), (cb,)), ((), ())), preferred_element_type=F32)


def halves(x):
    high = x.astype(BF16)
    return high, (x - high.astype(F32)).astype(BF16)


def thirds(x):
    high = x.astype(BF16).astype(F32)
    middle = (x - high).astype(BF16).astype(F32)
    return high, middle, x - high - middle


def mm(a, b, ca=1, cb=0):
    left = jnp.concatenate([a[0], a[0], a[1]], axis=ca)
    right = jnp.concatenate([b[0], b[1], b[0]], axis=cb)
    return dot(left, right, ca, cb)


def cat(pairs, axis):
    return tuple(jnp.concatenate(parts, axis=axis) for parts in zip(*pairs))


def iotas(rows, columns):
    shape = (rows, columns)
    return lax.broadcasted_iota(jnp.int32, shape, 0), lax.broadcasted_iota(jnp.int32, shape, 1)


def call(kernel, outs, smem=(), scratch=(), flops=0, inside=True, fetch=()):
    if inside:
        outs = jax.tree.map(lambda o: pltpu.VMEM(o.shape, o.dtype), outs)
    scoped = SPARE_VMEM + sum(x.dtype.itemsize * math.prod(x.shape) for x in scratch)

    def run(*args):
        spec = lambda i: pl.BlockSpec(memory_space=pltpu.SMEM if i in smem else pltpu.VMEM)
        space = lambda i: pltpu.HBM if i in fetch else pltpu.VMEM
        hold = pltpu.with_memory_space_constraint
        return pl.pallas_call(
            kernel,
            out_shape=outs,
            in_specs=[spec(i) for i in range(len(args))],
            out_specs=jax.tree.map(lambda _: pl.BlockSpec(memory_space=pltpu.VMEM), outs),
            scratch_shapes=list(scratch),
            compiler_params=pltpu.CompilerParams(vmem_limit_bytes=scoped),
            cost_estimate=pl.CostEstimate(flops=flops, bytes_accessed=0, transcendentals=0),
        )(*(hold(x, space(i)) if i in fetch or i not in smem else x for i, x in enumerate(args)))

    return run


def arr(dtype, *shape):
    return jax.ShapeDtypeStruct(shape, dtype)


class Ring:
    def __init__(self, size):
        self.size = size
        self.paired = size & (size - 1) == 0

    def source(self, i, d):
        return i ^ d if self.paired else (i + d) % self.size

    def target(self, i, d):
        return i ^ d if self.paired else (i + self.size - d) % self.size

    def seen(self, d, k):
        return d ^ k if self.paired else (k - d) % self.size

    def pairs(self, d):
        return [(self.source(i, d), i) for i in range(self.size)]


class Plan:
    def __init__(self, n, tok, hv, hk):
        self.n, self.tok, self.hv, self.hk = n, tok, hv, hk
        self.mates = n // hv
        self.v_at = 2 * tok
        self.aux_at = 2 * tok + DV
        self.rows = self.aux_at + AUX
        self.ring = Ring(hv)

    def key_head(self, head):
        return head * self.hk // self.hv

    def exchange(self, pieces):
        s = self.mates
        moved = [pieces[0]]
        for d in range(1, self.hv):
            pairs = [(i * s + b, j * s + b) for i, j in self.ring.pairs(d) for b in range(s)]
            moved.append(lax.ppermute(pieces[d], "ctx", pairs))
        return moved

    def from_mate(self, x, d):
        s = self.mates
        pairs = [(i // s * s + (i + d) % s, i) for i in range(self.n)]
        return lax.ppermute(x, "ctx", pairs)


def aux_rows(rows, columns):
    row_ids = lax.broadcasted_iota(jnp.int32, (AUX, columns), 0)
    out = jnp.zeros((AUX, columns), F32)
    for i, part in enumerate(p for r in rows for p in thirds(r)):
        out = jnp.where(row_ids == i, part, out)
    return out.astype(BF16)


def pack_kernel(plan, place_ref, q_ref, k_ref, v_ref, rate_ref, decay_ref, *refs):
    outs, out_ref = refs[:-1], refs[-1]
    tok = plan.tok
    for h in range(plan.hv):
        kh = plan.key_head(h)
        out_ref[h, :tok] = q_ref[:, kh * DK : (kh + 1) * DK]
        out_ref[h, tok : 2 * tok] = k_ref[:, kh * DK : (kh + 1) * DK]
        turned = jnp.transpose(v_ref[:, h * DV : (h + 1) * DV].astype(F32))
        out_ref[h, plan.v_at : plan.aux_at] = turned.astype(BF16)
        rows = [rate_ref[h : h + 1, :], decay_ref[h : h + 1, :]]
        out_ref[h, plan.aux_at :] = aux_rows(rows, tok)
    hand_out(plan, place_ref[0], out_ref, outs)


def hand_out(plan, place, all_ref, outs):
    for d, ref in enumerate(outs):
        ref[...] = all_ref[plan.ring.target(place, d)]


def unit(x):
    scale = lax.rsqrt(jnp.sum(x * x, axis=1, keepdims=True) + EPS)
    return x * scale, scale


def segments(off_ref, positions):
    total = jnp.zeros(positions.shape, jnp.int32)
    for j in range(off_ref.shape[0] - 1):
        total = total + (off_ref[j] <= positions).astype(jnp.int32)
    return total


def to_columns(rows, tok):
    row_ids = lax.broadcasted_iota(jnp.int32, (tok, tok), 0)
    stacked = jnp.zeros((tok, tok), F32)
    for i, r in enumerate(rows):
        stacked = jnp.where(row_ids == i, r, stacked)
    turned = jnp.transpose(stacked)
    return [turned[:, i : i + 1] for i in range(len(rows))]


def to_rows(columns, tok):
    column_ids = lax.broadcasted_iota(jnp.int32, (tok, tok), 1)
    stacked = jnp.zeros((tok, tok), F32)
    for i, c in enumerate(columns):
        stacked = jnp.where(column_ids == i, c, stacked)
    turned = jnp.transpose(stacked)
    return [turned[i : i + 1, :] for i in range(len(columns))]


def scalings(plan, off_ref, chunks, auxes):
    tok = plan.tok
    rows, columns = iotas(tok, tok)
    upto = (rows <= columns).astype(BF16)
    sums = [dot(a, upto, 1, 0) for a in auxes]
    rates = [jnp.sum(a[0:3].astype(F32), axis=0, keepdims=True) for a in auxes]
    cumuls = [s[3:4] + s[4:5] + s[5:6] for s in sums]
    turned = to_columns(rates + cumuls, tok)
    out = []
    for i, c in enumerate(chunks):
        b_col, c_col = turned[i], turned[len(chunks) + i]
        c_row = cumuls[i]
        start = c * tok
        seg_col = segments(off_ref, start + rows[:, :1])
        seg_row = segments(off_ref, start + columns[:1, :])
        before = jnp.int32(0)
        last = jnp.int32(0)
        for j in range(off_ref.shape[0] - 1):
            before = before + (off_ref[j] <= start - 1).astype(jnp.int32)
            last = last + (off_ref[j] <= start + tok - 1).astype(jnp.int32)
        c_last = c_row[:, tok - 1 : tok]
        together = (seg_col == seg_row) & (rows >= columns)
        ratio = jnp.where(together, jnp.exp(jnp.where(together, c_col - c_row, 0.0)), 0.0)
        start_col = jnp.where(seg_col == before, jnp.exp(c_col), 0.0)
        end_col = jnp.where(seg_col == last, jnp.exp(c_last - c_col), 0.0)
        whole = jnp.where(last == before, jnp.exp(c_last), 0.0)
        out.append((rates[i], b_col, ratio, start_col, end_col, whole))
    return out


def inverses(lowers):
    size = lowers[0].shape[0]
    rows, columns = iotas(size, size)
    identity = (rows == columns).astype(F32)
    block = min(16, size)
    near = (rows // block) == (columns // block)
    powers = [jnp.where(near, -m, 0.0) for m in lowers]
    results = [identity + p for p in powers]
    split = [halves(p) for p in powers]
    powers = [mm(s, s) for s in split]
    reach = 2
    while reach < block:
        split = [halves(p) for p in powers]
        more = reach * 2 < block
        both = []
        for r, s in zip(results, split):
            left = halves(r)
            if more:
                left = cat([left, s], 0)
            both.append(mm(left, s))
        results = [r + b[:size] for r, b in zip(results, both)]
        if more:
            powers = [b[size:] for b in both]
        reach *= 2
    while block < size:
        across = ((rows // (2 * block)) == (columns // (2 * block))) & (
            (rows // block) > (columns // block)
        )
        split = [halves(r) for r in results]
        middle = [mm(halves(jnp.where(across, m, 0.0)), s) for m, s in zip(lowers, split)]
        results = [r - mm(s, halves(m)) for r, s, m in zip(results, split, middle)]
        block *= 2
    return results


def chunks_of(plan, place, mate):
    return [mate + plan.mates * plan.ring.source(place, d) for d in range(plan.hv)]


def prepare_kernel(plan, off_ref, place_ref, mate_ref, *refs):
    in_refs, (link_ref, kept_ref) = refs[: plan.hv], refs[plan.hv :]
    tok = plan.tok
    rows, columns = iotas(tok, tok)
    key_rows, key_columns = iotas(DK, DK)
    identity = (key_rows == key_columns).astype(F32)
    mine = range(plan.hv)
    chunks = chunks_of(plan, place_ref[0], mate_ref[0])
    scales = scalings(plan, off_ref, chunks, [r[plan.aux_at :] for r in in_refs])
    qn = [unit(in_refs[m][:tok].astype(F32))[0] for m in mine]
    kn = [unit(in_refs[m][tok : 2 * tok].astype(F32))[0] for m in mine]
    kp = [halves(x) for x in kn]
    qp = [halves(x) for x in qn]
    dots = [mm(cat([q, k], 0), k, 1, 1) for q, k in zip(qp, kp)]
    strict = rows > columns
    lowers = [jnp.where(strict, s[1] * d[tok:] * s[2], 0.0) for s, d in zip(scales, dots)]
    scores = [d[:tok] * s[2] for s, d in zip(scales, dots)]
    inv = inverses(lowers)
    rated = [halves(x * s[0]) for x, s in zip(inv, scales)]
    w = [mm(x, halves(s[3] * k)) for x, s, k in zip(rated, scales, kn)]
    values = [in_refs[m][plan.v_at : plan.aux_at] for m in mine]
    u = [
        dot(jnp.concatenate([v, v], axis=1), jnp.concatenate(x, axis=1), 1, 1)
        for v, x in zip(values, rated)
    ]
    wp = [halves(x) for x in w]
    up = [halves(x) for x in u]
    ap = [halves(x) for x in scores]
    ke = [halves(s[4] * k) for s, k in zip(scales, kn)]
    for m in mine:
        link_ref[m, 0] = scales[m][5] * identity - mm(wp[m], ke[m], 0, 0)
        link_ref[m, 1] = mm(up[m], ke[m])
    for m in mine:
        kept_ref[m, INVERSE] = inv[m]
        kept_ref[m, SCORES] = scores[m]
        kept_ref[m, FROM_STATE] = w[m]
        kept_ref[m, READS] = scales[m][3] * qn[m] - mm(ap[m], wp[m])
        kept_ref[m, RATIO] = scales[m][2]
        kept_ref[m, WRITES] = u[m]
        kept_ref[m, LOCAL] = mm(up[m], ap[m], 1, 1)


def lay_out(plan, place, mate, refs, all_ref):
    for d, ref in enumerate(refs):
        for m in range(plan.hv):
            all_ref[lax.rem(mate + d, plan.mates), plan.ring.source(place, m)] = ref[m]


def scan_kernel(plan, place_ref, mate_ref, *refs):
    s, hv = plan.mates, plan.hv
    links, kept_ref, state_ref = refs[:s], refs[s], refs[s + 1]
    outs, (all_ref, states_ref) = refs[s + 2 : -2], refs[-2:]
    place, mate = place_ref[0], mate_ref[0]
    lay_out(plan, place, mate, links, all_ref)
    state = jnp.zeros((DV, DK), F32)
    for c in range(plan.n):
        states_ref[c] = state
        if c < plan.n - 1:
            link = all_ref.at[c % s, c // s]
            state = link[1] + mm(halves(state), halves(link[0]))
    cores = []
    for m, c in enumerate(chunks_of(plan, place, mate)):
        state = states_ref[c]
        state_ref[m] = state
        core = kept_ref[m, LOCAL] + mm(halves(state), halves(kept_ref[m, READS]), 1, 1)
        cores.append(core.astype(BF16))
    for d in range(hv):
        for k in range(hv):
            outs[d][k] = cores[plan.ring.seen(d, k)]


def state_cotangent_kernel(plan, kept_ref, *refs):
    for m in range(plan.hv):
        refs[-1][m] = mm(d_out(refs[m]), halves(kept_ref[m, READS]))


def d_out(ref):
    return ref[:DV], ref[DV:]


def backward_kernel(plan, off_ref, place_ref, mate_ref, *refs):
    s, n, tok, hv = plan.mates, plan.n, plan.tok, plan.hv
    links, backs, refs = refs[:s], refs[s : 2 * s], refs[2 * s :]
    in_refs, d_refs, kept_ref, state_ref = refs[:hv], refs[hv : 2 * hv], refs[2 * hv], refs[2 * hv + 1]
    outs, (links_ref, backs_ref, cots_ref) = refs[2 * hv + 2 : -3], refs[-3:]
    outs = [outs[plan.ring.seen(m, 0)] for m in range(hv)]
    place, mate = place_ref[0], mate_ref[0]
    lay_out(plan, place, mate, links, links_ref)
    lay_out(plan, place, mate, backs, backs_ref)
    d_state = jnp.zeros((DV, DK), F32)
    for c in reversed(range(n)):
        cots_ref[c] = d_state
        if c:
            d_state = backs_ref[c % s, c // s] + mm(
                halves(d_state), halves(links_ref[c % s, c // s, 0]), 1, 1
            )
    rows, columns = iotas(tok, tok)
    strict = rows > columns
    upto = (rows >= columns).astype(BF16)
    mine = range(hv)
    chunks = chunks_of(plan, place, mate)
    scales = scalings(plan, off_ref, chunks, [r[plan.aux_at :] for r in in_refs])
    qu = [unit(in_refs[m][:tok].astype(F32)) for m in mine]
    ku = [unit(in_refs[m][tok : 2 * tok].astype(F32)) for m in mine]
    qp = [halves(x[0]) for x in qu]
    kp = [halves(x[0]) for x in ku]
    do = [d_out(r) for r in d_refs]
    s0 = [state_ref[m] for m in mine]
    ds = [cots_ref[c] for c in chunks]
    s0p = [halves(x) for x in s0]
    dsp = [halves(x) for x in ds]
    pseudo = [kept_ref[m, WRITES] - mm(s0p[m], halves(kept_ref[m, FROM_STATE]), 1, 1) for m in mine]
    pp = [halves(x) for x in pseudo]
    ke = [halves(s[4] * k[0]) for s, k in zip(scales, ku)]
    dp = [mm(do[m], halves(kept_ref[m, SCORES])) + mm(dsp[m], ke[m], 1, 1) for m in mine]
    dr = [mm(halves(dp[m]), halves(kept_ref[m, INVERSE])) for m in mine]
    drp = [halves(x) for x in dr]
    big = [mm(cat([o, r], 1), cat([p, s], 1), 0, 0) for o, r, p, s in zip(do, drp, pp, s0p)]
    pds = [mm(p, d, 0, 0) for p, d in zip(pp, dsp)]
    da = [big[m][:tok, :tok] * kept_ref[m, RATIO] for m in mine]
    dm = [jnp.where(strict, -big[m][tok:, :tok] * kept_ref[m, RATIO], 0.0) for m in mine]
    dap = [halves(x) for x in da]
    dmp = [halves(x) for x in dm]
    dbm = [halves(s[1] * x) for s, x in zip(scales, dm)]
    by_row = [mm(cat([x, y], 0), k) for x, y, k in zip(dap, dmp, kp)]
    by_column = [
        mm(cat([x, y], 0), cat([q, k], 0), 0, 0) for x, y, q, k in zip(dap, dbm, qp, kp)
    ]
    sums = []
    for m in mine:
        _, b_col, _, start_col, end_col, whole = scales[m]
        (qn, q_scale), (kn, k_scale) = qu[m], ku[m]
        out = outs[m]
        dqn = by_row[m][:tok] + start_col * big[m][:tok, tok:]
        erase = by_row[m][tok:] - start_col * big[m][tok:, tok:]
        ends = end_col * pds[m]
        write = by_column[m] + ends
        dkn = b_col * erase + write
        s_q = jnp.sum(qn * dqn, axis=1, keepdims=True)
        s_e = jnp.sum(kn * erase, axis=1, keepdims=True)
        s_w = jnp.sum(kn * write, axis=1, keepdims=True)
        total = jnp.sum(jnp.sum(kn * ends, axis=1, keepdims=True), axis=0, keepdims=True)
        both = jnp.sum(jnp.sum(s0[m] * ds[m], axis=1, keepdims=True), axis=0, keepdims=True)
        out[:tok] = (q_scale * (dqn - qn * s_q)).astype(BF16)
        out[tok : 2 * tok] = (k_scale * (dkn - kn * (b_col * s_e + s_w))).astype(BF16)
        out[plan.v_at : plan.aux_at] = (scales[m][0] * dr[m]).astype(BF16)
        sums.append((s_e, s_q + b_col * s_e - s_w, total + whole * both))
    turned = to_rows([s[0] for s in sums] + [s[1] for s in sums], tok)
    for m in mine:
        values = in_refs[m][plan.v_at : plan.aux_at].astype(F32)
        d_rate = turned[m] + jnp.sum(dr[m] * values, axis=0, keepdims=True)
        parts = dot(aux_rows([turned[plan.hv + m]], tok), upto, 1, 0)
        d_decay = parts[0:1] + parts[1:2] + parts[2:3] + sums[m][2]
        outs[m][plan.aux_at :] = aux_rows([d_rate, d_decay], tok)


def gather_rows(head, pieces, all_ref):
    rows, ring = pieces[0].shape[0], Ring(len(pieces))
    for d, piece in enumerate(pieces):
        at = ring.source(head, d) * rows
        all_ref[pl.ds(pl.multiple_of(at, rows), rows), :] = piece[...]


def cotangent_kernel(plan, parts, head_ref, place_ref, *refs):
    pieces, w_ref, outs, (all_ref, core_ref) = refs[:parts], refs[parts], refs[parts + 1 : -2], refs[-2:]
    gather_rows(head_ref[0], pieces, all_ref)
    high, low = halves(dot(w_ref[...], all_ref[...], 1, 1))
    for m in range(plan.hv):
        core_ref[m, :DV] = high[m * DV : (m + 1) * DV]
        core_ref[m, DV:] = low[m * DV : (m + 1) * DV]
    hand_out(plan, place_ref[0], core_ref, outs)


def turn_kernel(plan, parts, head_ref, place_ref, *refs):
    pieces, outs, (all_ref, turned_ref) = refs[:parts], refs[parts:-2], refs[-2:]
    gather_rows(head_ref[0], pieces, all_ref)
    share = turned_ref.shape[1]
    for m in range(plan.hv):
        part = all_ref[:, m * share : (m + 1) * share].astype(F32)
        turned_ref[m] = jnp.transpose(part).astype(BF16)
    hand_out(plan, place_ref[0], turned_ref, outs)


def project_kernel(plan, parts, head_ref, place_ref, *refs):
    mixed_refs, w_ref, outs, (all_ref, total_ref) = (
        refs[: plan.hv],
        refs[plan.hv],
        refs[plan.hv + 1 : -2],
        refs[-2:],
    )
    for d, ref in enumerate(mixed_refs):
        all_ref[plan.ring.source(place_ref[0], d)] = ref[0]
    mixed = all_ref[...].reshape(plan.hv * DV, plan.tok)
    total_ref[...] = dot(mixed, w_ref[...], 0, 0)
    rows, ring = outs[0].shape[0], Ring(parts)
    for d in range(parts):
        at = ring.target(head_ref[0], d) * rows
        block = total_ref[pl.ds(pl.multiple_of(at, rows), rows), :]
        outs[d][...] = block.astype(outs[d].dtype)


def weight_kernel(plan, place_ref, mate_ref, *refs):
    hv = plan.hv
    turned, mixed_refs, outs, all_ref = refs[:hv], refs[hv : 2 * hv], refs[2 * hv : -1], refs[-1]
    for d, ref in enumerate(mixed_refs):
        head = plan.ring.source(place_ref[0], d)
        for k in range(hv):
            all_ref[k, head] = ref[k]
    share = outs[0].shape[0]
    for d, out_ref in enumerate(outs):
        at = lax.rem(mate_ref[0] + plan.mates - d, plan.mates) * share
        at = pl.multiple_of(at, share)
        total = None
        for k in range(hv):
            mixed = all_ref[k].reshape(hv * DV, plan.tok)
            part = dot(turned[k][pl.ds(at, share), :], mixed, 1, 1)
            total = part if total is None else total + part
        out_ref[...] = total


def finish_kernel(plan, place_ref, *refs):
    pieces, (q_ref, k_ref, v_ref, rate_ref, decay_ref, in_ref) = refs[: plan.hv], refs[plan.hv :]
    tok = plan.tok
    for d, ref in enumerate(pieces):
        in_ref[plan.ring.source(place_ref[0], d)] = ref[...]
    for kh in range(plan.hk):
        mine = [h for h in range(plan.hv) if plan.key_head(h) == kh]
        for ref, at in ((q_ref, 0), (k_ref, tok)):
            total = in_ref[mine[0], at : at + tok].astype(F32)
            for h in mine[1:]:
                total = total + in_ref[h, at : at + tok].astype(F32)
            ref[:, kh * DK : (kh + 1) * DK] = total
    for h in range(plan.hv):
        v_ref[:, h * DV : (h + 1) * DV] = jnp.transpose(
            in_ref[h, plan.v_at : plan.aux_at].astype(F32)
        )
        aux = in_ref[h, plan.aux_at :].astype(F32)
        rate_ref[h : h + 1, :] = aux[0:1] + aux[1:2] + aux[2:3]
        decay_ref[h : h + 1, :] = aux[3:4] + aux[4:5] + aux[5:6]


def after(x, y):
    return lax.optimization_barrier((x, y))[0]


def per_device(
    queries, key_vectors, value_rows, write_rate, log_decay, doc_offsets, out_weight, grad_out
):
    n, parts = lax.axis_size("ctx"), lax.axis_size("head")
    tok, hv = queries.shape[0], write_rate.shape[0]
    hk, model = queries.shape[1] // DK, grad_out.shape[1]
    plan = Plan(n, tok, hv, hk)
    s = plan.mates
    index = lax.axis_index("ctx").astype(jnp.int32)
    place, mate = (index // s).reshape(1), (index % s).reshape(1)
    head = lax.axis_index("head").astype(jnp.int32).reshape(1)

    def across_heads(pieces):
        moved = [lax.ppermute(pieces[d], "head", Ring(parts).pairs(d)) for d in range(1, parts)]
        return [pieces[0]] + moved

    vmem = lambda dtype, *shape: pltpu.VMEM(shape, dtype)

    packed = call(
        partial(pack_kernel, plan),
        [arr(BF16, plan.rows, DK)] * hv,
        smem=(0,),
        scratch=[vmem(BF16, hv, plan.rows, DK)],
        fetch=range(1, 6),
    )(place, queries, key_vectors, value_rows, write_rate, log_decay)
    got = plan.exchange(packed)
    rows = across_heads([grad_out] * parts)

    link, kept = call(
        partial(prepare_kernel, plan),
        (arr(F32, hv, 2, DK, DK), arr(F32, hv, KEPT, tok, DK)),
        smem=(0, 1, 2),
        fetch=(0,),
        flops=20_000_000_000,
    )(doc_offsets, place, mate, *got)
    links = [link] + [plan.from_mate(link, d) for d in range(1, s)]

    d_core = call(
        partial(cotangent_kernel, plan, parts),
        [arr(BF16, 2 * DV, tok)] * hv,
        smem=(0, 1),
        scratch=[vmem(BF16, tok, model), vmem(BF16, hv, 2 * DV, tok)],
        flops=30_000_000_000,
    )(head, place, *rows, after(out_weight, link))
    kept = after(kept, d_core[0])
    d_core = plan.exchange(d_core)

    states, *mixed = call(
        partial(scan_kernel, plan),
        [arr(F32, hv, DV, DK)] + [arr(BF16, hv, DV, tok)] * hv,
        smem=(0, 1),
        scratch=[vmem(F32, s, hv, 2, DK, DK), vmem(F32, n, DV, DK)],
        flops=2_500_000_000,
    )(place, mate, *links, kept)
    turned = call(
        partial(turn_kernel, plan, parts),
        [arr(BF16, model // hv, tok)] * hv,
        smem=(0, 1),
        scratch=[vmem(BF16, tok, model), vmem(BF16, hv, model // hv, tok)],
        flops=1_000_000_000,
    )(head, place, *after(rows, states))
    mixed = plan.exchange(mixed)
    turned = plan.exchange(turned)
    back = call(
        partial(state_cotangent_kernel, plan), arr(F32, hv, DV, DK), flops=30_000_000_000
    )(kept, *after(d_core, states))
    backs = [back] + [plan.from_mate(back, d) for d in range(1, s)]

    projected = call(
        partial(project_kernel, plan, parts),
        [arr(BF16 if d else F32, tok // parts, model) for d in range(parts)],
        smem=(0, 1),
        scratch=[vmem(BF16, hv, DV, tok), vmem(F32, tok, model)],
        flops=1_000_000_000,
    )(head, place, *mixed, out_weight)
    layer_parts = across_heads(projected)

    grads = call(
        partial(backward_kernel, plan),
        [arr(BF16, plan.rows, DK)] * hv,
        smem=(0, 1, 2),
        fetch=(0,),
        scratch=[
            vmem(F32, s, hv, 2, DK, DK),
            vmem(F32, s, hv, DV, DK),
            vmem(F32, n, DV, DK),
        ],
        flops=6_000_000_000,
    )(doc_offsets, place, mate, *links, *backs, *got, *d_core, kept, after(states, projected[1]))

    shares = call(
        partial(weight_kernel, plan),
        [arr(F32, model // n, hv * DV)] * s,
        smem=(0, 1),
        scratch=[vmem(BF16, hv, hv, DV, tok)],
        flops=1_000_000_000,
    )(place, mate, *turned, *mixed)
    grads = plan.exchange(after(grads, shares[0]))
    weight_grad = shares[0]
    for d in range(1, s):
        weight_grad = weight_grad + plan.from_mate(shares[d], d)

    layer_out = layer_parts[0]
    for part in layer_parts[1:]:
        layer_out = layer_out + part.astype(F32)
    grads = after(grads, (layer_out, weight_grad))
    grad_q, grad_k, grad_v, grad_rate, grad_decay = call(
        partial(finish_kernel, plan),
        (
            arr(F32, tok, hk * DK),
            arr(F32, tok, hk * DK),
            arr(F32, tok, hv * DV),
            arr(F32, hv, tok),
            arr(F32, hv, tok),
        ),
        smem=(0,),
        scratch=[vmem(BF16, hv, plan.rows, DK)],
        flops=1_000_000_000,
        inside=False,
    )(place, *grads)
    return (layer_out, grad_q, grad_k, grad_v, grad_rate, grad_decay, weight_grad)


def solution(mesh):
    placed = (
        P("ctx", "head"),
        P("ctx", "head"),
        P("ctx", "head"),
        P("head", "ctx"),
        P("head", "ctx"),
        P(),
        P("head", None),
        P(("ctx", "head"), None),
    )
    return jax.shard_map(
        per_device,
        mesh=mesh,
        in_specs=placed,
        out_specs=(
            P(("ctx", "head"), None),
            P("ctx", "head"),
            P("ctx", "head"),
            P("ctx", "head"),
            P("head", "ctx"),
            P("head", "ctx"),
            P("ctx", "head"),
        ),
        check_vma=False,
    )
```

```python
import math
from functools import partial

import jax
import jax.numpy as jnp
from jax import lax
from jax.experimental import pallas as pl
from jax.experimental.pallas import tpu as pltpu
from jax.sharding import PartitionSpec as P

DK = 128
DV = 128
AUX = 16
INVERSE, SCORES, FROM_STATE, READS, RATIO, WRITES, LOCAL, KEPT = range(8)
EPS = 1e-06
F32 = jnp.float32
BF16 = jnp.bfloat16
SPARE_VMEM = 8 * 1024 * 1024


def dot(a, b, ca, cb):
    return lax.dot_general(a, b, (((ca,), (cb,)), ((), ())), preferred_element_type=F32)


def halves(x):
    high = x.astype(BF16)
    return high, (x - high.astype(F32)).astype(BF16)


def thirds(x):
    high = x.astype(BF16).astype(F32)
    middle = (x - high).astype(BF16).astype(F32)
    return high, middle, x - high - middle


def mm(a, b, ca=1, cb=0):
    left = jnp.concatenate([a[0], a[0], a[1]], axis=ca)
    right = jnp.concatenate([b[0], b[1], b[0]], axis=cb)
    return dot(left, right, ca, cb)


def cat(pairs, axis):
    return tuple(jnp.concatenate(parts, axis=axis) for parts in zip(*pairs))


def iotas(rows, columns):
    shape = (rows, columns)
    return lax.broadcasted_iota(jnp.int32, shape, 0), lax.broadcasted_iota(jnp.int32, shape, 1)


def call(kernel, outs, smem=(), scratch=(), flops=0, inside=True, fetch=()):
    if inside:
        outs = jax.tree.map(lambda o: pltpu.VMEM(o.shape, o.dtype), outs)
    scoped = SPARE_VMEM + sum(x.dtype.itemsize * math.prod(x.shape) for x in scratch)

    def run(*args):
        spec = lambda i: pl.BlockSpec(memory_space=pltpu.SMEM if i in smem else pltpu.VMEM)
        space = lambda i: pltpu.HBM if i in fetch else pltpu.VMEM
        hold = pltpu.with_memory_space_constraint
        return pl.pallas_call(
            kernel,
            out_shape=outs,
            in_specs=[spec(i) for i in range(len(args))],
            out_specs=jax.tree.map(lambda _: pl.BlockSpec(memory_space=pltpu.VMEM), outs),
            scratch_shapes=list(scratch),
            compiler_params=pltpu.CompilerParams(vmem_limit_bytes=scoped),
            cost_estimate=pl.CostEstimate(flops=flops, bytes_accessed=0, transcendentals=0),
        )(*(hold(x, space(i)) if i in fetch or i not in smem else x for i, x in enumerate(args)))

    return run


def arr(dtype, *shape):
    return jax.ShapeDtypeStruct(shape, dtype)


class Ring:
    def __init__(self, size):
        self.size = size
        self.paired = size & (size - 1) == 0

    def source(self, i, d):
        return i ^ d if self.paired else (i + d) % self.size

    def target(self, i, d):
        return i ^ d if self.paired else (i + self.size - d) % self.size

    def seen(self, d, k):
        return d ^ k if self.paired else (k - d) % self.size

    def far_first(self):
        return sorted(range(self.size), key=lambda d: d != self.size // 2)

    def pairs(self, d):
        return [(self.source(i, d), i) for i in range(self.size)]


class Plan:
    def __init__(self, n, tok, hv, hk):
        self.n, self.tok, self.hv, self.hk = n, tok, hv, hk
        self.mates = n // hv
        self.v_at = 2 * tok
        self.aux_at = 2 * tok + DV
        self.rows = self.aux_at + AUX
        self.ring = Ring(hv)

    def key_head(self, head):
        return head * self.hk // self.hv

    def exchange(self, pieces, in_turn=False):
        s = self.mates
        moved = [pieces[0]]
        for d in range(1, self.hv):
            pairs = [(i * s + b, j * s + b) for i, j in self.ring.pairs(d) for b in range(s)]
            piece = after(pieces[d], moved[1]) if in_turn and d > 1 else pieces[d]
            moved.append(lax.ppermute(piece, "ctx", pairs))
        return moved

    def from_mate(self, x, d):
        s = self.mates
        pairs = [(i // s * s + (i + d) % s, i) for i in range(self.n)]
        return lax.ppermute(x, "ctx", pairs)


def aux_rows(rows, columns):
    row_ids = lax.broadcasted_iota(jnp.int32, (AUX, columns), 0)
    out = jnp.zeros((AUX, columns), F32)
    for i, part in enumerate(p for r in rows for p in thirds(r)):
        out = jnp.where(row_ids == i, part, out)
    return out.astype(BF16)


def pack_kernel(plan, place_ref, q_ref, k_ref, v_ref, rate_ref, decay_ref, *refs):
    outs, out_ref = refs[:-1], refs[-1]
    tok = plan.tok
    for h in range(plan.hv):
        kh = plan.key_head(h)
        out_ref[h, :tok] = q_ref[:, kh * DK : (kh + 1) * DK]
        out_ref[h, tok : 2 * tok] = k_ref[:, kh * DK : (kh + 1) * DK]
        turned = jnp.transpose(v_ref[:, h * DV : (h + 1) * DV].astype(F32))
        out_ref[h, plan.v_at : plan.aux_at] = turned.astype(BF16)
        rows = [rate_ref[h : h + 1, :], decay_ref[h : h + 1, :]]
        out_ref[h, plan.aux_at :] = aux_rows(rows, tok)
    hand_out(plan, place_ref[0], out_ref, outs)


def hand_out(plan, place, all_ref, outs):
    for d, ref in enumerate(outs):
        ref[...] = all_ref[plan.ring.target(place, d)]


def unit(x):
    scale = lax.rsqrt(jnp.sum(x * x, axis=1, keepdims=True) + EPS)
    return x * scale, scale


def segments(off_ref, positions):
    total = jnp.zeros(positions.shape, jnp.int32)
    for j in range(off_ref.shape[0] - 1):
        total = total + (off_ref[j] <= positions).astype(jnp.int32)
    return total


def to_columns(rows, tok):
    row_ids = lax.broadcasted_iota(jnp.int32, (tok, tok), 0)
    stacked = jnp.zeros((tok, tok), F32)
    for i, r in enumerate(rows):
        stacked = jnp.where(row_ids == i, r, stacked)
    turned = jnp.transpose(stacked)
    return [turned[:, i : i + 1] for i in range(len(rows))]


def to_rows(columns, tok):
    column_ids = lax.broadcasted_iota(jnp.int32, (tok, tok), 1)
    stacked = jnp.zeros((tok, tok), F32)
    for i, c in enumerate(columns):
        stacked = jnp.where(column_ids == i, c, stacked)
    turned = jnp.transpose(stacked)
    return [turned[i : i + 1, :] for i in range(len(columns))]


def scalings(plan, off_ref, chunks, auxes):
    tok = plan.tok
    rows, columns = iotas(tok, tok)
    upto = (rows <= columns).astype(BF16)
    sums = [dot(a, upto, 1, 0) for a in auxes]
    rates = [jnp.sum(a[0:3].astype(F32), axis=0, keepdims=True) for a in auxes]
    cumuls = [s[3:4] + s[4:5] + s[5:6] for s in sums]
    turned = to_columns(rates + cumuls, tok)
    out = []
    for i, c in enumerate(chunks):
        b_col, c_col = turned[i], turned[len(chunks) + i]
        c_row = cumuls[i]
        start = c * tok
        seg_col = segments(off_ref, start + rows[:, :1])
        seg_row = segments(off_ref, start + columns[:1, :])
        before = jnp.int32(0)
        last = jnp.int32(0)
        for j in range(off_ref.shape[0] - 1):
            before = before + (off_ref[j] <= start - 1).astype(jnp.int32)
            last = last + (off_ref[j] <= start + tok - 1).astype(jnp.int32)
        c_last = c_row[:, tok - 1 : tok]
        together = (seg_col == seg_row) & (rows >= columns)
        ratio = jnp.where(together, jnp.exp(jnp.where(together, c_col - c_row, 0.0)), 0.0)
        start_col = jnp.where(seg_col == before, jnp.exp(c_col), 0.0)
        end_col = jnp.where(seg_col == last, jnp.exp(c_last - c_col), 0.0)
        whole = jnp.where(last == before, jnp.exp(c_last), 0.0)
        out.append((rates[i], b_col, ratio, start_col, end_col, whole))
    return out


def inverses(lowers):
    size = lowers[0].shape[0]
    rows, columns = iotas(size, size)
    identity = (rows == columns).astype(F32)
    block = min(16, size)
    near = (rows // block) == (columns // block)
    powers = [jnp.where(near, -m, 0.0) for m in lowers]
    results = [identity + p for p in powers]
    split = [halves(p) for p in powers]
    powers = [mm(s, s) for s in split]
    reach = 2
    while reach < block:
        split = [halves(p) for p in powers]
        more = reach * 2 < block
        both = []
        for r, s in zip(results, split):
            left = halves(r)
            if more:
                left = cat([left, s], 0)
            both.append(mm(left, s))
        results = [r + b[:size] for r, b in zip(results, both)]
        if more:
            powers = [b[size:] for b in both]
        reach *= 2
    while block < size:
        across = ((rows // (2 * block)) == (columns // (2 * block))) & (
            (rows // block) > (columns // block)
        )
        split = [halves(r) for r in results]
        middle = [mm(halves(jnp.where(across, m, 0.0)), s) for m, s in zip(lowers, split)]
        results = [r - mm(s, halves(m)) for r, s, m in zip(results, split, middle)]
        block *= 2
    return results


def chunks_of(plan, place, mate):
    return [mate + plan.mates * plan.ring.source(place, d) for d in range(plan.hv)]


def prepare_kernel(plan, off_ref, place_ref, mate_ref, *refs):
    in_refs, (link_ref, kept_ref) = refs[: plan.hv], refs[plan.hv :]
    tok = plan.tok
    rows, columns = iotas(tok, tok)
    key_rows, key_columns = iotas(DK, DK)
    identity = (key_rows == key_columns).astype(F32)
    mine = range(plan.hv)
    chunks = chunks_of(plan, place_ref[0], mate_ref[0])
    scales = scalings(plan, off_ref, chunks, [r[plan.aux_at :] for r in in_refs])
    qn = [unit(in_refs[m][:tok].astype(F32))[0] for m in mine]
    kn = [unit(in_refs[m][tok : 2 * tok].astype(F32))[0] for m in mine]
    kp = [halves(x) for x in kn]
    qp = [halves(x) for x in qn]
    dots = [mm(cat([q, k], 0), k, 1, 1) for q, k in zip(qp, kp)]
    strict = rows > columns
    lowers = [jnp.where(strict, s[1] * d[tok:] * s[2], 0.0) for s, d in zip(scales, dots)]
    scores = [d[:tok] * s[2] for s, d in zip(scales, dots)]
    inv = inverses(lowers)
    rated = [halves(x * s[0]) for x, s in zip(inv, scales)]
    w = [mm(x, halves(s[3] * k)) for x, s, k in zip(rated, scales, kn)]
    values = [in_refs[m][plan.v_at : plan.aux_at] for m in mine]
    u = [
        dot(jnp.concatenate([v, v], axis=1), jnp.concatenate(x, axis=1), 1, 1)
        for v, x in zip(values, rated)
    ]
    wp = [halves(x) for x in w]
    up = [halves(x) for x in u]
    ap = [halves(x) for x in scores]
    ke = [halves(s[4] * k) for s, k in zip(scales, kn)]
    for m in mine:
        link_ref[m, 0] = scales[m][5] * identity - mm(wp[m], ke[m], 0, 0)
        link_ref[m, 1] = mm(up[m], ke[m])
    for m in mine:
        kept_ref[m, INVERSE] = inv[m]
        kept_ref[m, SCORES] = scores[m]
        kept_ref[m, FROM_STATE] = w[m]
        kept_ref[m, READS] = scales[m][3] * qn[m] - mm(ap[m], wp[m])
        kept_ref[m, RATIO] = scales[m][2]
        kept_ref[m, WRITES] = u[m]
        kept_ref[m, LOCAL] = mm(up[m], ap[m], 1, 1)


def lay_out(plan, place, mate, refs, all_ref):
    for d, ref in enumerate(refs):
        for m in range(plan.hv):
            all_ref[lax.rem(mate + d, plan.mates), plan.ring.source(place, m)] = ref[m]


def scan_kernel(plan, place_ref, mate_ref, *refs):
    s, hv = plan.mates, plan.hv
    links, kept_ref, d_refs, state_ref = refs[:s], refs[s], refs[s + 1 : s + 1 + hv], refs[s + 1 + hv]
    outs, (all_ref, states_ref) = refs[s + 2 + hv : -2], refs[-2:]
    place, mate = place_ref[0], mate_ref[0]
    lay_out(plan, place, mate, links, all_ref)
    state = jnp.zeros((DV, DK), F32)
    for c in range(plan.n):
        states_ref[c] = state
        if c < plan.n - 1:
            link = all_ref.at[c % s, c // s]
            state = link[1] + mm(halves(state), halves(link[0]))
    cores = []
    for m, c in enumerate(chunks_of(plan, place, mate)):
        state = states_ref[c]
        state_ref[m] = state
        core = kept_ref[m, LOCAL] + mm(halves(state), halves(kept_ref[m, READS]), 1, 1)
        cores.append(core.astype(BF16))
    for d in range(hv):
        outs[d][:2] = d_refs[d][...]
        for k in range(hv):
            outs[d][2 + k] = cores[plan.ring.seen(d, k)]


def state_cotangent_kernel(plan, kept_ref, *refs):
    for m in range(plan.hv):
        refs[-1][m] = mm(d_out(refs[m]), halves(kept_ref[m, READS]))


def d_out(ref):
    return ref[0], ref[1]


def backward_kernel(plan, off_ref, place_ref, mate_ref, *refs):
    s, n, tok, hv = plan.mates, plan.n, plan.tok, plan.hv
    links, backs, refs = refs[:s], refs[s : 2 * s], refs[2 * s :]
    in_refs, d_refs, kept_ref, state_ref = refs[:hv], refs[hv : 2 * hv], refs[2 * hv], refs[2 * hv + 1]
    outs, (links_ref, backs_ref, cots_ref) = refs[2 * hv + 2 : -3], refs[-3:]
    outs = [outs[plan.ring.seen(m, 0)] for m in range(hv)]
    place, mate = place_ref[0], mate_ref[0]
    lay_out(plan, place, mate, links, links_ref)
    lay_out(plan, place, mate, backs, backs_ref)
    d_state = jnp.zeros((DV, DK), F32)
    for c in reversed(range(n)):
        cots_ref[c] = d_state
        if c:
            d_state = backs_ref[c % s, c // s] + mm(
                halves(d_state), halves(links_ref[c % s, c // s, 0]), 1, 1
            )
    rows, columns = iotas(tok, tok)
    strict = rows > columns
    upto = (rows >= columns).astype(BF16)
    mine = range(hv)
    chunks = chunks_of(plan, place, mate)
    scales = scalings(plan, off_ref, chunks, [r[plan.aux_at :] for r in in_refs])
    qu = [unit(in_refs[m][:tok].astype(F32)) for m in mine]
    ku = [unit(in_refs[m][tok : 2 * tok].astype(F32)) for m in mine]
    qp = [halves(x[0]) for x in qu]
    kp = [halves(x[0]) for x in ku]
    do = [d_out(r) for r in d_refs]
    s0 = [state_ref[m] for m in mine]
    ds = [cots_ref[c] for c in chunks]
    s0p = [halves(x) for x in s0]
    dsp = [halves(x) for x in ds]
    pseudo = [kept_ref[m, WRITES] - mm(s0p[m], halves(kept_ref[m, FROM_STATE]), 1, 1) for m in mine]
    pp = [halves(x) for x in pseudo]
    ke = [halves(s[4] * k[0]) for s, k in zip(scales, ku)]
    dp = [mm(do[m], halves(kept_ref[m, SCORES])) + mm(dsp[m], ke[m], 1, 1) for m in mine]
    dr = [mm(halves(dp[m]), halves(kept_ref[m, INVERSE])) for m in mine]
    drp = [halves(x) for x in dr]
    big = [mm(cat([o, r], 1), cat([p, s], 1), 0, 0) for o, r, p, s in zip(do, drp, pp, s0p)]
    pds = [mm(p, d, 0, 0) for p, d in zip(pp, dsp)]
    da = [big[m][:tok, :tok] * kept_ref[m, RATIO] for m in mine]
    dm = [jnp.where(strict, -big[m][tok:, :tok] * kept_ref[m, RATIO], 0.0) for m in mine]
    dap = [halves(x) for x in da]
    dmp = [halves(x) for x in dm]
    dbm = [halves(s[1] * x) for s, x in zip(scales, dm)]
    by_row = [mm(cat([x, y], 0), k) for x, y, k in zip(dap, dmp, kp)]
    by_column = [
        mm(cat([x, y], 0), cat([q, k], 0), 0, 0) for x, y, q, k in zip(dap, dbm, qp, kp)
    ]
    sums = []
    for m in mine:
        _, b_col, _, start_col, end_col, whole = scales[m]
        (qn, q_scale), (kn, k_scale) = qu[m], ku[m]
        out = outs[m]
        dqn = by_row[m][:tok] + start_col * big[m][:tok, tok:]
        erase = by_row[m][tok:] - start_col * big[m][tok:, tok:]
        ends = end_col * pds[m]
        write = by_column[m] + ends
        dkn = b_col * erase + write
        s_q = jnp.sum(qn * dqn, axis=1, keepdims=True)
        s_e = jnp.sum(kn * erase, axis=1, keepdims=True)
        s_w = jnp.sum(kn * write, axis=1, keepdims=True)
        total = jnp.sum(jnp.sum(kn * ends, axis=1, keepdims=True), axis=0, keepdims=True)
        both = jnp.sum(jnp.sum(s0[m] * ds[m], axis=1, keepdims=True), axis=0, keepdims=True)
        out[:tok] = (q_scale * (dqn - qn * s_q)).astype(BF16)
        out[tok : 2 * tok] = (k_scale * (dkn - kn * (b_col * s_e + s_w))).astype(BF16)
        out[plan.v_at : plan.aux_at] = (scales[m][0] * dr[m]).astype(BF16)
        sums.append((s_e, s_q + b_col * s_e - s_w, total + whole * both))
    turned = to_rows([s[0] for s in sums] + [s[1] for s in sums], tok)
    for m in mine:
        values = in_refs[m][plan.v_at : plan.aux_at].astype(F32)
        d_rate = turned[m] + jnp.sum(dr[m] * values, axis=0, keepdims=True)
        parts = dot(aux_rows([turned[plan.hv + m]], tok), upto, 1, 0)
        d_decay = parts[0:1] + parts[1:2] + parts[2:3] + sums[m][2]
        outs[m][plan.aux_at :] = aux_rows([d_rate, d_decay], tok)


def gather_rows(head, pieces, all_ref):
    rows, ring = pieces[0].shape[0], Ring(len(pieces))
    for d, piece in zip(ring.far_first(), pieces):
        at = ring.source(head, d) * rows
        all_ref[pl.ds(pl.multiple_of(at, rows), rows), :] = piece[...]


def cotangent_kernel(plan, parts, head_ref, place_ref, *refs):
    pieces, w_ref, outs, (all_ref, core_ref) = refs[:parts], refs[parts], refs[parts + 1 : -2], refs[-2:]
    gather_rows(head_ref[0], pieces, all_ref)
    high, low = halves(dot(w_ref[...], all_ref[...], 1, 1))
    for m in range(plan.hv):
        core_ref[m, 0] = high[m * DV : (m + 1) * DV]
        core_ref[m, 1] = low[m * DV : (m + 1) * DV]
    hand_out(plan, place_ref[0], core_ref, outs)


def turn_kernel(plan, parts, head_ref, place_ref, *refs):
    pieces, outs, (all_ref, turned_ref) = refs[:parts], refs[parts:-2], refs[-2:]
    gather_rows(head_ref[0], pieces, all_ref)
    share = turned_ref.shape[1]
    for m in range(plan.hv):
        part = all_ref[:, m * share : (m + 1) * share].astype(F32)
        turned_ref[m] = jnp.transpose(part).astype(BF16)
    hand_out(plan, place_ref[0], turned_ref, outs)


def project_kernel(plan, parts, head_ref, place_ref, *refs):
    mixed_refs, w_ref, outs, (all_ref, total_ref) = (
        refs[: plan.hv],
        refs[plan.hv],
        refs[plan.hv + 1 : -2],
        refs[-2:],
    )
    for d, ref in enumerate(mixed_refs):
        all_ref[plan.ring.source(place_ref[0], d)] = ref[2]
    mixed = all_ref[...].reshape(plan.hv * DV, plan.tok)
    total_ref[...] = dot(mixed, w_ref[...], 0, 0)
    rows, ring = outs[0].shape[0], Ring(parts)
    for d in range(parts):
        at = ring.target(head_ref[0], d) * rows
        block = total_ref[pl.ds(pl.multiple_of(at, rows), rows), :]
        outs[d][...] = block.astype(outs[d].dtype)


def weight_kernel(plan, place_ref, mate_ref, *refs):
    hv = plan.hv
    turned, mixed_refs, outs, all_ref = refs[:hv], refs[hv : 2 * hv], refs[2 * hv : -1], refs[-1]
    for d, ref in enumerate(mixed_refs):
        head = plan.ring.source(place_ref[0], d)
        for k in range(hv):
            all_ref[k, head] = ref[2 + k]
    share = outs[0].shape[0]
    for d, out_ref in enumerate(outs):
        at = lax.rem(mate_ref[0] + plan.mates - d, plan.mates) * share
        at = pl.multiple_of(at, share)
        total = None
        for k in range(hv):
            mixed = all_ref[k].reshape(hv * DV, plan.tok)
            part = dot(turned[k][pl.ds(at, share), :], mixed, 1, 1)
            total = part if total is None else total + part
        out_ref[...] = total


def finish_kernel(plan, place_ref, *refs):
    pieces, (q_ref, k_ref, v_ref, rate_ref, decay_ref, in_ref) = refs[: plan.hv], refs[plan.hv :]
    tok = plan.tok
    for d, ref in enumerate(pieces):
        in_ref[plan.ring.source(place_ref[0], d)] = ref[...]
    for kh in range(plan.hk):
        mine = [h for h in range(plan.hv) if plan.key_head(h) == kh]
        for ref, at in ((q_ref, 0), (k_ref, tok)):
            total = in_ref[mine[0], at : at + tok].astype(F32)
            for h in mine[1:]:
                total = total + in_ref[h, at : at + tok].astype(F32)
            ref[:, kh * DK : (kh + 1) * DK] = total
    for h in range(plan.hv):
        v_ref[:, h * DV : (h + 1) * DV] = jnp.transpose(
            in_ref[h, plan.v_at : plan.aux_at].astype(F32)
        )
        aux = in_ref[h, plan.aux_at :].astype(F32)
        rate_ref[h : h + 1, :] = aux[0:1] + aux[1:2] + aux[2:3]
        decay_ref[h : h + 1, :] = aux[3:4] + aux[4:5] + aux[5:6]


def after(x, y):
    return lax.optimization_barrier((x, y))[0]


def per_device(
    queries, key_vectors, value_rows, write_rate, log_decay, doc_offsets, out_weight, grad_out
):
    n, parts = lax.axis_size("ctx"), lax.axis_size("head")
    tok, hv = queries.shape[0], write_rate.shape[0]
    hk, model = queries.shape[1] // DK, grad_out.shape[1]
    plan = Plan(n, tok, hv, hk)
    s = plan.mates
    index = lax.axis_index("ctx").astype(jnp.int32)
    place, mate = (index // s).reshape(1), (index % s).reshape(1)
    head = lax.axis_index("head").astype(jnp.int32).reshape(1)

    def across_heads(pieces):
        moved = list(pieces)
        for d in range(1, parts):
            moved[d] = lax.ppermute(pieces[d], "head", Ring(parts).pairs(d))
        return moved

    vmem = lambda dtype, *shape: pltpu.VMEM(shape, dtype)

    packed = call(
        partial(pack_kernel, plan),
        [arr(BF16, plan.rows, DK)] * hv,
        smem=(0,),
        scratch=[vmem(BF16, hv, plan.rows, DK)],
        fetch=range(1, 6),
    )(place, queries, key_vectors, value_rows, write_rate, log_decay)
    got = plan.exchange(packed)
    rows = across_heads([grad_out] * parts)
    rows = [rows[d] for d in Ring(parts).far_first()]

    link, kept = call(
        partial(prepare_kernel, plan),
        (arr(F32, hv, 2, DK, DK), arr(F32, hv, KEPT, tok, DK)),
        smem=(0, 1, 2),
        fetch=(0,),
        flops=20_000_000_000,
    )(doc_offsets, place, mate, *got)
    links = [link] + [plan.from_mate(link, d) for d in range(1, s)]

    d_core = call(
        partial(cotangent_kernel, plan, parts),
        [arr(BF16, 2, DV, tok)] * hv,
        smem=(0, 1),
        scratch=[vmem(BF16, tok, model), vmem(BF16, hv, 2, DV, tok)],
        flops=30_000_000_000,
    )(head, place, *rows, after(out_weight, link))

    states, *mixed = call(
        partial(scan_kernel, plan),
        [arr(F32, hv, DV, DK)] + [arr(BF16, 2 + hv, DV, tok)] * hv,
        smem=(0, 1),
        scratch=[vmem(F32, s, hv, 2, DK, DK), vmem(F32, n, DV, DK)],
        flops=2_500_000_000,
    )(place, mate, *links, kept, *d_core)
    turned = call(
        partial(turn_kernel, plan, parts),
        [arr(BF16, model // hv, tok)] * hv,
        smem=(0, 1),
        scratch=[vmem(BF16, tok, model), vmem(BF16, hv, model // hv, tok)],
        flops=1_000_000_000,
    )(head, place, *after(rows, states))
    mixed = plan.exchange(mixed)
    turned = plan.exchange(turned, in_turn=True)
    back = call(
        partial(state_cotangent_kernel, plan), arr(F32, hv, DV, DK), flops=30_000_000_000
    )(kept, *mixed)
    backs = [back] + [plan.from_mate(back, d) for d in range(1, s)]

    projected = call(
        partial(project_kernel, plan, parts),
        [arr(BF16 if d else F32, tok // parts, model) for d in range(parts)],
        smem=(0, 1),
        scratch=[vmem(BF16, hv, DV, tok), vmem(F32, tok, model)],
        flops=1_000_000_000,
    )(head, place, *mixed, out_weight)
    layer_parts = across_heads(projected)

    grads = call(
        partial(backward_kernel, plan),
        [arr(BF16, plan.rows, DK)] * hv,
        smem=(0, 1, 2),
        fetch=(0,),
        scratch=[
            vmem(F32, s, hv, 2, DK, DK),
            vmem(F32, s, hv, DV, DK),
            vmem(F32, n, DV, DK),
        ],
        flops=6_000_000_000,
    )(doc_offsets, place, mate, *links, *backs, *got, *mixed, kept, after(states, projected[1]))

    shares = call(
        partial(weight_kernel, plan),
        [arr(F32, model // n, hv * DV)] * s,
        smem=(0, 1),
        scratch=[vmem(BF16, hv, hv, DV, tok)],
        flops=1_000_000_000,
    )(place, mate, *turned, *mixed)
    grads = plan.exchange(after(grads, shares[0]))
    weight_grad = shares[0]
    for d in range(1, s):
        weight_grad = weight_grad + plan.from_mate(shares[d], d)

    layer_out = layer_parts[0]
    for part in layer_parts[1:]:
        layer_out = layer_out + part.astype(F32)
    grads = after(grads, (layer_out, weight_grad))
    grad_q, grad_k, grad_v, grad_rate, grad_decay = call(
        partial(finish_kernel, plan),
        (
            arr(F32, tok, hk * DK),
            arr(F32, tok, hk * DK),
            arr(F32, tok, hv * DV),
            arr(F32, hv, tok),
            arr(F32, hv, tok),
        ),
        smem=(0,),
        scratch=[vmem(BF16, hv, plan.rows, DK)],
        flops=1_000_000_000,
        inside=False,
    )(place, *grads)
    return (layer_out, grad_q, grad_k, grad_v, grad_rate, grad_decay, weight_grad)


def solution(mesh):
    placed = (
        P("ctx", "head"),
        P("ctx", "head"),
        P("ctx", "head"),
        P("head", "ctx"),
        P("head", "ctx"),
        P(),
        P("head", None),
        P(("ctx", "head"), None),
    )
    return jax.shard_map(
        per_device,
        mesh=mesh,
        in_specs=placed,
        out_specs=(
            P(("ctx", "head"), None),
            P("ctx", "head"),
            P("ctx", "head"),
            P("ctx", "head"),
            P("head", "ctx"),
            P("head", "ctx"),
            P("ctx", "head"),
        ),
        check_vma=False,
    )
```

```python
import math
from functools import partial

import jax
import jax.numpy as jnp
from jax import lax
from jax.experimental import pallas as pl
from jax.experimental.pallas import tpu as pltpu
from jax.sharding import PartitionSpec as P

DK = 128
DV = 128
AUX = 16
INVERSE, SCORES, FROM_STATE, READS, RATIO, WRITES, LOCAL, KEPT = range(8)
EPS = 1e-06
F32 = jnp.float32
BF16 = jnp.bfloat16
SPARE_VMEM = 8 * 1024 * 1024


def dot(a, b, ca, cb):
    return lax.dot_general(a, b, (((ca,), (cb,)), ((), ())), preferred_element_type=F32)


def halves(x):
    high = x.astype(BF16)
    return high, (x - high.astype(F32)).astype(BF16)


def thirds(x):
    high = x.astype(BF16).astype(F32)
    middle = (x - high).astype(BF16).astype(F32)
    return high, middle, x - high - middle


def mm(a, b, ca=1, cb=0):
    left = jnp.concatenate([a[0], a[0], a[1]], axis=ca)
    right = jnp.concatenate([b[0], b[1], b[0]], axis=cb)
    return dot(left, right, ca, cb)


def cat(pairs, axis):
    return tuple(jnp.concatenate(parts, axis=axis) for parts in zip(*pairs))


def iotas(rows, columns):
    shape = (rows, columns)
    return lax.broadcasted_iota(jnp.int32, shape, 0), lax.broadcasted_iota(jnp.int32, shape, 1)


def call(kernel, outs, smem=(), scratch=(), flops=0, inside=True, fetch=()):
    if inside:
        outs = jax.tree.map(lambda o: pltpu.VMEM(o.shape, o.dtype), outs)
    scoped = SPARE_VMEM + sum(x.dtype.itemsize * math.prod(x.shape) for x in scratch)

    def run(*args):
        spec = lambda i: pl.BlockSpec(memory_space=pltpu.SMEM if i in smem else pltpu.VMEM)
        space = lambda i: pltpu.HBM if i in fetch else pltpu.VMEM
        hold = pltpu.with_memory_space_constraint
        return pl.pallas_call(
            kernel,
            out_shape=outs,
            in_specs=[spec(i) for i in range(len(args))],
            out_specs=jax.tree.map(lambda _: pl.BlockSpec(memory_space=pltpu.VMEM), outs),
            scratch_shapes=list(scratch),
            compiler_params=pltpu.CompilerParams(vmem_limit_bytes=scoped),
            cost_estimate=pl.CostEstimate(flops=flops, bytes_accessed=0, transcendentals=0),
        )(*(hold(x, space(i)) if i in fetch or i not in smem else x for i, x in enumerate(args)))

    return run


def arr(dtype, *shape):
    return jax.ShapeDtypeStruct(shape, dtype)


class Ring:
    def __init__(self, size):
        self.size = size
        self.paired = size & (size - 1) == 0

    def source(self, i, d):
        return i ^ d if self.paired else (i + d) % self.size

    def target(self, i, d):
        return i ^ d if self.paired else (i + self.size - d) % self.size

    def seen(self, d, k):
        return d ^ k if self.paired else (k - d) % self.size

    def far_first(self):
        return sorted(range(self.size), key=lambda d: d != self.size // 2)

    def pairs(self, d):
        return [(self.source(i, d), i) for i in range(self.size)]


class Plan:
    def __init__(self, n, tok, hv, hk):
        self.n, self.tok, self.hv, self.hk = n, tok, hv, hk
        self.mates = n // hv
        self.v_at = 2 * tok
        self.aux_at = 2 * tok + DV
        self.rows = self.aux_at + AUX
        self.ring = Ring(hv)

    def key_head(self, head):
        return head * self.hk // self.hv

    def exchange(self, pieces):
        s = self.mates
        moved = [pieces[0]]
        for d in range(1, self.hv):
            pairs = [(i * s + b, j * s + b) for i, j in self.ring.pairs(d) for b in range(s)]
            moved.append(lax.ppermute(pieces[d], "ctx", pairs))
        return moved

    def from_mate(self, x, d):
        s = self.mates
        pairs = [(i // s * s + (i + d) % s, i) for i in range(self.n)]
        return lax.ppermute(x, "ctx", pairs)


def aux_rows(rows, columns):
    row_ids = lax.broadcasted_iota(jnp.int32, (AUX, columns), 0)
    out = jnp.zeros((AUX, columns), F32)
    for i, part in enumerate(p for r in rows for p in thirds(r)):
        out = jnp.where(row_ids == i, part, out)
    return out.astype(BF16)


def pack_kernel(plan, place_ref, q_ref, k_ref, v_ref, rate_ref, decay_ref, *refs):
    outs, out_ref = refs[:-1], refs[-1]
    tok = plan.tok
    for h in range(plan.hv):
        kh = plan.key_head(h)
        out_ref[h, :tok] = q_ref[:, kh * DK : (kh + 1) * DK]
        out_ref[h, tok : 2 * tok] = k_ref[:, kh * DK : (kh + 1) * DK]
        turned = jnp.transpose(v_ref[:, h * DV : (h + 1) * DV].astype(F32))
        out_ref[h, plan.v_at : plan.aux_at] = turned.astype(BF16)
        rows = [rate_ref[h : h + 1, :], decay_ref[h : h + 1, :]]
        out_ref[h, plan.aux_at :] = aux_rows(rows, tok)
    hand_out(plan, place_ref[0], out_ref, outs)


def hand_out(plan, place, all_ref, outs):
    for d, ref in enumerate(outs):
        ref[...] = all_ref[plan.ring.target(place, d)]


def unit(x):
    scale = lax.rsqrt(jnp.sum(x * x, axis=1, keepdims=True) + EPS)
    return x * scale, scale


def segments(off_ref, positions):
    total = jnp.zeros(positions.shape, jnp.int32)
    for j in range(off_ref.shape[0] - 1):
        total = total + (off_ref[j] <= positions).astype(jnp.int32)
    return total


def to_columns(rows, tok):
    row_ids = lax.broadcasted_iota(jnp.int32, (tok, tok), 0)
    stacked = jnp.zeros((tok, tok), F32)
    for i, r in enumerate(rows):
        stacked = jnp.where(row_ids == i, r, stacked)
    turned = jnp.transpose(stacked)
    return [turned[:, i : i + 1] for i in range(len(rows))]


def to_rows(columns, tok):
    column_ids = lax.broadcasted_iota(jnp.int32, (tok, tok), 1)
    stacked = jnp.zeros((tok, tok), F32)
    for i, c in enumerate(columns):
        stacked = jnp.where(column_ids == i, c, stacked)
    turned = jnp.transpose(stacked)
    return [turned[i : i + 1, :] for i in range(len(columns))]


def scalings(plan, off_ref, chunks, auxes):
    tok = plan.tok
    rows, columns = iotas(tok, tok)
    upto = (rows <= columns).astype(BF16)
    sums = [dot(a, upto, 1, 0) for a in auxes]
    rates = [jnp.sum(a[0:3].astype(F32), axis=0, keepdims=True) for a in auxes]
    cumuls = [s[3:4] + s[4:5] + s[5:6] for s in sums]
    turned = to_columns(rates + cumuls, tok)
    out = []
    for i, c in enumerate(chunks):
        b_col, c_col = turned[i], turned[len(chunks) + i]
        c_row = cumuls[i]
        start = c * tok
        seg_col = segments(off_ref, start + rows[:, :1])
        seg_row = segments(off_ref, start + columns[:1, :])
        before = jnp.int32(0)
        last = jnp.int32(0)
        for j in range(off_ref.shape[0] - 1):
            before = before + (off_ref[j] <= start - 1).astype(jnp.int32)
            last = last + (off_ref[j] <= start + tok - 1).astype(jnp.int32)
        c_last = c_row[:, tok - 1 : tok]
        together = (seg_col == seg_row) & (rows >= columns)
        ratio = jnp.where(together, jnp.exp(jnp.where(together, c_col - c_row, 0.0)), 0.0)
        start_col = jnp.where(seg_col == before, jnp.exp(c_col), 0.0)
        end_col = jnp.where(seg_col == last, jnp.exp(c_last - c_col), 0.0)
        whole = jnp.where(last == before, jnp.exp(c_last), 0.0)
        out.append((rates[i], b_col, ratio, start_col, end_col, whole))
    return out


def inverses(lowers):
    size = lowers[0].shape[0]
    rows, columns = iotas(size, size)
    identity = (rows == columns).astype(F32)
    block = min(16, size)
    near = (rows // block) == (columns // block)
    powers = [jnp.where(near, -m, 0.0) for m in lowers]
    results = [identity + p for p in powers]
    split = [halves(p) for p in powers]
    powers = [mm(s, s) for s in split]
    reach = 2
    while reach < block:
        split = [halves(p) for p in powers]
        more = reach * 2 < block
        both = []
        for r, s in zip(results, split):
            left = halves(r)
            if more:
                left = cat([left, s], 0)
            both.append(mm(left, s))
        results = [r + b[:size] for r, b in zip(results, both)]
        if more:
            powers = [b[size:] for b in both]
        reach *= 2
    while block < size:
        across = ((rows // (2 * block)) == (columns // (2 * block))) & (
            (rows // block) > (columns // block)
        )
        split = [halves(r) for r in results]
        middle = [mm(halves(jnp.where(across, m, 0.0)), s) for m, s in zip(lowers, split)]
        results = [r - mm(s, halves(m)) for r, s, m in zip(results, split, middle)]
        block *= 2
    return results


def chunks_of(plan, place, mate):
    return [mate + plan.mates * plan.ring.source(place, d) for d in range(plan.hv)]


def prepare_kernel(plan, off_ref, place_ref, mate_ref, *refs):
    in_refs, (link_ref, kept_ref) = refs[: plan.hv], refs[plan.hv :]
    tok = plan.tok
    rows, columns = iotas(tok, tok)
    key_rows, key_columns = iotas(DK, DK)
    identity = (key_rows == key_columns).astype(F32)
    mine = range(plan.hv)
    chunks = chunks_of(plan, place_ref[0], mate_ref[0])
    scales = scalings(plan, off_ref, chunks, [r[plan.aux_at :] for r in in_refs])
    qn = [unit(in_refs[m][:tok].astype(F32))[0] for m in mine]
    kn = [unit(in_refs[m][tok : 2 * tok].astype(F32))[0] for m in mine]
    kp = [halves(x) for x in kn]
    qp = [halves(x) for x in qn]
    dots = [mm(cat([q, k], 0), k, 1, 1) for q, k in zip(qp, kp)]
    strict = rows > columns
    lowers = [jnp.where(strict, s[1] * d[tok:] * s[2], 0.0) for s, d in zip(scales, dots)]
    scores = [d[:tok] * s[2] for s, d in zip(scales, dots)]
    inv = inverses(lowers)
    rated = [halves(x * s[0]) for x, s in zip(inv, scales)]
    w = [mm(x, halves(s[3] * k)) for x, s, k in zip(rated, scales, kn)]
    values = [in_refs[m][plan.v_at : plan.aux_at] for m in mine]
    u = [
        dot(jnp.concatenate([v, v], axis=1), jnp.concatenate(x, axis=1), 1, 1)
        for v, x in zip(values, rated)
    ]
    wp = [halves(x) for x in w]
    up = [halves(x) for x in u]
    ap = [halves(x) for x in scores]
    ke = [halves(s[4] * k) for s, k in zip(scales, kn)]
    for m in mine:
        link_ref[m, 0] = scales[m][5] * identity - mm(wp[m], ke[m], 0, 0)
        link_ref[m, 1] = mm(up[m], ke[m])
    for m in mine:
        kept_ref[m, INVERSE] = inv[m]
        kept_ref[m, SCORES] = scores[m]
        kept_ref[m, FROM_STATE] = w[m]
        kept_ref[m, READS] = scales[m][3] * qn[m] - mm(ap[m], wp[m])
        kept_ref[m, RATIO] = scales[m][2]
        kept_ref[m, WRITES] = u[m]
        kept_ref[m, LOCAL] = mm(up[m], ap[m], 1, 1)


def lay_out(plan, place, mate, refs, all_ref):
    for d, ref in enumerate(refs):
        for m in range(plan.hv):
            all_ref[lax.rem(mate + d, plan.mates), plan.ring.source(place, m)] = ref[m]


def scan_kernel(plan, place_ref, mate_ref, *refs):
    s, hv = plan.mates, plan.hv
    links, kept_ref, state_ref = refs[:s], refs[s], refs[s + 1]
    outs, (all_ref, states_ref) = refs[s + 2 : -2], refs[-2:]
    place, mate = place_ref[0], mate_ref[0]
    lay_out(plan, place, mate, links, all_ref)
    state = jnp.zeros((DV, DK), F32)
    for c in range(plan.n):
        states_ref[c] = state
        if c < plan.n - 1:
            link = all_ref.at[c % s, c // s]
            state = link[1] + mm(halves(state), halves(link[0]))
    cores = []
    for m, c in enumerate(chunks_of(plan, place, mate)):
        state = states_ref[c]
        state_ref[m] = state
        core = kept_ref[m, LOCAL] + mm(halves(state), halves(kept_ref[m, READS]), 1, 1)
        cores.append(core.astype(BF16))
    for d in range(hv):
        for k in range(hv):
            outs[d][k] = cores[plan.ring.seen(d, k)]


def state_cotangent_kernel(plan, kept_ref, *refs):
    for m in range(plan.hv):
        refs[-1][m] = mm(d_out(refs[m]), halves(kept_ref[m, READS]))


def d_out(ref):
    return ref[:DV], ref[DV:]


def backward_kernel(plan, off_ref, place_ref, mate_ref, *refs):
    s, n, tok, hv = plan.mates, plan.n, plan.tok, plan.hv
    links, backs, refs = refs[:s], refs[s : 2 * s], refs[2 * s :]
    in_refs, d_refs, kept_ref, state_ref = refs[:hv], refs[hv : 2 * hv], refs[2 * hv], refs[2 * hv + 1]
    outs, (links_ref, backs_ref, cots_ref) = refs[2 * hv + 2 : -3], refs[-3:]
    outs = [outs[plan.ring.seen(m, 0)] for m in range(hv)]
    place, mate = place_ref[0], mate_ref[0]
    lay_out(plan, place, mate, links, links_ref)
    lay_out(plan, place, mate, backs, backs_ref)
    d_state = jnp.zeros((DV, DK), F32)
    for c in reversed(range(n)):
        cots_ref[c] = d_state
        if c:
            d_state = backs_ref[c % s, c // s] + mm(
                halves(d_state), halves(links_ref[c % s, c // s, 0]), 1, 1
            )
    rows, columns = iotas(tok, tok)
    strict = rows > columns
    upto = (rows >= columns).astype(BF16)
    mine = range(hv)
    chunks = chunks_of(plan, place, mate)
    scales = scalings(plan, off_ref, chunks, [r[plan.aux_at :] for r in in_refs])
    qu = [unit(in_refs[m][:tok].astype(F32)) for m in mine]
    ku = [unit(in_refs[m][tok : 2 * tok].astype(F32)) for m in mine]
    qp = [halves(x[0]) for x in qu]
    kp = [halves(x[0]) for x in ku]
    do = [d_out(r) for r in d_refs]
    s0 = [state_ref[m] for m in mine]
    ds = [cots_ref[c] for c in chunks]
    s0p = [halves(x) for x in s0]
    dsp = [halves(x) for x in ds]
    pseudo = [kept_ref[m, WRITES] - mm(s0p[m], halves(kept_ref[m, FROM_STATE]), 1, 1) for m in mine]
    pp = [halves(x) for x in pseudo]
    ke = [halves(s[4] * k[0]) for s, k in zip(scales, ku)]
    dp = [mm(do[m], halves(kept_ref[m, SCORES])) + mm(dsp[m], ke[m], 1, 1) for m in mine]
    dr = [mm(halves(dp[m]), halves(kept_ref[m, INVERSE])) for m in mine]
    drp = [halves(x) for x in dr]
    big = [mm(cat([o, r], 1), cat([p, s], 1), 0, 0) for o, r, p, s in zip(do, drp, pp, s0p)]
    pds = [mm(p, d, 0, 0) for p, d in zip(pp, dsp)]
    da = [big[m][:tok, :tok] * kept_ref[m, RATIO] for m in mine]
    dm = [jnp.where(strict, -big[m][tok:, :tok] * kept_ref[m, RATIO], 0.0) for m in mine]
    dap = [halves(x) for x in da]
    dmp = [halves(x) for x in dm]
    dbm = [halves(s[1] * x) for s, x in zip(scales, dm)]
    by_row = [mm(cat([x, y], 0), k) for x, y, k in zip(dap, dmp, kp)]
    by_column = [
        mm(cat([x, y], 0), cat([q, k], 0), 0, 0) for x, y, q, k in zip(dap, dbm, qp, kp)
    ]
    sums = []
    for m in mine:
        _, b_col, _, start_col, end_col, whole = scales[m]
        (qn, q_scale), (kn, k_scale) = qu[m], ku[m]
        out = outs[m]
        dqn = by_row[m][:tok] + start_col * big[m][:tok, tok:]
        erase = by_row[m][tok:] - start_col * big[m][tok:, tok:]
        ends = end_col * pds[m]
        write = by_column[m] + ends
        dkn = b_col * erase + write
        s_q = jnp.sum(qn * dqn, axis=1, keepdims=True)
        s_e = jnp.sum(kn * erase, axis=1, keepdims=True)
        s_w = jnp.sum(kn * write, axis=1, keepdims=True)
        total = jnp.sum(jnp.sum(kn * ends, axis=1, keepdims=True), axis=0, keepdims=True)
        both = jnp.sum(jnp.sum(s0[m] * ds[m], axis=1, keepdims=True), axis=0, keepdims=True)
        out[:tok] = (q_scale * (dqn - qn * s_q)).astype(BF16)
        out[tok : 2 * tok] = (k_scale * (dkn - kn * (b_col * s_e + s_w))).astype(BF16)
        out[plan.v_at : plan.aux_at] = (scales[m][0] * dr[m]).astype(BF16)
        sums.append((s_e, s_q + b_col * s_e - s_w, total + whole * both))
    turned = to_rows([s[0] for s in sums] + [s[1] for s in sums], tok)
    for m in mine:
        values = in_refs[m][plan.v_at : plan.aux_at].astype(F32)
        d_rate = turned[m] + jnp.sum(dr[m] * values, axis=0, keepdims=True)
        parts = dot(aux_rows([turned[plan.hv + m]], tok), upto, 1, 0)
        d_decay = parts[0:1] + parts[1:2] + parts[2:3] + sums[m][2]
        outs[m][plan.aux_at :] = aux_rows([d_rate, d_decay], tok)


def gather_rows(head, pieces, all_ref):
    rows, ring = pieces[0].shape[0], Ring(len(pieces))
    for d, piece in zip(ring.far_first(), pieces):
        at = ring.source(head, d) * rows
        all_ref[pl.ds(pl.multiple_of(at, rows), rows), :] = piece[...]


def cotangent_kernel(plan, parts, head_ref, place_ref, *refs):
    pieces, w_ref, outs, (all_ref, core_ref) = refs[:parts], refs[parts], refs[parts + 1 : -2], refs[-2:]
    gather_rows(head_ref[0], pieces, all_ref)
    high, low = halves(dot(w_ref[...], all_ref[...], 1, 1))
    for m in range(plan.hv):
        core_ref[m, :DV] = high[m * DV : (m + 1) * DV]
        core_ref[m, DV:] = low[m * DV : (m + 1) * DV]
    hand_out(plan, place_ref[0], core_ref, outs)


def turn_kernel(plan, parts, head_ref, place_ref, *refs):
    pieces, outs, (all_ref, turned_ref) = refs[:parts], refs[parts:-2], refs[-2:]
    gather_rows(head_ref[0], pieces, all_ref)
    share = turned_ref.shape[1]
    for m in range(plan.hv):
        part = all_ref[:, m * share : (m + 1) * share].astype(F32)
        turned_ref[m] = jnp.transpose(part).astype(BF16)
    hand_out(plan, place_ref[0], turned_ref, outs)


def project_kernel(plan, parts, head_ref, place_ref, *refs):
    mixed_refs, w_ref, outs, (all_ref, total_ref) = (
        refs[: plan.hv],
        refs[plan.hv],
        refs[plan.hv + 1 : -2],
        refs[-2:],
    )
    for d, ref in enumerate(mixed_refs):
        all_ref[plan.ring.source(place_ref[0], d)] = ref[0]
    mixed = all_ref[...].reshape(plan.hv * DV, plan.tok)
    total_ref[...] = dot(mixed, w_ref[...], 0, 0)
    rows, ring = outs[0].shape[0], Ring(parts)
    for d in range(parts):
        at = ring.target(head_ref[0], d) * rows
        block = total_ref[pl.ds(pl.multiple_of(at, rows), rows), :]
        outs[d][...] = block.astype(outs[d].dtype)


def weight_kernel(plan, place_ref, mate_ref, *refs):
    hv = plan.hv
    turned, mixed_refs, outs, all_ref = refs[:hv], refs[hv : 2 * hv], refs[2 * hv : -1], refs[-1]
    for d, ref in enumerate(mixed_refs):
        head = plan.ring.source(place_ref[0], d)
        for k in range(hv):
            all_ref[k, head] = ref[k]
    share = outs[0].shape[0]
    for d, out_ref in enumerate(outs):
        at = lax.rem(mate_ref[0] + plan.mates - d, plan.mates) * share
        at = pl.multiple_of(at, share)
        total = None
        for k in range(hv):
            mixed = all_ref[k].reshape(hv * DV, plan.tok)
            part = dot(turned[k][pl.ds(at, share), :], mixed, 1, 1)
            total = part if total is None else total + part
        out_ref[...] = total


def finish_kernel(plan, place_ref, *refs):
    pieces, (q_ref, k_ref, v_ref, rate_ref, decay_ref, in_ref) = refs[: plan.hv], refs[plan.hv :]
    tok = plan.tok
    for d, ref in enumerate(pieces):
        in_ref[plan.ring.source(place_ref[0], d)] = ref[...]
    for kh in range(plan.hk):
        mine = [h for h in range(plan.hv) if plan.key_head(h) == kh]
        for ref, at in ((q_ref, 0), (k_ref, tok)):
            total = in_ref[mine[0], at : at + tok].astype(F32)
            for h in mine[1:]:
                total = total + in_ref[h, at : at + tok].astype(F32)
            ref[:, kh * DK : (kh + 1) * DK] = total
    for h in range(plan.hv):
        v_ref[:, h * DV : (h + 1) * DV] = jnp.transpose(
            in_ref[h, plan.v_at : plan.aux_at].astype(F32)
        )
        aux = in_ref[h, plan.aux_at :].astype(F32)
        rate_ref[h : h + 1, :] = aux[0:1] + aux[1:2] + aux[2:3]
        decay_ref[h : h + 1, :] = aux[3:4] + aux[4:5] + aux[5:6]


def after(x, y):
    return lax.optimization_barrier((x, y))[0]


def per_device(
    queries, key_vectors, value_rows, write_rate, log_decay, doc_offsets, out_weight, grad_out
):
    n, parts = lax.axis_size("ctx"), lax.axis_size("head")
    tok, hv = queries.shape[0], write_rate.shape[0]
    hk, model = queries.shape[1] // DK, grad_out.shape[1]
    plan = Plan(n, tok, hv, hk)
    s = plan.mates
    index = lax.axis_index("ctx").astype(jnp.int32)
    place, mate = (index // s).reshape(1), (index % s).reshape(1)
    head = lax.axis_index("head").astype(jnp.int32).reshape(1)

    def across_heads(pieces):
        moved = [lax.ppermute(pieces[d], "head", Ring(parts).pairs(d)) for d in range(1, parts)]
        return [pieces[0]] + moved

    vmem = lambda dtype, *shape: pltpu.VMEM(shape, dtype)

    packed = call(
        partial(pack_kernel, plan),
        [arr(BF16, plan.rows, DK)] * hv,
        smem=(0,),
        scratch=[vmem(BF16, hv, plan.rows, DK)],
        fetch=range(1, 6),
    )(place, queries, key_vectors, value_rows, write_rate, log_decay)
    got = plan.exchange(packed)
    rows = across_heads([grad_out] * parts)
    rows = [rows[d] for d in Ring(parts).far_first()]

    link, kept = call(
        partial(prepare_kernel, plan),
        (arr(F32, hv, 2, DK, DK), arr(F32, hv, KEPT, tok, DK)),
        smem=(0, 1, 2),
        fetch=(0,),
        flops=20_000_000_000,
    )(doc_offsets, place, mate, *got)
    links = [link] + [plan.from_mate(link, d) for d in range(1, s)]

    d_core = call(
        partial(cotangent_kernel, plan, parts),
        [arr(BF16, 2 * DV, tok)] * hv,
        smem=(0, 1),
        scratch=[vmem(BF16, tok, model), vmem(BF16, hv, 2 * DV, tok)],
        flops=30_000_000_000,
    )(head, place, *rows, after(out_weight, link))
    kept = after(kept, d_core[0])
    d_core = plan.exchange(d_core)

    states, *mixed = call(
        partial(scan_kernel, plan),
        [arr(F32, hv, DV, DK)] + [arr(BF16, hv, DV, tok)] * hv,
        smem=(0, 1),
        scratch=[vmem(F32, s, hv, 2, DK, DK), vmem(F32, n, DV, DK)],
        flops=2_500_000_000,
    )(place, mate, *links, kept)
    turned = call(
        partial(turn_kernel, plan, parts),
        [arr(BF16, model // hv, tok)] * hv,
        smem=(0, 1),
        scratch=[vmem(BF16, tok, model), vmem(BF16, hv, model // hv, tok)],
        flops=1_000_000_000,
    )(head, place, *after(rows, states))
    mixed = plan.exchange(mixed)
    turned = plan.exchange(turned)
    back = call(
        partial(state_cotangent_kernel, plan), arr(F32, hv, DV, DK), flops=30_000_000_000
    )(kept, *after(d_core, states))
    backs = [back] + [plan.from_mate(back, d) for d in range(1, s)]

    projected = call(
        partial(project_kernel, plan, parts),
        [arr(BF16 if d else F32, tok // parts, model) for d in range(parts)],
        smem=(0, 1),
        scratch=[vmem(BF16, hv, DV, tok), vmem(F32, tok, model)],
        flops=1_000_000_000,
    )(head, place, *mixed, out_weight)
    layer_parts = across_heads(projected)

    grads = call(
        partial(backward_kernel, plan),
        [arr(BF16, plan.rows, DK)] * hv,
        smem=(0, 1, 2),
        fetch=(0,),
        scratch=[
            vmem(F32, s, hv, 2, DK, DK),
            vmem(F32, s, hv, DV, DK),
            vmem(F32, n, DV, DK),
        ],
        flops=6_000_000_000,
    )(doc_offsets, place, mate, *links, *backs, *got, *d_core, kept, after(states, projected[1]))

    shares = call(
        partial(weight_kernel, plan),
        [arr(F32, model // n, hv * DV)] * s,
        smem=(0, 1),
        scratch=[vmem(BF16, hv, hv, DV, tok)],
        flops=1_000_000_000,
    )(place, mate, *turned, *mixed)
    grads = plan.exchange(after(grads, shares[0]))
    weight_grad = shares[0]
    for d in range(1, s):
        weight_grad = weight_grad + plan.from_mate(shares[d], d)

    layer_out = layer_parts[0]
    for part in layer_parts[:0:-1]:
        layer_out = layer_out + part.astype(F32)
    grads = after(grads, (layer_out, weight_grad))
    grad_q, grad_k, grad_v, grad_rate, grad_decay = call(
        partial(finish_kernel, plan),
        (
            arr(F32, tok, hk * DK),
            arr(F32, tok, hk * DK),
            arr(F32, tok, hv * DV),
            arr(F32, hv, tok),
            arr(F32, hv, tok),
        ),
        smem=(0,),
        scratch=[vmem(BF16, hv, plan.rows, DK)],
        flops=1_000_000_000,
        inside=False,
    )(place, *grads)
    return (layer_out, grad_q, grad_k, grad_v, grad_rate, grad_decay, weight_grad)


def solution(mesh):
    placed = (
        P("ctx", "head"),
        P("ctx", "head"),
        P("ctx", "head"),
        P("head", "ctx"),
        P("head", "ctx"),
        P(),
        P("head", None),
        P(("ctx", "head"), None),
    )
    return jax.shard_map(
        per_device,
        mesh=mesh,
        in_specs=placed,
        out_specs=(
            P(("ctx", "head"), None),
            P("ctx", "head"),
            P("ctx", "head"),
            P("ctx", "head"),
            P("head", "ctx"),
            P("head", "ctx"),
            P("ctx", "head"),
        ),
        check_vma=False,
    )
```

```python
import math
from functools import partial

import jax
import jax.numpy as jnp
from jax import lax
from jax.experimental import pallas as pl
from jax.experimental.pallas import tpu as pltpu
from jax.sharding import PartitionSpec as P

DK = 128
DV = 128
AUX = 16
INVERSE, SCORES, FROM_STATE, READS, RATIO, WRITES, LOCAL, KEPT = range(8)
EPS = 1e-06
F32 = jnp.float32
BF16 = jnp.bfloat16
SPARE_VMEM = 8 * 1024 * 1024


def dot(a, b, ca, cb):
    return lax.dot_general(a, b, (((ca,), (cb,)), ((), ())), preferred_element_type=F32)


def halves(x):
    high = x.astype(BF16)
    return high, (x - high.astype(F32)).astype(BF16)


def thirds(x):
    high = x.astype(BF16).astype(F32)
    middle = (x - high).astype(BF16).astype(F32)
    return high, middle, x - high - middle


def mm(a, b, ca=1, cb=0):
    left = jnp.concatenate([a[0], a[0], a[1]], axis=ca)
    right = jnp.concatenate([b[0], b[1], b[0]], axis=cb)
    return dot(left, right, ca, cb)


def cat(pairs, axis):
    return tuple(jnp.concatenate(parts, axis=axis) for parts in zip(*pairs))


def iotas(rows, columns):
    shape = (rows, columns)
    return lax.broadcasted_iota(jnp.int32, shape, 0), lax.broadcasted_iota(jnp.int32, shape, 1)


def call(kernel, outs, smem=(), scratch=(), flops=0, inside=True, fetch=()):
    if inside:
        outs = jax.tree.map(lambda o: pltpu.VMEM(o.shape, o.dtype), outs)
    scoped = SPARE_VMEM + sum(x.dtype.itemsize * math.prod(x.shape) for x in scratch)

    def run(*args):
        spec = lambda i: pl.BlockSpec(memory_space=pltpu.SMEM if i in smem else pltpu.VMEM)
        space = lambda i: pltpu.HBM if i in fetch else pltpu.VMEM
        hold = pltpu.with_memory_space_constraint
        return pl.pallas_call(
            kernel,
            out_shape=outs,
            in_specs=[spec(i) for i in range(len(args))],
            out_specs=jax.tree.map(lambda _: pl.BlockSpec(memory_space=pltpu.VMEM), outs),
            scratch_shapes=list(scratch),
            compiler_params=pltpu.CompilerParams(vmem_limit_bytes=scoped),
            cost_estimate=pl.CostEstimate(flops=flops, bytes_accessed=0, transcendentals=0),
        )(*(hold(x, space(i)) if i in fetch or i not in smem else x for i, x in enumerate(args)))

    return run


def arr(dtype, *shape):
    return jax.ShapeDtypeStruct(shape, dtype)


class Ring:
    def __init__(self, size):
        self.size = size
        self.paired = size & (size - 1) == 0

    def source(self, i, d):
        return i ^ d if self.paired else (i + d) % self.size

    def target(self, i, d):
        return i ^ d if self.paired else (i + self.size - d) % self.size

    def seen(self, d, k):
        return d ^ k if self.paired else (k - d) % self.size

    def far_first(self):
        return sorted(range(self.size), key=lambda d: (d != self.size // 2, -d))

    def pairs(self, d):
        return [(self.source(i, d), i) for i in range(self.size)]


class Plan:
    def __init__(self, n, tok, hv, hk):
        self.n, self.tok, self.hv, self.hk = n, tok, hv, hk
        self.mates = n // hv
        self.v_at = 2 * tok
        self.aux_at = 2 * tok + DV
        self.rows = self.aux_at + AUX
        self.ring = Ring(hv)

    def key_head(self, head):
        return head * self.hk // self.hv

    def exchange(self, pieces):
        s = self.mates
        moved = [pieces[0]]
        for d in range(1, self.hv):
            pairs = [(i * s + b, j * s + b) for i, j in self.ring.pairs(d) for b in range(s)]
            moved.append(lax.ppermute(pieces[d], "ctx", pairs))
        return moved

    def from_mate(self, x, d):
        s = self.mates
        pairs = [(i // s * s + (i + d) % s, i) for i in range(self.n)]
        return lax.ppermute(x, "ctx", pairs)


def aux_rows(rows, columns):
    row_ids = lax.broadcasted_iota(jnp.int32, (AUX, columns), 0)
    out = jnp.zeros((AUX, columns), F32)
    for i, part in enumerate(p for r in rows for p in thirds(r)):
        out = jnp.where(row_ids == i, part, out)
    return out.astype(BF16)


def pack_kernel(plan, place_ref, q_ref, k_ref, v_ref, rate_ref, decay_ref, *refs):
    outs, out_ref = refs[:-1], refs[-1]
    tok = plan.tok
    for h in range(plan.hv):
        kh = plan.key_head(h)
        out_ref[h, :tok] = q_ref[:, kh * DK : (kh + 1) * DK]
        out_ref[h, tok : 2 * tok] = k_ref[:, kh * DK : (kh + 1) * DK]
        turned = jnp.transpose(v_ref[:, h * DV : (h + 1) * DV].astype(F32))
        out_ref[h, plan.v_at : plan.aux_at] = turned.astype(BF16)
        rows = [rate_ref[h : h + 1, :], decay_ref[h : h + 1, :]]
        out_ref[h, plan.aux_at :] = aux_rows(rows, tok)
    hand_out(plan, place_ref[0], out_ref, outs)


def hand_out(plan, place, all_ref, outs):
    for d, ref in enumerate(outs):
        ref[...] = all_ref[plan.ring.target(place, d)]


def unit(x):
    scale = lax.rsqrt(jnp.sum(x * x, axis=1, keepdims=True) + EPS)
    return x * scale, scale


def segments(off_ref, positions):
    total = jnp.zeros(positions.shape, jnp.int32)
    for j in range(off_ref.shape[0] - 1):
        total = total + (off_ref[j] <= positions).astype(jnp.int32)
    return total


def to_columns(rows, tok):
    row_ids = lax.broadcasted_iota(jnp.int32, (tok, tok), 0)
    stacked = jnp.zeros((tok, tok), F32)
    for i, r in enumerate(rows):
        stacked = jnp.where(row_ids == i, r, stacked)
    turned = jnp.transpose(stacked)
    return [turned[:, i : i + 1] for i in range(len(rows))]


def to_rows(columns, tok):
    column_ids = lax.broadcasted_iota(jnp.int32, (tok, tok), 1)
    stacked = jnp.zeros((tok, tok), F32)
    for i, c in enumerate(columns):
        stacked = jnp.where(column_ids == i, c, stacked)
    turned = jnp.transpose(stacked)
    return [turned[i : i + 1, :] for i in range(len(columns))]


def scalings(plan, off_ref, chunks, auxes):
    tok = plan.tok
    rows, columns = iotas(tok, tok)
    upto = (rows <= columns).astype(BF16)
    sums = [dot(a, upto, 1, 0) for a in auxes]
    rates = [jnp.sum(a[0:3].astype(F32), axis=0, keepdims=True) for a in auxes]
    cumuls = [s[3:4] + s[4:5] + s[5:6] for s in sums]
    turned = to_columns(rates + cumuls, tok)
    out = []
    for i, c in enumerate(chunks):
        b_col, c_col = turned[i], turned[len(chunks) + i]
        c_row = cumuls[i]
        start = c * tok
        seg_col = segments(off_ref, start + rows[:, :1])
        seg_row = segments(off_ref, start + columns[:1, :])
        before = jnp.int32(0)
        last = jnp.int32(0)
        for j in range(off_ref.shape[0] - 1):
            before = before + (off_ref[j] <= start - 1).astype(jnp.int32)
            last = last + (off_ref[j] <= start + tok - 1).astype(jnp.int32)
        c_last = c_row[:, tok - 1 : tok]
        together = (seg_col == seg_row) & (rows >= columns)
        ratio = jnp.where(together, jnp.exp(jnp.where(together, c_col - c_row, 0.0)), 0.0)
        start_col = jnp.where(seg_col == before, jnp.exp(c_col), 0.0)
        end_col = jnp.where(seg_col == last, jnp.exp(c_last - c_col), 0.0)
        whole = jnp.where(last == before, jnp.exp(c_last), 0.0)
        out.append((rates[i], b_col, ratio, start_col, end_col, whole))
    return out


def inverses(lowers):
    size = lowers[0].shape[0]
    rows, columns = iotas(size, size)
    identity = (rows == columns).astype(F32)
    block = min(16, size)
    near = (rows // block) == (columns // block)
    powers = [jnp.where(near, -m, 0.0) for m in lowers]
    results = [identity + p for p in powers]
    split = [halves(p) for p in powers]
    powers = [mm(s, s) for s in split]
    reach = 2
    while reach < block:
        split = [halves(p) for p in powers]
        more = reach * 2 < block
        both = []
        for r, s in zip(results, split):
            left = halves(r)
            if more:
                left = cat([left, s], 0)
            both.append(mm(left, s))
        results = [r + b[:size] for r, b in zip(results, both)]
        if more:
            powers = [b[size:] for b in both]
        reach *= 2
    while block < size:
        across = ((rows // (2 * block)) == (columns // (2 * block))) & (
            (rows // block) > (columns // block)
        )
        split = [halves(r) for r in results]
        middle = [mm(halves(jnp.where(across, m, 0.0)), s) for m, s in zip(lowers, split)]
        results = [r - mm(s, halves(m)) for r, s, m in zip(results, split, middle)]
        block *= 2
    return results


def chunks_of(plan, place, mate):
    return [mate + plan.mates * plan.ring.source(place, d) for d in range(plan.hv)]


def prepare_kernel(plan, off_ref, place_ref, mate_ref, *refs):
    in_refs, (link_ref, kept_ref) = refs[: plan.hv], refs[plan.hv :]
    tok = plan.tok
    rows, columns = iotas(tok, tok)
    key_rows, key_columns = iotas(DK, DK)
    identity = (key_rows == key_columns).astype(F32)
    mine = range(plan.hv)
    chunks = chunks_of(plan, place_ref[0], mate_ref[0])
    scales = scalings(plan, off_ref, chunks, [r[plan.aux_at :] for r in in_refs])
    qn = [unit(in_refs[m][:tok].astype(F32))[0] for m in mine]
    kn = [unit(in_refs[m][tok : 2 * tok].astype(F32))[0] for m in mine]
    kp = [halves(x) for x in kn]
    qp = [halves(x) for x in qn]
    dots = [mm(cat([q, k], 0), k, 1, 1) for q, k in zip(qp, kp)]
    strict = rows > columns
    lowers = [jnp.where(strict, s[1] * d[tok:] * s[2], 0.0) for s, d in zip(scales, dots)]
    scores = [d[:tok] * s[2] for s, d in zip(scales, dots)]
    inv = inverses(lowers)
    rated = [halves(x * s[0]) for x, s in zip(inv, scales)]
    w = [mm(x, halves(s[3] * k)) for x, s, k in zip(rated, scales, kn)]
    values = [in_refs[m][plan.v_at : plan.aux_at] for m in mine]
    u = [
        dot(jnp.concatenate([v, v], axis=1), jnp.concatenate(x, axis=1), 1, 1)
        for v, x in zip(values, rated)
    ]
    wp = [halves(x) for x in w]
    up = [halves(x) for x in u]
    ap = [halves(x) for x in scores]
    ke = [halves(s[4] * k) for s, k in zip(scales, kn)]
    for m in mine:
        link_ref[m, 0] = scales[m][5] * identity - mm(wp[m], ke[m], 0, 0)
        link_ref[m, 1] = mm(up[m], ke[m])
    for m in mine:
        kept_ref[m, INVERSE] = inv[m]
        kept_ref[m, SCORES] = scores[m]
        kept_ref[m, FROM_STATE] = w[m]
        kept_ref[m, READS] = scales[m][3] * qn[m] - mm(ap[m], wp[m])
        kept_ref[m, RATIO] = scales[m][2]
        kept_ref[m, WRITES] = u[m]
        kept_ref[m, LOCAL] = mm(up[m], ap[m], 1, 1)


def lay_out(plan, place, mate, refs, all_ref):
    for d, ref in enumerate(refs):
        for m in range(plan.hv):
            all_ref[lax.rem(mate + d, plan.mates), plan.ring.source(place, m)] = ref[m]


def scan_kernel(plan, place_ref, mate_ref, *refs):
    s, hv = plan.mates, plan.hv
    links, kept_ref, state_ref = refs[:s], refs[s], refs[s + 1]
    outs, (all_ref, states_ref) = refs[s + 2 : -2], refs[-2:]
    place, mate = place_ref[0], mate_ref[0]
    lay_out(plan, place, mate, links, all_ref)
    state = jnp.zeros((DV, DK), F32)
    for c in range(plan.n):
        states_ref[c] = state
        if c < plan.n - 1:
            link = all_ref.at[c % s, c // s]
            state = link[1] + mm(halves(state), halves(link[0]))
    cores = []
    for m, c in enumerate(chunks_of(plan, place, mate)):
        state = states_ref[c]
        state_ref[m] = state
        core = kept_ref[m, LOCAL] + mm(halves(state), halves(kept_ref[m, READS]), 1, 1)
        cores.append(core.astype(BF16))
    for d in range(hv):
        for k in range(hv):
            outs[d][k] = cores[plan.ring.seen(d, k)]


def state_cotangent_kernel(plan, kept_ref, *refs):
    for m in range(plan.hv):
        refs[-1][m] = mm(d_out(refs[m]), halves(kept_ref[m, READS]))


def d_out(ref):
    return ref[:DV], ref[DV:]


def backward_kernel(plan, off_ref, place_ref, mate_ref, *refs):
    s, n, tok, hv = plan.mates, plan.n, plan.tok, plan.hv
    links, backs, refs = refs[:s], refs[s : 2 * s], refs[2 * s :]
    in_refs, d_refs, kept_ref, state_ref = refs[:hv], refs[hv : 2 * hv], refs[2 * hv], refs[2 * hv + 1]
    outs, (links_ref, backs_ref, cots_ref) = refs[2 * hv + 2 : -3], refs[-3:]
    outs = [outs[plan.ring.seen(m, 0)] for m in range(hv)]
    place, mate = place_ref[0], mate_ref[0]
    lay_out(plan, place, mate, links, links_ref)
    lay_out(plan, place, mate, backs, backs_ref)
    d_state = jnp.zeros((DV, DK), F32)
    for c in reversed(range(n)):
        cots_ref[c] = d_state
        if c:
            d_state = backs_ref[c % s, c // s] + mm(
                halves(d_state), halves(links_ref[c % s, c // s, 0]), 1, 1
            )
    rows, columns = iotas(tok, tok)
    strict = rows > columns
    upto = (rows >= columns).astype(BF16)
    mine = range(hv)
    chunks = chunks_of(plan, place, mate)
    scales = scalings(plan, off_ref, chunks, [r[plan.aux_at :] for r in in_refs])
    qu = [unit(in_refs[m][:tok].astype(F32)) for m in mine]
    ku = [unit(in_refs[m][tok : 2 * tok].astype(F32)) for m in mine]
    qp = [halves(x[0]) for x in qu]
    kp = [halves(x[0]) for x in ku]
    do = [d_out(r) for r in d_refs]
    s0 = [state_ref[m] for m in mine]
    ds = [cots_ref[c] for c in chunks]
    s0p = [halves(x) for x in s0]
    dsp = [halves(x) for x in ds]
    pseudo = [kept_ref[m, WRITES] - mm(s0p[m], halves(kept_ref[m, FROM_STATE]), 1, 1) for m in mine]
    pp = [halves(x) for x in pseudo]
    ke = [halves(s[4] * k[0]) for s, k in zip(scales, ku)]
    dp = [mm(do[m], halves(kept_ref[m, SCORES])) + mm(dsp[m], ke[m], 1, 1) for m in mine]
    dr = [mm(halves(dp[m]), halves(kept_ref[m, INVERSE])) for m in mine]
    drp = [halves(x) for x in dr]
    big = [mm(cat([o, r], 1), cat([p, s], 1), 0, 0) for o, r, p, s in zip(do, drp, pp, s0p)]
    pds = [mm(p, d, 0, 0) for p, d in zip(pp, dsp)]
    da = [big[m][:tok, :tok] * kept_ref[m, RATIO] for m in mine]
    dm = [jnp.where(strict, -big[m][tok:, :tok] * kept_ref[m, RATIO], 0.0) for m in mine]
    dap = [halves(x) for x in da]
    dmp = [halves(x) for x in dm]
    dbm = [halves(s[1] * x) for s, x in zip(scales, dm)]
    by_row = [mm(cat([x, y], 0), k) for x, y, k in zip(dap, dmp, kp)]
    by_column = [
        mm(cat([x, y], 0), cat([q, k], 0), 0, 0) for x, y, q, k in zip(dap, dbm, qp, kp)
    ]
    sums = []
    for m in mine:
        _, b_col, _, start_col, end_col, whole = scales[m]
        (qn, q_scale), (kn, k_scale) = qu[m], ku[m]
        out = outs[m]
        dqn = by_row[m][:tok] + start_col * big[m][:tok, tok:]
        erase = by_row[m][tok:] - start_col * big[m][tok:, tok:]
        ends = end_col * pds[m]
        write = by_column[m] + ends
        dkn = b_col * erase + write
        s_q = jnp.sum(qn * dqn, axis=1, keepdims=True)
        s_e = jnp.sum(kn * erase, axis=1, keepdims=True)
        s_w = jnp.sum(kn * write, axis=1, keepdims=True)
        total = jnp.sum(jnp.sum(kn * ends, axis=1, keepdims=True), axis=0, keepdims=True)
        both = jnp.sum(jnp.sum(s0[m] * ds[m], axis=1, keepdims=True), axis=0, keepdims=True)
        out[:tok] = (q_scale * (dqn - qn * s_q)).astype(BF16)
        out[tok : 2 * tok] = (k_scale * (dkn - kn * (b_col * s_e + s_w))).astype(BF16)
        out[plan.v_at : plan.aux_at] = (scales[m][0] * dr[m]).astype(BF16)
        sums.append((s_e, s_q + b_col * s_e - s_w, total + whole * both))
    turned = to_rows([s[0] for s in sums] + [s[1] for s in sums], tok)
    for m in mine:
        values = in_refs[m][plan.v_at : plan.aux_at].astype(F32)
        d_rate = turned[m] + jnp.sum(dr[m] * values, axis=0, keepdims=True)
        parts = dot(aux_rows([turned[plan.hv + m]], tok), upto, 1, 0)
        d_decay = parts[0:1] + parts[1:2] + parts[2:3] + sums[m][2]
        outs[m][plan.aux_at :] = aux_rows([d_rate, d_decay], tok)


def gather_rows(head, pieces, all_ref):
    rows, ring = pieces[0].shape[0], Ring(len(pieces))
    for d, piece in zip(ring.far_first(), pieces):
        at = ring.source(head, d) * rows
        all_ref[pl.ds(pl.multiple_of(at, rows), rows), :] = piece[...]


def cotangent_kernel(plan, parts, head_ref, place_ref, *refs):
    pieces, w_ref, outs, (all_ref, core_ref) = refs[:parts], refs[parts], refs[parts + 1 : -2], refs[-2:]
    gather_rows(head_ref[0], pieces, all_ref)
    high, low = halves(dot(w_ref[...], all_ref[...], 1, 1))
    for m in range(plan.hv):
        core_ref[m, :DV] = high[m * DV : (m + 1) * DV]
        core_ref[m, DV:] = low[m * DV : (m + 1) * DV]
    hand_out(plan, place_ref[0], core_ref, outs)


def turn_kernel(plan, parts, head_ref, place_ref, *refs):
    pieces, outs, (all_ref, turned_ref) = refs[:parts], refs[parts:-2], refs[-2:]
    gather_rows(head_ref[0], pieces, all_ref)
    share = turned_ref.shape[1]
    for m in range(plan.hv):
        part = all_ref[:, m * share : (m + 1) * share].astype(F32)
        turned_ref[m] = jnp.transpose(part).astype(BF16)
    hand_out(plan, place_ref[0], turned_ref, outs)


def project_kernel(plan, parts, head_ref, place_ref, *refs):
    mixed_refs, w_ref, outs, (all_ref, total_ref) = (
        refs[: plan.hv],
        refs[plan.hv],
        refs[plan.hv + 1 : -2],
        refs[-2:],
    )
    for d, ref in enumerate(mixed_refs):
        all_ref[plan.ring.source(place_ref[0], d)] = ref[0]
    mixed = all_ref[...].reshape(plan.hv * DV, plan.tok)
    total_ref[...] = dot(mixed, w_ref[...], 0, 0)
    rows, ring = outs[0].shape[0], Ring(parts)
    for d in range(parts):
        at = ring.target(head_ref[0], d) * rows
        block = total_ref[pl.ds(pl.multiple_of(at, rows), rows), :]
        outs[d][...] = block.astype(outs[d].dtype)


def weight_kernel(plan, place_ref, mate_ref, *refs):
    hv = plan.hv
    turned, mixed_refs, outs, all_ref = refs[:hv], refs[hv : 2 * hv], refs[2 * hv : -1], refs[-1]
    for d, ref in enumerate(mixed_refs):
        head = plan.ring.source(place_ref[0], d)
        for k in range(hv):
            all_ref[k, head] = ref[k]
    share = outs[0].shape[0]
    for d, out_ref in enumerate(outs):
        at = lax.rem(mate_ref[0] + plan.mates - d, plan.mates) * share
        at = pl.multiple_of(at, share)
        total = None
        for k in range(hv):
            mixed = all_ref[k].reshape(hv * DV, plan.tok)
            part = dot(turned[k][pl.ds(at, share), :], mixed, 1, 1)
            total = part if total is None else total + part
        out_ref[...] = total


def finish_kernel(plan, place_ref, *refs):
    pieces, (q_ref, k_ref, v_ref, rate_ref, decay_ref, in_ref) = refs[: plan.hv], refs[plan.hv :]
    tok = plan.tok
    for d, ref in enumerate(reversed(pieces)):
        in_ref[plan.ring.source(place_ref[0], d)] = ref[...]
    for kh in range(plan.hk):
        mine = [h for h in range(plan.hv) if plan.key_head(h) == kh]
        for ref, at in ((q_ref, 0), (k_ref, tok)):
            total = in_ref[mine[0], at : at + tok].astype(F32)
            for h in mine[1:]:
                total = total + in_ref[h, at : at + tok].astype(F32)
            ref[:, kh * DK : (kh + 1) * DK] = total
    for h in range(plan.hv):
        v_ref[:, h * DV : (h + 1) * DV] = jnp.transpose(
            in_ref[h, plan.v_at : plan.aux_at].astype(F32)
        )
        aux = in_ref[h, plan.aux_at :].astype(F32)
        rate_ref[h : h + 1, :] = aux[0:1] + aux[1:2] + aux[2:3]
        decay_ref[h : h + 1, :] = aux[3:4] + aux[4:5] + aux[5:6]


def after(x, y):
    return lax.optimization_barrier((x, y))[0]


def per_device(
    queries, key_vectors, value_rows, write_rate, log_decay, doc_offsets, out_weight, grad_out
):
    n, parts = lax.axis_size("ctx"), lax.axis_size("head")
    tok, hv = queries.shape[0], write_rate.shape[0]
    hk, model = queries.shape[1] // DK, grad_out.shape[1]
    plan = Plan(n, tok, hv, hk)
    s = plan.mates
    index = lax.axis_index("ctx").astype(jnp.int32)
    place, mate = (index // s).reshape(1), (index % s).reshape(1)
    head = lax.axis_index("head").astype(jnp.int32).reshape(1)

    def across_heads(pieces):
        moved = [lax.ppermute(pieces[d], "head", Ring(parts).pairs(d)) for d in range(1, parts)]
        return [pieces[0]] + moved

    vmem = lambda dtype, *shape: pltpu.VMEM(shape, dtype)

    packed = call(
        partial(pack_kernel, plan),
        [arr(BF16, plan.rows, DK)] * hv,
        smem=(0,),
        scratch=[vmem(BF16, hv, plan.rows, DK)],
        fetch=range(1, 6),
    )(place, queries, key_vectors, value_rows, write_rate, log_decay)
    got = plan.exchange(packed)
    rows = across_heads([grad_out] * parts)
    rows = [rows[d] for d in Ring(parts).far_first()]

    link, kept = call(
        partial(prepare_kernel, plan),
        (arr(F32, hv, 2, DK, DK), arr(F32, hv, KEPT, tok, DK)),
        smem=(0, 1, 2),
        fetch=(0,),
        flops=20_000_000_000,
    )(doc_offsets, place, mate, *got)
    links = [link] + [plan.from_mate(link, d) for d in range(1, s)]

    d_core = call(
        partial(cotangent_kernel, plan, parts),
        [arr(BF16, 2 * DV, tok)] * hv,
        smem=(0, 1),
        scratch=[vmem(BF16, tok, model), vmem(BF16, hv, 2 * DV, tok)],
        flops=30_000_000_000,
    )(head, place, *rows, after(out_weight, link))
    kept = after(kept, d_core[0])
    d_core = plan.exchange(d_core)

    states, *mixed = call(
        partial(scan_kernel, plan),
        [arr(F32, hv, DV, DK)] + [arr(BF16, hv, DV, tok)] * hv,
        smem=(0, 1),
        scratch=[vmem(F32, s, hv, 2, DK, DK), vmem(F32, n, DV, DK)],
        flops=2_500_000_000,
    )(place, mate, *links, kept)
    turned = call(
        partial(turn_kernel, plan, parts),
        [arr(BF16, model // hv, tok)] * hv,
        smem=(0, 1),
        scratch=[vmem(BF16, tok, model), vmem(BF16, hv, model // hv, tok)],
        flops=1_000_000_000,
    )(head, place, *after(rows, states))
    mixed = plan.exchange(mixed)
    turned = plan.exchange(turned)
    back = call(
        partial(state_cotangent_kernel, plan), arr(F32, hv, DV, DK), flops=30_000_000_000
    )(kept, *after(d_core, states))
    backs = [back] + [plan.from_mate(back, d) for d in range(1, s)]

    projected = call(
        partial(project_kernel, plan, parts),
        [arr(BF16 if d else F32, tok // parts, model) for d in range(parts)],
        smem=(0, 1),
        scratch=[vmem(BF16, hv, DV, tok), vmem(F32, tok, model)],
        flops=1_000_000_000,
    )(head, place, *mixed, out_weight)
    layer_parts = across_heads(projected)

    grads = call(
        partial(backward_kernel, plan),
        [arr(BF16, plan.rows, DK)] * hv,
        smem=(0, 1, 2),
        fetch=(0,),
        scratch=[
            vmem(F32, s, hv, 2, DK, DK),
            vmem(F32, s, hv, DV, DK),
            vmem(F32, n, DV, DK),
        ],
        flops=6_000_000_000,
    )(doc_offsets, place, mate, *links, *backs, *got, *d_core, kept, after(states, projected[1]))

    shares = call(
        partial(weight_kernel, plan),
        [arr(F32, model // n, hv * DV)] * s,
        smem=(0, 1),
        scratch=[vmem(BF16, hv, hv, DV, tok)],
        flops=1_000_000_000,
    )(place, mate, *turned, *mixed)
    grads = plan.exchange(after(grads, shares[0]))
    weight_grad = shares[0]
    for d in range(1, s):
        weight_grad = weight_grad + plan.from_mate(shares[d], d)

    layer_out = layer_parts[0]
    for d in Ring(parts).far_first()[-2::-1]:
        layer_out = layer_out + layer_parts[d].astype(F32)
    grads = after(grads[::-1], (layer_out, weight_grad))
    grad_q, grad_k, grad_v, grad_rate, grad_decay = call(
        partial(finish_kernel, plan),
        (
            arr(F32, tok, hk * DK),
            arr(F32, tok, hk * DK),
            arr(F32, tok, hv * DV),
            arr(F32, hv, tok),
            arr(F32, hv, tok),
        ),
        smem=(0,),
        scratch=[vmem(BF16, hv, plan.rows, DK)],
        flops=1_000_000_000,
        inside=False,
    )(place, *grads)
    return (layer_out, grad_q, grad_k, grad_v, grad_rate, grad_decay, weight_grad)


def solution(mesh):
    placed = (
        P("ctx", "head"),
        P("ctx", "head"),
        P("ctx", "head"),
        P("head", "ctx"),
        P("head", "ctx"),
        P(),
        P("head", None),
        P(("ctx", "head"), None),
    )
    return jax.shard_map(
        per_device,
        mesh=mesh,
        in_specs=placed,
        out_specs=(
            P(("ctx", "head"), None),
            P("ctx", "head"),
            P("ctx", "head"),
            P("ctx", "head"),
            P("head", "ctx"),
            P("head", "ctx"),
            P("ctx", "head"),
        ),
        check_vma=False,
    )
```

```python
import math
from functools import partial

import jax
import jax.numpy as jnp
from jax import lax
from jax.experimental import pallas as pl
from jax.experimental.pallas import tpu as pltpu
from jax.sharding import PartitionSpec as P

DK = 128
DV = 128
AUX = 16
INVERSE, SCORES, FROM_STATE, READS, KEYS, QUERIES, ENDS, SPLIT = range(8)
RATIO, WRITES, LOCAL, COLUMNS, KEPT = range(5)
SCALES = 6
EPS = 1e-06
F32 = jnp.float32
BF16 = jnp.bfloat16
SPARE_VMEM = 8 * 1024 * 1024


def dot(a, b, ca, cb):
    return lax.dot_general(a, b, (((ca,), (cb,)), ((), ())), preferred_element_type=F32)


def halves(x):
    high = x.astype(BF16)
    return high, (x - high.astype(F32)).astype(BF16)


def thirds(x):
    high = x.astype(BF16).astype(F32)
    middle = (x - high).astype(BF16).astype(F32)
    return high, middle, x - high - middle


def mm(a, b, ca=1, cb=0):
    left = jnp.concatenate([a[0], a[0], a[1]], axis=ca)
    right = jnp.concatenate([b[0], b[1], b[0]], axis=cb)
    return dot(left, right, ca, cb)


def cat(pairs, axis):
    return tuple(jnp.concatenate(parts, axis=axis) for parts in zip(*pairs))


def iotas(rows, columns):
    shape = (rows, columns)
    return lax.broadcasted_iota(jnp.int32, shape, 0), lax.broadcasted_iota(jnp.int32, shape, 1)


def call(kernel, outs, smem=(), scratch=(), flops=0, inside=True, fetch=()):
    if inside:
        outs = jax.tree.map(lambda o: pltpu.VMEM(o.shape, o.dtype), outs)
    scoped = SPARE_VMEM + sum(x.dtype.itemsize * math.prod(x.shape) for x in scratch)

    def run(*args):
        spec = lambda i: pl.BlockSpec(memory_space=pltpu.SMEM if i in smem else pltpu.VMEM)
        space = lambda i: pltpu.HBM if i in fetch else pltpu.VMEM
        hold = pltpu.with_memory_space_constraint
        return pl.pallas_call(
            kernel,
            out_shape=outs,
            in_specs=[spec(i) for i in range(len(args))],
            out_specs=jax.tree.map(lambda _: pl.BlockSpec(memory_space=pltpu.VMEM), outs),
            scratch_shapes=list(scratch),
            compiler_params=pltpu.CompilerParams(vmem_limit_bytes=scoped),
            cost_estimate=pl.CostEstimate(flops=flops, bytes_accessed=0, transcendentals=0),
        )(*(hold(x, space(i)) if i in fetch or i not in smem else x for i, x in enumerate(args)))

    return run


def arr(dtype, *shape):
    return jax.ShapeDtypeStruct(shape, dtype)


class Ring:
    def __init__(self, size):
        self.size = size
        self.paired = size & (size - 1) == 0

    def source(self, i, d):
        return i ^ d if self.paired else (i + d) % self.size

    def target(self, i, d):
        return i ^ d if self.paired else (i + self.size - d) % self.size

    def seen(self, d, k):
        return d ^ k if self.paired else (k - d) % self.size

    def far_first(self):
        return sorted(range(self.size), key=lambda d: d != self.size // 2)

    def pairs(self, d):
        return [(self.source(i, d), i) for i in range(self.size)]


class Plan:
    def __init__(self, n, tok, hv, hk):
        self.n, self.tok, self.hv, self.hk = n, tok, hv, hk
        self.mates = n // hv
        self.v_at = 2 * tok
        self.aux_at = 2 * tok + DV
        self.rows = self.aux_at + AUX
        self.ring = Ring(hv)

    def key_head(self, head):
        return head * self.hk // self.hv

    def exchange(self, pieces):
        s = self.mates
        moved = [pieces[0]]
        for d in range(1, self.hv):
            pairs = [(i * s + b, j * s + b) for i, j in self.ring.pairs(d) for b in range(s)]
            moved.append(lax.ppermute(pieces[d], "ctx", pairs))
        return moved

    def from_mate(self, x, d):
        s = self.mates
        pairs = [(i // s * s + (i + d) % s, i) for i in range(self.n)]
        return lax.ppermute(x, "ctx", pairs)


def aux_rows(rows, columns):
    row_ids = lax.broadcasted_iota(jnp.int32, (AUX, columns), 0)
    out = jnp.zeros((AUX, columns), F32)
    for i, part in enumerate(p for r in rows for p in thirds(r)):
        out = jnp.where(row_ids == i, part, out)
    return out.astype(BF16)


def pack_kernel(plan, place_ref, q_ref, k_ref, v_ref, rate_ref, decay_ref, *refs):
    outs, out_ref = refs[:-1], refs[-1]
    tok = plan.tok
    for h in range(plan.hv):
        kh = plan.key_head(h)
        out_ref[h, :tok] = q_ref[:, kh * DK : (kh + 1) * DK]
        out_ref[h, tok : 2 * tok] = k_ref[:, kh * DK : (kh + 1) * DK]
        turned = jnp.transpose(v_ref[:, h * DV : (h + 1) * DV].astype(F32))
        out_ref[h, plan.v_at : plan.aux_at] = turned.astype(BF16)
        rows = [rate_ref[h : h + 1, :], decay_ref[h : h + 1, :]]
        out_ref[h, plan.aux_at :] = aux_rows(rows, tok)
    hand_out(plan, place_ref[0], out_ref, outs)


def hand_out(plan, place, all_ref, outs):
    for d, ref in enumerate(outs):
        ref[...] = all_ref[plan.ring.target(place, d)]


def unit(x):
    scale = lax.rsqrt(jnp.sum(x * x, axis=1, keepdims=True) + EPS)
    return x * scale, scale


def segments(off_ref, positions):
    total = jnp.zeros(positions.shape, jnp.int32)
    for j in range(off_ref.shape[0] - 1):
        total = total + (off_ref[j] <= positions).astype(jnp.int32)
    return total


def to_columns(rows, tok):
    row_ids = lax.broadcasted_iota(jnp.int32, (tok, tok), 0)
    stacked = jnp.zeros((tok, tok), F32)
    for i, r in enumerate(rows):
        stacked = jnp.where(row_ids == i, r, stacked)
    turned = jnp.transpose(stacked)
    return [turned[:, i : i + 1] for i in range(len(rows))]


def to_rows(columns, tok):
    column_ids = lax.broadcasted_iota(jnp.int32, (tok, tok), 1)
    stacked = jnp.zeros((tok, tok), F32)
    for i, c in enumerate(columns):
        stacked = jnp.where(column_ids == i, c, stacked)
    turned = jnp.transpose(stacked)
    return [turned[i : i + 1, :] for i in range(len(columns))]


def scalings(plan, off_ref, chunks, auxes):
    tok = plan.tok
    rows, columns = iotas(tok, tok)
    upto = (rows <= columns).astype(BF16)
    sums = [dot(a, upto, 1, 0) for a in auxes]
    rates = [jnp.sum(a[0:3].astype(F32), axis=0, keepdims=True) for a in auxes]
    cumuls = [s[3:4] + s[4:5] + s[5:6] for s in sums]
    turned = to_columns(rates + cumuls, tok)
    out = []
    for i, c in enumerate(chunks):
        b_col, c_col = turned[i], turned[len(chunks) + i]
        c_row = cumuls[i]
        start = c * tok
        seg_col = segments(off_ref, start + rows[:, :1])
        seg_row = segments(off_ref, start + columns[:1, :])
        before = jnp.int32(0)
        last = jnp.int32(0)
        for j in range(off_ref.shape[0] - 1):
            before = before + (off_ref[j] <= start - 1).astype(jnp.int32)
            last = last + (off_ref[j] <= start + tok - 1).astype(jnp.int32)
        c_last = c_row[:, tok - 1 : tok]
        together = (seg_col == seg_row) & (rows >= columns)
        ratio = jnp.where(together, jnp.exp(jnp.where(together, c_col - c_row, 0.0)), 0.0)
        start_col = jnp.where(seg_col == before, jnp.exp(c_col), 0.0)
        end_col = jnp.where(seg_col == last, jnp.exp(c_last - c_col), 0.0)
        whole = jnp.where(last == before, jnp.exp(c_last), 0.0)
        out.append((rates[i], b_col, ratio, start_col, end_col, whole))
    return out


def inverses(lowers):
    size = lowers[0].shape[0]
    rows, columns = iotas(size, size)
    identity = (rows == columns).astype(F32)
    block = min(16, size)
    near = (rows // block) == (columns // block)
    powers = [jnp.where(near, -m, 0.0) for m in lowers]
    results = [identity + p for p in powers]
    split = [halves(p) for p in powers]
    powers = [mm(s, s) for s in split]
    reach = 2
    while reach < block:
        split = [halves(p) for p in powers]
        more = reach * 2 < block
        both = []
        for r, s in zip(results, split):
            left = halves(r)
            if more:
                left = cat([left, s], 0)
            both.append(mm(left, s))
        results = [r + b[:size] for r, b in zip(results, both)]
        if more:
            powers = [b[size:] for b in both]
        reach *= 2
    while block < size:
        across = ((rows // (2 * block)) == (columns // (2 * block))) & (
            (rows // block) > (columns // block)
        )
        split = [halves(r) for r in results]
        middle = [mm(halves(jnp.where(across, m, 0.0)), s) for m, s in zip(lowers, split)]
        results = [r - mm(s, halves(m)) for r, s, m in zip(results, split, middle)]
        block *= 2
    return results


def chunks_of(plan, place, mate):
    return [mate + plan.mates * plan.ring.source(place, d) for d in range(plan.hv)]


def prepare_kernel(plan, off_ref, place_ref, mate_ref, *refs):
    in_refs, (link_ref, split_ref, kept_ref) = refs[: plan.hv], refs[plan.hv :]
    tok = plan.tok
    rows, columns = iotas(tok, tok)
    key_rows, key_columns = iotas(DK, DK)
    identity = (key_rows == key_columns).astype(F32)
    mine = range(plan.hv)
    chunks = chunks_of(plan, place_ref[0], mate_ref[0])
    scales = scalings(plan, off_ref, chunks, [r[plan.aux_at :] for r in in_refs])
    qu = [unit(in_refs[m][:tok].astype(F32)) for m in mine]
    ku = [unit(in_refs[m][tok : 2 * tok].astype(F32)) for m in mine]
    qn, kn = [x[0] for x in qu], [x[0] for x in ku]
    kp = [halves(x) for x in kn]
    qp = [halves(x) for x in qn]
    dots = [mm(cat([q, k], 0), k, 1, 1) for q, k in zip(qp, kp)]
    strict = rows > columns
    lowers = [jnp.where(strict, s[1] * d[tok:] * s[2], 0.0) for s, d in zip(scales, dots)]
    scores = [d[:tok] * s[2] for s, d in zip(scales, dots)]
    inv = inverses(lowers)
    rated = [halves(x * s[0]) for x, s in zip(inv, scales)]
    w = [mm(x, halves(s[3] * k)) for x, s, k in zip(rated, scales, kn)]
    values = [in_refs[m][plan.v_at : plan.aux_at] for m in mine]
    u = [
        dot(jnp.concatenate([v, v], axis=1), jnp.concatenate(x, axis=1), 1, 1)
        for v, x in zip(values, rated)
    ]
    wp = [halves(x) for x in w]
    up = [halves(x) for x in u]
    ap = [halves(x) for x in scores]
    ke = [halves(s[4] * k) for s, k in zip(scales, kn)]
    for m in mine:
        link_ref[m, 0] = scales[m][5] * identity - mm(wp[m], ke[m], 0, 0)
        link_ref[m, 1] = mm(up[m], ke[m])
    lanes = lax.broadcasted_iota(jnp.int32, (tok, DK), 1)
    for m in mine:
        _, b_col, ratio, start_col, end_col, whole = scales[m]
        reads = start_col * qn[m] - mm(ap[m], wp[m])
        for i, pair in enumerate((halves(inv[m]), ap[m], wp[m], halves(reads), kp[m], qp[m], ke[m])):
            split_ref[m, i, 0], split_ref[m, i, 1] = pair
        kept_ref[m, RATIO] = ratio
        kept_ref[m, WRITES] = u[m]
        kept_ref[m, LOCAL] = mm(up[m], ap[m], 1, 1)
        columns_of = jnp.zeros((tok, DK), F32)
        for i, x in enumerate((b_col, start_col, end_col, qu[m][1], ku[m][1], whole)):
            columns_of = jnp.where(lanes == i, x, columns_of)
        kept_ref[m, COLUMNS] = columns_of


def get(split_ref, m, i):
    return split_ref[m, i, 0], split_ref[m, i, 1]


def lay_out(plan, place, mate, refs, all_ref):
    for d, ref in enumerate(refs):
        for m in range(plan.hv):
            all_ref[lax.rem(mate + d, plan.mates), plan.ring.source(place, m)] = ref[m]


def scan_kernel(plan, place_ref, mate_ref, *refs):
    s, hv = plan.mates, plan.hv
    links, split_ref, kept_ref, state_ref = refs[:s], refs[s], refs[s + 1], refs[s + 2]
    outs, (all_ref, states_ref) = refs[s + 3 : -2], refs[-2:]
    place, mate = place_ref[0], mate_ref[0]
    lay_out(plan, place, mate, links, all_ref)
    state = jnp.zeros((DV, DK), F32)
    for c in range(plan.n):
        states_ref[c] = state
        if c < plan.n - 1:
            link = all_ref.at[c % s, c // s]
            state = link[1] + mm(halves(state), halves(link[0]))
    cores = []
    for m, c in enumerate(chunks_of(plan, place, mate)):
        state = states_ref[c]
        state_ref[m] = state
        core = kept_ref[m, LOCAL] + mm(halves(state), get(split_ref, m, READS), 1, 1)
        cores.append(core.astype(BF16))
    for d in range(hv):
        for k in range(hv):
            outs[d][k] = cores[plan.ring.seen(d, k)]


def state_cotangent_kernel(plan, split_ref, *refs):
    for m in range(plan.hv):
        refs[-1][m] = mm(d_out(refs[m]), get(split_ref, m, READS))


def d_out(ref):
    return ref[:DV], ref[DV:]


def backward_kernel(plan, place_ref, mate_ref, *refs):
    s, n, tok, hv = plan.mates, plan.n, plan.tok, plan.hv
    links, backs, refs = refs[:s], refs[s : 2 * s], refs[2 * s :]
    in_refs, d_refs = refs[:hv], refs[hv : 2 * hv]
    split_ref, kept_ref, state_ref = refs[2 * hv : 2 * hv + 3]
    outs, (links_ref, backs_ref, cots_ref) = refs[2 * hv + 3 : -3], refs[-3:]
    outs = [outs[plan.ring.seen(m, 0)] for m in range(hv)]
    place, mate = place_ref[0], mate_ref[0]
    lay_out(plan, place, mate, links, links_ref)
    lay_out(plan, place, mate, backs, backs_ref)
    d_state = jnp.zeros((DV, DK), F32)
    for c in reversed(range(n)):
        cots_ref[c] = d_state
        if c:
            d_state = backs_ref[c % s, c // s] + mm(
                halves(d_state), halves(links_ref[c % s, c // s, 0]), 1, 1
            )
    rows, columns = iotas(tok, tok)
    strict = rows > columns
    upto = (rows >= columns).astype(BF16)
    mine = range(hv)
    chunks = chunks_of(plan, place, mate)
    scales = []
    for m in mine:
        held = kept_ref[m, COLUMNS]
        columns_of = [held[:, i : i + 1] for i in range(SCALES)]
        rate = jnp.sum(in_refs[m][plan.aux_at :][0:3].astype(F32), axis=0, keepdims=True)
        scales.append([rate] + columns_of[:-1] + [columns_of[-1][:1]])
    qp = [get(split_ref, m, QUERIES) for m in mine]
    kp = [get(split_ref, m, KEYS) for m in mine]
    ke = [get(split_ref, m, ENDS) for m in mine]
    whole_of = lambda pair: pair[0].astype(F32) + pair[1].astype(F32)
    do = [d_out(r) for r in d_refs]
    s0 = [state_ref[m] for m in mine]
    ds = [cots_ref[c] for c in chunks]
    s0p = [halves(x) for x in s0]
    dsp = [halves(x) for x in ds]
    pseudo = [kept_ref[m, WRITES] - mm(s0p[m], get(split_ref, m, FROM_STATE), 1, 1) for m in mine]
    pp = [halves(x) for x in pseudo]
    dp = [mm(do[m], get(split_ref, m, SCORES)) + mm(dsp[m], ke[m], 1, 1) for m in mine]
    dr = [mm(halves(dp[m]), get(split_ref, m, INVERSE)) for m in mine]
    drp = [halves(x) for x in dr]
    big = [mm(cat([o, r], 1), cat([p, s], 1), 0, 0) for o, r, p, s in zip(do, drp, pp, s0p)]
    pds = [mm(p, d, 0, 0) for p, d in zip(pp, dsp)]
    da = [big[m][:tok, :tok] * kept_ref[m, RATIO] for m in mine]
    dm = [jnp.where(strict, -big[m][tok:, :tok] * kept_ref[m, RATIO], 0.0) for m in mine]
    dap = [halves(x) for x in da]
    dmp = [halves(x) for x in dm]
    dbm = [halves(s[1] * x) for s, x in zip(scales, dm)]
    by_row = [mm(cat([x, y], 0), k) for x, y, k in zip(dap, dmp, kp)]
    by_column = [
        mm(cat([x, y], 0), cat([q, k], 0), 0, 0) for x, y, q, k in zip(dap, dbm, qp, kp)
    ]
    sums = []
    for m in mine:
        _, b_col, start_col, end_col, q_scale, k_scale, whole = scales[m]
        qn, kn = whole_of(qp[m]), whole_of(kp[m])
        out = outs[m]
        dqn = by_row[m][:tok] + start_col * big[m][:tok, tok:]
        erase = by_row[m][tok:] - start_col * big[m][tok:, tok:]
        ends = end_col * pds[m]
        write = by_column[m] + ends
        dkn = b_col * erase + write
        s_q = jnp.sum(qn * dqn, axis=1, keepdims=True)
        s_e = jnp.sum(kn * erase, axis=1, keepdims=True)
        s_w = jnp.sum(kn * write, axis=1, keepdims=True)
        total = jnp.sum(jnp.sum(kn * ends, axis=1, keepdims=True), axis=0, keepdims=True)
        both = jnp.sum(jnp.sum(s0[m] * ds[m], axis=1, keepdims=True), axis=0, keepdims=True)
        out[:tok] = (q_scale * (dqn - qn * s_q)).astype(BF16)
        out[tok : 2 * tok] = (k_scale * (dkn - kn * (b_col * s_e + s_w))).astype(BF16)
        out[plan.v_at : plan.aux_at] = (scales[m][0] * dr[m]).astype(BF16)
        sums.append((s_e, s_q + b_col * s_e - s_w, total + whole * both))
    turned = to_rows([s[0] for s in sums] + [s[1] for s in sums], tok)
    for m in mine:
        values = in_refs[m][plan.v_at : plan.aux_at].astype(F32)
        d_rate = turned[m] + jnp.sum(dr[m] * values, axis=0, keepdims=True)
        parts = dot(aux_rows([turned[plan.hv + m]], tok), upto, 1, 0)
        d_decay = parts[0:1] + parts[1:2] + parts[2:3] + sums[m][2]
        outs[m][plan.aux_at :] = aux_rows([d_rate, d_decay], tok)


def gather_rows(head, pieces, all_ref):
    rows, ring = pieces[0].shape[0], Ring(len(pieces))
    for d, piece in zip(ring.far_first(), pieces):
        at = ring.source(head, d) * rows
        all_ref[pl.ds(pl.multiple_of(at, rows), rows), :] = piece[...]


def cotangent_kernel(plan, parts, head_ref, place_ref, *refs):
    pieces, w_ref, outs, (all_ref, core_ref) = refs[:parts], refs[parts], refs[parts + 1 : -2], refs[-2:]
    gather_rows(head_ref[0], pieces, all_ref)
    high, low = halves(dot(w_ref[...], all_ref[...], 1, 1))
    for m in range(plan.hv):
        core_ref[m, :DV] = high[m * DV : (m + 1) * DV]
        core_ref[m, DV:] = low[m * DV : (m + 1) * DV]
    hand_out(plan, place_ref[0], core_ref, outs)


def turn_kernel(plan, parts, head_ref, place_ref, *refs):
    pieces, outs, (all_ref, turned_ref) = refs[:parts], refs[parts:-2], refs[-2:]
    gather_rows(head_ref[0], pieces, all_ref)
    share = turned_ref.shape[1]
    for m in range(plan.hv):
        part = all_ref[:, m * share : (m + 1) * share].astype(F32)
        turned_ref[m] = jnp.transpose(part).astype(BF16)
    hand_out(plan, place_ref[0], turned_ref, outs)


def project_kernel(plan, parts, head_ref, place_ref, *refs):
    mixed_refs, w_ref, outs, (all_ref, total_ref) = (
        refs[: plan.hv],
        refs[plan.hv],
        refs[plan.hv + 1 : -2],
        refs[-2:],
    )
    for d, ref in enumerate(mixed_refs):
        all_ref[plan.ring.source(place_ref[0], d)] = ref[0]
    mixed = all_ref[...].reshape(plan.hv * DV, plan.tok)
    total_ref[...] = dot(mixed, w_ref[...], 0, 0)
    rows, ring = outs[0].shape[0], Ring(parts)
    for d in range(parts):
        at = ring.target(head_ref[0], d) * rows
        block = total_ref[pl.ds(pl.multiple_of(at, rows), rows), :]
        outs[d][...] = block.astype(outs[d].dtype)


def weight_kernel(plan, place_ref, mate_ref, *refs):
    hv = plan.hv
    turned, mixed_refs, outs, all_ref = refs[:hv], refs[hv : 2 * hv], refs[2 * hv : -1], refs[-1]
    for d, ref in enumerate(mixed_refs):
        head = plan.ring.source(place_ref[0], d)
        for k in range(hv):
            all_ref[k, head] = ref[k]
    share = outs[0].shape[0]
    for d, out_ref in enumerate(outs):
        at = lax.rem(mate_ref[0] + plan.mates - d, plan.mates) * share
        at = pl.multiple_of(at, share)
        total = None
        for k in range(hv):
            mixed = all_ref[k].reshape(hv * DV, plan.tok)
            part = dot(turned[k][pl.ds(at, share), :], mixed, 1, 1)
            total = part if total is None else total + part
        out_ref[...] = total


def finish_kernel(plan, place_ref, *refs):
    pieces, (q_ref, k_ref, v_ref, rate_ref, decay_ref, in_ref) = refs[: plan.hv], refs[plan.hv :]
    tok = plan.tok
    for d, ref in enumerate(pieces):
        in_ref[plan.ring.source(place_ref[0], d)] = ref[...]
    for kh in range(plan.hk):
        mine = [h for h in range(plan.hv) if plan.key_head(h) == kh]
        for ref, at in ((q_ref, 0), (k_ref, tok)):
            total = in_ref[mine[0], at : at + tok].astype(F32)
            for h in mine[1:]:
                total = total + in_ref[h, at : at + tok].astype(F32)
            ref[:, kh * DK : (kh + 1) * DK] = total
    for h in range(plan.hv):
        v_ref[:, h * DV : (h + 1) * DV] = jnp.transpose(
            in_ref[h, plan.v_at : plan.aux_at].astype(F32)
        )
        aux = in_ref[h, plan.aux_at :].astype(F32)
        rate_ref[h : h + 1, :] = aux[0:1] + aux[1:2] + aux[2:3]
        decay_ref[h : h + 1, :] = aux[3:4] + aux[4:5] + aux[5:6]


def after(x, y):
    return lax.optimization_barrier((x, y))[0]


def per_device(
    queries, key_vectors, value_rows, write_rate, log_decay, doc_offsets, out_weight, grad_out
):
    n, parts = lax.axis_size("ctx"), lax.axis_size("head")
    tok, hv = queries.shape[0], write_rate.shape[0]
    hk, model = queries.shape[1] // DK, grad_out.shape[1]
    plan = Plan(n, tok, hv, hk)
    s = plan.mates
    index = lax.axis_index("ctx").astype(jnp.int32)
    place, mate = (index // s).reshape(1), (index % s).reshape(1)
    head = lax.axis_index("head").astype(jnp.int32).reshape(1)

    def across_heads(pieces):
        moved = [lax.ppermute(pieces[d], "head", Ring(parts).pairs(d)) for d in range(1, parts)]
        return [pieces[0]] + moved

    vmem = lambda dtype, *shape: pltpu.VMEM(shape, dtype)

    packed = call(
        partial(pack_kernel, plan),
        [arr(BF16, plan.rows, DK)] * hv,
        smem=(0,),
        scratch=[vmem(BF16, hv, plan.rows, DK)],
        fetch=range(1, 6),
    )(place, queries, key_vectors, value_rows, write_rate, log_decay)
    got = plan.exchange(packed)
    rows = across_heads([grad_out] * parts)
    rows = [rows[d] for d in Ring(parts).far_first()]

    link, split, kept = call(
        partial(prepare_kernel, plan),
        (
            arr(F32, hv, 2, DK, DK),
            arr(BF16, hv, SPLIT, 2, tok, DK),
            arr(F32, hv, KEPT, tok, DK),
        ),
        smem=(0, 1, 2),
        fetch=(0,),
        flops=20_000_000_000,
    )(doc_offsets, place, mate, *got)
    links = [link] + [plan.from_mate(link, d) for d in range(1, s)]

    d_core = call(
        partial(cotangent_kernel, plan, parts),
        [arr(BF16, 2 * DV, tok)] * hv,
        smem=(0, 1),
        scratch=[vmem(BF16, tok, model), vmem(BF16, hv, 2 * DV, tok)],
        flops=30_000_000_000,
    )(head, place, *rows, after(out_weight, link))
    kept = after(kept, d_core[0])
    d_core = plan.exchange(d_core)

    states, *mixed = call(
        partial(scan_kernel, plan),
        [arr(F32, hv, DV, DK)] + [arr(BF16, hv, DV, tok)] * hv,
        smem=(0, 1),
        scratch=[vmem(F32, s, hv, 2, DK, DK), vmem(F32, n, DV, DK)],
        flops=2_500_000_000,
    )(place, mate, *links, split, kept)
    turned = call(
        partial(turn_kernel, plan, parts),
        [arr(BF16, model // hv, tok)] * hv,
        smem=(0, 1),
        scratch=[vmem(BF16, tok, model), vmem(BF16, hv, model // hv, tok)],
        flops=1_000_000_000,
    )(head, place, *after(rows, states))
    mixed = plan.exchange(mixed)
    turned = plan.exchange(turned)
    back = call(
        partial(state_cotangent_kernel, plan), arr(F32, hv, DV, DK), flops=30_000_000_000
    )(split, *after(d_core, states))
    backs = [back] + [plan.from_mate(back, d) for d in range(1, s)]

    projected = call(
        partial(project_kernel, plan, parts),
        [arr(BF16 if d else F32, tok // parts, model) for d in range(parts)],
        smem=(0, 1),
        scratch=[vmem(BF16, hv, DV, tok), vmem(F32, tok, model)],
        flops=1_000_000_000,
    )(head, place, *mixed, out_weight)
    layer_parts = across_heads(projected)

    grads = call(
        partial(backward_kernel, plan),
        [arr(BF16, plan.rows, DK)] * hv,
        smem=(0, 1),
        scratch=[
            vmem(F32, s, hv, 2, DK, DK),
            vmem(F32, s, hv, DV, DK),
            vmem(F32, n, DV, DK),
        ],
        flops=6_000_000_000,
    )(place, mate, *links, *backs, *got, *d_core, split, kept, after(states, projected[1]))

    shares = call(
        partial(weight_kernel, plan),
        [arr(F32, model // n, hv * DV)] * s,
        smem=(0, 1),
        scratch=[vmem(BF16, hv, hv, DV, tok)],
        flops=1_000_000_000,
    )(place, mate, *turned, *mixed)
    grads = plan.exchange(after(grads, shares[0]))
    weight_grad = shares[0]
    for d in range(1, s):
        weight_grad = weight_grad + plan.from_mate(shares[d], d)

    layer_out = layer_parts[0]
    for part in layer_parts[:0:-1]:
        layer_out = layer_out + part.astype(F32)
    grads = after(grads, (layer_out, weight_grad))
    grad_q, grad_k, grad_v, grad_rate, grad_decay = call(
        partial(finish_kernel, plan),
        (
            arr(F32, tok, hk * DK),
            arr(F32, tok, hk * DK),
            arr(F32, tok, hv * DV),
            arr(F32, hv, tok),
            arr(F32, hv, tok),
        ),
        smem=(0,),
        scratch=[vmem(BF16, hv, plan.rows, DK)],
        flops=1_000_000_000,
        inside=False,
    )(place, *grads)
    return (layer_out, grad_q, grad_k, grad_v, grad_rate, grad_decay, weight_grad)


def solution(mesh):
    placed = (
        P("ctx", "head"),
        P("ctx", "head"),
        P("ctx", "head"),
        P("head", "ctx"),
        P("head", "ctx"),
        P(),
        P("head", None),
        P(("ctx", "head"), None),
    )
    return jax.shard_map(
        per_device,
        mesh=mesh,
        in_specs=placed,
        out_specs=(
            P(("ctx", "head"), None),
            P("ctx", "head"),
            P("ctx", "head"),
            P("ctx", "head"),
            P("head", "ctx"),
            P("head", "ctx"),
            P("ctx", "head"),
        ),
        check_vma=False,
    )
```

```python
import math
from functools import partial

import jax
import jax.numpy as jnp
from jax import lax
from jax.experimental import pallas as pl
from jax.experimental.pallas import tpu as pltpu
from jax.sharding import PartitionSpec as P

DK = 128
DV = 128
AUX = 16
INVERSE, SCORES, FROM_STATE, READS, KEYS, QUERIES, ENDS, SPLIT = range(8)
RATIO, WRITES, LOCAL, COLUMNS, KEPT = range(5)
SCALES = 6
EPS = 1e-06
F32 = jnp.float32
BF16 = jnp.bfloat16
SPARE_VMEM = 8 * 1024 * 1024


def dot(a, b, ca, cb):
    return lax.dot_general(a, b, (((ca,), (cb,)), ((), ())), preferred_element_type=F32)


def halves(x):
    high = x.astype(BF16)
    return high, (x - high.astype(F32)).astype(BF16)


def thirds(x):
    high = x.astype(BF16).astype(F32)
    middle = (x - high).astype(BF16).astype(F32)
    return high, middle, x - high - middle


def mm(a, b, ca=1, cb=0):
    left = jnp.concatenate([a[0], a[0], a[1]], axis=ca)
    right = jnp.concatenate([b[0], b[1], b[0]], axis=cb)
    return dot(left, right, ca, cb)


def cat(pairs, axis):
    return tuple(jnp.concatenate(parts, axis=axis) for parts in zip(*pairs))


def iotas(rows, columns):
    shape = (rows, columns)
    return lax.broadcasted_iota(jnp.int32, shape, 0), lax.broadcasted_iota(jnp.int32, shape, 1)


def call(kernel, outs, smem=(), scratch=(), flops=0, inside=True, fetch=()):
    if inside:
        outs = jax.tree.map(lambda o: pltpu.VMEM(o.shape, o.dtype), outs)
    scoped = SPARE_VMEM + sum(x.dtype.itemsize * math.prod(x.shape) for x in scratch)

    def run(*args):
        spec = lambda i: pl.BlockSpec(memory_space=pltpu.SMEM if i in smem else pltpu.VMEM)
        space = lambda i: pltpu.HBM if i in fetch else pltpu.VMEM
        hold = pltpu.with_memory_space_constraint
        return pl.pallas_call(
            kernel,
            out_shape=outs,
            in_specs=[spec(i) for i in range(len(args))],
            out_specs=jax.tree.map(lambda _: pl.BlockSpec(memory_space=pltpu.VMEM), outs),
            scratch_shapes=list(scratch),
            compiler_params=pltpu.CompilerParams(vmem_limit_bytes=scoped),
            cost_estimate=pl.CostEstimate(flops=flops, bytes_accessed=0, transcendentals=0),
        )(*(hold(x, space(i)) if i in fetch or i not in smem else x for i, x in enumerate(args)))

    return run


def arr(dtype, *shape):
    return jax.ShapeDtypeStruct(shape, dtype)


class Ring:
    def __init__(self, size):
        self.size = size
        self.paired = size & (size - 1) == 0

    def source(self, i, d):
        return i ^ d if self.paired else (i + d) % self.size

    def target(self, i, d):
        return i ^ d if self.paired else (i + self.size - d) % self.size

    def seen(self, d, k):
        return d ^ k if self.paired else (k - d) % self.size

    def far_first(self):
        return sorted(range(self.size), key=lambda d: d != self.size // 2)

    def pairs(self, d):
        return [(self.source(i, d), i) for i in range(self.size)]


class Plan:
    def __init__(self, n, tok, hv, hk):
        self.n, self.tok, self.hv, self.hk = n, tok, hv, hk
        self.mates = n // hv
        self.v_at = 2 * tok
        self.aux_at = 2 * tok + DV
        self.rows = self.aux_at + AUX
        self.ring = Ring(hv)

    def key_head(self, head):
        return head * self.hk // self.hv

    def exchange(self, pieces):
        s = self.mates
        moved = [pieces[0]]
        for d in range(1, self.hv):
            pairs = [(i * s + b, j * s + b) for i, j in self.ring.pairs(d) for b in range(s)]
            moved.append(lax.ppermute(pieces[d], "ctx", pairs))
        return moved

    def from_mate(self, x, d):
        s = self.mates
        pairs = [(i // s * s + (i + d) % s, i) for i in range(self.n)]
        return lax.ppermute(x, "ctx", pairs)


def aux_rows(rows, columns):
    row_ids = lax.broadcasted_iota(jnp.int32, (AUX, columns), 0)
    out = jnp.zeros((AUX, columns), F32)
    for i, part in enumerate(p for r in rows for p in thirds(r)):
        out = jnp.where(row_ids == i, part, out)
    return out.astype(BF16)


def pack_kernel(plan, place_ref, q_ref, k_ref, v_ref, rate_ref, decay_ref, *refs):
    outs, out_ref = refs[:-1], refs[-1]
    tok = plan.tok
    for h in range(plan.hv):
        kh = plan.key_head(h)
        out_ref[h, :tok] = q_ref[:, kh * DK : (kh + 1) * DK]
        out_ref[h, tok : 2 * tok] = k_ref[:, kh * DK : (kh + 1) * DK]
        turned = jnp.transpose(v_ref[:, h * DV : (h + 1) * DV].astype(F32))
        out_ref[h, plan.v_at : plan.aux_at] = turned.astype(BF16)
        rows = [rate_ref[h : h + 1, :], decay_ref[h : h + 1, :]]
        out_ref[h, plan.aux_at :] = aux_rows(rows, tok)
    hand_out(plan, place_ref[0], out_ref, outs)


def hand_out(plan, place, all_ref, outs):
    for d, ref in enumerate(outs):
        ref[...] = all_ref[plan.ring.target(place, d)]


def unit(x):
    scale = lax.rsqrt(jnp.sum(x * x, axis=1, keepdims=True) + EPS)
    return x * scale, scale


def segments(off_ref, positions):
    total = jnp.zeros(positions.shape, jnp.int32)
    for j in range(off_ref.shape[0] - 1):
        total = total + (off_ref[j] <= positions).astype(jnp.int32)
    return total


def to_columns(rows, tok):
    row_ids = lax.broadcasted_iota(jnp.int32, (tok, tok), 0)
    stacked = jnp.zeros((tok, tok), F32)
    for i, r in enumerate(rows):
        stacked = jnp.where(row_ids == i, r, stacked)
    turned = jnp.transpose(stacked)
    return [turned[:, i : i + 1] for i in range(len(rows))]


def to_rows(columns, tok):
    column_ids = lax.broadcasted_iota(jnp.int32, (tok, tok), 1)
    stacked = jnp.zeros((tok, tok), F32)
    for i, c in enumerate(columns):
        stacked = jnp.where(column_ids == i, c, stacked)
    turned = jnp.transpose(stacked)
    return [turned[i : i + 1, :] for i in range(len(columns))]


def scalings(plan, off_ref, chunks, auxes):
    tok = plan.tok
    rows, columns = iotas(tok, tok)
    upto = (rows <= columns).astype(BF16)
    sums = [dot(a, upto, 1, 0) for a in auxes]
    rates = [jnp.sum(a[0:3].astype(F32), axis=0, keepdims=True) for a in auxes]
    cumuls = [s[3:4] + s[4:5] + s[5:6] for s in sums]
    turned = to_columns(rates + cumuls, tok)
    out = []
    for i, c in enumerate(chunks):
        b_col, c_col = turned[i], turned[len(chunks) + i]
        c_row = cumuls[i]
        start = c * tok
        seg_col = segments(off_ref, start + rows[:, :1])
        seg_row = segments(off_ref, start + columns[:1, :])
        before = jnp.int32(0)
        last = jnp.int32(0)
        for j in range(off_ref.shape[0] - 1):
            before = before + (off_ref[j] <= start - 1).astype(jnp.int32)
            last = last + (off_ref[j] <= start + tok - 1).astype(jnp.int32)
        c_last = c_row[:, tok - 1 : tok]
        together = (seg_col == seg_row) & (rows >= columns)
        ratio = jnp.where(together, jnp.exp(jnp.where(together, c_col - c_row, 0.0)), 0.0)
        start_col = jnp.where(seg_col == before, jnp.exp(c_col), 0.0)
        end_col = jnp.where(seg_col == last, jnp.exp(c_last - c_col), 0.0)
        whole = jnp.where(last == before, jnp.exp(c_last), 0.0)
        out.append((rates[i], b_col, ratio, start_col, end_col, whole))
    return out


def inverses(lowers):
    size = lowers[0].shape[0]
    rows, columns = iotas(size, size)
    identity = (rows == columns).astype(F32)
    block = min(16, size)
    near = (rows // block) == (columns // block)
    powers = [jnp.where(near, -m, 0.0) for m in lowers]
    results = [identity + p for p in powers]
    split = [halves(p) for p in powers]
    powers = [mm(s, s) for s in split]
    reach = 2
    while reach < block:
        split = [halves(p) for p in powers]
        more = reach * 2 < block
        both = []
        for r, s in zip(results, split):
            left = halves(r)
            if more:
                left = cat([left, s], 0)
            both.append(mm(left, s))
        results = [r + b[:size] for r, b in zip(results, both)]
        if more:
            powers = [b[size:] for b in both]
        reach *= 2
    while block < size:
        across = ((rows // (2 * block)) == (columns // (2 * block))) & (
            (rows // block) > (columns // block)
        )
        split = [halves(r) for r in results]
        middle = [mm(halves(jnp.where(across, m, 0.0)), s) for m, s in zip(lowers, split)]
        results = [r - mm(s, halves(m)) for r, s, m in zip(results, split, middle)]
        block *= 2
    return results


def chunks_of(plan, place, mate):
    return [mate + plan.mates * plan.ring.source(place, d) for d in range(plan.hv)]


def prepare_kernel(plan, off_ref, place_ref, mate_ref, *refs):
    in_refs, (link_ref, split_ref, kept_ref) = refs[: plan.hv], refs[plan.hv :]
    tok = plan.tok
    rows, columns = iotas(tok, tok)
    key_rows, key_columns = iotas(DK, DK)
    identity = (key_rows == key_columns).astype(F32)
    mine = range(plan.hv)
    chunks = chunks_of(plan, place_ref[0], mate_ref[0])
    scales = scalings(plan, off_ref, chunks, [r[plan.aux_at :] for r in in_refs])
    qu = [unit(in_refs[m][:tok].astype(F32)) for m in mine]
    ku = [unit(in_refs[m][tok : 2 * tok].astype(F32)) for m in mine]
    qn, kn = [x[0] for x in qu], [x[0] for x in ku]
    kp = [halves(x) for x in kn]
    qp = [halves(x) for x in qn]
    dots = [mm(cat([q, k], 0), k, 1, 1) for q, k in zip(qp, kp)]
    strict = rows > columns
    lowers = [jnp.where(strict, s[1] * d[tok:] * s[2], 0.0) for s, d in zip(scales, dots)]
    scores = [d[:tok] * s[2] for s, d in zip(scales, dots)]
    inv = inverses(lowers)
    rated = [halves(x * s[0]) for x, s in zip(inv, scales)]
    w = [mm(x, halves(s[3] * k)) for x, s, k in zip(rated, scales, kn)]
    values = [in_refs[m][plan.v_at : plan.aux_at] for m in mine]
    u = [
        dot(jnp.concatenate([v, v], axis=1), jnp.concatenate(x, axis=1), 1, 1)
        for v, x in zip(values, rated)
    ]
    wp = [halves(x) for x in w]
    up = [halves(x) for x in u]
    ap = [halves(x) for x in scores]
    ke = [halves(s[4] * k) for s, k in zip(scales, kn)]
    for m in mine:
        link_ref[m, 0] = scales[m][5] * identity - mm(wp[m], ke[m], 0, 0)
        link_ref[m, 1] = mm(up[m], ke[m])
    lanes = lax.broadcasted_iota(jnp.int32, (tok, DK), 1)
    for m in mine:
        _, b_col, ratio, start_col, end_col, whole = scales[m]
        reads = start_col * qn[m] - mm(ap[m], wp[m])
        for i, pair in enumerate((halves(inv[m]), ap[m], wp[m], halves(reads), kp[m], qp[m], ke[m])):
            split_ref[m, i, 0], split_ref[m, i, 1] = pair
        kept_ref[m, RATIO] = ratio
        kept_ref[m, WRITES] = u[m]
        kept_ref[m, LOCAL] = mm(up[m], ap[m], 1, 1)
        columns_of = jnp.zeros((tok, DK), F32)
        for i, x in enumerate((b_col, start_col, end_col, qu[m][1], ku[m][1], whole)):
            columns_of = jnp.where(lanes == i, x, columns_of)
        kept_ref[m, COLUMNS] = columns_of


def get(split_ref, m, i):
    return split_ref[m, i, 0], split_ref[m, i, 1]


def lay_out(plan, place, mate, refs, all_ref):
    for d, ref in enumerate(refs):
        for m in range(plan.hv):
            all_ref[lax.rem(mate + d, plan.mates), plan.ring.source(place, m)] = ref[m]


def scan_kernel(plan, place_ref, mate_ref, *refs):
    s, hv = plan.mates, plan.hv
    links, split_ref, kept_ref, state_ref = refs[:s], refs[s], refs[s + 1], refs[s + 2]
    outs, (all_ref, states_ref) = refs[s + 3 : -2], refs[-2:]
    place, mate = place_ref[0], mate_ref[0]
    lay_out(plan, place, mate, links, all_ref)
    state = jnp.zeros((DV, DK), F32)
    for c in range(plan.n):
        states_ref[c] = state
        if c < plan.n - 1:
            link = all_ref.at[c % s, c // s]
            state = link[1] + mm(halves(state), halves(link[0]))
    cores = []
    for m, c in enumerate(chunks_of(plan, place, mate)):
        state = states_ref[c]
        state_ref[m] = state
        core = kept_ref[m, LOCAL] + mm(halves(state), get(split_ref, m, READS), 1, 1)
        cores.append(core.astype(BF16))
    for d in range(hv):
        for k in range(hv):
            outs[d][k] = cores[plan.ring.seen(d, k)]


def state_cotangent_kernel(plan, split_ref, *refs):
    for m in range(plan.hv):
        refs[-1][m] = mm(d_out(refs[m]), get(split_ref, m, READS))


def d_out(ref):
    return ref[:DV], ref[DV:]


def backward_kernel(plan, place_ref, mate_ref, *refs):
    s, n, tok, hv = plan.mates, plan.n, plan.tok, plan.hv
    links, backs, refs = refs[:s], refs[s : 2 * s], refs[2 * s :]
    in_refs, d_refs = refs[:hv], refs[hv : 2 * hv]
    split_ref, kept_ref, state_ref = refs[2 * hv : 2 * hv + 3]
    outs, (links_ref, backs_ref, cots_ref) = refs[2 * hv + 3 : -3], refs[-3:]
    outs = [outs[plan.ring.seen(m, 0)] for m in range(hv)]
    place, mate = place_ref[0], mate_ref[0]
    lay_out(plan, place, mate, links, links_ref)
    lay_out(plan, place, mate, backs, backs_ref)
    d_state = jnp.zeros((DV, DK), F32)
    for c in reversed(range(n)):
        cots_ref[c] = d_state
        if c:
            d_state = backs_ref[c % s, c // s] + mm(
                halves(d_state), halves(links_ref[c % s, c // s, 0]), 1, 1
            )
    rows, columns = iotas(tok, tok)
    strict = rows > columns
    upto = (rows >= columns).astype(BF16)
    mine = range(hv)
    chunks = chunks_of(plan, place, mate)
    scales = []
    for m in mine:
        held = kept_ref[m, COLUMNS]
        columns_of = [held[:, i : i + 1] for i in range(SCALES)]
        rate = jnp.sum(in_refs[m][plan.aux_at :][0:3].astype(F32), axis=0, keepdims=True)
        scales.append([rate] + columns_of[:-1] + [columns_of[-1][:1]])
    qp = [get(split_ref, m, QUERIES) for m in mine]
    kp = [get(split_ref, m, KEYS) for m in mine]
    ke = [get(split_ref, m, ENDS) for m in mine]
    whole_of = lambda pair: pair[0].astype(F32) + pair[1].astype(F32)
    do = [d_out(r) for r in d_refs]
    s0 = [state_ref[m] for m in mine]
    ds = [cots_ref[c] for c in chunks]
    s0p = [halves(x) for x in s0]
    dsp = [halves(x) for x in ds]
    pseudo = [kept_ref[m, WRITES] - mm(s0p[m], get(split_ref, m, FROM_STATE), 1, 1) for m in mine]
    pp = [halves(x) for x in pseudo]
    dp = [mm(do[m], get(split_ref, m, SCORES)) + mm(dsp[m], ke[m], 1, 1) for m in mine]
    dr = [mm(halves(dp[m]), get(split_ref, m, INVERSE)) for m in mine]
    drp = [halves(x) for x in dr]
    big = [mm(cat([o, r], 1), cat([p, s], 1), 0, 0) for o, r, p, s in zip(do, drp, pp, s0p)]
    pds = [mm(p, d, 0, 0) for p, d in zip(pp, dsp)]
    da = [big[m][:tok, :tok] * kept_ref[m, RATIO] for m in mine]
    dm = [jnp.where(strict, -big[m][tok:, :tok] * kept_ref[m, RATIO], 0.0) for m in mine]
    dap = [halves(x) for x in da]
    dmp = [halves(x) for x in dm]
    dbm = [halves(s[1] * x) for s, x in zip(scales, dm)]
    by_row = [mm(cat([x, y], 0), k) for x, y, k in zip(dap, dmp, kp)]
    by_column = [
        mm(cat([x, y], 0), cat([q, k], 0), 0, 0) for x, y, q, k in zip(dap, dbm, qp, kp)
    ]
    sums = []
    for m in mine:
        _, b_col, start_col, end_col, q_scale, k_scale, whole = scales[m]
        qn, kn = whole_of(qp[m]), whole_of(kp[m])
        out = outs[m]
        dqn = by_row[m][:tok] + start_col * big[m][:tok, tok:]
        erase = by_row[m][tok:] - start_col * big[m][tok:, tok:]
        ends = end_col * pds[m]
        write = by_column[m] + ends
        dkn = b_col * erase + write
        s_q = jnp.sum(qn * dqn, axis=1, keepdims=True)
        s_e = jnp.sum(kn * erase, axis=1, keepdims=True)
        s_w = jnp.sum(kn * write, axis=1, keepdims=True)
        total = jnp.sum(jnp.sum(kn * ends, axis=1, keepdims=True), axis=0, keepdims=True)
        both = jnp.sum(jnp.sum(s0[m] * ds[m], axis=1, keepdims=True), axis=0, keepdims=True)
        out[:tok] = (q_scale * (dqn - qn * s_q)).astype(BF16)
        out[tok : 2 * tok] = (k_scale * (dkn - kn * (b_col * s_e + s_w))).astype(BF16)
        out[plan.v_at : plan.aux_at] = (scales[m][0] * dr[m]).astype(BF16)
        sums.append((s_e, s_q + b_col * s_e - s_w, total + whole * both))
    turned = to_rows([s[0] for s in sums] + [s[1] for s in sums], tok)
    for m in mine:
        values = in_refs[m][plan.v_at : plan.aux_at].astype(F32)
        d_rate = turned[m] + jnp.sum(dr[m] * values, axis=0, keepdims=True)
        parts = dot(aux_rows([turned[plan.hv + m]], tok), upto, 1, 0)
        d_decay = parts[0:1] + parts[1:2] + parts[2:3] + sums[m][2]
        outs[m][plan.aux_at :] = aux_rows([d_rate, d_decay], tok)


def gather_rows(head, pieces, all_ref):
    rows, ring = pieces[0].shape[0], Ring(len(pieces))
    for d, piece in zip(ring.far_first(), pieces):
        at = ring.source(head, d) * rows
        all_ref[pl.ds(pl.multiple_of(at, rows), rows), :] = piece[...]


def cotangent_kernel(plan, parts, head_ref, place_ref, *refs):
    pieces, w_ref, outs, (all_ref, core_ref) = refs[:parts], refs[parts], refs[parts + 1 : -2], refs[-2:]
    gather_rows(head_ref[0], pieces, all_ref)
    high, low = halves(dot(w_ref[...], all_ref[...], 1, 1))
    for m in range(plan.hv):
        core_ref[m, :DV] = high[m * DV : (m + 1) * DV]
        core_ref[m, DV:] = low[m * DV : (m + 1) * DV]
    hand_out(plan, place_ref[0], core_ref, outs)


def turn_kernel(plan, parts, head_ref, place_ref, *refs):
    pieces, outs, (all_ref, turned_ref) = refs[:parts], refs[parts:-2], refs[-2:]
    gather_rows(head_ref[0], pieces, all_ref)
    share = turned_ref.shape[1]
    for m in range(plan.hv):
        part = all_ref[:, m * share : (m + 1) * share].astype(F32)
        turned_ref[m] = jnp.transpose(part).astype(BF16)
    hand_out(plan, place_ref[0], turned_ref, outs)


def project_kernel(plan, parts, head_ref, place_ref, *refs):
    mixed_refs, w_ref, outs, (all_ref, total_ref) = (
        refs[: plan.hv],
        refs[plan.hv],
        refs[plan.hv + 1 : -2],
        refs[-2:],
    )
    for d, ref in enumerate(mixed_refs):
        all_ref[plan.ring.source(place_ref[0], d)] = ref[0]
    mixed = all_ref[...].reshape(plan.hv * DV, plan.tok)
    total_ref[...] = dot(mixed, w_ref[...], 0, 0)
    rows, ring = outs[0].shape[0], Ring(parts)
    for d in range(parts):
        at = ring.target(head_ref[0], d) * rows
        block = total_ref[pl.ds(pl.multiple_of(at, rows), rows), :]
        outs[d][...] = block.astype(outs[d].dtype)


def weight_kernel(plan, place_ref, mate_ref, *refs):
    hv = plan.hv
    turned, mixed_refs, outs, all_ref = refs[:hv], refs[hv : 2 * hv], refs[2 * hv : -1], refs[-1]
    for d, ref in enumerate(mixed_refs):
        head = plan.ring.source(place_ref[0], d)
        for k in range(hv):
            all_ref[k, head] = ref[k]
    share = outs[0].shape[0]
    for d, out_ref in enumerate(outs):
        at = lax.rem(mate_ref[0] + plan.mates - d, plan.mates) * share
        at = pl.multiple_of(at, share)
        total = None
        for k in range(hv):
            mixed = all_ref[k].reshape(hv * DV, plan.tok)
            part = dot(turned[k][pl.ds(at, share), :], mixed, 1, 1)
            total = part if total is None else total + part
        out_ref[...] = total


def finish_kernel(plan, place_ref, *refs):
    pieces, (q_ref, k_ref, v_ref, rate_ref, decay_ref, in_ref) = refs[: plan.hv], refs[plan.hv :]
    tok = plan.tok
    for d, ref in enumerate(pieces):
        in_ref[plan.ring.source(place_ref[0], d)] = ref[...]
    for kh in range(plan.hk):
        mine = [h for h in range(plan.hv) if plan.key_head(h) == kh]
        for ref, at in ((q_ref, 0), (k_ref, tok)):
            total = in_ref[mine[0], at : at + tok].astype(F32)
            for h in mine[1:]:
                total = total + in_ref[h, at : at + tok].astype(F32)
            ref[:, kh * DK : (kh + 1) * DK] = total
    for h in range(plan.hv):
        v_ref[:, h * DV : (h + 1) * DV] = jnp.transpose(
            in_ref[h, plan.v_at : plan.aux_at].astype(F32)
        )
        aux = in_ref[h, plan.aux_at :].astype(F32)
        rate_ref[h : h + 1, :] = aux[0:1] + aux[1:2] + aux[2:3]
        decay_ref[h : h + 1, :] = aux[3:4] + aux[4:5] + aux[5:6]


def after(x, y):
    return lax.optimization_barrier((x, y))[0]


def per_device(
    queries, key_vectors, value_rows, write_rate, log_decay, doc_offsets, out_weight, grad_out
):
    n, parts = lax.axis_size("ctx"), lax.axis_size("head")
    tok, hv = queries.shape[0], write_rate.shape[0]
    hk, model = queries.shape[1] // DK, grad_out.shape[1]
    plan = Plan(n, tok, hv, hk)
    s = plan.mates
    index = lax.axis_index("ctx").astype(jnp.int32)
    place, mate = (index // s).reshape(1), (index % s).reshape(1)
    head = lax.axis_index("head").astype(jnp.int32).reshape(1)

    def across_heads(pieces):
        moved = [lax.ppermute(pieces[d], "head", Ring(parts).pairs(d)) for d in range(1, parts)]
        return [pieces[0]] + moved

    vmem = lambda dtype, *shape: pltpu.VMEM(shape, dtype)

    packed = call(
        partial(pack_kernel, plan),
        [arr(BF16, plan.rows, DK)] * hv,
        smem=(0,),
        scratch=[vmem(BF16, hv, plan.rows, DK)],
        fetch=range(1, 6),
    )(place, queries, key_vectors, value_rows, write_rate, log_decay)
    got = plan.exchange(packed)
    rows = across_heads([grad_out] * parts)
    rows = [rows[d] for d in Ring(parts).far_first()]

    link, split, kept = call(
        partial(prepare_kernel, plan),
        (
            arr(F32, hv, 2, DK, DK),
            arr(BF16, hv, SPLIT, 2, tok, DK),
            arr(F32, hv, KEPT, tok, DK),
        ),
        smem=(0, 1, 2),
        fetch=(0,),
        flops=0,
    )(doc_offsets, place, mate, *got)
    links = [link] + [plan.from_mate(link, d) for d in range(1, s)]

    d_core = call(
        partial(cotangent_kernel, plan, parts),
        [arr(BF16, 2 * DV, tok)] * hv,
        smem=(0, 1),
        scratch=[vmem(BF16, tok, model), vmem(BF16, hv, 2 * DV, tok)],
        flops=30_000_000_000,
    )(head, place, *rows, after(out_weight, link))
    kept = after(kept, d_core[0])
    d_core = plan.exchange(d_core)

    states, *mixed = call(
        partial(scan_kernel, plan),
        [arr(F32, hv, DV, DK)] + [arr(BF16, hv, DV, tok)] * hv,
        smem=(0, 1),
        scratch=[vmem(F32, s, hv, 2, DK, DK), vmem(F32, n, DV, DK)],
        flops=2_500_000_000,
    )(place, mate, *links, split, kept)
    turned = call(
        partial(turn_kernel, plan, parts),
        [arr(BF16, model // hv, tok)] * hv,
        smem=(0, 1),
        scratch=[vmem(BF16, tok, model), vmem(BF16, hv, model // hv, tok)],
        flops=1_000_000_000,
    )(head, place, *after(rows, states))
    mixed = plan.exchange(mixed)
    turned = plan.exchange(turned)
    back = call(
        partial(state_cotangent_kernel, plan), arr(F32, hv, DV, DK), flops=30_000_000_000
    )(split, *after(d_core, states))
    backs = [back] + [plan.from_mate(back, d) for d in range(1, s)]

    projected = call(
        partial(project_kernel, plan, parts),
        [arr(BF16 if d else F32, tok // parts, model) for d in range(parts)],
        smem=(0, 1),
        scratch=[vmem(BF16, hv, DV, tok), vmem(F32, tok, model)],
        flops=1_000_000_000,
    )(head, place, *mixed, out_weight)
    layer_parts = across_heads(projected)

    grads = call(
        partial(backward_kernel, plan),
        [arr(BF16, plan.rows, DK)] * hv,
        smem=(0, 1),
        scratch=[
            vmem(F32, s, hv, 2, DK, DK),
            vmem(F32, s, hv, DV, DK),
            vmem(F32, n, DV, DK),
        ],
        flops=6_000_000_000,
    )(place, mate, *links, *backs, *got, *d_core, split, kept, after(states, projected[1]))

    shares = call(
        partial(weight_kernel, plan),
        [arr(F32, model // n, hv * DV)] * s,
        smem=(0, 1),
        scratch=[vmem(BF16, hv, hv, DV, tok)],
        flops=1_000_000_000,
    )(place, mate, *turned, *mixed)
    grads = plan.exchange(after(grads, shares[0]))
    weight_grad = shares[0]
    for d in range(1, s):
        weight_grad = weight_grad + plan.from_mate(shares[d], d)

    layer_out = layer_parts[0]
    for part in layer_parts[:0:-1]:
        layer_out = layer_out + part.astype(F32)
    grads = after(grads, (layer_out, weight_grad))
    grad_q, grad_k, grad_v, grad_rate, grad_decay = call(
        partial(finish_kernel, plan),
        (
            arr(F32, tok, hk * DK),
            arr(F32, tok, hk * DK),
            arr(F32, tok, hv * DV),
            arr(F32, hv, tok),
            arr(F32, hv, tok),
        ),
        smem=(0,),
        scratch=[vmem(BF16, hv, plan.rows, DK)],
        flops=1_000_000_000,
        inside=False,
    )(place, *grads)
    return (layer_out, grad_q, grad_k, grad_v, grad_rate, grad_decay, weight_grad)


def solution(mesh):
    placed = (
        P("ctx", "head"),
        P("ctx", "head"),
        P("ctx", "head"),
        P("head", "ctx"),
        P("head", "ctx"),
        P(),
        P("head", None),
        P(("ctx", "head"), None),
    )
    return jax.shard_map(
        per_device,
        mesh=mesh,
        in_specs=placed,
        out_specs=(
            P(("ctx", "head"), None),
            P("ctx", "head"),
            P("ctx", "head"),
            P("ctx", "head"),
            P("head", "ctx"),
            P("head", "ctx"),
            P("ctx", "head"),
        ),
        check_vma=False,
    )
```

```python
import math
from functools import partial

import jax
import jax.numpy as jnp
from jax import lax
from jax.experimental import pallas as pl
from jax.experimental.pallas import tpu as pltpu
from jax.sharding import PartitionSpec as P

DK = 128
DV = 128
AUX = 16
INVERSE, SCORES, FROM_STATE, READS, KEYS, QUERIES, ENDS, SPLIT = range(8)
RATIO, WRITES, LOCAL, COLUMNS, KEPT = range(5)
SCALES = 6
EPS = 1e-06
F32 = jnp.float32
BF16 = jnp.bfloat16
SPARE_VMEM = 8 * 1024 * 1024


def dot(a, b, ca, cb):
    return lax.dot_general(a, b, (((ca,), (cb,)), ((), ())), preferred_element_type=F32)


def halves(x):
    high = x.astype(BF16)
    return high, (x - high.astype(F32)).astype(BF16)


def thirds(x):
    high = x.astype(BF16).astype(F32)
    middle = (x - high).astype(BF16).astype(F32)
    return high, middle, x - high - middle


def mm(a, b, ca=1, cb=0):
    left = jnp.concatenate([a[0], a[0], a[1]], axis=ca)
    right = jnp.concatenate([b[0], b[1], b[0]], axis=cb)
    return dot(left, right, ca, cb)


def cat(pairs, axis):
    return tuple(jnp.concatenate(parts, axis=axis) for parts in zip(*pairs))


def iotas(rows, columns):
    shape = (rows, columns)
    return lax.broadcasted_iota(jnp.int32, shape, 0), lax.broadcasted_iota(jnp.int32, shape, 1)


def call(kernel, outs, smem=(), scratch=(), flops=0, inside=True, fetch=()):
    if inside:
        outs = jax.tree.map(lambda o: pltpu.VMEM(o.shape, o.dtype), outs)
    scoped = SPARE_VMEM + sum(x.dtype.itemsize * math.prod(x.shape) for x in scratch)

    def run(*args):
        spec = lambda i: pl.BlockSpec(memory_space=pltpu.SMEM if i in smem else pltpu.VMEM)
        space = lambda i: pltpu.HBM if i in fetch else pltpu.VMEM
        hold = pltpu.with_memory_space_constraint
        return pl.pallas_call(
            kernel,
            out_shape=outs,
            in_specs=[spec(i) for i in range(len(args))],
            out_specs=jax.tree.map(lambda _: pl.BlockSpec(memory_space=pltpu.VMEM), outs),
            scratch_shapes=list(scratch),
            compiler_params=pltpu.CompilerParams(vmem_limit_bytes=scoped),
            cost_estimate=pl.CostEstimate(flops=flops, bytes_accessed=0, transcendentals=0),
        )(*(hold(x, space(i)) if i in fetch or i not in smem else x for i, x in enumerate(args)))

    return run


def arr(dtype, *shape):
    return jax.ShapeDtypeStruct(shape, dtype)


class Ring:
    def __init__(self, size):
        self.size = size
        self.paired = size & (size - 1) == 0

    def source(self, i, d):
        return i ^ d if self.paired else (i + d) % self.size

    def target(self, i, d):
        return i ^ d if self.paired else (i + self.size - d) % self.size

    def seen(self, d, k):
        return d ^ k if self.paired else (k - d) % self.size

    def far_first(self):
        return sorted(range(self.size), key=lambda d: d != self.size // 2)

    def pairs(self, d):
        return [(self.source(i, d), i) for i in range(self.size)]


class Plan:
    def __init__(self, n, tok, hv, hk):
        self.n, self.tok, self.hv, self.hk = n, tok, hv, hk
        self.mates = n // hv
        self.v_at = 2 * tok
        self.aux_at = 2 * tok + DV
        self.rows = self.aux_at + AUX
        self.ring = Ring(hv)

    def key_head(self, head):
        return head * self.hk // self.hv

    def exchange(self, pieces):
        s = self.mates
        moved = [pieces[0]]
        for d in range(1, self.hv):
            pairs = [(i * s + b, j * s + b) for i, j in self.ring.pairs(d) for b in range(s)]
            moved.append(lax.ppermute(pieces[d], "ctx", pairs))
        return moved

    def from_mate(self, x, d):
        s = self.mates
        pairs = [(i // s * s + (i + d) % s, i) for i in range(self.n)]
        return lax.ppermute(x, "ctx", pairs)


def aux_rows(rows, columns):
    row_ids = lax.broadcasted_iota(jnp.int32, (AUX, columns), 0)
    out = jnp.zeros((AUX, columns), F32)
    for i, part in enumerate(p for r in rows for p in thirds(r)):
        out = jnp.where(row_ids == i, part, out)
    return out.astype(BF16)


def pack_kernel(plan, place_ref, q_ref, k_ref, v_ref, rate_ref, decay_ref, *refs):
    outs, out_ref = refs[:-1], refs[-1]
    tok = plan.tok
    for h in range(plan.hv):
        kh = plan.key_head(h)
        out_ref[h, :tok] = q_ref[:, kh * DK : (kh + 1) * DK]
        out_ref[h, tok : 2 * tok] = k_ref[:, kh * DK : (kh + 1) * DK]
        turned = jnp.transpose(v_ref[:, h * DV : (h + 1) * DV].astype(F32))
        out_ref[h, plan.v_at : plan.aux_at] = turned.astype(BF16)
        rows = [rate_ref[h : h + 1, :], decay_ref[h : h + 1, :]]
        out_ref[h, plan.aux_at :] = aux_rows(rows, tok)
    hand_out(plan, place_ref[0], out_ref, outs)


def hand_out(plan, place, all_ref, outs):
    for d, ref in enumerate(outs):
        ref[...] = all_ref[plan.ring.target(place, d)]


def unit(x):
    scale = lax.rsqrt(jnp.sum(x * x, axis=1, keepdims=True) + EPS)
    return x * scale, scale


def segments(off_ref, positions):
    total = jnp.zeros(positions.shape, jnp.int32)
    for j in range(off_ref.shape[0] - 1):
        total = total + (off_ref[j] <= positions).astype(jnp.int32)
    return total


def to_columns(rows, tok):
    row_ids = lax.broadcasted_iota(jnp.int32, (tok, tok), 0)
    stacked = jnp.zeros((tok, tok), F32)
    for i, r in enumerate(rows):
        stacked = jnp.where(row_ids == i, r, stacked)
    turned = jnp.transpose(stacked)
    return [turned[:, i : i + 1] for i in range(len(rows))]


def to_rows(columns, tok):
    column_ids = lax.broadcasted_iota(jnp.int32, (tok, tok), 1)
    stacked = jnp.zeros((tok, tok), F32)
    for i, c in enumerate(columns):
        stacked = jnp.where(column_ids == i, c, stacked)
    turned = jnp.transpose(stacked)
    return [turned[i : i + 1, :] for i in range(len(columns))]


def scalings(plan, off_ref, chunks, auxes):
    tok = plan.tok
    rows, columns = iotas(tok, tok)
    upto = (rows <= columns).astype(BF16)
    sums = [dot(a, upto, 1, 0) for a in auxes]
    rates = [jnp.sum(a[0:3].astype(F32), axis=0, keepdims=True) for a in auxes]
    cumuls = [s[3:4] + s[4:5] + s[5:6] for s in sums]
    turned = to_columns(rates + cumuls, tok)
    out = []
    for i, c in enumerate(chunks):
        b_col, c_col = turned[i], turned[len(chunks) + i]
        c_row = cumuls[i]
        start = c * tok
        seg_col = segments(off_ref, start + rows[:, :1])
        seg_row = segments(off_ref, start + columns[:1, :])
        before = jnp.int32(0)
        last = jnp.int32(0)
        for j in range(off_ref.shape[0] - 1):
            before = before + (off_ref[j] <= start - 1).astype(jnp.int32)
            last = last + (off_ref[j] <= start + tok - 1).astype(jnp.int32)
        c_last = c_row[:, tok - 1 : tok]
        together = (seg_col == seg_row) & (rows >= columns)
        ratio = jnp.where(together, jnp.exp(jnp.where(together, c_col - c_row, 0.0)), 0.0)
        start_col = jnp.where(seg_col == before, jnp.exp(c_col), 0.0)
        end_col = jnp.where(seg_col == last, jnp.exp(c_last - c_col), 0.0)
        whole = jnp.where(last == before, jnp.exp(c_last), 0.0)
        out.append((rates[i], b_col, ratio, start_col, end_col, whole))
    return out


def inverses(lowers):
    size = lowers[0].shape[0]
    rows, columns = iotas(size, size)
    identity = (rows == columns).astype(F32)
    block = min(16, size)
    near = (rows // block) == (columns // block)
    powers = [jnp.where(near, -m, 0.0) for m in lowers]
    results = [identity + p for p in powers]
    split = [halves(p) for p in powers]
    powers = [mm(s, s) for s in split]
    reach = 2
    while reach < block:
        split = [halves(p) for p in powers]
        more = reach * 2 < block
        both = []
        for r, s in zip(results, split):
            left = halves(r)
            if more:
                left = cat([left, s], 0)
            both.append(mm(left, s))
        results = [r + b[:size] for r, b in zip(results, both)]
        if more:
            powers = [b[size:] for b in both]
        reach *= 2
    while block < size:
        across = ((rows // (2 * block)) == (columns // (2 * block))) & (
            (rows // block) > (columns // block)
        )
        split = [halves(r) for r in results]
        middle = [mm(halves(jnp.where(across, m, 0.0)), s) for m, s in zip(lowers, split)]
        results = [r - mm(s, halves(m)) for r, s, m in zip(results, split, middle)]
        block *= 2
    return results


def chunks_of(plan, place, mate):
    return [mate + plan.mates * plan.ring.source(place, d) for d in range(plan.hv)]


def prepare_kernel(plan, off_ref, place_ref, mate_ref, *refs):
    in_refs, (link_ref, split_ref, kept_ref) = refs[: plan.hv], refs[plan.hv :]
    tok = plan.tok
    rows, columns = iotas(tok, tok)
    key_rows, key_columns = iotas(DK, DK)
    identity = (key_rows == key_columns).astype(F32)
    mine = range(plan.hv)
    chunks = chunks_of(plan, place_ref[0], mate_ref[0])
    scales = scalings(plan, off_ref, chunks, [r[plan.aux_at :] for r in in_refs])
    qu = [unit(in_refs[m][:tok].astype(F32)) for m in mine]
    ku = [unit(in_refs[m][tok : 2 * tok].astype(F32)) for m in mine]
    qn, kn = [x[0] for x in qu], [x[0] for x in ku]
    kp = [halves(x) for x in kn]
    qp = [halves(x) for x in qn]
    dots = [mm(cat([q, k], 0), k, 1, 1) for q, k in zip(qp, kp)]
    strict = rows > columns
    lowers = [jnp.where(strict, s[1] * d[tok:] * s[2], 0.0) for s, d in zip(scales, dots)]
    scores = [d[:tok] * s[2] for s, d in zip(scales, dots)]
    inv = inverses(lowers)
    rated = [halves(x * s[0]) for x, s in zip(inv, scales)]
    w = [mm(x, halves(s[3] * k)) for x, s, k in zip(rated, scales, kn)]
    values = [in_refs[m][plan.v_at : plan.aux_at] for m in mine]
    u = [
        dot(jnp.concatenate([v, v], axis=1), jnp.concatenate(x, axis=1), 1, 1)
        for v, x in zip(values, rated)
    ]
    wp = [halves(x) for x in w]
    up = [halves(x) for x in u]
    ap = [halves(x) for x in scores]
    ke = [halves(s[4] * k) for s, k in zip(scales, kn)]
    for m in mine:
        link_ref[m, 0] = scales[m][5] * identity - mm(wp[m], ke[m], 0, 0)
        link_ref[m, 1] = mm(up[m], ke[m])
    lanes = lax.broadcasted_iota(jnp.int32, (tok, DK), 1)
    for m in mine:
        _, b_col, ratio, start_col, end_col, whole = scales[m]
        reads = start_col * qn[m] - mm(ap[m], wp[m])
        for i, pair in enumerate((halves(inv[m]), ap[m], wp[m], halves(reads), kp[m], qp[m], ke[m])):
            split_ref[m, i, 0], split_ref[m, i, 1] = pair
        kept_ref[m, RATIO] = ratio
        kept_ref[m, WRITES] = u[m]
        kept_ref[m, LOCAL] = mm(up[m], ap[m], 1, 1)
        columns_of = jnp.zeros((tok, DK), F32)
        for i, x in enumerate((b_col, start_col, end_col, qu[m][1], ku[m][1], whole)):
            columns_of = jnp.where(lanes == i, x, columns_of)
        kept_ref[m, COLUMNS] = columns_of


def get(split_ref, m, i):
    return split_ref[m, i, 0], split_ref[m, i, 1]


def lay_out(plan, place, mate, refs, all_ref):
    for d, ref in enumerate(refs):
        for m in range(plan.hv):
            all_ref[lax.rem(mate + d, plan.mates), plan.ring.source(place, m)] = ref[m]


def scan_kernel(plan, place_ref, mate_ref, *refs):
    s, hv = plan.mates, plan.hv
    links, split_ref, kept_ref, state_ref = refs[:s], refs[s], refs[s + 1], refs[s + 2]
    outs, (all_ref, states_ref) = refs[s + 3 : -2], refs[-2:]
    place, mate = place_ref[0], mate_ref[0]
    lay_out(plan, place, mate, links, all_ref)
    state = jnp.zeros((DV, DK), F32)
    for c in range(plan.n):
        states_ref[c] = state
        if c < plan.n - 1:
            link = all_ref.at[c % s, c // s]
            state = link[1] + mm(halves(state), halves(link[0]))
    cores = []
    for m, c in enumerate(chunks_of(plan, place, mate)):
        state = states_ref[c]
        state_ref[m] = state
        core = kept_ref[m, LOCAL] + mm(halves(state), get(split_ref, m, READS), 1, 1)
        cores.append(core.astype(BF16))
    for d in range(hv):
        for k in range(hv):
            outs[d][k] = cores[plan.ring.seen(d, k)]


def state_cotangent_kernel(plan, split_ref, *refs):
    for m in range(plan.hv):
        refs[-1][m] = mm(d_out(refs[m]), get(split_ref, m, READS))


def d_out(ref):
    return ref[:DV], ref[DV:]


def backward_kernel(plan, place_ref, mate_ref, *refs):
    s, n, tok, hv = plan.mates, plan.n, plan.tok, plan.hv
    links, backs, refs = refs[:s], refs[s : 2 * s], refs[2 * s :]
    in_refs, d_refs = refs[:hv], refs[hv : 2 * hv]
    split_ref, kept_ref, state_ref = refs[2 * hv : 2 * hv + 3]
    outs, (links_ref, backs_ref, cots_ref) = refs[2 * hv + 3 : -3], refs[-3:]
    outs = [outs[plan.ring.seen(m, 0)] for m in range(hv)]
    place, mate = place_ref[0], mate_ref[0]
    lay_out(plan, place, mate, links, links_ref)
    lay_out(plan, place, mate, backs, backs_ref)
    d_state = jnp.zeros((DV, DK), F32)
    for c in reversed(range(n)):
        cots_ref[c] = d_state
        if c:
            d_state = backs_ref[c % s, c // s] + mm(
                halves(d_state), halves(links_ref[c % s, c // s, 0]), 1, 1
            )
    rows, columns = iotas(tok, tok)
    strict = rows > columns
    upto = (rows >= columns).astype(BF16)
    mine = range(hv)
    chunks = chunks_of(plan, place, mate)
    scales = []
    for m in mine:
        held = kept_ref[m, COLUMNS]
        columns_of = [held[:, i : i + 1] for i in range(SCALES)]
        rate = jnp.sum(in_refs[m][plan.aux_at :][0:3].astype(F32), axis=0, keepdims=True)
        scales.append([rate] + columns_of[:-1] + [columns_of[-1][:1]])
    qp = [get(split_ref, m, QUERIES) for m in mine]
    kp = [get(split_ref, m, KEYS) for m in mine]
    ke = [get(split_ref, m, ENDS) for m in mine]
    whole_of = lambda pair: pair[0].astype(F32) + pair[1].astype(F32)
    do = [d_out(r) for r in d_refs]
    s0 = [state_ref[m] for m in mine]
    ds = [cots_ref[c] for c in chunks]
    s0p = [halves(x) for x in s0]
    dsp = [halves(x) for x in ds]
    pseudo = [kept_ref[m, WRITES] - mm(s0p[m], get(split_ref, m, FROM_STATE), 1, 1) for m in mine]
    pp = [halves(x) for x in pseudo]
    dp = [mm(do[m], get(split_ref, m, SCORES)) + mm(dsp[m], ke[m], 1, 1) for m in mine]
    dr = [mm(halves(dp[m]), get(split_ref, m, INVERSE)) for m in mine]
    drp = [halves(x) for x in dr]
    big = [mm(cat([o, r], 1), cat([p, s], 1), 0, 0) for o, r, p, s in zip(do, drp, pp, s0p)]
    pds = [mm(p, d, 0, 0) for p, d in zip(pp, dsp)]
    da = [big[m][:tok, :tok] * kept_ref[m, RATIO] for m in mine]
    dm = [jnp.where(strict, -big[m][tok:, :tok] * kept_ref[m, RATIO], 0.0) for m in mine]
    dap = [halves(x) for x in da]
    dmp = [halves(x) for x in dm]
    dbm = [halves(s[1] * x) for s, x in zip(scales, dm)]
    by_row = [mm(cat([x, y], 0), k) for x, y, k in zip(dap, dmp, kp)]
    by_column = [
        mm(cat([x, y], 0), cat([q, k], 0), 0, 0) for x, y, q, k in zip(dap, dbm, qp, kp)
    ]
    sums = []
    for m in mine:
        _, b_col, start_col, end_col, q_scale, k_scale, whole = scales[m]
        qn, kn = whole_of(qp[m]), whole_of(kp[m])
        out = outs[m]
        dqn = by_row[m][:tok] + start_col * big[m][:tok, tok:]
        erase = by_row[m][tok:] - start_col * big[m][tok:, tok:]
        ends = end_col * pds[m]
        write = by_column[m] + ends
        dkn = b_col * erase + write
        s_q = jnp.sum(qn * dqn, axis=1, keepdims=True)
        s_e = jnp.sum(kn * erase, axis=1, keepdims=True)
        s_w = jnp.sum(kn * write, axis=1, keepdims=True)
        total = jnp.sum(jnp.sum(kn * ends, axis=1, keepdims=True), axis=0, keepdims=True)
        both = jnp.sum(jnp.sum(s0[m] * ds[m], axis=1, keepdims=True), axis=0, keepdims=True)
        out[:tok] = (q_scale * (dqn - qn * s_q)).astype(BF16)
        out[tok : 2 * tok] = (k_scale * (dkn - kn * (b_col * s_e + s_w))).astype(BF16)
        out[plan.v_at : plan.aux_at] = (scales[m][0] * dr[m]).astype(BF16)
        sums.append((s_e, s_q + b_col * s_e - s_w, total + whole * both))
    turned = to_rows([s[0] for s in sums] + [s[1] for s in sums], tok)
    for m in mine:
        values = in_refs[m][plan.v_at : plan.aux_at].astype(F32)
        d_rate = turned[m] + jnp.sum(dr[m] * values, axis=0, keepdims=True)
        parts = dot(aux_rows([turned[plan.hv + m]], tok), upto, 1, 0)
        d_decay = parts[0:1] + parts[1:2] + parts[2:3] + sums[m][2]
        outs[m][plan.aux_at :] = aux_rows([d_rate, d_decay], tok)


def gather_rows(head, pieces, all_ref):
    rows, ring = pieces[0].shape[0], Ring(len(pieces))
    for d, piece in zip(ring.far_first(), pieces):
        at = ring.source(head, d) * rows
        all_ref[pl.ds(pl.multiple_of(at, rows), rows), :] = piece[...]


def cotangent_kernel(plan, parts, head_ref, place_ref, *refs):
    pieces, w_ref, outs, (all_ref, core_ref) = refs[:parts], refs[parts], refs[parts + 1 : -2], refs[-2:]
    gather_rows(head_ref[0], pieces, all_ref)
    high, low = halves(dot(w_ref[...], all_ref[...], 1, 1))
    for m in range(plan.hv):
        core_ref[m, :DV] = high[m * DV : (m + 1) * DV]
        core_ref[m, DV:] = low[m * DV : (m + 1) * DV]
    hand_out(plan, place_ref[0], core_ref, outs)


def turn_kernel(plan, parts, head_ref, place_ref, *refs):
    pieces, outs, (all_ref, turned_ref) = refs[:parts], refs[parts:-2], refs[-2:]
    gather_rows(head_ref[0], pieces, all_ref)
    share = turned_ref.shape[1]
    for m in range(plan.hv):
        part = all_ref[:, m * share : (m + 1) * share].astype(F32)
        turned_ref[m] = jnp.transpose(part).astype(BF16)
    hand_out(plan, place_ref[0], turned_ref, outs)


def project_kernel(plan, parts, head_ref, place_ref, *refs):
    mixed_refs, w_ref, outs, (all_ref, total_ref) = (
        refs[: plan.hv],
        refs[plan.hv],
        refs[plan.hv + 1 : -2],
        refs[-2:],
    )
    for d, ref in enumerate(mixed_refs):
        all_ref[plan.ring.source(place_ref[0], d)] = ref[0]
    mixed = all_ref[...].reshape(plan.hv * DV, plan.tok)
    total_ref[...] = dot(mixed, w_ref[...], 0, 0)
    rows, ring = outs[0].shape[0], Ring(parts)
    for d in range(parts):
        at = ring.target(head_ref[0], d) * rows
        block = total_ref[pl.ds(pl.multiple_of(at, rows), rows), :]
        outs[d][...] = block.astype(outs[d].dtype)


def weight_kernel(plan, place_ref, mate_ref, *refs):
    hv = plan.hv
    turned, mixed_refs, outs, all_ref = refs[:hv], refs[hv : 2 * hv], refs[2 * hv : -1], refs[-1]
    for d, ref in enumerate(mixed_refs):
        head = plan.ring.source(place_ref[0], d)
        for k in range(hv):
            all_ref[k, head] = ref[k]
    share = outs[0].shape[0]
    for d, out_ref in enumerate(outs):
        at = lax.rem(mate_ref[0] + plan.mates - d, plan.mates) * share
        at = pl.multiple_of(at, share)
        total = None
        for k in range(hv):
            mixed = all_ref[k].reshape(hv * DV, plan.tok)
            part = dot(turned[k][pl.ds(at, share), :], mixed, 1, 1)
            total = part if total is None else total + part
        out_ref[...] = total


def finish_kernel(plan, place_ref, *refs):
    pieces, (q_ref, k_ref, v_ref, rate_ref, decay_ref, in_ref) = refs[: plan.hv], refs[plan.hv :]
    tok = plan.tok
    for d, ref in enumerate(reversed(pieces)):
        in_ref[plan.ring.source(place_ref[0], d)] = ref[...]
    for kh in range(plan.hk):
        mine = [h for h in range(plan.hv) if plan.key_head(h) == kh]
        for ref, at in ((q_ref, 0), (k_ref, tok)):
            total = in_ref[mine[0], at : at + tok].astype(F32)
            for h in mine[1:]:
                total = total + in_ref[h, at : at + tok].astype(F32)
            ref[:, kh * DK : (kh + 1) * DK] = total
    for h in range(plan.hv):
        v_ref[:, h * DV : (h + 1) * DV] = jnp.transpose(
            in_ref[h, plan.v_at : plan.aux_at].astype(F32)
        )
        aux = in_ref[h, plan.aux_at :].astype(F32)
        rate_ref[h : h + 1, :] = aux[0:1] + aux[1:2] + aux[2:3]
        decay_ref[h : h + 1, :] = aux[3:4] + aux[4:5] + aux[5:6]


def after(x, y):
    return lax.optimization_barrier((x, y))[0]


def per_device(
    queries, key_vectors, value_rows, write_rate, log_decay, doc_offsets, out_weight, grad_out
):
    n, parts = lax.axis_size("ctx"), lax.axis_size("head")
    tok, hv = queries.shape[0], write_rate.shape[0]
    hk, model = queries.shape[1] // DK, grad_out.shape[1]
    plan = Plan(n, tok, hv, hk)
    s = plan.mates
    index = lax.axis_index("ctx").astype(jnp.int32)
    place, mate = (index // s).reshape(1), (index % s).reshape(1)
    head = lax.axis_index("head").astype(jnp.int32).reshape(1)

    def across_heads(pieces):
        moved = [lax.ppermute(pieces[d], "head", Ring(parts).pairs(d)) for d in range(1, parts)]
        return [pieces[0]] + moved

    vmem = lambda dtype, *shape: pltpu.VMEM(shape, dtype)

    packed = call(
        partial(pack_kernel, plan),
        [arr(BF16, plan.rows, DK)] * hv,
        smem=(0,),
        scratch=[vmem(BF16, hv, plan.rows, DK)],
        fetch=range(1, 6),
    )(place, queries, key_vectors, value_rows, write_rate, log_decay)
    got = plan.exchange(packed)
    rows = across_heads([grad_out] * parts)
    rows = [rows[d] for d in Ring(parts).far_first()]

    link, split, kept = call(
        partial(prepare_kernel, plan),
        (
            arr(F32, hv, 2, DK, DK),
            arr(BF16, hv, SPLIT, 2, tok, DK),
            arr(F32, hv, KEPT, tok, DK),
        ),
        smem=(0, 1, 2),
        fetch=(0,),
        flops=20_000_000_000,
    )(doc_offsets, place, mate, *got)
    links = [link] + [plan.from_mate(link, d) for d in range(1, s)]

    d_core = call(
        partial(cotangent_kernel, plan, parts),
        [arr(BF16, 2 * DV, tok)] * hv,
        smem=(0, 1),
        scratch=[vmem(BF16, tok, model), vmem(BF16, hv, 2 * DV, tok)],
        flops=30_000_000_000,
    )(head, place, *rows, after(out_weight, link))
    kept = after(kept, d_core[0])
    d_core = plan.exchange(d_core)

    states, *mixed = call(
        partial(scan_kernel, plan),
        [arr(F32, hv, DV, DK)] + [arr(BF16, hv, DV, tok)] * hv,
        smem=(0, 1),
        scratch=[vmem(F32, s, hv, 2, DK, DK), vmem(F32, n, DV, DK)],
        flops=2_500_000_000,
    )(place, mate, *links, split, kept)
    turned = call(
        partial(turn_kernel, plan, parts),
        [arr(BF16, model // hv, tok)] * hv,
        smem=(0, 1),
        scratch=[vmem(BF16, tok, model), vmem(BF16, hv, model // hv, tok)],
        flops=1_000_000_000,
    )(head, place, *after(rows, states))
    mixed = plan.exchange(mixed)
    turned = plan.exchange(turned)
    back = call(
        partial(state_cotangent_kernel, plan), arr(F32, hv, DV, DK), flops=30_000_000_000
    )(split, *after(d_core, states))
    backs = [back] + [plan.from_mate(back, d) for d in range(1, s)]

    projected = call(
        partial(project_kernel, plan, parts),
        [arr(BF16 if d else F32, tok // parts, model) for d in range(parts)],
        smem=(0, 1),
        scratch=[vmem(BF16, hv, DV, tok), vmem(F32, tok, model)],
        flops=1_000_000_000,
    )(head, place, *mixed, out_weight)
    layer_parts = across_heads(projected)

    grads = call(
        partial(backward_kernel, plan),
        [arr(BF16, plan.rows, DK)] * hv,
        smem=(0, 1),
        scratch=[
            vmem(F32, s, hv, 2, DK, DK),
            vmem(F32, s, hv, DV, DK),
            vmem(F32, n, DV, DK),
        ],
        flops=6_000_000_000,
    )(place, mate, *links, *backs, *got, *d_core, split, kept, after(states, projected[1]))

    shares = call(
        partial(weight_kernel, plan),
        [arr(F32, model // n, hv * DV)] * s,
        smem=(0, 1),
        scratch=[vmem(BF16, hv, hv, DV, tok)],
        flops=1_000_000_000,
    )(place, mate, *turned, *mixed)
    grads = plan.exchange(after(grads, shares[0]))
    weight_grad = shares[0]
    for d in range(1, s):
        weight_grad = weight_grad + plan.from_mate(shares[d], d)

    layer_out = layer_parts[0]
    for part in layer_parts[:0:-1]:
        layer_out = layer_out + part.astype(F32)
    grads = after(grads[::-1], (layer_out, weight_grad))
    grad_q, grad_k, grad_v, grad_rate, grad_decay = call(
        partial(finish_kernel, plan),
        (
            arr(F32, tok, hk * DK),
            arr(F32, tok, hk * DK),
            arr(F32, tok, hv * DV),
            arr(F32, hv, tok),
            arr(F32, hv, tok),
        ),
        smem=(0,),
        scratch=[vmem(BF16, hv, plan.rows, DK)],
        flops=1_000_000_000,
        inside=False,
    )(place, *grads)
    return (layer_out, grad_q, grad_k, grad_v, grad_rate, grad_decay, weight_grad)


def solution(mesh):
    placed = (
        P("ctx", "head"),
        P("ctx", "head"),
        P("ctx", "head"),
        P("head", "ctx"),
        P("head", "ctx"),
        P(),
        P("head", None),
        P(("ctx", "head"), None),
    )
    return jax.shard_map(
        per_device,
        mesh=mesh,
        in_specs=placed,
        out_specs=(
            P(("ctx", "head"), None),
            P("ctx", "head"),
            P("ctx", "head"),
            P("ctx", "head"),
            P("head", "ctx"),
            P("head", "ctx"),
            P("ctx", "head"),
        ),
        check_vma=False,
    )
```
